32 devices in a mesh: fsdp: 16 (over z, y, core), tp: 2 (over x).
Axes of the slice: x: 2, y: 2, z: 4, core: 2. Of those that a mesh axis runs over, the one named last changes fastest.
Arguments:
- latents_in: bfloat16 [1024, 16, 1024], P('tp', 'fsdp'), may hold values from -6 to 6
- condition: bfloat16 [16, 1024], P('fsdp'), may hold values from -6 to 6
- grad_out: bfloat16 [1024, 16, 1024], P('tp', 'fsdp'), may hold values from -6 to 6
- qkv_weight: bfloat16 [1024, 3, 1024], P('fsdp', None, 'tp'), may hold values from -0.1875 to 0.1875
- proj_weight: bfloat16 [1024, 1024], P('tp', 'fsdp'), may hold values from -3 to 3
- up_weight: bfloat16 [1024, 4096], P('fsdp', 'tp'), may hold values from -0.1875 to 0.1875
- down_weight: bfloat16 [4096, 1024], P('tp', 'fsdp'), may hold values from -0.09375 to 0.09375
- ada_weight: bfloat16 [1024, 6, 1024], P('fsdp', None, 'tp'), may hold values from -0.1875 to 0.1875
- query_bias: bfloat16 [1024], P(('fsdp', 'tp')), may hold values from -1.75 to 1.75
- value_bias: bfloat16 [1024], P(('fsdp', 'tp')), may hold values from -1.75 to 1.75
- proj_bias: bfloat16 [1024], P(('fsdp', 'tp')), may hold values from -1.75 to 1.75
- up_bias: bfloat16 [4096], P(('fsdp', 'tp')), may hold values from -1.75 to 1.75
- down_bias: bfloat16 [1024], P(('fsdp', 'tp')), may hold values from -1.75 to 1.75
- ada_bias: bfloat16 [6, 1024], P(None, ('fsdp', 'tp')), may hold values from -1.75 to 1.75
Outputs:
- block_out: bfloat16 [1024, 16, 1024], P('tp', 'fsdp')
- input_grad: float32 [1024, 16, 1024], P('tp', 'fsdp')
- cond_grad: float32 [16, 1024], P('fsdp', 'tp')
- qkv_weight_grad: float32 [1024, 3, 1024], P('fsdp', None, 'tp')
- proj_weight_grad: float32 [1024, 1024], P('tp', 'fsdp')
- up_weight_grad: float32 [1024, 4096], P('fsdp', 'tp')
- down_weight_grad: float32 [4096, 1024], P('tp', 'fsdp')
- ada_weight_grad: float32 [1024, 6, 1024], P('fsdp', None, 'tp')
- query_bias_grad: float32 [1024], P(('fsdp', 'tp'))
- value_bias_grad: float32 [1024], P(('fsdp', 'tp'))
- proj_bias_grad: float32 [1024], P(('fsdp', 'tp'))
- up_bias_grad: float32 [4096], P(('fsdp', 'tp'))
- down_bias_grad: float32 [1024], P(('fsdp', 'tp'))
- ada_bias_grad: float32 [6, 1024], P(None, ('fsdp', 'tp'))
The draws below stay inside these ranges and needn't reach their ends.
All inputs are finite; a program needn't handle non-finite values.
Results may differ from the reference program's by a relative error of at most 0.019.
Values may be sent and summed in bfloat16 or wider, within the bound.
A program may use at most 192 MiB of HBM per device.

```python
import math
import jax
import jax.numpy as jnp
from jax import lax

D = 1024
FF = 4096
C = 1024
HD = 64
HEADS = 16
SEQ = 1024
LATENTS = 16


def level_of(rng, shape, cuts, smallest, largest):
    def one(axis_at, parts):
        heights = jax.random.uniform(jax.random.fold_in(jax.random.fold_in(rng, 6), axis_at), (parts,), jnp.float32, smallest / len(cuts), largest / len(cuts))
        return jnp.repeat(jnp.exp(heights), shape[axis_at] // parts).reshape((-1,) + (1,) * (len(shape) - axis_at - 1))

    level = one(*cuts[0])
    for cut in cuts[1:]:
        level = level * one(*cut)
    return level


def scatter_about(stream_key, dims, spread, most, pieces=(), held_as=jnp.bfloat16):
    values = jax.random.normal(stream_key, dims, jnp.float32) * spread
    if len(pieces) > 0:
        values = level_of(stream_key, dims, pieces, -0.22, 0.18) * values
    return jnp.clip(values, min=-most, max=most).astype(held_as)


def setup_inputs(seed: int = 0) -> dict:
    key_list = jax.random.split(jax.random.key(seed), 15)
    latents_in = scatter_about(key_list[0], (SEQ, LATENTS, D), 1.0, 6.0, ((0, 2), (1, 16)))
    condition = scatter_about(key_list[1], (LATENTS, C), 1.0, 6.0, ((0, 16),))
    grad_out = scatter_about(key_list[2], (SEQ, LATENTS, D), 1.0, 6.0, ((0, 2), (1, 16)))
    qkv_weight = scatter_about(key_list[3], (D, 3, D), D ** -0.5, 0.1875, ((0, 16), (2, 2)))
    proj_weight = scatter_about(key_list[4], (D, D), (max(4, 4 * D // SEQ)) ** -0.5, 3.0, ((0, 2), (1, 16)))
    up_weight = scatter_about(key_list[5], (D, FF), D ** -0.5, 0.1875, ((0, 16), (1, 2)))
    down_weight = scatter_about(key_list[6], (FF, D), FF ** -0.5, 0.09375, ((0, 2), (1, 16)))
    ada_weight = scatter_about(key_list[7], (C, 6, D), C ** -0.5, 0.1875, ((0, 16), (2, 2)))
    query_bias = scatter_about(key_list[8], (D,), 0.3, 1.75, ((0, 32),))
    value_bias = scatter_about(key_list[9], (D,), 0.3, 1.75, ((0, 32),))
    proj_bias = scatter_about(key_list[10], (D,), 0.3, 1.75, ((0, 32),))
    up_bias = scatter_about(key_list[11], (FF,), 0.3, 1.75, ((0, 32),))
    down_bias = scatter_about(key_list[12], (D,), 0.3, 1.75, ((0, 32),))
    ada_bias = scatter_about(key_list[13], (6, D), 0.3, 1.75, ((1, 32),))
    return dict(latents_in=latents_in, condition=condition, grad_out=grad_out, qkv_weight=qkv_weight, proj_weight=proj_weight, up_weight=up_weight, down_weight=down_weight, ada_weight=ada_weight, query_bias=query_bias, value_bias=value_bias, proj_bias=proj_bias, up_bias=up_bias, down_bias=down_bias, ada_bias=ada_bias)


@jax.custom_vjp
def low(v):
    return lax.optimization_barrier(v.astype(jnp.bfloat16)).astype(jnp.float32)

@jax.custom_vjp
def low_back(v):
    return v

def low_keep(v):
    return (low(v), None)

def low_pass(kept, grad):
    return (grad,)

def back_keep(v):
    return (v, None)

def back_low(kept, grad):
    return (low(grad),)
low.defvjp(low_keep, low_pass)
low_back.defvjp(back_keep, back_low)
highest = lax.Precision.HIGHEST
epsilon = 1e-06

def layer_norm(values):
    centred = values - lax.optimization_barrier(jnp.mean(values, axis=-1, keepdims=True))
    return centred * lax.rsqrt(lax.optimization_barrier(jnp.mean(centred * centred, axis=-1, keepdims=True)) + epsilon)

def attend(queries, key_rows, value_rows):
    block_rows = min(512, SEQ)
    score_scale = 1.0 / math.sqrt(HD)
    blocks = queries.reshape(SEQ // block_rows, block_rows, HEADS, HD)

    def one_block(q_rows):
        scores = low_back(jnp.einsum('qhd,khd->hqk', q_rows, key_rows, precision=highest) * score_scale)
        weights_soft = low(jax.nn.softmax(scores, axis=-1))
        return jnp.einsum('hqk,khd->qhd', weights_soft, value_rows, precision=highest)
    return lax.map(jax.checkpoint(one_block), blocks).reshape(SEQ, HEADS * HD)

def forward(latent, condition, params):
    qkv_weight, proj_weight, up_weight, down_weight, ada_weight, query_bias, value_bias, proj_bias, up_bias, down_bias, ada_bias = params
    silu_cond = low(jax.nn.silu(condition))
    modulation = jnp.dot(silu_cond, ada_weight.reshape(C, 6 * D), precision=highest).reshape(6, D) + ada_bias
    attn_in = low(layer_norm(latent) * (1.0 + modulation[1]) + modulation[0])
    projected = jnp.einsum('sd,dtf->stf', attn_in, qkv_weight, precision=highest)
    queries = low(low_back(projected[:, 0] + query_bias))
    key_rows = low(low_back(projected[:, 1]))
    value_rows = low(low_back(projected[:, 2] + value_bias))
    heads_out = attend(queries.reshape(SEQ, HEADS, HD), key_rows.reshape(SEQ, HEADS, HD), value_rows.reshape(SEQ, HEADS, HD))
    heads_out = low(low_back(heads_out))
    branch_one = low_back(jnp.dot(heads_out, proj_weight, precision=highest) + proj_bias)
    middle = latent + modulation[2] * branch_one
    mlp_in = low(layer_norm(middle) * (1.0 + modulation[4]) + modulation[3])
    hidden = low_back(jnp.dot(mlp_in, up_weight, precision=highest) + up_bias)
    active = low(jax.nn.gelu(hidden, approximate=True))
    branch_two = low_back(jnp.dot(active, down_weight, precision=highest) + down_bias)
    return middle + modulation[5] * branch_two

def reference(latents_in, condition, grad_out, qkv_weight, proj_weight, up_weight, down_weight, ada_weight, query_bias, value_bias, proj_bias, up_bias, down_bias, ada_bias):
    params = tuple((weight_item.astype(jnp.float32) for weight_item in (qkv_weight, proj_weight, up_weight, down_weight, ada_weight, query_bias, value_bias, proj_bias, up_bias, down_bias, ada_bias)))

    def per_latent(totals, inputs):
        latent, cond_row, grad_row = inputs
        result, pull = jax.vjp(forward, latent.astype(jnp.float32), cond_row.astype(jnp.float32), params)
        latent_grad, cond_row_grad, param_grads = pull(grad_row.astype(jnp.float32))
        totals = jax.tree.map(lambda first, second: first + second, totals, param_grads)
        return (totals, (result.astype(jnp.bfloat16), latent_grad, cond_row_grad))
    zero_grads = tuple((jnp.zeros_like(weight_item) for weight_item in params))
    totals, (results, latent_grads, cond_grads) = lax.scan(per_latent, zero_grads, (jnp.swapaxes(latents_in, 0, 1), condition, jnp.swapaxes(grad_out, 0, 1)))
    return (jnp.swapaxes(results, 0, 1), jnp.swapaxes(latent_grads, 0, 1), cond_grads, totals[0], totals[1], totals[2], totals[3], totals[4], totals[5], totals[6], totals[7], totals[8], totals[9], totals[10])
```

```python
import functools
import math

import jax
import jax.numpy as jnp
from jax import lax
from jax.experimental import pallas as pl
from jax.experimental.pallas import tpu as pltpu
from jax.sharding import PartitionSpec as P


HD = 64


epsilon = 1e-06


def layer_norm(values):
    centred = values - jnp.mean(values, axis=-1, keepdims=True)
    return centred * lax.rsqrt(jnp.mean(centred * centred, axis=-1, keepdims=True) + epsilon)


def modulate(values, shift_part, scale_part):
    return layer_norm(values) * (1.0 + scale_part) + shift_part


def gelu_tanh(values):
    return jax.nn.gelu(values, approximate=True)


def gather_rows(piece):
    return lax.all_gather(piece, "tp", axis=0, tiled=True)


def gather_grads(piece):
    return lax.all_gather(piece, "tp", axis=0, tiled=True)


def scatter_rows(product, row_count):
    return lax.psum_scatter(
        product(jnp.int32(0), row_count * lax.axis_size("tp")).astype(jnp.bfloat16),
        "tp",
        scatter_dimension=0,
        tiled=True,
    ).astype(jnp.float32)


def scatter_grads(product, row_count):
    return lax.psum_scatter(
        product(jnp.int32(0), row_count * lax.axis_size("tp")).astype(jnp.bfloat16),
        "tp",
        scatter_dimension=0,
        tiled=True,
    ).astype(jnp.float32)


def split_heads(packed):
    head_count = packed.shape[3] // HD
    shaped = packed.reshape(packed.shape[0], packed.shape[1], 3, head_count, HD)
    return (shaped[:, :, 0], shaped[:, :, 1], shaped[:, :, 2])


def attend_forward(packed):
    length, latents, local_width = (packed.shape[0], packed.shape[1], packed.shape[3])
    queries, key_rows, value_rows = split_heads(packed)
    block_rows = min(512, length)
    score_scale = 1.0 / math.sqrt(HD)
    blocks = queries.reshape(length // block_rows, block_rows, latents, local_width // HD, HD)

    def one_block(q_rows):
        scores = (
            jnp.einsum("qbhd,kbhd->bhqk", q_rows, key_rows, preferred_element_type=jnp.float32)
            * score_scale
        )
        largest = jnp.max(scores, axis=-1, keepdims=True)
        exponent = jnp.exp(scores - largest)
        summed = jnp.sum(exponent, axis=-1, keepdims=True)
        weights_soft = (exponent / summed).astype(jnp.bfloat16)
        mixture = jnp.einsum(
            "bhqk,kbhd->qbhd", weights_soft, value_rows, preferred_element_type=jnp.float32
        )
        return (mixture.astype(jnp.bfloat16), largest[..., 0] + jnp.log(summed[..., 0]))

    mixture_all, log_sums = lax.map(one_block, blocks)
    return (mixture_all.reshape(length, latents, local_width), log_sums)


def attend_backward(packed, log_sums, heads_grad):
    length, latents, local_width = (packed.shape[0], packed.shape[1], packed.shape[3])
    head_count = local_width // HD
    queries, key_rows, value_rows = split_heads(packed)
    block_rows = min(512, length)
    count_blocks = length // block_rows
    score_scale = 1.0 / math.sqrt(HD)
    q_blocks = queries.reshape(count_blocks, block_rows, latents, head_count, HD)
    g_blocks = heads_grad.reshape(count_blocks, block_rows, latents, head_count, HD)

    def one_block(carried, inputs):
        key_grad, value_grad = carried
        q_rows, g_rows, log_rows = inputs
        scores = (
            jnp.einsum("qbhd,kbhd->bhqk", q_rows, key_rows, preferred_element_type=jnp.float32)
            * score_scale
        )
        weights_soft = jnp.exp(scores - log_rows[..., None])
        soft_grad = jnp.einsum(
            "qbhd,kbhd->bhqk", g_rows, value_rows, preferred_element_type=jnp.float32
        )
        inner_sum = jnp.sum(weights_soft * soft_grad, axis=-1, keepdims=True)
        score_grad = (weights_soft * (soft_grad - inner_sum)).astype(jnp.bfloat16)
        query_grad = (
            jnp.einsum("bhqk,kbhd->qbhd", score_grad, key_rows, preferred_element_type=jnp.float32)
            * score_scale
        )
        key_grad = (
            key_grad
            + jnp.einsum("bhqk,qbhd->kbhd", score_grad, q_rows, preferred_element_type=jnp.float32)
            * score_scale
        )
        value_grad = value_grad + jnp.einsum(
            "bhqk,qbhd->kbhd",
            weights_soft.astype(jnp.bfloat16),
            g_rows,
            preferred_element_type=jnp.float32,
        )
        return ((key_grad, value_grad), query_grad)

    zero_rows = jnp.zeros((length, latents, head_count, HD), jnp.float32)
    (key_grad, value_grad), query_grad = lax.scan(
        one_block, (zero_rows, zero_rows), (q_blocks, g_blocks, log_sums)
    )
    stacked = jnp.stack(
        [
            query_grad.reshape(length, latents, local_width),
            key_grad.reshape(length, latents, local_width),
            value_grad.reshape(length, latents, local_width),
        ],
        axis=2,
    )
    return stacked.astype(jnp.bfloat16)


def on_device_general(
    latents_in,
    condition,
    grad_out,
    qkv_weight,
    proj_weight,
    up_weight,
    down_weight,
    ada_weight,
    query_bias,
    value_bias,
    proj_bias,
    up_bias,
    down_bias,
    ada_bias,
):
    tp_index = lax.axis_index("tp")
    local_rows = latents_in.shape[0]
    local_width = qkv_weight.shape[2]
    local_hidden = up_weight.shape[1]
    model_width = latents_in.shape[2]
    width_start = tp_index * local_width
    hidden_start = tp_index * local_hidden
    full_qkv, full_proj, full_up, full_down, full_ada = (
        lax.all_gather(qkv_weight, "fsdp", axis=0, tiled=True),
        lax.all_gather(proj_weight, "fsdp", axis=1, tiled=True),
        lax.all_gather(up_weight, "fsdp", axis=0, tiled=True),
        lax.all_gather(down_weight, "fsdp", axis=1, tiled=True),
        lax.all_gather(ada_weight, "fsdp", axis=0, tiled=True),
    )
    bias_list = (
        lax.all_gather(query_bias, ("fsdp", "tp"), axis=0, tiled=True),
        lax.all_gather(value_bias, ("fsdp", "tp"), axis=0, tiled=True),
        lax.all_gather(proj_bias, ("fsdp", "tp"), axis=0, tiled=True),
        lax.all_gather(up_bias, ("fsdp", "tp"), axis=0, tiled=True),
        lax.all_gather(down_bias, ("fsdp", "tp"), axis=0, tiled=True),
        lax.all_gather(ada_bias, ("fsdp", "tp"), axis=1, tiled=True),
    )
    all_query, all_value, all_proj, all_up, all_down, all_ada = [
        item_bias.astype(jnp.float32) for item_bias in bias_list
    ]
    hidden_total = all_up.shape[0]
    cond_float = condition.astype(jnp.float32)
    silu_cond = jax.nn.silu(cond_float).astype(jnp.bfloat16)
    ada_cols = lax.dynamic_slice_in_dim(all_ada, width_start, local_width, 1)
    mod_part = (
        jnp.einsum("bc,ctf->btf", silu_cond, full_ada, preferred_element_type=jnp.float32)
        + ada_cols
    )
    modulation = lax.all_gather(mod_part, "tp", axis=2, tiled=True)
    shift_one, scale_one, gate_one = (modulation[:, 0], modulation[:, 1], modulation[:, 2])
    shift_two, scale_two, gate_two = (modulation[:, 3], modulation[:, 4], modulation[:, 5])
    input_float = latents_in.astype(jnp.float32)
    attn_in = modulate(input_float, shift_one, scale_one).astype(jnp.bfloat16)
    attn_full = gather_rows(attn_in)
    query_cols = lax.dynamic_slice_in_dim(all_query, width_start, local_width, 0)
    value_cols = lax.dynamic_slice_in_dim(all_value, width_start, local_width, 0)
    bias_three = jnp.stack([query_cols, jnp.zeros_like(query_cols), value_cols])
    packed = (
        jnp.einsum("sbd,dtf->sbtf", attn_full, full_qkv, preferred_element_type=jnp.float32)
        + bias_three
    ).astype(jnp.bfloat16)
    heads_out, log_sums = attend_forward(packed)

    def project_heads(first_row, row_count):
        return jnp.einsum("sbf,fd->sbd", heads_out, full_proj, preferred_element_type=jnp.float32)

    branch_one = scatter_rows(project_heads, local_rows) + all_proj
    middle = input_float + gate_one * branch_one
    mlp_in = modulate(middle, shift_two, scale_two).astype(jnp.bfloat16)
    mlp_full = gather_rows(mlp_in)
    up_cols = lax.dynamic_slice_in_dim(all_up, hidden_start, local_hidden, 0)
    hidden = (
        jnp.einsum("sbd,df->sbf", mlp_full, full_up, preferred_element_type=jnp.float32) + up_cols
    )
    active = gelu_tanh(hidden).astype(jnp.bfloat16)

    def project_hidden(first_row, row_count):
        return jnp.einsum("sbf,fd->sbd", active, full_down, preferred_element_type=jnp.float32)

    branch_two = scatter_rows(project_hidden, local_rows) + all_down
    block_out = (middle + gate_two * branch_two).astype(jnp.bfloat16)
    grad_float = grad_out.astype(jnp.float32)
    gate_two_grad = jnp.sum(grad_float * branch_two, axis=0)
    branch_two_grad = (grad_float * gate_two).astype(jnp.bfloat16)
    down_bias_part = jnp.sum(branch_two_grad.astype(jnp.float32), axis=(0, 1))
    _, gelu_pull = jax.vjp(gelu_tanh, hidden)
    branch_two_full = gather_grads(branch_two_grad)
    active_grad = jnp.einsum(
        "sbd,fd->sbf", branch_two_full, full_down, preferred_element_type=jnp.float32
    )
    down_grad = jnp.einsum(
        "sbf,sbd->fd", active, branch_two_full, preferred_element_type=jnp.float32
    )
    hidden_grad = gelu_pull(active_grad)[0].astype(jnp.bfloat16)
    up_grad = jnp.einsum("sbd,sbf->df", mlp_full, hidden_grad, preferred_element_type=jnp.float32)
    up_bias_part = lax.dynamic_update_slice(
        jnp.zeros((hidden_total,), jnp.float32),
        jnp.sum(hidden_grad.astype(jnp.float32), axis=(0, 1)),
        (hidden_start,),
    )

    def back_hidden(first_row, row_count):
        return jnp.einsum("sbf,df->sbd", hidden_grad, full_up, preferred_element_type=jnp.float32)

    mlp_in_grad = scatter_grads(back_hidden, local_rows)
    _, second_pull = jax.vjp(modulate, middle, shift_two, scale_two)
    middle_part, shift_two_grad, scale_two_grad = second_pull(mlp_in_grad)
    middle_grad = grad_float + middle_part
    gate_one_grad = jnp.sum(middle_grad * branch_one, axis=0)
    branch_one_grad = (middle_grad * gate_one).astype(jnp.bfloat16)
    proj_bias_part = jnp.sum(branch_one_grad.astype(jnp.float32), axis=(0, 1))
    branch_one_full = gather_grads(branch_one_grad)
    heads_grad = jnp.einsum(
        "sbd,fd->sbf", branch_one_full, full_proj, preferred_element_type=jnp.float32
    ).astype(jnp.bfloat16)
    proj_grad = jnp.einsum(
        "sbf,sbd->fd", heads_out, branch_one_full, preferred_element_type=jnp.float32
    )
    packed_grad = attend_backward(packed, log_sums, heads_grad)
    qkv_grad = jnp.einsum(
        "sbd,sbtf->dtf", attn_full, packed_grad, preferred_element_type=jnp.float32
    )
    packed_sums = jnp.sum(packed_grad.astype(jnp.float32), axis=(0, 1))
    zero_width = jnp.zeros((model_width,), jnp.float32)
    query_bias_part = lax.dynamic_update_slice(zero_width, packed_sums[0], (width_start,))
    value_bias_part = lax.dynamic_update_slice(zero_width, packed_sums[2], (width_start,))

    def back_packed(first_row, row_count):
        return jnp.einsum(
            "sbtf,dtf->sbd", packed_grad, full_qkv, preferred_element_type=jnp.float32
        )

    attn_in_grad = scatter_grads(back_packed, local_rows)
    _, first_pull = jax.vjp(modulate, input_float, shift_one, scale_one)
    input_part, shift_one_grad, scale_one_grad = first_pull(attn_in_grad)
    input_grad = middle_grad + input_part
    mod_grad = jnp.stack(
        [
            shift_one_grad,
            scale_one_grad,
            gate_one_grad,
            shift_two_grad,
            scale_two_grad,
            gate_two_grad,
        ],
        axis=1,
    )
    mod_cols_grad = lax.psum_scatter(
        mod_grad.astype(jnp.bfloat16), "tp", scatter_dimension=2, tiled=True
    ).astype(jnp.float32)
    ada_grad = jnp.einsum(
        "bc,btf->ctf", silu_cond.astype(jnp.float32), mod_cols_grad, precision=lax.Precision.HIGHEST
    )
    ada_bias_part = lax.dynamic_update_slice(
        jnp.zeros((6, model_width), jnp.float32), jnp.sum(mod_cols_grad, axis=0), (0, width_start)
    )
    silu_grad = jnp.einsum(
        "btf,ctf->bc", mod_cols_grad, full_ada.astype(jnp.float32), precision=lax.Precision.HIGHEST
    )
    silu_cols = lax.psum_scatter(silu_grad, "tp", scatter_dimension=1, tiled=True)
    cond_width = silu_cols.shape[1]
    cond_cols = lax.dynamic_slice_in_dim(cond_float, tp_index * cond_width, cond_width, 1)
    _, silu_pull = jax.vjp(jax.nn.silu, cond_cols)
    cond_grad = silu_pull(silu_cols)[0]
    qkv_sum, proj_sum, up_sum, down_sum, ada_sum = (
        lax.psum_scatter(
            qkv_grad.astype(jnp.bfloat16), "fsdp", scatter_dimension=0, tiled=True
        ).astype(jnp.float32),
        lax.psum_scatter(
            proj_grad.astype(jnp.bfloat16), "fsdp", scatter_dimension=1, tiled=True
        ).astype(jnp.float32),
        lax.psum_scatter(
            up_grad.astype(jnp.bfloat16), "fsdp", scatter_dimension=0, tiled=True
        ).astype(jnp.float32),
        lax.psum_scatter(
            down_grad.astype(jnp.bfloat16), "fsdp", scatter_dimension=1, tiled=True
        ).astype(jnp.float32),
        lax.psum_scatter(
            ada_grad.astype(jnp.bfloat16), "fsdp", scatter_dimension=0, tiled=True
        ).astype(jnp.float32),
    )
    query_sum, value_sum, proj_bias_sum, up_bias_sum, down_bias_sum, ada_bias_sum = (
        lax.psum_scatter(query_bias_part, ("fsdp", "tp"), scatter_dimension=0, tiled=True),
        lax.psum_scatter(value_bias_part, ("fsdp", "tp"), scatter_dimension=0, tiled=True),
        lax.psum_scatter(proj_bias_part, ("fsdp", "tp"), scatter_dimension=0, tiled=True),
        lax.psum_scatter(up_bias_part, ("fsdp", "tp"), scatter_dimension=0, tiled=True),
        lax.psum_scatter(down_bias_part, ("fsdp", "tp"), scatter_dimension=0, tiled=True),
        lax.psum_scatter(ada_bias_part, ("fsdp", "tp"), scatter_dimension=1, tiled=True),
    )
    return (
        block_out,
        input_grad,
        cond_grad,
        qkv_sum,
        proj_sum,
        up_sum,
        down_sum,
        ada_sum,
        query_sum,
        value_sum,
        proj_bias_sum,
        up_bias_sum,
        down_bias_sum,
        ada_bias_sum,
    )


MESH = pl.DeviceIdType.MESH
ANY = pl.ANY
BF = jnp.bfloat16
F32 = jnp.float32


def place():
    f, x = lax.axis_index("fsdp"), lax.axis_index("tp")
    z, y, c = f // 4, lax.rem(f // 2, 2), lax.rem(f, 2)
    return z, y, c, x


def at(z, y, c, x):
    return ((z * 2 + y) * 2 + c, x)


def remote(src, dst, send, recv, device):
    return pltpu.make_async_remote_copy(
        src_ref=src, dst_ref=dst, send_sem=send, recv_sem=recv, device_id=device, device_id_type=MESH
    )


def greet(devices):
    barrier = pltpu.get_barrier_semaphore()
    for device in devices:
        pl.semaphore_signal(barrier, inc=1, device_id=device, device_id_type=MESH)
    pl.semaphore_wait(barrier, len(devices))


def partners(z, y, c, x, diagonal=False):
    out = [at(z, y, 1 - c, x), at(z, 1 - y, c, x), at(z, y, c, 1 - x)]
    out += [at(lax.rem(z + d, 4), y, c, x) for d in (1, 2, 3)]
    if diagonal:
        out.append(at(z, y, 1 - c, 1 - x))
    return out


class Gather:
    sems = 8

    def __init__(self, own, full, send, recv, local):
        self.own, self.full, self.send, self.recv, self.local = own, full, send, recv, local

    def _core(self):
        z, y, c, x = place()
        rows = pl.ds(pl.multiple_of(c * 64, 64), 64)
        spot = self.full.at[x, z, y, rows]
        return (
            pltpu.make_async_copy(self.own.at[c], spot, self.local),
            remote(self.own.at[1 - c], spot, self.send.at[0], self.recv.at[0], at(z, y, 1 - c, x)),
        )

    def _z(self, d):
        z, y, c, x = place()
        spot = self.full.at[x, z, y]
        return remote(spot, spot, self.send.at[d], self.recv.at[d], at(lax.rem(z + d, 4), y, c, x))

    def _xy(self, k):
        z, y, c, x = place()
        if k == 0:
            spot, to = self.full.at[x, pl.ds(0, 2), y], at(z, y, c, 1 - x)
        elif k == 1:
            spot, to = self.full.at[x, pl.ds(2, 2), y], at(z, 1 - y, c, x)
        elif k == 2:
            spot, to = self.full.at[:, pl.ds(0, 2), y], at(z, 1 - y, c, x)
        else:
            spot, to = self.full.at[x, pl.ds(2, 2)], at(z, y, c, 1 - x)
        return remote(spot, spot, self.send.at[4 + k], self.recv.at[4 + k], to)

    def start_core(self):
        for copy in self._core():
            copy.start()

    def core_to_z(self):
        local, far = self._core()
        local.wait()
        far.wait()
        for d in (1, 2, 3):
            self._z(d).start()

    def z_to_xy(self):
        for d in (1, 2, 3):
            self._z(d).wait()
        self._xy(0).start()
        self._xy(1).start()

    def xy_to_last(self):
        self._xy(0).wait()
        self._xy(2).start()
        self._xy(1).wait()
        self._xy(3).start()

    def finish(self):
        self._xy(2).wait()
        self._xy(3).wait()


class Scatter:
    sems = 8

    def __init__(self, part, first_a, first_b, second, third, total, out, send, recv, local):
        self.part, self.first_a, self.first_b = part, first_a, first_b
        self.second, self.third, self.total, self.out = second, third, total, out
        self.send, self.recv, self.local = send, recv, local

    def _copy(self, k):
        z, y, c, x = place()
        send, recv = self.send.at[k], self.recv.at[k]
        if k == 0:
            return remote(self.part.at[:, pl.ds(0, 2), 1 - y], self.first_a, send, recv, at(z, 1 - y, c, x))
        if k == 1:
            return remote(self.part.at[1 - x, pl.ds(2, 2)], self.first_b, send, recv, at(z, y, c, 1 - x))
        if k == 2:
            return remote(self.first_a.at[1 - x], self.second.at[pl.ds(0, 2)], send, recv, at(z, y, c, 1 - x))
        if k == 3:
            return remote(self.first_b.at[:, 1 - y], self.second.at[pl.ds(2, 2)], send, recv, at(z, 1 - y, c, x))
        if k <= 6:
            d = k - 3
            to = lax.rem(z + d, 4)
            return remote(self.second.at[to], self.third.at[d - 1], send, recv, at(to, y, c, x))
        rows = pl.ds(pl.multiple_of((1 - c) * 64, 64), 64)
        return remote(self.total.at[rows], self.out.at[c], send, recv, at(z, y, 1 - c, x))

    def _own(self):
        z, y, c, x = place()
        rows = pl.ds(pl.multiple_of(c * 64, 64), 64)
        return pltpu.make_async_copy(self.total.at[rows], self.out.at[c], self.local)

    def start(self):
        self._copy(0).start()
        self._copy(1).start()

    def first(self):
        z, y, c, x = place()
        self._copy(0).wait()

        def add_a(i, carry):
            self.first_a[i // 2, i % 2] = (
                self.first_a[i // 2, i % 2].astype(F32) + self.part[i // 2, i % 2, y].astype(F32)
            ).astype(BF)
            return carry

        lax.fori_loop(0, 4, add_a, 0)
        self._copy(2).start()
        self._copy(1).wait()

        def add_b(i, carry):
            self.first_b[i // 2, i % 2] = (
                self.first_b[i // 2, i % 2].astype(F32) + self.part[x, 2 + i // 2, i % 2].astype(F32)
            ).astype(BF)
            return carry

        lax.fori_loop(0, 4, add_b, 0)
        self._copy(3).start()

    def next(self):
        z, y, c, x = place()
        self._copy(2).wait()

        def add_a(i, carry):
            self.second[i] = (self.second[i].astype(F32) + self.first_a[x, i].astype(F32)).astype(BF)
            return carry

        lax.fori_loop(0, 2, add_a, 0)
        self._copy(3).wait()

        def add_b(i, carry):
            self.second[2 + i] = (self.second[2 + i].astype(F32) + self.first_b[i, y].astype(F32)).astype(BF)
            return carry

        lax.fori_loop(0, 2, add_b, 0)
        for k in (4, 5, 6):
            self._copy(k).start()

    def last(self):
        z, y, c, x = place()
        for k in (4, 5, 6):
            self._copy(k).wait()

        def add(i, carry):
            rows = pl.ds(pl.multiple_of(i * 64, 64), 64)
            total = self.second[z, rows].astype(F32)
            for d in range(3):
                total = total + self.third[d, rows].astype(F32)
            self.total[rows] = total
            return carry

        lax.fori_loop(0, 2, add, 0)
        self._copy(7).start()
        self._own().start()

    def finish(self):
        self._copy(7).wait()
        self._own().wait()


class Swap:
    sems = 2

    def __init__(self, own, full, send, recv, local):
        self.own, self.full, self.send, self.recv, self.local = own, full, send, recv, local

    def _far(self):
        z, y, c, x = place()
        return remote(self.own, self.full.at[1 - c], self.send.at[0], self.recv.at[0], at(z, y, 1 - c, 1 - x))

    def _near(self):
        z, y, c, x = place()
        return pltpu.make_async_copy(self.own, self.full.at[c], self.local)

    def _core(self):
        z, y, c, x = place()
        spot = self.full.at[c]
        return remote(spot, spot, self.send.at[1], self.recv.at[1], at(z, y, 1 - c, x))

    def start(self):
        z, y, c, x = place()

        @pl.when(c != x)
        def _():
            self._far().start()

        @pl.when(c == x)
        def _():
            self._near().start()

    def share(self):
        z, y, c, x = place()

        @pl.when(c != x)
        def _():
            self._far().wait()

        @pl.when(c == x)
        def _():
            self._near().wait()

        self._core().start()

    def finish(self):
        self._core().wait()


COLS = (768, 256, 1024, 1024)


def gather_kernel(lat, grad, wq, wp, wu, wd, lat_full, grad_full, gq, gp, gu, gd, send, recv, local):
    z, y, c, x = place()
    greet(partners(z, y, c, x, True))
    swaps = [
        Swap(own, full, send.at[4 + i], recv.at[4 + i], local.at[4 + i])
        for i, (own, full) in enumerate(((lat, lat_full), (grad, grad_full)))
    ]
    groups = [
        Gather(own, full, send.at[i], recv.at[i], local.at[i])
        for i, (own, full) in enumerate(((wq, gq), (wp, gp), (wu, gu), (wd, gd)))
    ]
    for group in groups:
        group.start_core()
    swaps[0].start()
    for group in groups:
        group.core_to_z()
    for group in groups:
        group.z_to_xy()
    swaps[0].share()
    swaps[1].start()
    for group in groups:
        group.xy_to_last()
    for group in groups:
        group.finish()
    swaps[1].share()
    for swap in swaps:
        swap.finish()


def gather_all(lat, grad, wq, wp, wu, wd):
    outs = [jax.ShapeDtypeStruct((2, 512, 1024), BF)] * 2
    outs += [jax.ShapeDtypeStruct((2, 4, 2, 128, n), BF) for n in COLS]
    return pl.pallas_call(
        gather_kernel,
        out_shape=outs,
        in_specs=[pl.BlockSpec(memory_space=ANY)] * 6,
        out_specs=[pl.BlockSpec(memory_space=ANY)] * 6,
        scratch_shapes=[
            pltpu.SemaphoreType.DMA((6, 8)),
            pltpu.SemaphoreType.DMA((6, 8)),
            pltpu.SemaphoreType.DMA((6,)),
        ],
        compiler_params=pltpu.CompilerParams(collective_id=0, has_side_effects=True),
        name="gather_all",
    )(lat, grad, wq, wp, wu, wd)


def scatter_buffers(n):
    return [
        pltpu.VMEM((2, 2, 128, n), BF),
        pltpu.VMEM((2, 2, 128, n), BF),
        pltpu.VMEM((4, 128, n), BF),
        pltpu.VMEM((3, 128, n), BF),
        pltpu.VMEM((128, n), F32),
    ]


def scatter_kernel(dq, dp, du, dd, oq, op, ou, od, *rest):
    buffers, (send, recv, local) = rest[:-3], rest[-3:]
    z, y, c, x = place()
    greet(partners(z, y, c, x))
    groups = []
    for i, (part, out) in enumerate(((dq, oq), (dp, op), (du, ou), (dd, od))):
        groups.append(Scatter(part, *buffers[5 * i : 5 * i + 5], out, send.at[i], recv.at[i], local.at[i]))
    groups = [groups[i] for i in (3, 2, 1, 0)]
    for group in groups:
        group.start()
    for group in groups:
        group.first()
    for group in groups:
        group.next()
    for group in groups:
        group.last()
    for group in groups:
        group.finish()


def scatter_all(*parts):
    scratch = []
    for n in COLS:
        scratch += scatter_buffers(n)
    return pl.pallas_call(
        scatter_kernel,
        out_shape=[jax.ShapeDtypeStruct((2, 64, n), F32) for n in COLS],
        in_specs=[pl.BlockSpec(memory_space=pltpu.VMEM)] * 4,
        out_specs=[pl.BlockSpec(memory_space=ANY)] * 4,
        scratch_shapes=scratch
        + [
            pltpu.SemaphoreType.DMA((4, 8)),
            pltpu.SemaphoreType.DMA((4, 8)),
            pltpu.SemaphoreType.DMA((4,)),
        ],
        compiler_params=pltpu.CompilerParams(
            collective_id=1, has_side_effects=True, vmem_limit_bytes=56 * 2**20
        ),
        name="scatter_all",
    )(*parts)


def swap_back_kernel(block, grad, block_out, grad_out, send, recv, local):
    z, y, c, x = place()
    greet([at(z, y, 1 - c, 1 - x)])

    @pl.when(c != x)
    def _():
        copies = [
            remote(a, b, send.at[i], recv.at[i], at(z, y, 1 - c, 1 - x))
            for i, (a, b) in enumerate(((block, block_out), (grad, grad_out)))
        ]
        for copy in copies:
            copy.start()
        for copy in copies:
            copy.wait()

    @pl.when(c == x)
    def _():
        copies = [
            pltpu.make_async_copy(a, b, local.at[i]) for i, (a, b) in enumerate(((block, block_out), (grad, grad_out)))
        ]
        for copy in copies:
            copy.start()
        for copy in copies:
            copy.wait()


def swap_back(block, grad):
    return pl.pallas_call(
        swap_back_kernel,
        out_shape=[jax.ShapeDtypeStruct(a.shape, a.dtype) for a in (block, grad)],
        in_specs=[pl.BlockSpec(memory_space=ANY)] * 2,
        out_specs=[pl.BlockSpec(memory_space=ANY)] * 2,
        scratch_shapes=[
            pltpu.SemaphoreType.DMA((2,)),
            pltpu.SemaphoreType.DMA((2,)),
            pltpu.SemaphoreType.DMA((2,)),
        ],
        compiler_params=pltpu.CompilerParams(collective_id=2, has_side_effects=True),
        name="swap_back",
    )(block, grad)


def pair_sum(partial):
    pairs = [(i, i ^ 1) for i in range(16)]
    rounded = partial.astype(BF)
    return partial + lax.ppermute(rounded, "fsdp", pairs).astype(F32)


def spread(vectors, sizes):
    everyone = lax.all_gather(vectors, ("fsdp", "tp"), axis=0, tiled=False)
    parts, first = [], 0
    for size in sizes:
        parts.append(everyone[:, first : first + size])
        first += size
    return parts


def on_device_pairs(
    latents_in,
    condition,
    grad_out,
    qkv_weight,
    proj_weight,
    up_weight,
    down_weight,
    ada_weight,
    query_bias,
    value_bias,
    proj_bias,
    up_bias,
    down_bias,
    ada_bias,
):
    z, y, c, x = place()
    wq = qkv_weight.reshape(64, 3, 2, 256).transpose(2, 0, 1, 3).reshape(2, 64, 768)
    wp = proj_weight.T.reshape(64, 2, 256).transpose(1, 0, 2)
    wu = up_weight.reshape(64, 2, 1024).transpose(1, 0, 2)
    wd = down_weight.T.reshape(64, 2, 1024).transpose(1, 0, 2)
    lat_full, grad_full, gq, gp, gu, gd = gather_all(
        latents_in.reshape(512, 1024), grad_out.reshape(512, 1024), wq, wp, wu, wd
    )
    gq, gp, gu, gd = [g.reshape(2, 1024, -1) for g in (gq, gp, gu, gd)]
    biases = jnp.concatenate([query_bias, value_bias, proj_bias, down_bias, up_bias, ada_bias.reshape(-1)])
    all_q, all_v, all_p, all_d, all_u, all_a = [
        b.astype(F32) for b in spread(biases, (32, 32, 32, 32, 128, 192))
    ]
    all_q, all_v, all_p, all_d, all_u = [b.reshape(-1) for b in (all_q, all_v, all_p, all_d, all_u)]
    all_a = all_a.reshape(32, 6, 32).transpose(1, 0, 2).reshape(6, 1024)
    conditions = lax.all_gather(condition, "fsdp", axis=0, tiled=True)
    silu_all = jax.nn.silu(conditions.astype(F32)).astype(BF)
    my_rows = (z * 4 + y * 2 + c) * 64
    silu_mine = lax.dynamic_slice_in_dim(silu_all, my_rows, 64, 1)
    mod_part = jnp.einsum("bc,ctf->btf", silu_mine, ada_weight, preferred_element_type=F32)
    mod_half = lax.psum_scatter(mod_part, "fsdp", scatter_dimension=0, tiled=True)
    mods = lax.all_gather(mod_half, ("fsdp", "tp"), axis=0, tiled=True)
    latent = (z * 2 + y) * 2 + x
    modulation = (
        lax.dynamic_slice_in_dim(mods, latent * 2, 2, 0).transpose(1, 0, 2).reshape(6, 1024) + all_a
    )
    m = [modulation[i : i + 1] for i in range(6)]
    half = lambda v, width: jnp.stack(
        [lax.dynamic_slice_in_dim(v, b * 2 * width + c * width, width, 0) for b in range(2)]
    )
    q_cols, v_cols, u_cols = half(all_q, 256), half(all_v, 256), half(all_u, 1024)

    xin = lat_full.reshape(1024, 1024).astype(F32)
    attn_in = modulate(xin, m[0], m[1]).astype(BF)
    bias_three = jnp.stack([q_cols, jnp.zeros_like(q_cols), v_cols], 1).reshape(2, 1, 768)
    packed = (jnp.einsum("sd,xdn->xsn", attn_in, gq, preferred_element_type=F32) + bias_three).astype(BF)
    packed4 = packed.reshape(2, 1024, 3, 256).transpose(1, 2, 0, 3).reshape(1024, 1, 3, 512)
    heads_out, log_sums = attend_forward(packed4)
    heads_out = heads_out.reshape(1024, 512)
    wproj = gp.transpose(1, 0, 2).reshape(1024, 512)
    branch_one = pair_sum(jnp.einsum("sf,df->sd", heads_out, wproj, preferred_element_type=F32)) + all_p
    middle = xin + m[2] * branch_one
    mlp_in = modulate(middle, m[3], m[4]).astype(BF)
    hidden = jnp.einsum("sd,xdn->xsn", mlp_in, gu, preferred_element_type=F32) + u_cols[:, None]
    active = gelu_tanh(hidden).astype(BF)
    branch_two = pair_sum(jnp.einsum("xsn,xdn->sd", active, gd, preferred_element_type=F32)) + all_d
    block_out = (middle + m[5] * branch_two).astype(BF)
    g = grad_full.reshape(1024, 1024).astype(F32)
    gate_two_grad = jnp.sum(g * branch_two, 0)
    g2 = (g * m[5]).astype(BF)
    own_rows = lambda a: lax.dynamic_slice_in_dim(a, c * 512, 512, 0)
    down_bias_part = jnp.sum(own_rows(g2).astype(F32), 0)
    _, gelu_pull = jax.vjp(gelu_tanh, hidden)
    active_grad = jnp.einsum("sd,xdn->xsn", g2, gd, preferred_element_type=F32)
    down_grad = jnp.einsum("sd,xsn->xdn", g2, active, preferred_element_type=F32).astype(BF)
    hidden_grad = gelu_pull(active_grad)[0].astype(BF)
    up_grad = jnp.einsum("sd,xsn->xdn", mlp_in, hidden_grad, preferred_element_type=F32).astype(BF)
    up_bias_part = jnp.sum(hidden_grad.astype(F32), 1)
    mlp_in_grad = pair_sum(jnp.einsum("xsn,xdn->sd", hidden_grad, gu, preferred_element_type=F32))
    _, second_pull = jax.vjp(modulate, middle, m[3], m[4])
    middle_part, shift_two_grad, scale_two_grad = second_pull(mlp_in_grad)
    middle_grad = g + middle_part
    gate_one_grad = jnp.sum(middle_grad * branch_one, 0)
    g1 = (middle_grad * m[2]).astype(BF)
    proj_bias_part = jnp.sum(own_rows(g1).astype(F32), 0)
    heads_grad = jnp.einsum("sd,df->sf", g1, wproj, preferred_element_type=F32).astype(BF)
    proj_grad = jnp.einsum("sd,sf->df", g1, heads_out, preferred_element_type=F32).astype(BF)
    proj_grad = proj_grad.reshape(1024, 2, 256).transpose(1, 0, 2)
    packed_grad = attend_backward(packed4, log_sums, heads_grad.reshape(1024, 1, 512)).reshape(1024, 3, 2, 256)
    packed_grad = packed_grad.transpose(2, 0, 1, 3).reshape(2, 1024, 768)
    qkv_grad = jnp.einsum("sd,xsn->xdn", attn_in, packed_grad, preferred_element_type=F32).astype(BF)
    packed_sums = jnp.sum(packed_grad.astype(F32), 1)
    attn_in_grad = pair_sum(jnp.einsum("xsn,xdn->sd", packed_grad, gq, preferred_element_type=F32))
    _, first_pull = jax.vjp(modulate, xin, m[0], m[1])
    input_part, shift_one_grad, scale_one_grad = first_pull(attn_in_grad)
    input_grad = middle_grad + input_part

    block_mine, grad_mine = swap_back(own_rows(block_out), own_rows(input_grad.astype(BF)))
    parts = scatter_all(
        *[p.reshape(2, 4, 2, 128, -1) for p in (qkv_grad, proj_grad, up_grad, down_grad)]
    )
    oq, op, ou, od = parts
    qkv_sum = oq.reshape(2, 64, 3, 256).transpose(1, 2, 0, 3).reshape(64, 3, 512)
    proj_sum = op.transpose(1, 0, 2).reshape(64, 512).T
    up_sum = ou.transpose(1, 0, 2).reshape(64, 2048)
    down_sum = od.transpose(1, 0, 2).reshape(64, 2048).T
    mod_grad = jnp.stack(
        [shift_one_grad[0], scale_one_grad[0], gate_one_grad, shift_two_grad[0], scale_two_grad[0], gate_two_grad]
    )
    mine = lax.dynamic_slice_in_dim(mod_grad, c * 512, 512, 1)
    every = lax.all_gather(mine, ("fsdp", "tp"), axis=0, tiled=False).reshape(4, 2, 2, 2, 6, 512)
    mod_cols = lax.dynamic_index_in_dim(every, x, 2, False).reshape(16, 6, 512)
    ada_sum = jnp.einsum(
        "bc,btf->ctf", silu_mine.astype(F32), mod_cols, precision=lax.Precision.HIGHEST
    )
    ada_bias_cols = jnp.sum(mod_cols, 0)
    ada_bias_sum = lax.dynamic_slice_in_dim(ada_bias_cols, (z * 4 + y * 2 + c) % 8 * 64 + x * 32, 32, 1)
    every_bias = jnp.sum(every, axis=(0, 1, 3))
    own_col = ((z * 4 + y * 2 + c) * 2 + x) * 32
    ada_bias_sum = lax.dynamic_slice_in_dim(
        every_bias.transpose(1, 0, 2).reshape(6, 1024), own_col, 32, 1
    )
    silu_part = jnp.einsum(
        "btf,ctf->bc", mod_cols, ada_weight.astype(F32), precision=lax.Precision.HIGHEST
    )
    silu_every = lax.all_gather(silu_part, ("fsdp", "tp"), axis=0, tiled=False).reshape(16, 2, 16, 64).sum(1)
    f = z * 4 + y * 2 + c
    silu_row = lax.dynamic_index_in_dim(silu_every, f, 1, False).reshape(1, 1024)
    silu_cols = lax.dynamic_slice_in_dim(silu_row, x * 512, 512, 1)
    cond_cols = lax.dynamic_slice_in_dim(condition.astype(F32), x * 512, 512, 1)
    _, silu_pull = jax.vjp(jax.nn.silu, cond_cols)
    cond_grad = silu_pull(silu_cols)[0]
    put = lambda v, width: sum(
        lax.dynamic_update_slice(
            jnp.zeros((4 * width,), F32), v[b], (b * 2 * width + c * width,)
        )
        for b in range(2)
    )
    q_part, v_part = put(packed_sums[:, :256], 256), put(packed_sums[:, 512:], 256)
    u_part = put(up_bias_part, 1024)
    bias_parts = jnp.concatenate(
        [b.reshape(32, -1) for b in (q_part, v_part, proj_bias_part, down_bias_part, u_part)], 1
    )
    bias_sums = lax.psum_scatter(bias_parts, ("fsdp", "tp"), scatter_dimension=0, tiled=True)[0]
    return (
        block_mine.reshape(512, 1, 1024),
        grad_mine.astype(F32).reshape(512, 1, 1024),
        cond_grad,
        qkv_sum,
        proj_sum,
        up_sum,
        down_sum,
        ada_sum,
        bias_sums[0:32],
        bias_sums[32:64],
        bias_sums[64:96],
        bias_sums[128:256],
        bias_sums[96:128],
        ada_bias_sum,
    )


def solution(mesh):
    shape = dict(mesh.shape)
    pairs = shape["fsdp"] == 16 and shape["tp"] == 2
    return jax.shard_map(
        on_device_pairs if pairs else on_device_general,
        mesh=mesh,
        in_specs=(
            P("tp", "fsdp", None),
            P("fsdp", None),
            P("tp", "fsdp", None),
            P("fsdp", None, "tp"),
            P("tp", "fsdp"),
            P("fsdp", "tp"),
            P("tp", "fsdp"),
            P("fsdp", None, "tp"),
            P(("fsdp", "tp")),
            P(("fsdp", "tp")),
            P(("fsdp", "tp")),
            P(("fsdp", "tp")),
            P(("fsdp", "tp")),
            P(None, ("fsdp", "tp")),
        ),
        out_specs=(
            P("tp", "fsdp", None),
            P("tp", "fsdp", None),
            P("fsdp", "tp"),
            P("fsdp", None, "tp"),
            P("tp", "fsdp"),
            P("fsdp", "tp"),
            P("tp", "fsdp"),
            P("fsdp", None, "tp"),
            P(("fsdp", "tp")),
            P(("fsdp", "tp")),
            P(("fsdp", "tp")),
            P(("fsdp", "tp")),
            P(("fsdp", "tp")),
            P(None, ("fsdp", "tp")),
        ),
        check_vma=False,
    )
```

```python
import functools
import math

import jax
import jax.numpy as jnp
from jax import lax
from jax.experimental import pallas as pl
from jax.experimental.pallas import tpu as pltpu
from jax.sharding import PartitionSpec as P


HD = 64


epsilon = 1e-06


def layer_norm(values):
    centred = values - jnp.mean(values, axis=-1, keepdims=True)
    return centred * lax.rsqrt(jnp.mean(centred * centred, axis=-1, keepdims=True) + epsilon)


def modulate(values, shift_part, scale_part):
    return layer_norm(values) * (1.0 + scale_part) + shift_part


def gelu_tanh(values):
    return jax.nn.gelu(values, approximate=True)


def gather_rows(piece):
    return lax.all_gather(piece, "tp", axis=0, tiled=True)


def gather_grads(piece):
    return lax.all_gather(piece, "tp", axis=0, tiled=True)


def scatter_rows(product, row_count):
    return lax.psum_scatter(
        product(jnp.int32(0), row_count * lax.axis_size("tp")).astype(jnp.bfloat16),
        "tp",
        scatter_dimension=0,
        tiled=True,
    ).astype(jnp.float32)


def scatter_grads(product, row_count):
    return lax.psum_scatter(
        product(jnp.int32(0), row_count * lax.axis_size("tp")).astype(jnp.bfloat16),
        "tp",
        scatter_dimension=0,
        tiled=True,
    ).astype(jnp.float32)


def split_heads(packed):
    head_count = packed.shape[3] // HD
    shaped = packed.reshape(packed.shape[0], packed.shape[1], 3, head_count, HD)
    return (shaped[:, :, 0], shaped[:, :, 1], shaped[:, :, 2])


def attend_forward(packed):
    length, latents, local_width = (packed.shape[0], packed.shape[1], packed.shape[3])
    queries, key_rows, value_rows = split_heads(packed)
    block_rows = min(512, length)
    score_scale = 1.0 / math.sqrt(HD)
    blocks = queries.reshape(length // block_rows, block_rows, latents, local_width // HD, HD)

    def one_block(q_rows):
        scores = (
            jnp.einsum("qbhd,kbhd->bhqk", q_rows, key_rows, preferred_element_type=jnp.float32)
            * score_scale
        )
        largest = jnp.max(scores, axis=-1, keepdims=True)
        exponent = jnp.exp(scores - largest)
        summed = jnp.sum(exponent, axis=-1, keepdims=True)
        weights_soft = (exponent / summed).astype(jnp.bfloat16)
        mixture = jnp.einsum(
            "bhqk,kbhd->qbhd", weights_soft, value_rows, preferred_element_type=jnp.float32
        )
        return (mixture.astype(jnp.bfloat16), largest[..., 0] + jnp.log(summed[..., 0]))

    mixture_all, log_sums = lax.map(one_block, blocks)
    return (mixture_all.reshape(length, latents, local_width), log_sums)


def attend_backward(packed, log_sums, heads_grad):
    length, latents, local_width = (packed.shape[0], packed.shape[1], packed.shape[3])
    head_count = local_width // HD
    queries, key_rows, value_rows = split_heads(packed)
    block_rows = min(512, length)
    count_blocks = length // block_rows
    score_scale = 1.0 / math.sqrt(HD)
    q_blocks = queries.reshape(count_blocks, block_rows, latents, head_count, HD)
    g_blocks = heads_grad.reshape(count_blocks, block_rows, latents, head_count, HD)

    def one_block(carried, inputs):
        key_grad, value_grad = carried
        q_rows, g_rows, log_rows = inputs
        scores = (
            jnp.einsum("qbhd,kbhd->bhqk", q_rows, key_rows, preferred_element_type=jnp.float32)
            * score_scale
        )
        weights_soft = jnp.exp(scores - log_rows[..., None])
        soft_grad = jnp.einsum(
            "qbhd,kbhd->bhqk", g_rows, value_rows, preferred_element_type=jnp.float32
        )
        inner_sum = jnp.sum(weights_soft * soft_grad, axis=-1, keepdims=True)
        score_grad = (weights_soft * (soft_grad - inner_sum)).astype(jnp.bfloat16)
        query_grad = (
            jnp.einsum("bhqk,kbhd->qbhd", score_grad, key_rows, preferred_element_type=jnp.float32)
            * score_scale
        )
        key_grad = (
            key_grad
            + jnp.einsum("bhqk,qbhd->kbhd", score_grad, q_rows, preferred_element_type=jnp.float32)
            * score_scale
        )
        value_grad = value_grad + jnp.einsum(
            "bhqk,qbhd->kbhd",
            weights_soft.astype(jnp.bfloat16),
            g_rows,
            preferred_element_type=jnp.float32,
        )
        return ((key_grad, value_grad), query_grad)

    zero_rows = jnp.zeros((length, latents, head_count, HD), jnp.float32)
    (key_grad, value_grad), query_grad = lax.scan(
        one_block, (zero_rows, zero_rows), (q_blocks, g_blocks, log_sums)
    )
    stacked = jnp.stack(
        [
            query_grad.reshape(length, latents, local_width),
            key_grad.reshape(length, latents, local_width),
            value_grad.reshape(length, latents, local_width),
        ],
        axis=2,
    )
    return stacked.astype(jnp.bfloat16)


def on_device_general(
    latents_in,
    condition,
    grad_out,
    qkv_weight,
    proj_weight,
    up_weight,
    down_weight,
    ada_weight,
    query_bias,
    value_bias,
    proj_bias,
    up_bias,
    down_bias,
    ada_bias,
):
    tp_index = lax.axis_index("tp")
    local_rows = latents_in.shape[0]
    local_width = qkv_weight.shape[2]
    local_hidden = up_weight.shape[1]
    model_width = latents_in.shape[2]
    width_start = tp_index * local_width
    hidden_start = tp_index * local_hidden
    full_qkv, full_proj, full_up, full_down, full_ada = (
        lax.all_gather(qkv_weight, "fsdp", axis=0, tiled=True),
        lax.all_gather(proj_weight, "fsdp", axis=1, tiled=True),
        lax.all_gather(up_weight, "fsdp", axis=0, tiled=True),
        lax.all_gather(down_weight, "fsdp", axis=1, tiled=True),
        lax.all_gather(ada_weight, "fsdp", axis=0, tiled=True),
    )
    bias_list = (
        lax.all_gather(query_bias, ("fsdp", "tp"), axis=0, tiled=True),
        lax.all_gather(value_bias, ("fsdp", "tp"), axis=0, tiled=True),
        lax.all_gather(proj_bias, ("fsdp", "tp"), axis=0, tiled=True),
        lax.all_gather(up_bias, ("fsdp", "tp"), axis=0, tiled=True),
        lax.all_gather(down_bias, ("fsdp", "tp"), axis=0, tiled=True),
        lax.all_gather(ada_bias, ("fsdp", "tp"), axis=1, tiled=True),
    )
    all_query, all_value, all_proj, all_up, all_down, all_ada = [
        item_bias.astype(jnp.float32) for item_bias in bias_list
    ]
    hidden_total = all_up.shape[0]
    cond_float = condition.astype(jnp.float32)
    silu_cond = jax.nn.silu(cond_float).astype(jnp.bfloat16)
    ada_cols = lax.dynamic_slice_in_dim(all_ada, width_start, local_width, 1)
    mod_part = (
        jnp.einsum("bc,ctf->btf", silu_cond, full_ada, preferred_element_type=jnp.float32)
        + ada_cols
    )
    modulation = lax.all_gather(mod_part, "tp", axis=2, tiled=True)
    shift_one, scale_one, gate_one = (modulation[:, 0], modulation[:, 1], modulation[:, 2])
    shift_two, scale_two, gate_two = (modulation[:, 3], modulation[:, 4], modulation[:, 5])
    input_float = latents_in.astype(jnp.float32)
    attn_in = modulate(input_float, shift_one, scale_one).astype(jnp.bfloat16)
    attn_full = gather_rows(attn_in)
    query_cols = lax.dynamic_slice_in_dim(all_query, width_start, local_width, 0)
    value_cols = lax.dynamic_slice_in_dim(all_value, width_start, local_width, 0)
    bias_three = jnp.stack([query_cols, jnp.zeros_like(query_cols), value_cols])
    packed = (
        jnp.einsum("sbd,dtf->sbtf", attn_full, full_qkv, preferred_element_type=jnp.float32)
        + bias_three
    ).astype(jnp.bfloat16)
    heads_out, log_sums = attend_forward(packed)

    def project_heads(first_row, row_count):
        return jnp.einsum("sbf,fd->sbd", heads_out, full_proj, preferred_element_type=jnp.float32)

    branch_one = scatter_rows(project_heads, local_rows) + all_proj
    middle = input_float + gate_one * branch_one
    mlp_in = modulate(middle, shift_two, scale_two).astype(jnp.bfloat16)
    mlp_full = gather_rows(mlp_in)
    up_cols = lax.dynamic_slice_in_dim(all_up, hidden_start, local_hidden, 0)
    hidden = (
        jnp.einsum("sbd,df->sbf", mlp_full, full_up, preferred_element_type=jnp.float32) + up_cols
    )
    active = gelu_tanh(hidden).astype(jnp.bfloat16)

    def project_hidden(first_row, row_count):
        return jnp.einsum("sbf,fd->sbd", active, full_down, preferred_element_type=jnp.float32)

    branch_two = scatter_rows(project_hidden, local_rows) + all_down
    block_out = (middle + gate_two * branch_two).astype(jnp.bfloat16)
    grad_float = grad_out.astype(jnp.float32)
    gate_two_grad = jnp.sum(grad_float * branch_two, axis=0)
    branch_two_grad = (grad_float * gate_two).astype(jnp.bfloat16)
    down_bias_part = jnp.sum(branch_two_grad.astype(jnp.float32), axis=(0, 1))
    _, gelu_pull = jax.vjp(gelu_tanh, hidden)
    branch_two_full = gather_grads(branch_two_grad)
    active_grad = jnp.einsum(
        "sbd,fd->sbf", branch_two_full, full_down, preferred_element_type=jnp.float32
    )
    down_grad = jnp.einsum(
        "sbf,sbd->fd", active, branch_two_full, preferred_element_type=jnp.float32
    )
    hidden_grad = gelu_pull(active_grad)[0].astype(jnp.bfloat16)
    up_grad = jnp.einsum("sbd,sbf->df", mlp_full, hidden_grad, preferred_element_type=jnp.float32)
    up_bias_part = lax.dynamic_update_slice(
        jnp.zeros((hidden_total,), jnp.float32),
        jnp.sum(hidden_grad.astype(jnp.float32), axis=(0, 1)),
        (hidden_start,),
    )

    def back_hidden(first_row, row_count):
        return jnp.einsum("sbf,df->sbd", hidden_grad, full_up, preferred_element_type=jnp.float32)

    mlp_in_grad = scatter_grads(back_hidden, local_rows)
    _, second_pull = jax.vjp(modulate, middle, shift_two, scale_two)
    middle_part, shift_two_grad, scale_two_grad = second_pull(mlp_in_grad)
    middle_grad = grad_float + middle_part
    gate_one_grad = jnp.sum(middle_grad * branch_one, axis=0)
    branch_one_grad = (middle_grad * gate_one).astype(jnp.bfloat16)
    proj_bias_part = jnp.sum(branch_one_grad.astype(jnp.float32), axis=(0, 1))
    branch_one_full = gather_grads(branch_one_grad)
    heads_grad = jnp.einsum(
        "sbd,fd->sbf", branch_one_full, full_proj, preferred_element_type=jnp.float32
    ).astype(jnp.bfloat16)
    proj_grad = jnp.einsum(
        "sbf,sbd->fd", heads_out, branch_one_full, preferred_element_type=jnp.float32
    )
    packed_grad = attend_backward(packed, log_sums, heads_grad)
    qkv_grad = jnp.einsum(
        "sbd,sbtf->dtf", attn_full, packed_grad, preferred_element_type=jnp.float32
    )
    packed_sums = jnp.sum(packed_grad.astype(jnp.float32), axis=(0, 1))
    zero_width = jnp.zeros((model_width,), jnp.float32)
    query_bias_part = lax.dynamic_update_slice(zero_width, packed_sums[0], (width_start,))
    value_bias_part = lax.dynamic_update_slice(zero_width, packed_sums[2], (width_start,))

    def back_packed(first_row, row_count):
        return jnp.einsum(
            "sbtf,dtf->sbd", packed_grad, full_qkv, preferred_element_type=jnp.float32
        )

    attn_in_grad = scatter_grads(back_packed, local_rows)
    _, first_pull = jax.vjp(modulate, input_float, shift_one, scale_one)
    input_part, shift_one_grad, scale_one_grad = first_pull(attn_in_grad)
    input_grad = middle_grad + input_part
    mod_grad = jnp.stack(
        [
            shift_one_grad,
            scale_one_grad,
            gate_one_grad,
            shift_two_grad,
            scale_two_grad,
            gate_two_grad,
        ],
        axis=1,
    )
    mod_cols_grad = lax.psum_scatter(
        mod_grad.astype(jnp.bfloat16), "tp", scatter_dimension=2, tiled=True
    ).astype(jnp.float32)
    ada_grad = jnp.einsum(
        "bc,btf->ctf", silu_cond.astype(jnp.float32), mod_cols_grad, precision=lax.Precision.HIGHEST
    )
    ada_bias_part = lax.dynamic_update_slice(
        jnp.zeros((6, model_width), jnp.float32), jnp.sum(mod_cols_grad, axis=0), (0, width_start)
    )
    silu_grad = jnp.einsum(
        "btf,ctf->bc", mod_cols_grad, full_ada.astype(jnp.float32), precision=lax.Precision.HIGHEST
    )
    silu_cols = lax.psum_scatter(silu_grad, "tp", scatter_dimension=1, tiled=True)
    cond_width = silu_cols.shape[1]
    cond_cols = lax.dynamic_slice_in_dim(cond_float, tp_index * cond_width, cond_width, 1)
    _, silu_pull = jax.vjp(jax.nn.silu, cond_cols)
    cond_grad = silu_pull(silu_cols)[0]
    qkv_sum, proj_sum, up_sum, down_sum, ada_sum = (
        lax.psum_scatter(
            qkv_grad.astype(jnp.bfloat16), "fsdp", scatter_dimension=0, tiled=True
        ).astype(jnp.float32),
        lax.psum_scatter(
            proj_grad.astype(jnp.bfloat16), "fsdp", scatter_dimension=1, tiled=True
        ).astype(jnp.float32),
        lax.psum_scatter(
            up_grad.astype(jnp.bfloat16), "fsdp", scatter_dimension=0, tiled=True
        ).astype(jnp.float32),
        lax.psum_scatter(
            down_grad.astype(jnp.bfloat16), "fsdp", scatter_dimension=1, tiled=True
        ).astype(jnp.float32),
        lax.psum_scatter(
            ada_grad.astype(jnp.bfloat16), "fsdp", scatter_dimension=0, tiled=True
        ).astype(jnp.float32),
    )
    query_sum, value_sum, proj_bias_sum, up_bias_sum, down_bias_sum, ada_bias_sum = (
        lax.psum_scatter(query_bias_part, ("fsdp", "tp"), scatter_dimension=0, tiled=True),
        lax.psum_scatter(value_bias_part, ("fsdp", "tp"), scatter_dimension=0, tiled=True),
        lax.psum_scatter(proj_bias_part, ("fsdp", "tp"), scatter_dimension=0, tiled=True),
        lax.psum_scatter(up_bias_part, ("fsdp", "tp"), scatter_dimension=0, tiled=True),
        lax.psum_scatter(down_bias_part, ("fsdp", "tp"), scatter_dimension=0, tiled=True),
        lax.psum_scatter(ada_bias_part, ("fsdp", "tp"), scatter_dimension=1, tiled=True),
    )
    return (
        block_out,
        input_grad,
        cond_grad,
        qkv_sum,
        proj_sum,
        up_sum,
        down_sum,
        ada_sum,
        query_sum,
        value_sum,
        proj_bias_sum,
        up_bias_sum,
        down_bias_sum,
        ada_bias_sum,
    )


MESH = pl.DeviceIdType.MESH
ANY = pl.ANY
BF = jnp.bfloat16
F32 = jnp.float32
MIB = 2**20
IN_VMEM = pl.BlockSpec(memory_space=pltpu.VMEM)
IN_ANY = pl.BlockSpec(memory_space=ANY)


def place():
    f, x = lax.axis_index("fsdp"), lax.axis_index("tp")
    z, y, c = f // 4, lax.rem(f // 2, 2), lax.rem(f, 2)
    return z, y, c, x


def at(z, y, c, x):
    return ((z * 2 + y) * 2 + c, x)


def block(index, size):
    return pl.ds(pl.multiple_of(index * size, size), size)


def remote(src, dst, send, recv, device):
    return pltpu.make_async_remote_copy(
        src_ref=src, dst_ref=dst, send_sem=send, recv_sem=recv, device_id=device, device_id_type=MESH
    )


def greet(devices):
    barrier = pltpu.get_barrier_semaphore()
    for device in devices:
        pl.semaphore_signal(barrier, inc=1, device_id=device, device_id_type=MESH)
    pl.semaphore_wait(barrier, len(devices))


def partners(diagonal=False):
    z, y, c, x = place()
    out = [at(z, y, 1 - c, x), at(z, 1 - y, c, x), at(z, y, c, 1 - x)]
    out += [at(lax.rem(z + d, 4), y, c, x) for d in (1, 2, 3)]
    if diagonal:
        out.append(at(z, y, 1 - c, 1 - x))
    return out


class Gather:
    def __init__(self, own, full, send, recv, local):
        self.own, self.full, self.send, self.recv, self.local = own, full, send, recv, local

    def _core(self):
        z, y, c, x = place()
        spot = self.full.at[x, z, y, block(c, 64)]
        return (
            pltpu.make_async_copy(self.own.at[c], spot, self.local),
            remote(self.own.at[1 - c], spot, self.send.at[0], self.recv.at[0], at(z, y, 1 - c, x)),
        )

    def _z(self, d):
        z, y, c, x = place()
        spot = self.full.at[x, z, y]
        return remote(spot, spot, self.send.at[d], self.recv.at[d], at(lax.rem(z + d, 4), y, c, x))

    def _xy(self, k):
        z, y, c, x = place()
        if k == 0:
            spot, to = self.full.at[x, pl.ds(0, 2), y], at(z, y, c, 1 - x)
        elif k == 1:
            spot, to = self.full.at[x, pl.ds(2, 2), y], at(z, 1 - y, c, x)
        elif k == 2:
            spot, to = self.full.at[:, pl.ds(0, 2), y], at(z, 1 - y, c, x)
        else:
            spot, to = self.full.at[x, pl.ds(2, 2)], at(z, y, c, 1 - x)
        return remote(spot, spot, self.send.at[4 + k], self.recv.at[4 + k], to)

    def start_core(self):
        for copy in self._core():
            copy.start()

    def wait_core(self):
        for copy in self._core():
            copy.wait()

    def start_z(self):
        for d in (1, 2, 3):
            self._z(d).start()

    def wait_z(self):
        for d in (1, 2, 3):
            self._z(d).wait()

    def start_xy(self):
        self._xy(0).start()
        self._xy(1).start()

    def xy_to_last(self):
        self._xy(0).wait()
        self._xy(2).start()
        self._xy(1).wait()
        self._xy(3).start()

    def finish(self):
        self._xy(2).wait()
        self._xy(3).wait()


class Swap:
    def __init__(self, own, full, send, recv, local):
        self.own, self.full, self.send, self.recv, self.local = own, full, send, recv, local

    def _far(self):
        z, y, c, x = place()
        return remote(self.own, self.full.at[1 - c], self.send.at[0], self.recv.at[0], at(z, y, 1 - c, 1 - x))

    def _near(self):
        z, y, c, x = place()
        return pltpu.make_async_copy(self.own, self.full.at[c], self.local)

    def _core(self):
        z, y, c, x = place()
        spot = self.full.at[c]
        return remote(spot, spot, self.send.at[1], self.recv.at[1], at(z, y, 1 - c, x))

    def start(self):
        z, y, c, x = place()

        @pl.when(c != x)
        def _():
            self._far().start()

        @pl.when(c == x)
        def _():
            self._near().start()

    def share(self):
        z, y, c, x = place()

        @pl.when(c != x)
        def _():
            self._far().wait()

        @pl.when(c == x)
        def _():
            self._near().wait()

        self._core().start()

    def finish(self):
        self._core().wait()


COLS = (768, 256, 1024, 1024)


class SmallGather:
    def __init__(self, own, full, send, recv):
        self.own, self.full, self.send, self.recv = own, full, send, recv

    def _copy(self, k):
        z, y, c, x = place()
        send, recv = self.send.at[k], self.recv.at[k]
        if k == 0:
            return remote(self.own, self.full.at[x, z, y, c], send, recv, at(z, y, 1 - c, x))
        if k <= 3:
            spot = self.full.at[x, z, y]
            return remote(spot, spot, send, recv, at(lax.rem(z + k, 4), y, c, x))
        if k == 4:
            spot = self.full.at[x, :, y]
            return remote(spot, spot, send, recv, at(z, 1 - y, c, x))
        spot = self.full.at[x]
        return remote(spot, spot, send, recv, at(z, y, c, 1 - x))

    def start(self):
        z, y, c, x = place()
        self.full[x, z, y, c] = self.own[...]
        self._copy(0).start()

    def step(self, done, begin):
        for k in done:
            self._copy(k).wait()
        for k in begin:
            self._copy(k).start()


def ada_products(small_full, ada, wide, part, silu_out):
    z, y, c, x = place()
    wide[...] = jnp.zeros_like(wide)
    wide[block(c, 64), :] = ada[...]
    row = z * 2 + y
    lhs = jnp.concatenate(
        [small_full[x, zz, yy, cc, pl.ds(row, 1), :] for zz in range(4) for yy in range(2) for cc in range(2)], 0
    )
    silu_out[...] = lhs
    lhs = lhs.astype(BF)
    part[...] = jnp.zeros_like(part)
    for j in range(6):
        product = jnp.dot(lhs, wide[:, j * 512 : (j + 1) * 512], preferred_element_type=F32)
        for b in range(16):
            part[b // 4, b // 2 % 2, b % 2, j : j + 1, :] = product[b : b + 1, :]


def widen(small_full, row, k, width=1024):
    pieces = jnp.concatenate(
        [
            small_full[xx, zz, yy, cc, row : row + 1, :]
            for zz in range(4)
            for yy in range(2)
            for cc in range(2)
            for xx in range(2)
        ],
        0,
    ).astype(BF)
    lane = lax.broadcasted_iota(jnp.int32, (128, width), 1)
    source = lax.broadcasted_iota(jnp.int32, (128, width), 0)
    pick = jnp.where(source == k * 32 + lax.rem(lane, 32), 1.0, 0.0).astype(BF)
    spread_out = jnp.dot(pieces, pick, preferred_element_type=F32)
    device = lax.broadcasted_iota(jnp.int32, (32, width), 0)
    lane = lax.broadcasted_iota(jnp.int32, (32, width), 1)
    return jnp.sum(jnp.where(lane // 32 == device, spread_out, 0.0), 0, keepdims=True)


def start_kernel(
    lat, wq, wp, wu, wd, small, ada,
    lat_full, gq, gp, gu, gd, vectors, up_bias, silu_out,
    small_full, wide, part, near_c, near_y, near_z, mods, send, recv, local,
):
    z, y, c, x = place()
    greet(partners(True))
    swap = Swap(lat, lat_full, send.at[4], recv.at[4], local.at[4])
    q, p, u, d = [
        Gather(own, full, send.at[i], recv.at[i], local.at[i])
        for i, (own, full) in enumerate(((wq, gq), (wp, gp), (wu, gu), (wd, gd)))
    ]
    little = SmallGather(small, small_full, send.at[5], recv.at[5])
    little.start()
    q.start_core()
    swap.start()
    for group in (p, u, d):
        group.start_core()
    q.wait_core()
    q.start_z()
    little.step((0,), (1, 2, 3))
    little.step((1, 2, 3), (4,))
    little.step((4,), (5,))
    ada_products(small_full, ada, wide, part, silu_out)
    first = remote(part.at[:, :, 1 - c], near_c, send.at[6, 0], recv.at[6, 0], at(z, y, 1 - c, x))
    first.start()
    first.wait()
    for zz in range(4):
        for yy in range(2):
            near_c[zz, yy] = near_c[zz, yy] + part[zz, yy, c]
    second = remote(near_c.at[:, 1 - y], near_y, send.at[6, 1], recv.at[6, 1], at(z, 1 - y, c, x))
    second.start()
    second.wait()
    for zz in range(4):
        near_y[zz] = near_y[zz] + near_c[zz, y]
    thirds = []
    for s in (1, 2, 3):
        to = lax.rem(z + s, 4)
        copy = remote(near_y.at[to], near_z.at[s - 1], send.at[6, 1 + s], recv.at[6, 1 + s], at(to, y, c, x))
        copy.start()
        thirds.append(copy)
    for copy in thirds:
        copy.wait()
    near_z[3] = near_y[z] + near_z[0] + near_z[1] + near_z[2]
    fourth = remote(near_z.at[3], mods.at[1 - c], send.at[6, 5], recv.at[6, 5], at(z, y, 1 - c, 1 - x))

    @pl.when(c != x)
    def _():
        fourth.start()

    q.wait_z()
    q.start_xy()
    for group in (p, u):
        group.wait_core()
        group.start_z()

    @pl.when(c != x)
    def _():
        fourth.wait()

    @pl.when(c == x)
    def _():
        mods[c] = near_z[3]

    fifth = remote(mods.at[c], mods.at[c], send.at[6, 6], recv.at[6, 6], at(z, y, 1 - c, x))
    fifth.start()
    swap.share()
    little.step((5,), ())
    bias = [widen(small_full, 8, k) for k in range(4)]
    ada_bias = [widen(small_full, 10 + j // 4, j % 4) for j in range(6)]
    for zz in range(4):
        for yy in range(2):
            for cc in range(2):
                for xx in range(2):
                    device = ((zz * 2 + yy) * 2 + cc) * 2 + xx
                    up_bias[:, device * 128 : (device + 1) * 128] = small_full[xx, zz, yy, cc, 9:10, :]
    fifth.wait()
    for j in range(6):
        for h in range(2):
            lanes = slice(h * 512, (h + 1) * 512)
            vectors[j : j + 1, lanes] = mods[h, j : j + 1, :] + ada_bias[j][:, lanes]
    for k in range(4):
        vectors[6 + k : 7 + k, :] = bias[k]
    q.xy_to_last()
    swap.finish()
    d.wait_core()
    p.wait_z()
    u.wait_z()
    q.finish()


def start(lat, wq, wp, wu, wd, small, ada):
    outs = [jax.ShapeDtypeStruct((2, 512, 1024), BF)]
    outs += [jax.ShapeDtypeStruct((2, 4, 2, 128, n), BF) for n in COLS]
    outs += [jax.ShapeDtypeStruct((16, 1024), F32), jax.ShapeDtypeStruct((1, 4096), F32)]
    outs += [jax.ShapeDtypeStruct((16, 128), F32)]
    return pl.pallas_call(
        start_kernel,
        out_shape=outs,
        in_specs=[IN_ANY] * 5 + [IN_VMEM] * 2,
        out_specs=[IN_ANY] * 5 + [IN_VMEM] * 3,
        scratch_shapes=[
            pltpu.VMEM((2, 4, 2, 2, 16, 128), F32),
            pltpu.VMEM((128, 3072), BF),
            pltpu.VMEM((4, 2, 2, 8, 512), F32),
            pltpu.VMEM((4, 2, 8, 512), F32),
            pltpu.VMEM((4, 8, 512), F32),
            pltpu.VMEM((4, 8, 512), F32),
            pltpu.VMEM((2, 8, 512), F32),
            pltpu.SemaphoreType.DMA((7, 8)),
            pltpu.SemaphoreType.DMA((7, 8)),
            pltpu.SemaphoreType.DMA((5,)),
        ],
        compiler_params=pltpu.CompilerParams(
            collective_id=0, has_side_effects=True, vmem_limit_bytes=60 * MIB
        ),
        name="start",
    )(lat, wq, wp, wu, wd, small, ada)


def normalise(values):
    centred = values - jnp.mean(values, axis=-1, keepdims=True)
    scale = lax.rsqrt(jnp.mean(centred * centred, axis=-1, keepdims=True) + epsilon)
    return centred * scale, scale


def nn(a, b):
    return jnp.dot(a, b, preferred_element_type=F32)


def nt(a, b):
    return lax.dot_general(a, b, (((1,), (1,)), ((), ())), preferred_element_type=F32)


def tn(a, b):
    return lax.dot_general(a, b, (((0,), (0,)), ((), ())), preferred_element_type=F32)


def in_half(h):
    return lax.broadcasted_iota(jnp.int32, (1, 128), 1) // 64 == h


class Pair:
    def __init__(self, mine, theirs, send, recv):
        self.mine, self.theirs, self.send, self.recv = mine, theirs, send, recv

    def _copy(self, i):
        z, y, c, x = place()
        rows = block(i, 256)
        return remote(
            self.mine.at[rows], self.theirs.at[rows], self.send.at[i], self.recv.at[i], at(z, y, 1 - c, x)
        )

    def give(self, i, partial):
        self.mine[block(i, 256), :] = partial.astype(BF)
        self._copy(i).start()

    def take(self, i):
        self._copy(i).wait()
        rows = block(i, 256)
        return self.mine[rows, :].astype(F32) + self.theirs[rows, :].astype(F32)


def loop(count, body):
    def step(i, carry):
        body(i)
        return carry

    lax.fori_loop(0, count, step, 0)


def attend_kernel(
    lat, vectors, gq, gp_in, gu_in, gd_in, grad,
    attn_in, packed, heads_out, lse, branch_one, middle, grad_full, gp, gu, gd,
    wp, mine, theirs, send, recv, local,
):
    z, y, c, x = place()
    greet(partners(True))
    swap = Swap(grad, grad_full, send.at[3], recv.at[3], local.at[3])
    p, u, d = [Gather(None, full, send.at[i], recv.at[i], local.at[i]) for i, full in enumerate((gp, gu, gd))]
    p.start_xy()
    u.start_xy()
    d.start_z()
    swap.start()

    def modulated(i):
        rows = lat[i // 2, block(lax.rem(i, 2), 256), :].astype(F32)
        normal, _ = normalise(rows)
        attn_in[block(i, 256), :] = (normal * (1.0 + vectors[1:2, :]) + vectors[0:1, :]).astype(BF)

    loop(4, modulated)

    def project(i):
        b, rows = i // 2, block(lax.rem(i, 2), 512)
        columns = pl.ds(pl.multiple_of(b * 512 + c * 256, 256), 256)
        values = nn(attn_in[rows, :], gq[b])
        packed[b, rows, 0:256] = (values[:, 0:256] + vectors[6:7, columns]).astype(BF)
        packed[b, rows, 256:512] = values[:, 256:512].astype(BF)
        packed[b, rows, 512:768] = (values[:, 512:768] + vectors[7:8, columns]).astype(BF)

    loop(4, project)
    p.xy_to_last()
    lane = lax.broadcasted_iota(jnp.int32, (1, 128), 1)

    def attend(i):
        pair, rows = i // 2, block(lax.rem(i, 2), 512)
        b, q_at = pair // 2, pl.multiple_of(lax.rem(pair, 2) * 128, 128)
        queries = packed[b, rows, pl.ds(q_at, 128)] * BF(0.125)
        keys = packed[b, :, pl.ds(q_at + 256, 128)]
        values = packed[b, :, pl.ds(q_at + 512, 128)]
        result = None
        logs = lse[rows, :]
        for h in range(2):
            scores = nt(jnp.where(in_half(h), queries, jnp.zeros_like(queries)), keys)
            largest = jnp.max(scores, -1, keepdims=True)
            exponent = jnp.exp(scores - largest)
            summed = jnp.sum(exponent, -1, keepdims=True)
            mixture = nn(exponent.astype(BF), values) * (1.0 / summed)
            result = mixture if h == 0 else jnp.where(in_half(0), result, mixture)
            logs = jnp.where(lane == pair * 2 + h, largest + jnp.log(summed), logs)
        heads_out[b, rows, pl.ds(q_at, 128)] = result.astype(BF)
        lse[rows, :] = logs

        @pl.when(i == 3)
        def _():
            u.xy_to_last()

    lse[...] = jnp.zeros_like(lse)
    loop(8, attend)
    p.finish()
    load = pltpu.make_async_copy(gp, wp, local.at[0])
    load.start()
    load.wait()
    pair = Pair(mine, theirs, send.at[4], recv.at[4])

    def out(i):
        rows = block(i, 256)
        partial = nt(heads_out[0, rows, :], wp[0].reshape(1024, 256))
        pair.give(i, partial + nt(heads_out[1, rows, :], wp[1].reshape(1024, 256)))

    loop(4, out)

    def residual(i):
        rows = block(i, 256)
        branch = pair.take(i) + vectors[8:9, :]
        branch_one[rows, :] = branch.astype(BF)
        middle[rows, :] = lat[i // 2, block(lax.rem(i, 2), 256), :].astype(F32) + vectors[2:3, :] * branch

    loop(4, residual)
    swap.share()
    d.wait_z()
    u.finish()
    swap.finish()


def attend_pairs(lat, vectors, gq, gp, gu, gd, grad):
    full = lambda n: jax.ShapeDtypeStruct((2, 4, 2, 128, n), BF)
    tokens = lambda dtype: jax.ShapeDtypeStruct((1024, 1024), dtype)
    return pl.pallas_call(
        attend_kernel,
        out_shape=[
            tokens(BF),
            jax.ShapeDtypeStruct((2, 1024, 768), BF),
            jax.ShapeDtypeStruct((2, 1024, 256), BF),
            jax.ShapeDtypeStruct((1024, 128), F32),
            tokens(BF),
            tokens(F32),
            jax.ShapeDtypeStruct((2, 512, 1024), BF),
            full(256),
            full(1024),
            full(1024),
        ],
        in_specs=[IN_VMEM] * 3 + [IN_ANY] * 4,
        out_specs=[IN_VMEM] * 6 + [IN_ANY] * 4,
        scratch_shapes=[
            pltpu.VMEM((2, 4, 2, 128, 256), BF),
            pltpu.VMEM((1024, 1024), BF),
            pltpu.VMEM((1024, 1024), BF),
            pltpu.SemaphoreType.DMA((5, 8)),
            pltpu.SemaphoreType.DMA((5, 8)),
            pltpu.SemaphoreType.DMA((4,)),
        ],
        input_output_aliases={3: 7, 4: 8, 5: 9},
        compiler_params=pltpu.CompilerParams(
            collective_id=1, has_side_effects=True, vmem_limit_bytes=60 * MIB
        ),
        name="attend",
    )(lat, vectors, gq, gp, gu, gd, grad)


class Scatter:
    def __init__(self, send, recv, part=None, first_a=None, first_b=None, second=None, third=None, total=None, out=None):
        self.part, self.first_a, self.first_b = part, first_a, first_b
        self.second, self.third, self.total, self.out = second, third, total, out
        self.send, self.recv = send, recv

    def _copy(self, k):
        z, y, c, x = place()
        send, recv = self.send.at[k], self.recv.at[k]
        if k == 0:
            return remote(self.part.at[:, pl.ds(0, 2), 1 - y], self.first_a, send, recv, at(z, 1 - y, c, x))
        if k == 1:
            return remote(self.part.at[1 - x, pl.ds(2, 2)], self.first_b, send, recv, at(z, y, c, 1 - x))
        if k == 2:
            return remote(self.first_a.at[1 - x], self.second.at[pl.ds(0, 2)], send, recv, at(z, y, c, 1 - x))
        if k == 3:
            return remote(self.first_b.at[:, 1 - y], self.second.at[pl.ds(2, 2)], send, recv, at(z, 1 - y, c, x))
        if k <= 6:
            d = k - 3
            to = lax.rem(z + d, 4)
            return remote(self.second.at[to], self.third.at[d - 1], send, recv, at(to, y, c, x))
        return remote(self.total.at[block(1 - c, 64)], self.out.at[c], send, recv, at(z, y, 1 - c, x))

    def start(self):
        self._copy(0).start()
        self._copy(1).start()

    def turn(self):
        z, y, c, x = place()
        self._copy(0).wait()

        def add_a(i):
            b, zz = i // 2, lax.rem(i, 2)
            total = self.first_a[b, zz].astype(F32) + self.part[b, zz, y].astype(F32)
            self.first_a[b, zz] = total.astype(BF)

        loop(4, add_a)
        self._copy(2).start()
        self._copy(1).wait()

        def add_b(i):
            zz, yy = i // 2, lax.rem(i, 2)
            total = self.first_b[zz, yy].astype(F32) + self.part[x, 2 + zz, yy].astype(F32)
            self.first_b[zz, yy] = total.astype(BF)

        loop(4, add_b)
        self._copy(3).start()

    def finish_xy(self):
        z, y, c, x = place()
        self._copy(2).wait()

        def add_a(i):
            self.second[i] = (self.second[i].astype(F32) + self.first_a[x, i].astype(F32)).astype(BF)

        loop(2, add_a)
        self._copy(3).wait()

        def add_b(i):
            self.second[2 + i] = (self.second[2 + i].astype(F32) + self.first_b[i, y].astype(F32)).astype(BF)

        loop(2, add_b)

    def start_z(self):
        for k in (4, 5, 6):
            self._copy(k).start()

    def finish_z(self):
        z, y, c, x = place()
        for k in (4, 5, 6):
            self._copy(k).wait()

        def add(i):
            rows = block(i, 64)
            total = self.second[z, rows].astype(F32)
            for d in range(3):
                total = total + self.third[d, rows].astype(F32)
            self.total[rows] = total

        loop(2, add)
        self._copy(7).start()
        self.out[c] = self.total[block(c, 64)]

    def finish(self):
        self._copy(7).wait()


def scatter_xy_buffers(n):
    return [
        pltpu.VMEM((2, 2, 128, n), BF),
        pltpu.VMEM((2, 2, 128, n), BF),
    ]


def gelu_parts(v):
    k = math.sqrt(2.0 / math.pi)
    square = v * v
    t = jnp.tanh(k * v * (1.0 + 0.044715 * square))
    half = 0.5 * (1.0 + t)
    return v * half, half + 0.5 * k * v * (1.0 - t * t) * (1.0 + 3.0 * 0.044715 * square)


def mlp_kernel(
    middle_in, grad, branch_one, vectors, up_bias, gu, gd_in,
    block_out, middle_grad, g_one, up_grad, second, stats, up_sums, gd,
    mlp_in, g_two, slope, part, first_a, first_b, wd, mine, theirs, theirs_two, send, recv, local,
):
    z, y, c, x = place()
    active, hidden_grad = up_grad, slope
    load = pltpu.make_async_copy(middle_in, middle_grad, local.at[1])
    load.start()
    greet(partners())
    d = Gather(None, gd, send.at[0], recv.at[0], local.at[0])
    down = Scatter(send.at[1], recv.at[1], part=part, first_a=first_a, first_b=first_b, second=second)
    d.start_xy()
    stats[...] = jnp.zeros_like(stats)
    up_sums[...] = jnp.zeros_like(up_sums)
    load.wait()

    def enter(i):
        rows = block(i, 128)
        normal, _ = normalise(middle_grad[rows, :])
        mlp_in[rows, :] = (normal * (1.0 + vectors[4:5, :]) + vectors[3:4, :]).astype(BF)
        g = (grad[i // 4, block(lax.rem(i, 4), 128), :].astype(F32) * vectors[5:6, :]).astype(BF)
        g_two[rows, :] = g
        mine_too = jnp.where(i // 4 == c, 1.0, 0.0)
        stats[1:2, :] += jnp.sum(g.astype(F32), 0, keepdims=True) * mine_too

    loop(8, enter)

    def ascend(i):
        b, quarter = i // 4, lax.rem(i, 4)
        rows = block(quarter, 256)
        columns = pl.ds(pl.multiple_of(b * 2048 + c * 1024, 1024), 1024)
        value, gradient = gelu_parts(nn(mlp_in[rows, :], gu[b]) + up_bias[:, columns])
        active[b, quarter] = value.astype(BF).reshape(2, 128, 1024)
        slope[b, rows, :] = gradient.astype(BF)

    loop(8, ascend)
    d.xy_to_last()

    def down_gradient(i):
        b, zz = i // 2, lax.rem(i, 2)
        value = tn(g_two[:, block(zz, 512)], active[b].reshape(1024, 1024))
        part[b, pl.ds(zz * 2, 2)] = value.astype(BF).reshape(2, 2, 128, 1024)

    loop(4, down_gradient)
    down.start()
    d.finish()
    load = pltpu.make_async_copy(gd, wd, local.at[0])
    load.start()
    load.wait()
    pair = Pair(mine, theirs, send.at[2], recv.at[2])

    def descend(i):
        partial = nt(active[0, i].reshape(256, 1024), wd[0].reshape(1024, 1024))
        pair.give(i, partial + nt(active[1, i].reshape(256, 1024), wd[1].reshape(1024, 1024)))

    loop(4, descend)

    def hidden_gradient(i):
        b, rows = i // 4, block(lax.rem(i, 4), 256)
        value = nn(g_two[rows, :], wd[b].reshape(1024, 1024)) * slope[b, rows, :].astype(F32)
        value = value.astype(BF)
        hidden_grad[b, rows, :] = value
        up_sums[b] += jnp.sum(value.astype(F32), 0, keepdims=True)

    loop(8, hidden_gradient)

    def leave(i):
        rows = block(i, 256)
        g = grad[i // 2, block(lax.rem(i, 2), 256), :].astype(F32)
        branch_two = pair.take(i) + vectors[9:10, :]
        block_out[rows, :] = (middle_grad[rows, :] + vectors[5:6, :] * branch_two).astype(BF)
        stats[0:1, :] += jnp.sum(g * branch_two, 0, keepdims=True)

    loop(4, leave)
    back = Pair(mine, theirs_two, send.at[3], recv.at[3])

    def descend_back(i):
        rows = block(i, 256)
        back.give(i, nt(hidden_grad[0, rows, :], gu[0]) + nt(hidden_grad[1, rows, :], gu[1]))

    loop(4, descend_back)
    down.turn()

    def up_gradient(i):
        b, zz = i // 2, lax.rem(i, 2)
        value = tn(mlp_in[:, block(zz, 512)], hidden_grad[b])
        up_grad[b, pl.ds(zz * 2, 2)] = value.astype(BF).reshape(2, 2, 128, 1024)

    loop(4, up_gradient)

    def residual(i):
        rows = block(i, 256)
        dy = back.take(i)
        normal, scale = normalise(middle_grad[rows, :])
        stats[2:3, :] += jnp.sum(dy, 0, keepdims=True)
        stats[3:4, :] += jnp.sum(dy * normal, 0, keepdims=True)
        dn = dy * (1.0 + vectors[4:5, :])
        dn = dn - jnp.mean(dn, -1, keepdims=True) - normal * jnp.mean(dn * normal, -1, keepdims=True)
        total = grad[i // 2, block(lax.rem(i, 2), 256), :].astype(F32) + scale * dn
        middle_grad[rows, :] = total
        stats[4:5, :] += jnp.sum(total * branch_one[rows, :].astype(F32), 0, keepdims=True)
        g = (total * vectors[2:3, :]).astype(BF)
        g_one[rows, :] = g
        mine_too = jnp.where(i // 2 == c, 1.0, 0.0)
        stats[5:6, :] += jnp.sum(g.astype(F32), 0, keepdims=True) * mine_too

    loop(4, residual)
    down.finish_xy()


def mlp(middle, grad, branch_one, vectors, up_bias, gu, gd):
    full = jax.ShapeDtypeStruct((2, 4, 2, 128, 1024), BF)
    tokens = lambda dtype: jax.ShapeDtypeStruct((1024, 1024), dtype)
    wide = pltpu.VMEM((1024, 1024), BF)
    return pl.pallas_call(
        mlp_kernel,
        out_shape=[
            tokens(BF),
            tokens(F32),
            tokens(BF),
            full,
            jax.ShapeDtypeStruct((4, 128, 1024), BF),
            jax.ShapeDtypeStruct((8, 1024), F32),
            jax.ShapeDtypeStruct((2, 1, 1024), F32),
            full,
        ],
        in_specs=[IN_ANY] + [IN_VMEM] * 5 + [IN_ANY],
        out_specs=[IN_VMEM] * 7 + [IN_ANY],
        scratch_shapes=[
            wide,
            wide,
            pltpu.VMEM((2, 1024, 1024), BF),
            pltpu.VMEM((2, 4, 2, 128, 1024), BF),
            *scatter_xy_buffers(1024),
            pltpu.VMEM((2, 4, 2, 128, 1024), BF),
            wide,
            wide,
            wide,
            pltpu.SemaphoreType.DMA((4, 8)),
            pltpu.SemaphoreType.DMA((4, 8)),
            pltpu.SemaphoreType.DMA((2,)),
        ],
        input_output_aliases={6: 7},
        compiler_params=pltpu.CompilerParams(
            collective_id=2, has_side_effects=True, vmem_limit_bytes=62 * MIB
        ),
        name="mlp",
    )(middle, grad, branch_one, vectors, up_bias, gu, gd)


def back_kernel(
    lat, vectors, g_one, gp, gq, attn_in, packed_in, heads_out, lse, middle_grad_in, up_in, down_second, block_in,
    input_grad, qkv_grad, proj_grad, up_second, down_out, stats, sums, block_out,
    heads_grad, packed, packed_grad, delta, key_total, value_total, part, first_a, first_b, third, total_rows,
    mine, theirs, middle_grad, send, recv, local,
):
    z, y, c, x = place()
    loads = [
        pltpu.make_async_copy(source, target, local.at[i])
        for i, (source, target) in enumerate(((up_in, part), (packed_in, packed), (middle_grad_in, middle_grad)))
    ]
    for load in loads:
        load.start()
    greet(partners(True))
    up = Scatter(send.at[0], recv.at[0], part=part, first_a=first_a, first_b=first_b, second=up_second)
    down = Scatter(send.at[1], recv.at[1], second=down_second, third=third, total=total_rows, out=down_out)
    loads[0].wait()
    up.start()
    down.start_z()
    swap = SwapBack(block_in, block_out, send.at[3, 0], recv.at[3, 0], local.at[3])
    swap.start()
    loads[1].wait()
    sums[...] = jnp.zeros_like(sums)
    stats[...] = jnp.zeros_like(stats)
    lane = lax.broadcasted_iota(jnp.int32, (1, 128), 1)

    def enter(i):
        b, rows = i // 2, block(lax.rem(i, 2), 512)
        value = nn(g_one[rows, :], gp[b]).astype(BF)
        heads_grad[b, rows, :] = value
        products = value.astype(F32) * heads_out[b, rows, :].astype(F32)
        found = delta[rows, :]
        for h in range(4):
            wide = products[:, h // 2 * 128 : h // 2 * 128 + 128]
            total = jnp.sum(jnp.where(in_half(h % 2), wide, 0.0), -1, keepdims=True)
            found = jnp.where(lane == b * 4 + h, total, found)
        delta[rows, :] = found

    delta[...] = jnp.zeros_like(delta)
    loop(4, enter)

    def proj_gradient(i):
        b, half = i // 2, lax.rem(i, 2)
        value = tn(g_one[:, block(half, 512)], heads_out[b])
        proj_grad[b, pl.ds(half * 2, 2)] = value.astype(BF).reshape(2, 2, 128, 256)

    loop(4, proj_gradient)

    def attend(i):
        pair, quarter = i // 4, lax.rem(i, 4)
        rows = block(quarter, 256)
        b, at_lane = pair // 2, pl.multiple_of(lax.rem(pair, 2) * 128, 128)
        queries = packed[b, rows, pl.ds(at_lane, 128)] * BF(0.125)
        keys = packed[b, :, pl.ds(at_lane + 256, 128)]
        values = packed[b, :, pl.ds(at_lane + 512, 128)]
        grads = heads_grad[b, rows, pl.ds(at_lane, 128)]

        @pl.when(quarter == 0)
        def _():
            key_total[...] = jnp.zeros_like(key_total)
            value_total[...] = jnp.zeros_like(value_total)

        result = None
        logs, deltas = lse[rows, :], delta[rows, :]
        for h in range(2):
            column = lane == pair * 2 + h
            log = jnp.sum(jnp.where(column, logs, 0.0), -1, keepdims=True)
            inner = jnp.sum(jnp.where(column, deltas, 0.0), -1, keepdims=True)
            query = jnp.where(in_half(h), queries, jnp.zeros_like(queries))
            grad = jnp.where(in_half(h), grads, jnp.zeros_like(grads))
            probs = jnp.exp(nt(query, keys) - log)
            score_grad = (probs * (nt(grad, values) - inner)).astype(BF)
            query_grad = nn(score_grad, keys)
            result = query_grad if h == 0 else jnp.where(in_half(0), result, query_grad)
            key_total[...] += tn(score_grad, query)
            value_total[...] += tn(probs.astype(BF), grad)
        result = (result * 0.125).astype(BF)
        packed_grad[b, rows, pl.ds(at_lane, 128)] = result
        sums[b, :, pl.ds(at_lane, 128)] += jnp.sum(result.astype(F32), 0, keepdims=True)

        @pl.when(quarter == 3)
        def _():
            packed_grad[b, :, pl.ds(at_lane + 256, 128)] = key_total[...].astype(BF)
            total = value_total[...].astype(BF)
            packed_grad[b, :, pl.ds(at_lane + 512, 128)] = total
            sums[b, :, pl.ds(at_lane + 512, 128)] = jnp.sum(total.astype(F32), 0, keepdims=True)

        @pl.when(i == 9)
        def _():
            up.turn()

    loop(16, attend)
    down.finish_z()
    pair = Pair(mine, theirs, send.at[2], recv.at[2])

    def descend(i):
        rows = block(i, 256)
        pair.give(i, nt(packed_grad[0, rows, :], gq[0]) + nt(packed_grad[1, rows, :], gq[1]))

    loop(4, descend)

    def qkv_gradient(i):
        b, half = i // 2, lax.rem(i, 2)
        value = tn(attn_in[:, block(half, 512)], packed_grad[b])
        qkv_grad[b, pl.ds(half * 2, 2)] = value.astype(BF).reshape(2, 2, 128, 768)

    loop(4, qkv_gradient)
    loads[2].wait()

    def leave(i):
        rows = block(i, 256)
        dy = pair.take(i)
        normal, scale = normalise(lat[i // 2, block(lax.rem(i, 2), 256), :].astype(F32))
        stats[0:1, :] += jnp.sum(dy, 0, keepdims=True)
        stats[1:2, :] += jnp.sum(dy * normal, 0, keepdims=True)
        dn = dy * (1.0 + vectors[1:2, :])
        dn = dn - jnp.mean(dn, -1, keepdims=True) - normal * jnp.mean(dn * normal, -1, keepdims=True)
        input_grad[i // 2, block(lax.rem(i, 2), 256), :] = (middle_grad[rows, :] + scale * dn).astype(BF)

    loop(4, leave)
    down.finish()
    swap.finish()
    up.finish_xy()


class SwapBack:
    def __init__(self, full, out, send, recv, local):
        self.full, self.out, self.send, self.recv, self.local = full, out, send, recv, local

    def _far(self):
        z, y, c, x = place()
        return remote(self.full.at[c], self.out, self.send, self.recv, at(z, y, 1 - c, 1 - x))

    def _near(self):
        z, y, c, x = place()
        return pltpu.make_async_copy(self.full.at[c], self.out, self.local)

    def _both(self, act):
        z, y, c, x = place()

        @pl.when(c != x)
        def _():
            act(self._far())

        @pl.when(c == x)
        def _():
            act(self._near())

    def start(self):
        self._both(lambda copy: copy.start())

    def finish(self):
        self._both(lambda copy: copy.wait())


def attend_back(*args):
    wide = pltpu.VMEM((1024, 1024), BF)
    return pl.pallas_call(
        back_kernel,
        out_shape=[
            jax.ShapeDtypeStruct((2, 512, 1024), BF),
            jax.ShapeDtypeStruct((2, 4, 2, 128, 768), BF),
            jax.ShapeDtypeStruct((2, 4, 2, 128, 256), BF),
            jax.ShapeDtypeStruct((4, 128, 1024), BF),
            jax.ShapeDtypeStruct((2, 64, 1024), F32),
            jax.ShapeDtypeStruct((8, 1024), F32),
            jax.ShapeDtypeStruct((2, 1, 768), F32),
            jax.ShapeDtypeStruct((512, 1024), BF),
        ],
        in_specs=[IN_VMEM] * 6 + [IN_ANY] + [IN_VMEM] * 2 + [IN_ANY] * 2 + [IN_VMEM] + [IN_ANY],
        out_specs=[IN_VMEM] * 7 + [IN_ANY],
        scratch_shapes=[
            pltpu.VMEM((2, 1024, 256), BF),
            pltpu.VMEM((2, 1024, 768), BF),
            pltpu.VMEM((2, 1024, 768), BF),
            pltpu.VMEM((1024, 128), F32),
            pltpu.VMEM((1024, 128), F32),
            pltpu.VMEM((1024, 128), F32),
            pltpu.VMEM((2, 4, 2, 128, 1024), BF),
            *scatter_xy_buffers(1024),
            pltpu.VMEM((3, 128, 1024), BF),
            pltpu.VMEM((128, 1024), F32),
            wide,
            wide,
            pltpu.VMEM((1024, 1024), F32),
            pltpu.SemaphoreType.DMA((4, 8)),
            pltpu.SemaphoreType.DMA((4, 8)),
            pltpu.SemaphoreType.DMA((4,)),
        ],
        compiler_params=pltpu.CompilerParams(
            collective_id=3, has_side_effects=True, vmem_limit_bytes=62 * MIB
        ),
        name="attend_back",
    )(*args)


class SmallScatter:
    def __init__(self, part, near_c, near_x, near_y, near_z, send, recv):
        self.part, self.near_c, self.near_x, self.near_y, self.near_z = part, near_c, near_x, near_y, near_z
        self.send, self.recv = send, recv

    def _copy(self, k):
        z, y, c, x = place()
        send, recv = self.send.at[k], self.recv.at[k]
        if k == 0:
            return remote(self.part.at[1 - c], self.near_c, send, recv, at(z, y, 1 - c, x))
        if k == 1:
            return remote(self.near_c.at[1 - x], self.near_x, send, recv, at(z, y, c, 1 - x))
        if k == 2:
            return remote(self.near_x.at[1 - y], self.near_y, send, recv, at(z, 1 - y, c, x))
        d = k - 2
        to = lax.rem(z + d, 4)
        return remote(self.near_y.at[to], self.near_z.at[d - 1], send, recv, at(to, y, c, x))

    def start(self):
        self._copy(0).start()

    def step(self, k):
        z, y, c, x = place()
        self._copy(k).wait()
        if k == 0:
            self.near_c[...] = self.near_c[...] + self.part[c]
            self._copy(1).start()
        elif k == 1:
            self.near_x[...] = self.near_x[...] + self.near_c[x]
            self._copy(2).start()
        else:
            self.near_y[...] = self.near_y[...] + self.near_x[y]
            for j in (3, 4, 5):
                self._copy(j).start()

    def finish(self):
        z, y, c, x = place()
        for j in (3, 4, 5):
            self._copy(j).wait()
        return self.near_y[z] + self.near_z[0] + self.near_z[1] + self.near_z[2]


def split_bf(values):
    high = values.astype(BF)
    return high, (values - high.astype(F32)).astype(BF)


def exact_nn(values, chosen):
    high, low = split_bf(values)
    lower = (values - high.astype(F32) - low.astype(F32)).astype(BF)
    return nn(high, chosen) + nn(low, chosen) + nn(lower, chosen)


def narrow(vector, k):
    device = lax.broadcasted_iota(jnp.int32, (32, 1024), 0)
    lane = lax.broadcasted_iota(jnp.int32, (32, 1024), 1)
    source = lax.broadcasted_iota(jnp.int32, (1024, 128), 0)
    target = lax.broadcasted_iota(jnp.int32, (1024, 128), 1)
    chosen = jnp.where(target == k * 32 + lax.rem(source, 32), 1.0, 0.0).astype(BF)
    return exact_nn(jnp.where(lane // 32 == device, vector, 0.0), chosen)


def finish_kernel(
    stats_mlp, stats, sums, up_sums, silu, cond, ada, input_grad, qkv_grad, proj_grad, up_second,
    input_out, q_out, p_out, u_out, ada_out, cond_out, ada_bias_out, bias_out,
    q_a, q_b, q_second, q_third, q_total, p_a, p_b, p_second, p_third, p_total, u_third, u_total,
    columns, bias_part, near_c, near_x, near_y, near_z, own_mods, mods, wide, tall,
    found, other, spread_x, spread_c, spread_y, spread_z, picked, picked_other,
    send, recv, local,
):
    z, y, c, x = place()
    greet(partners(True))
    q = Scatter(send.at[0], recv.at[0], qkv_grad, q_a, q_b, q_second, q_third, q_total, q_out)
    p = Scatter(send.at[1], recv.at[1], proj_grad, p_a, p_b, p_second, p_third, p_total, p_out)
    u = Scatter(send.at[2], recv.at[2], second=up_second, third=u_third, total=u_total, out=u_out)
    swap = SwapBack(input_grad, input_out, send.at[3, 0], recv.at[3, 0], local.at[0])
    q.start()
    p.start()
    u.start_z()
    swap.start()
    rows = (stats[0:1, :], stats[1:2, :], stats_mlp[4:5, :], stats_mlp[2:3, :], stats_mlp[3:4, :], stats_mlp[0:1, :])
    own_mods[...] = jnp.zeros_like(own_mods)
    for j in range(6):
        for h in range(2):
            own_mods[h, j : j + 1, :] = rows[j][:, h * 512 : (h + 1) * 512]
    far = remote(own_mods.at[1 - x], mods.at[z, y, 1 - c], send.at[4, 0], recv.at[4, 0], at(z, y, 1 - c, 1 - x))

    @pl.when(c != x)
    def _():
        far.start()

    @pl.when(c == x)
    def _():
        mods[z, y, c] = own_mods[x]

    columns[...] = jnp.zeros_like(columns)
    bias_part[...] = jnp.zeros_like(bias_part)
    for b in range(2):
        spot = pl.ds(pl.multiple_of(b * 512 + c * 256, 256), 256)
        columns[0:1, spot] = sums[b, :, 0:256]
        columns[1:2, spot] = sums[b, :, 512:768]
    columns[2:3, :] = stats_mlp[5:6, :]
    columns[3:4, :] = stats_mlp[1:2, :]
    pieces = narrow(columns[0:1, :], 0) + narrow(columns[1:2, :], 1)
    pieces = pieces + narrow(columns[2:3, :], 2) + narrow(columns[3:4, :], 3)
    for k in range(32):
        bias_part[k // 2 % 2, k % 2, k // 4 % 2, k // 8, 0:1, :] = pieces[k : k + 1, :]
    for b in range(2):
        for i in range(8):
            bias_part[i // 2 % 2, i % 2, i // 4, b * 2 + c, 1:2, :] = up_sums[b, :, i * 128 : (i + 1) * 128]
    bias = SmallScatter(bias_part, near_c, near_x, near_y, near_z, send.at[5], recv.at[5])
    bias.start()

    @pl.when(c != x)
    def _():
        far.wait()

    spot = mods.at[z, y, c]
    core = remote(spot, spot, send.at[4, 1], recv.at[4, 1], at(z, y, 1 - c, x))
    core.start()
    bias.step(0)
    core.wait()
    spot_y = mods.at[z, y]
    across = remote(spot_y, spot_y, send.at[4, 2], recv.at[4, 2], at(z, 1 - y, c, x))
    across.start()
    bias.step(1)
    across.wait()
    spot_z = mods.at[z]
    along = [
        remote(spot_z, spot_z, send.at[4, 2 + d], recv.at[4, 2 + d], at(lax.rem(z + d, 4), y, c, x)) for d in (1, 2, 3)
    ]
    for copy in along:
        copy.start()
    bias.step(2)
    wide[...] = jnp.zeros_like(wide)
    wide[block(c, 64), :] = ada[...]
    silu_rows = silu[...].astype(BF)
    for copy in along:
        copy.wait()
    total = jnp.zeros((16, 128), F32)
    bias_rows = []
    for j in range(6):
        values = jnp.concatenate([mods[b // 4, b // 2 % 2, b % 2, j : j + 1, :] for b in range(16)], 0)
        high, low = split_bf(values)
        lanes = slice(j * 512, (j + 1) * 512)
        tall[...] = tn(silu_rows, high) + tn(silu_rows, low)
        ada_out[:, lanes] = tall[block(c, 64), :]
        total = total + nt(high, wide[:, lanes]) + nt(low, wide[:, lanes])
        bias_rows.append(jnp.sum(values, 0, keepdims=True))
    found[...] = total
    group = (lax.rem(z, 2) * 2 + y) * 2 + c
    source = lax.broadcasted_iota(jnp.int32, (512, 128), 0)
    target = lax.broadcasted_iota(jnp.int32, (512, 128), 1)
    chosen = jnp.where((source == group * 64 + target) & (target < 64), 1.0, 0.0).astype(BF)
    picked[...] = exact_nn(jnp.concatenate(bias_rows + [jnp.zeros((2, 512), F32)], 0), chosen)
    to_x = at(z, y, c, 1 - x)
    first = [
        remote(found, other, send.at[6, 0], recv.at[6, 0], to_x),
        remote(picked, picked_other, send.at[6, 1], recv.at[6, 1], to_x),
    ]
    for copy in first:
        copy.start()
    for copy in first:
        copy.wait()
    ada_bias_out[...] = jnp.where(z // 2 == x, picked[...], picked_other[...])
    total = found[...] + other[...]
    for b in range(16):
        spread_x[b % 2, b // 2 % 2, b // 4] = total[b : b + 1, :]
    second = remote(spread_x.at[1 - c], spread_c, send.at[6, 2], recv.at[6, 2], at(z, y, 1 - c, x))
    second.start()
    bias_out[...] = bias.finish()
    second.wait()
    spread_c[...] = spread_c[...] + spread_x[c]
    third = remote(spread_c.at[1 - y], spread_y.at[y], send.at[6, 3], recv.at[6, 3], at(z, 1 - y, c, x))
    third.start()
    spread_y[y] = spread_c[y]
    third.wait()
    fourth = [
        remote(
            spread_y.at[:, lax.rem(z + d, 4)], spread_z.at[z], send.at[6, 3 + d], recv.at[6, 3 + d],
            at(lax.rem(z + d, 4), y, c, x),
        )
        for d in (1, 2, 3)
    ]
    for copy in fourth:
        copy.start()
    spread_z[z] = spread_y[:, z]
    for copy in fourth:
        copy.wait()
    v = cond[...]
    gate = 1.0 / (1.0 + jnp.exp(-v))
    row = jnp.concatenate([spread_z[b // 2, b % 2] for b in range(8)], 0)
    cond_out[...] = row * gate * (1.0 + v * (1.0 - gate))
    q.turn()
    p.turn()
    u.finish_z()
    p.finish_xy()
    p.start_z()
    q.finish_xy()
    q.start_z()
    u.finish()
    p.finish_z()
    q.finish_z()
    p.finish()
    swap.finish()
    q.finish()


def scatter_rest(n):
    return [
        *scatter_xy_buffers(n),
        pltpu.VMEM((4, 128, n), BF),
        pltpu.VMEM((3, 128, n), BF),
        pltpu.VMEM((128, n), F32),
    ]


def finish(*args):
    small = lambda *shape: pltpu.VMEM(shape, F32)
    out = lambda *shape: jax.ShapeDtypeStruct(shape, F32)
    return pl.pallas_call(
        finish_kernel,
        out_shape=[
            jax.ShapeDtypeStruct((512, 1024), BF),
            out(2, 64, 768),
            out(2, 64, 256),
            out(2, 64, 1024),
            out(64, 3072),
            out(8, 128),
            out(8, 128),
            out(2, 128),
        ],
        in_specs=[IN_VMEM] * 7 + [IN_ANY] + [IN_VMEM] * 3,
        out_specs=[IN_ANY] + [IN_VMEM] * 7,
        scratch_shapes=[
            *scatter_rest(768),
            *scatter_rest(256),
            pltpu.VMEM((3, 128, 1024), BF),
            small(128, 1024),
            small(8, 1024),
            small(2, 2, 2, 4, 2, 128),
            small(2, 2, 4, 2, 128),
            small(2, 4, 2, 128),
            small(4, 2, 128),
            small(3, 2, 128),
            small(2, 8, 512),
            small(4, 2, 2, 8, 512),
            pltpu.VMEM((128, 3072), BF),
            small(128, 512),
            small(16, 128),
            small(16, 128),
            small(2, 2, 4, 1, 128),
            small(2, 4, 1, 128),
            small(2, 4, 1, 128),
            small(4, 2, 1, 128),
            small(8, 128),
            small(8, 128),
            pltpu.SemaphoreType.DMA((7, 8)),
            pltpu.SemaphoreType.DMA((7, 8)),
            pltpu.SemaphoreType.DMA((1,)),
        ],
        compiler_params=pltpu.CompilerParams(
            collective_id=4, has_side_effects=True, vmem_limit_bytes=60 * MIB
        ),
        name="finish",
    )(*args)


def on_device_pairs(
    latents_in,
    condition,
    grad_out,
    qkv_weight,
    proj_weight,
    up_weight,
    down_weight,
    ada_weight,
    query_bias,
    value_bias,
    proj_bias,
    up_bias,
    down_bias,
    ada_bias,
):
    x = lax.axis_index("tp")
    wq = qkv_weight.reshape(64, 3, 2, 256).transpose(2, 0, 1, 3).reshape(2, 64, 768)
    wp = proj_weight.T.reshape(64, 2, 256).transpose(1, 0, 2)
    wu = up_weight.reshape(64, 2, 1024).transpose(1, 0, 2)
    wd = down_weight.T.reshape(64, 2, 1024).transpose(1, 0, 2)
    ada = ada_weight.reshape(64, 3072)
    cond = condition.astype(F32).reshape(8, 128)
    biases = [query_bias, value_bias, proj_bias, down_bias, up_bias, ada_bias.reshape(-1), jnp.zeros((576,), BF)]
    small = jnp.concatenate(
        [jax.nn.silu(cond).astype(BF).astype(F32), jnp.concatenate(biases).astype(F32).reshape(8, 128)], 0
    )
    lat_full, gq, gp, gu, gd, vectors, up_all, silu = start(
        latents_in.reshape(512, 1024), wq, wp, wu, wd, small, ada
    )
    gq = gq.reshape(2, 1024, 768)
    attn_in, packed, heads_out, lse, branch_one, middle, grad_full, gp, gu, gd = attend_pairs(
        lat_full, vectors, gq, gp, gu, gd, grad_out.reshape(512, 1024)
    )
    gp, gu = gp.reshape(2, 1024, 256), gu.reshape(2, 1024, 1024)
    block_out, middle_grad, g_one, up_grad, down_second, stats_mlp, up_sums, _ = mlp(
        middle, grad_full, branch_one, vectors, up_all, gu, gd
    )
    input_grad, qkv_grad, proj_grad, up_second, down_out, stats, sums, block_mine = attend_back(
        lat_full, vectors, g_one, gp, gq, attn_in, packed, heads_out, lse, middle_grad, up_grad, down_second,
        block_out.reshape(2, 512, 1024),
    )
    input_mine, q_out, p_out, u_out, ada_out, cond_out, ada_bias_out, bias_out = finish(
        stats_mlp, stats, sums, up_sums, silu, cond, ada, input_grad, qkv_grad, proj_grad, up_second
    )
    rows = lax.dynamic_slice_in_dim(cond_out, x * 4, 4, 0)
    return (
        block_mine.reshape(512, 1, 1024),
        input_mine.astype(F32).reshape(512, 1, 1024),
        rows.reshape(1, 512),
        q_out.reshape(2, 64, 3, 256).transpose(1, 2, 0, 3).reshape(64, 3, 512),
        p_out.transpose(1, 0, 2).reshape(64, 512).T,
        u_out.transpose(1, 0, 2).reshape(64, 2048),
        down_out.transpose(1, 0, 2).reshape(64, 2048).T,
        ada_out.reshape(64, 6, 512),
        bias_out[0, 0:32],
        bias_out[0, 32:64],
        bias_out[0, 64:96],
        bias_out[1],
        bias_out[0, 96:128],
        lax.dynamic_slice_in_dim(ada_bias_out, x * 32, 32, 1)[:6],
    )


def solution(mesh):
    shape = dict(mesh.shape)
    pairs = shape["fsdp"] == 16 and shape["tp"] == 2
    return jax.shard_map(
        on_device_pairs if pairs else on_device_general,
        mesh=mesh,
        in_specs=(
            P("tp", "fsdp", None),
            P("fsdp", None),
            P("tp", "fsdp", None),
            P("fsdp", None, "tp"),
            P("tp", "fsdp"),
            P("fsdp", "tp"),
            P("tp", "fsdp"),
            P("fsdp", None, "tp"),
            P(("fsdp", "tp")),
            P(("fsdp", "tp")),
            P(("fsdp", "tp")),
            P(("fsdp", "tp")),
            P(("fsdp", "tp")),
            P(None, ("fsdp", "tp")),
        ),
        out_specs=(
            P("tp", "fsdp", None),
            P("tp", "fsdp", None),
            P("fsdp", "tp"),
            P("fsdp", None, "tp"),
            P("tp", "fsdp"),
            P("fsdp", "tp"),
            P("tp", "fsdp"),
            P("fsdp", None, "tp"),
            P(("fsdp", "tp")),
            P(("fsdp", "tp")),
            P(("fsdp", "tp")),
            P(("fsdp", "tp")),
            P(("fsdp", "tp")),
            P(None, ("fsdp", "tp")),
        ),
        check_vma=False,
    )
```

```python
import functools
import math

import jax
import jax.numpy as jnp
from jax import lax
from jax.experimental import pallas as pl
from jax.experimental.pallas import tpu as pltpu
from jax.sharding import PartitionSpec as P


HD = 64


epsilon = 1e-06


def layer_norm(values):
    centred = values - jnp.mean(values, axis=-1, keepdims=True)
    return centred * lax.rsqrt(jnp.mean(centred * centred, axis=-1, keepdims=True) + epsilon)


def modulate(values, shift_part, scale_part):
    return layer_norm(values) * (1.0 + scale_part) + shift_part


def gelu_tanh(values):
    return jax.nn.gelu(values, approximate=True)


def gather_rows(piece):
    return lax.all_gather(piece, "tp", axis=0, tiled=True)


def gather_grads(piece):
    return lax.all_gather(piece, "tp", axis=0, tiled=True)


def scatter_rows(product, row_count):
    return lax.psum_scatter(
        product(jnp.int32(0), row_count * lax.axis_size("tp")).astype(jnp.bfloat16),
        "tp",
        scatter_dimension=0,
        tiled=True,
    ).astype(jnp.float32)


def scatter_grads(product, row_count):
    return lax.psum_scatter(
        product(jnp.int32(0), row_count * lax.axis_size("tp")).astype(jnp.bfloat16),
        "tp",
        scatter_dimension=0,
        tiled=True,
    ).astype(jnp.float32)


def split_heads(packed):
    head_count = packed.shape[3] // HD
    shaped = packed.reshape(packed.shape[0], packed.shape[1], 3, head_count, HD)
    return (shaped[:, :, 0], shaped[:, :, 1], shaped[:, :, 2])


def attend_forward(packed):
    length, latents, local_width = (packed.shape[0], packed.shape[1], packed.shape[3])
    queries, key_rows, value_rows = split_heads(packed)
    block_rows = min(512, length)
    score_scale = 1.0 / math.sqrt(HD)
    blocks = queries.reshape(length // block_rows, block_rows, latents, local_width // HD, HD)

    def one_block(q_rows):
        scores = (
            jnp.einsum("qbhd,kbhd->bhqk", q_rows, key_rows, preferred_element_type=jnp.float32)
            * score_scale
        )
        largest = jnp.max(scores, axis=-1, keepdims=True)
        exponent = jnp.exp(scores - largest)
        summed = jnp.sum(exponent, axis=-1, keepdims=True)
        weights_soft = (exponent / summed).astype(jnp.bfloat16)
        mixture = jnp.einsum(
            "bhqk,kbhd->qbhd", weights_soft, value_rows, preferred_element_type=jnp.float32
        )
        return (mixture.astype(jnp.bfloat16), largest[..., 0] + jnp.log(summed[..., 0]))

    mixture_all, log_sums = lax.map(one_block, blocks)
    return (mixture_all.reshape(length, latents, local_width), log_sums)


def attend_backward(packed, log_sums, heads_grad):
    length, latents, local_width = (packed.shape[0], packed.shape[1], packed.shape[3])
    head_count = local_width // HD
    queries, key_rows, value_rows = split_heads(packed)
    block_rows = min(512, length)
    count_blocks = length // block_rows
    score_scale = 1.0 / math.sqrt(HD)
    q_blocks = queries.reshape(count_blocks, block_rows, latents, head_count, HD)
    g_blocks = heads_grad.reshape(count_blocks, block_rows, latents, head_count, HD)

    def one_block(carried, inputs):
        key_grad, value_grad = carried
        q_rows, g_rows, log_rows = inputs
        scores = (
            jnp.einsum("qbhd,kbhd->bhqk", q_rows, key_rows, preferred_element_type=jnp.float32)
            * score_scale
        )
        weights_soft = jnp.exp(scores - log_rows[..., None])
        soft_grad = jnp.einsum(
            "qbhd,kbhd->bhqk", g_rows, value_rows, preferred_element_type=jnp.float32
        )
        inner_sum = jnp.sum(weights_soft * soft_grad, axis=-1, keepdims=True)
        score_grad = (weights_soft * (soft_grad - inner_sum)).astype(jnp.bfloat16)
        query_grad = (
            jnp.einsum("bhqk,kbhd->qbhd", score_grad, key_rows, preferred_element_type=jnp.float32)
            * score_scale
        )
        key_grad = (
            key_grad
            + jnp.einsum("bhqk,qbhd->kbhd", score_grad, q_rows, preferred_element_type=jnp.float32)
            * score_scale
        )
        value_grad = value_grad + jnp.einsum(
            "bhqk,qbhd->kbhd",
            weights_soft.astype(jnp.bfloat16),
            g_rows,
            preferred_element_type=jnp.float32,
        )
        return ((key_grad, value_grad), query_grad)

    zero_rows = jnp.zeros((length, latents, head_count, HD), jnp.float32)
    (key_grad, value_grad), query_grad = lax.scan(
        one_block, (zero_rows, zero_rows), (q_blocks, g_blocks, log_sums)
    )
    stacked = jnp.stack(
        [
            query_grad.reshape(length, latents, local_width),
            key_grad.reshape(length, latents, local_width),
            value_grad.reshape(length, latents, local_width),
        ],
        axis=2,
    )
    return stacked.astype(jnp.bfloat16)


def on_device_general(
    latents_in,
    condition,
    grad_out,
    qkv_weight,
    proj_weight,
    up_weight,
    down_weight,
    ada_weight,
    query_bias,
    value_bias,
    proj_bias,
    up_bias,
    down_bias,
    ada_bias,
):
    tp_index = lax.axis_index("tp")
    local_rows = latents_in.shape[0]
    local_width = qkv_weight.shape[2]
    local_hidden = up_weight.shape[1]
    model_width = latents_in.shape[2]
    width_start = tp_index * local_width
    hidden_start = tp_index * local_hidden
    full_qkv, full_proj, full_up, full_down, full_ada = (
        lax.all_gather(qkv_weight, "fsdp", axis=0, tiled=True),
        lax.all_gather(proj_weight, "fsdp", axis=1, tiled=True),
        lax.all_gather(up_weight, "fsdp", axis=0, tiled=True),
        lax.all_gather(down_weight, "fsdp", axis=1, tiled=True),
        lax.all_gather(ada_weight, "fsdp", axis=0, tiled=True),
    )
    bias_list = (
        lax.all_gather(query_bias, ("fsdp", "tp"), axis=0, tiled=True),
        lax.all_gather(value_bias, ("fsdp", "tp"), axis=0, tiled=True),
        lax.all_gather(proj_bias, ("fsdp", "tp"), axis=0, tiled=True),
        lax.all_gather(up_bias, ("fsdp", "tp"), axis=0, tiled=True),
        lax.all_gather(down_bias, ("fsdp", "tp"), axis=0, tiled=True),
        lax.all_gather(ada_bias, ("fsdp", "tp"), axis=1, tiled=True),
    )
    all_query, all_value, all_proj, all_up, all_down, all_ada = [
        item_bias.astype(jnp.float32) for item_bias in bias_list
    ]
    hidden_total = all_up.shape[0]
    cond_float = condition.astype(jnp.float32)
    silu_cond = jax.nn.silu(cond_float).astype(jnp.bfloat16)
    ada_cols = lax.dynamic_slice_in_dim(all_ada, width_start, local_width, 1)
    mod_part = (
        jnp.einsum("bc,ctf->btf", silu_cond, full_ada, preferred_element_type=jnp.float32)
        + ada_cols
    )
    modulation = lax.all_gather(mod_part, "tp", axis=2, tiled=True)
    shift_one, scale_one, gate_one = (modulation[:, 0], modulation[:, 1], modulation[:, 2])
    shift_two, scale_two, gate_two = (modulation[:, 3], modulation[:, 4], modulation[:, 5])
    input_float = latents_in.astype(jnp.float32)
    attn_in = modulate(input_float, shift_one, scale_one).astype(jnp.bfloat16)
    attn_full = gather_rows(attn_in)
    query_cols = lax.dynamic_slice_in_dim(all_query, width_start, local_width, 0)
    value_cols = lax.dynamic_slice_in_dim(all_value, width_start, local_width, 0)
    bias_three = jnp.stack([query_cols, jnp.zeros_like(query_cols), value_cols])
    packed = (
        jnp.einsum("sbd,dtf->sbtf", attn_full, full_qkv, preferred_element_type=jnp.float32)
        + bias_three
    ).astype(jnp.bfloat16)
    heads_out, log_sums = attend_forward(packed)

    def project_heads(first_row, row_count):
        return jnp.einsum("sbf,fd->sbd", heads_out, full_proj, preferred_element_type=jnp.float32)

    branch_one = scatter_rows(project_heads, local_rows) + all_proj
    middle = input_float + gate_one * branch_one
    mlp_in = modulate(middle, shift_two, scale_two).astype(jnp.bfloat16)
    mlp_full = gather_rows(mlp_in)
    up_cols = lax.dynamic_slice_in_dim(all_up, hidden_start, local_hidden, 0)
    hidden = (
        jnp.einsum("sbd,df->sbf", mlp_full, full_up, preferred_element_type=jnp.float32) + up_cols
    )
    active = gelu_tanh(hidden).astype(jnp.bfloat16)

    def project_hidden(first_row, row_count):
        return jnp.einsum("sbf,fd->sbd", active, full_down, preferred_element_type=jnp.float32)

    branch_two = scatter_rows(project_hidden, local_rows) + all_down
    block_out = (middle + gate_two * branch_two).astype(jnp.bfloat16)
    grad_float = grad_out.astype(jnp.float32)
    gate_two_grad = jnp.sum(grad_float * branch_two, axis=0)
    branch_two_grad = (grad_float * gate_two).astype(jnp.bfloat16)
    down_bias_part = jnp.sum(branch_two_grad.astype(jnp.float32), axis=(0, 1))
    _, gelu_pull = jax.vjp(gelu_tanh, hidden)
    branch_two_full = gather_grads(branch_two_grad)
    active_grad = jnp.einsum(
        "sbd,fd->sbf", branch_two_full, full_down, preferred_element_type=jnp.float32
    )
    down_grad = jnp.einsum(
        "sbf,sbd->fd", active, branch_two_full, preferred_element_type=jnp.float32
    )
    hidden_grad = gelu_pull(active_grad)[0].astype(jnp.bfloat16)
    up_grad = jnp.einsum("sbd,sbf->df", mlp_full, hidden_grad, preferred_element_type=jnp.float32)
    up_bias_part = lax.dynamic_update_slice(
        jnp.zeros((hidden_total,), jnp.float32),
        jnp.sum(hidden_grad.astype(jnp.float32), axis=(0, 1)),
        (hidden_start,),
    )

    def back_hidden(first_row, row_count):
        return jnp.einsum("sbf,df->sbd", hidden_grad, full_up, preferred_element_type=jnp.float32)

    mlp_in_grad = scatter_grads(back_hidden, local_rows)
    _, second_pull = jax.vjp(modulate, middle, shift_two, scale_two)
    middle_part, shift_two_grad, scale_two_grad = second_pull(mlp_in_grad)
    middle_grad = grad_float + middle_part
    gate_one_grad = jnp.sum(middle_grad * branch_one, axis=0)
    branch_one_grad = (middle_grad * gate_one).astype(jnp.bfloat16)
    proj_bias_part = jnp.sum(branch_one_grad.astype(jnp.float32), axis=(0, 1))
    branch_one_full = gather_grads(branch_one_grad)
    heads_grad = jnp.einsum(
        "sbd,fd->sbf", branch_one_full, full_proj, preferred_element_type=jnp.float32
    ).astype(jnp.bfloat16)
    proj_grad = jnp.einsum(
        "sbf,sbd->fd", heads_out, branch_one_full, preferred_element_type=jnp.float32
    )
    packed_grad = attend_backward(packed, log_sums, heads_grad)
    qkv_grad = jnp.einsum(
        "sbd,sbtf->dtf", attn_full, packed_grad, preferred_element_type=jnp.float32
    )
    packed_sums = jnp.sum(packed_grad.astype(jnp.float32), axis=(0, 1))
    zero_width = jnp.zeros((model_width,), jnp.float32)
    query_bias_part = lax.dynamic_update_slice(zero_width, packed_sums[0], (width_start,))
    value_bias_part = lax.dynamic_update_slice(zero_width, packed_sums[2], (width_start,))

    def back_packed(first_row, row_count):
        return jnp.einsum(
            "sbtf,dtf->sbd", packed_grad, full_qkv, preferred_element_type=jnp.float32
        )

    attn_in_grad = scatter_grads(back_packed, local_rows)
    _, first_pull = jax.vjp(modulate, input_float, shift_one, scale_one)
    input_part, shift_one_grad, scale_one_grad = first_pull(attn_in_grad)
    input_grad = middle_grad + input_part
    mod_grad = jnp.stack(
        [
            shift_one_grad,
            scale_one_grad,
            gate_one_grad,
            shift_two_grad,
            scale_two_grad,
            gate_two_grad,
        ],
        axis=1,
    )
    mod_cols_grad = lax.psum_scatter(
        mod_grad.astype(jnp.bfloat16), "tp", scatter_dimension=2, tiled=True
    ).astype(jnp.float32)
    ada_grad = jnp.einsum(
        "bc,btf->ctf", silu_cond.astype(jnp.float32), mod_cols_grad, precision=lax.Precision.HIGHEST
    )
    ada_bias_part = lax.dynamic_update_slice(
        jnp.zeros((6, model_width), jnp.float32), jnp.sum(mod_cols_grad, axis=0), (0, width_start)
    )
    silu_grad = jnp.einsum(
        "btf,ctf->bc", mod_cols_grad, full_ada.astype(jnp.float32), precision=lax.Precision.HIGHEST
    )
    silu_cols = lax.psum_scatter(silu_grad, "tp", scatter_dimension=1, tiled=True)
    cond_width = silu_cols.shape[1]
    cond_cols = lax.dynamic_slice_in_dim(cond_float, tp_index * cond_width, cond_width, 1)
    _, silu_pull = jax.vjp(jax.nn.silu, cond_cols)
    cond_grad = silu_pull(silu_cols)[0]
    qkv_sum, proj_sum, up_sum, down_sum, ada_sum = (
        lax.psum_scatter(
            qkv_grad.astype(jnp.bfloat16), "fsdp", scatter_dimension=0, tiled=True
        ).astype(jnp.float32),
        lax.psum_scatter(
            proj_grad.astype(jnp.bfloat16), "fsdp", scatter_dimension=1, tiled=True
        ).astype(jnp.float32),
        lax.psum_scatter(
            up_grad.astype(jnp.bfloat16), "fsdp", scatter_dimension=0, tiled=True
        ).astype(jnp.float32),
        lax.psum_scatter(
            down_grad.astype(jnp.bfloat16), "fsdp", scatter_dimension=1, tiled=True
        ).astype(jnp.float32),
        lax.psum_scatter(
            ada_grad.astype(jnp.bfloat16), "fsdp", scatter_dimension=0, tiled=True
        ).astype(jnp.float32),
    )
    query_sum, value_sum, proj_bias_sum, up_bias_sum, down_bias_sum, ada_bias_sum = (
        lax.psum_scatter(query_bias_part, ("fsdp", "tp"), scatter_dimension=0, tiled=True),
        lax.psum_scatter(value_bias_part, ("fsdp", "tp"), scatter_dimension=0, tiled=True),
        lax.psum_scatter(proj_bias_part, ("fsdp", "tp"), scatter_dimension=0, tiled=True),
        lax.psum_scatter(up_bias_part, ("fsdp", "tp"), scatter_dimension=0, tiled=True),
        lax.psum_scatter(down_bias_part, ("fsdp", "tp"), scatter_dimension=0, tiled=True),
        lax.psum_scatter(ada_bias_part, ("fsdp", "tp"), scatter_dimension=1, tiled=True),
    )
    return (
        block_out,
        input_grad,
        cond_grad,
        qkv_sum,
        proj_sum,
        up_sum,
        down_sum,
        ada_sum,
        query_sum,
        value_sum,
        proj_bias_sum,
        up_bias_sum,
        down_bias_sum,
        ada_bias_sum,
    )


MESH = pl.DeviceIdType.MESH
ANY = pl.ANY
BF = jnp.bfloat16
F32 = jnp.float32
MIB = 2**20
IN_VMEM = pl.BlockSpec(memory_space=pltpu.VMEM)
IN_ANY = pl.BlockSpec(memory_space=ANY)
SPLIT = 80


def place():
    f, x = lax.axis_index("fsdp"), lax.axis_index("tp")
    z, y, c = f // 4, lax.rem(f // 2, 2), lax.rem(f, 2)
    return z, y, c, x


def at(z, y, c, x):
    return ((z * 2 + y) * 2 + c, x)


def block(index, size):
    return pl.ds(pl.multiple_of(index * size, size), size)


def remote(src, dst, send, recv, device):
    return pltpu.make_async_remote_copy(
        src_ref=src, dst_ref=dst, send_sem=send, recv_sem=recv, device_id=device, device_id_type=MESH
    )


def loop(count, body):
    def step(i, carry):
        body(i)
        return carry

    lax.fori_loop(0, count, step, 0)


def greet(devices):
    barrier = pltpu.get_barrier_semaphore()
    for device in devices:
        pl.semaphore_signal(barrier, inc=1, device_id=device, device_id_type=MESH)
    pl.semaphore_wait(barrier, len(devices))


def partners():
    z, y, c, x = place()
    out = [at(z, y, 1 - c, x), at(z, 1 - y, c, x), at(z, y, c, 1 - x), at(z, y, 1 - c, 1 - x)]
    return out + [at(lax.rem(z + d, 4), y, c, x) for d in (1, 2, 3)]


class Gather:
    def __init__(self, own, full, lanes, send, recv, local):
        self.own, self.full, self.lanes = own, full, pl.ds(*lanes)
        self.send, self.recv, self.local = send, recv, local

    def _core(self):
        z, y, c, x = place()
        copies = []
        for i, ((near, first, width), (far, _, _)) in enumerate(zip(self.own(c), self.own(1 - c))):
            spot = self.full.at[x, z, y, block(c, 64), pl.ds(first, width)]
            copies.append(pltpu.make_async_copy(near, spot, self.local.at[i]))
            copies.append(remote(far, spot, self.send.at[i], self.recv.at[i], at(z, y, 1 - c, x)))
        return copies

    def _copy(self, kind, d):
        z, y, c, x = place()
        a, b, from_z = pl.ds(0, SPLIT), pl.ds(SPLIT, 128 - SPLIT), lax.rem(z - d + 4, 4)
        if kind == 0:
            spot, to = self.full.at[x, z, y, :, self.lanes], at(lax.rem(z + d, 4), y, c, x)
        elif kind == 1:
            spot, to = self.full.at[x, from_z, y, a, self.lanes], at(z, y, c, 1 - x)
        elif kind == 2:
            spot, to = self.full.at[x, from_z, y, b, self.lanes], at(z, 1 - y, c, x)
        elif kind == 3:
            spot, to = self.full.at[:, from_z, y, a, self.lanes], at(z, 1 - y, c, x)
        else:
            spot, to = self.full.at[x, from_z, :, b, self.lanes], at(z, y, c, 1 - x)
        return remote(spot, spot, self.send.at[4 + 4 * kind + d], self.recv.at[4 + 4 * kind + d], to)

    def start_core(self):
        for copy in self._core():
            copy.start()

    def enter(self):
        for copy in self._core():
            copy.wait()
        for d in (2, 1, 3):
            self._copy(0, d).start()
        self._copy(1, 0).start()
        self._copy(2, 0).start()

    def arrived(self, d):
        self._copy(0, d).wait()
        self._copy(1, d).start()
        self._copy(2, d).start()

    def turn(self, d):
        self._copy(1, d).wait()
        self._copy(3, d).start()
        self._copy(2, d).wait()
        self._copy(4, d).start()

    def finish(self):
        for d in range(4):
            self._copy(3, d).wait()
            self._copy(4, d).wait()


class Scatter:
    def __init__(self, part, first_a, first_b, second, third, total, out, send, recv):
        self.part, self.first_a, self.first_b = part, first_a, first_b
        self.second, self.third, self.total, self.out = second, third, total, out
        self.send, self.recv = send, recv

    def _copy(self, kind, d):
        z, y, c, x = place()
        a, b, to_z = pl.ds(0, SPLIT), pl.ds(SPLIT, 128 - SPLIT), lax.rem(z + d, 4)
        send, recv = self.send.at[4 * kind + d], self.recv.at[4 * kind + d]
        to_x, to_y = at(z, y, c, 1 - x), at(z, 1 - y, c, x)
        if kind == 0:
            return remote(self.part.at[:, to_z, 1 - y, a], self.first_a.at[to_z], send, recv, to_y)
        if kind == 1:
            return remote(self.part.at[1 - x, to_z, :, b], self.first_b.at[to_z], send, recv, to_x)
        if kind == 2:
            return remote(self.first_a.at[to_z, 1 - x], self.second.at[to_z, a], send, recv, to_x)
        if kind == 3:
            return remote(self.first_b.at[to_z, 1 - y], self.second.at[to_z, b], send, recv, to_y)
        return remote(self.second.at[to_z], self.third.at[d - 1], send, recv, at(to_z, y, c, x))

    def _core(self):
        z, y, c, x = place()
        copies = []
        for i, (target, first, width) in enumerate(self.out(c)):
            lanes = pl.ds(first, width)
            copies.append(
                remote(
                    self.total.at[block(1 - c, 64), lanes], target, self.send.at[20 + i], self.recv.at[20 + i],
                    at(z, y, 1 - c, x),
                )
            )
            copies.append(pltpu.make_async_copy(self.total.at[block(c, 64), lanes], target, self.send.at[24 + i]))
        return copies

    def start(self):
        for d in (2, 1, 3, 0):
            self._copy(0, d).start()
            self._copy(1, d).start()

    def turn(self, d):
        z, y, c, x = place()
        to_z = lax.rem(z + d, 4)
        a, b = pl.ds(0, SPLIT), pl.ds(SPLIT, 128 - SPLIT)
        self._copy(0, d).wait()
        for k in range(2):
            total = self.first_a[to_z, k].astype(F32) + self.part[k, to_z, y, a].astype(F32)
            self.first_a[to_z, k] = total.astype(BF)
        self._copy(2, d).start()
        self._copy(1, d).wait()
        for k in range(2):
            total = self.first_b[to_z, k].astype(F32) + self.part[x, to_z, k, b].astype(F32)
            self.first_b[to_z, k] = total.astype(BF)
        self._copy(3, d).start()

    def leave(self, d):
        z, y, c, x = place()
        to_z = lax.rem(z + d, 4)
        a, b = pl.ds(0, SPLIT), pl.ds(SPLIT, 128 - SPLIT)
        self._copy(2, d).wait()
        self.second[to_z, a] = (self.second[to_z, a].astype(F32) + self.first_a[to_z, x].astype(F32)).astype(BF)
        self._copy(3, d).wait()
        self.second[to_z, b] = (self.second[to_z, b].astype(F32) + self.first_b[to_z, y].astype(F32)).astype(BF)
        if d:
            self._copy(4, d).start()

    def last(self):
        z, y, c, x = place()
        for d in (1, 2, 3):
            self._copy(4, d).wait()

        def add(i):
            rows = block(i, 64)
            total = self.second[z, rows].astype(F32)
            for d in range(3):
                total = total + self.third[d, rows].astype(F32)
            self.total[rows] = total

        loop(2, add)
        for copy in self._core():
            copy.start()

    def finish(self):
        for copy in self._core():
            copy.wait()


class Swap:
    def __init__(self, own, full, send, recv, local):
        self.own, self.full, self.send, self.recv, self.local = own, full, send, recv, local

    def _both(self, act):
        z, y, c, x = place()

        @pl.when(c != x)
        def _():
            to = at(z, y, 1 - c, 1 - x)
            act(remote(self.own, self.full.at[block(1 - c, 512)], self.send.at[0], self.recv.at[0], to))

        @pl.when(c == x)
        def _():
            act(pltpu.make_async_copy(self.own, self.full.at[block(c, 512)], self.local))

    def _core(self):
        z, y, c, x = place()
        spot = self.full.at[block(c, 512)]
        return remote(spot, spot, self.send.at[1], self.recv.at[1], at(z, y, 1 - c, x))

    def start(self):
        self._both(lambda copy: copy.start())

    def share(self):
        self._both(lambda copy: copy.wait())
        self._core().start()

    def finish(self):
        self._core().wait()


class SwapBack:
    def __init__(self, full, out, send, recv, local):
        self.full, self.out, self.send, self.recv, self.local = full, out, send, recv, local

    def _both(self, act):
        z, y, c, x = place()
        rows = self.full.at[block(c, 512)]

        @pl.when(c != x)
        def _():
            act(remote(rows, self.out, self.send, self.recv, at(z, y, 1 - c, 1 - x)))

        @pl.when(c == x)
        def _():
            act(pltpu.make_async_copy(rows, self.out, self.local))

    def start(self):
        self._both(lambda copy: copy.start())

    def finish(self):
        self._both(lambda copy: copy.wait())


class SmallGather:
    def __init__(self, own, full, send, recv):
        self.own, self.full, self.send, self.recv = own, full, send, recv

    def _copy(self, k):
        z, y, c, x = place()
        send, recv = self.send.at[k], self.recv.at[k]
        if k == 0:
            return remote(self.own, self.full.at[x, z, y, c], send, recv, at(z, y, 1 - c, x))
        if k <= 3:
            spot = self.full.at[x, z, y]
            return remote(spot, spot, send, recv, at(lax.rem(z + k, 4), y, c, x))
        if k == 4:
            spot = self.full.at[x, :, y]
            return remote(spot, spot, send, recv, at(z, 1 - y, c, x))
        spot = self.full.at[x]
        return remote(spot, spot, send, recv, at(z, y, c, 1 - x))

    def start(self):
        z, y, c, x = place()
        self.full[x, z, y, c] = self.own[...]
        self._copy(0).start()

    def step(self, done, begin):
        for k in done:
            self._copy(k).wait()
        for k in begin:
            self._copy(k).start()


class SmallScatter:
    def __init__(self, part, near_c, near_x, near_y, near_z, send, recv):
        self.part, self.near_c, self.near_x, self.near_y, self.near_z = part, near_c, near_x, near_y, near_z
        self.send, self.recv = send, recv

    def _copy(self, k):
        z, y, c, x = place()
        send, recv = self.send.at[k], self.recv.at[k]
        if k == 0:
            return remote(self.part.at[1 - c], self.near_c, send, recv, at(z, y, 1 - c, x))
        if k == 1:
            return remote(self.near_c.at[1 - x], self.near_x, send, recv, at(z, y, c, 1 - x))
        if k == 2:
            return remote(self.near_x.at[1 - y], self.near_y, send, recv, at(z, 1 - y, c, x))
        to = lax.rem(z + k - 2, 4)
        return remote(self.near_y.at[to], self.near_z.at[k - 3], send, recv, at(to, y, c, x))

    def start(self):
        self._copy(0).start()

    def step(self, k):
        z, y, c, x = place()
        self._copy(k).wait()
        if k == 0:
            self.near_c[...] = self.near_c[...] + self.part[c]
            self._copy(1).start()
        elif k == 1:
            self.near_x[...] = self.near_x[...] + self.near_c[x]
            self._copy(2).start()
        else:
            self.near_y[...] = self.near_y[...] + self.near_x[y]
            for j in (3, 4, 5):
                self._copy(j).start()

    def finish(self):
        z, y, c, x = place()
        for j in (3, 4, 5):
            self._copy(j).wait()
        return self.near_y[z] + self.near_z[0] + self.near_z[1] + self.near_z[2]


class Pair:
    def __init__(self, mine, theirs, send, recv):
        self.mine, self.theirs, self.send, self.recv = mine, theirs, send, recv

    def _copy(self, i):
        z, y, c, x = place()
        rows = block(i, 256)
        return remote(
            self.mine.at[rows], self.theirs.at[rows], self.send.at[i], self.recv.at[i], at(z, y, 1 - c, x)
        )

    def give(self, i, partial):
        self.mine[block(i, 256), :] = partial.astype(BF)
        self._copy(i).start()

    def take(self, i):
        self._copy(i).wait()
        rows = block(i, 256)
        return self.mine[rows, :].astype(F32) + self.theirs[rows, :].astype(F32)


def normalise(values):
    centred = values - jnp.mean(values, axis=-1, keepdims=True)
    scale = lax.rsqrt(jnp.mean(centred * centred, axis=-1, keepdims=True) + epsilon)
    return centred * scale, scale


def nn(a, b):
    return jnp.dot(a, b, preferred_element_type=F32)


def nt(a, b):
    return lax.dot_general(a, b, (((1,), (1,)), ((), ())), preferred_element_type=F32)


def tn(a, b):
    return lax.dot_general(a, b, (((0,), (0,)), ((), ())), preferred_element_type=F32)


def in_half(h):
    return lax.broadcasted_iota(jnp.int32, (1, 128), 1) // 64 == h


def column_sum(values):
    return jnp.sum(values, 0, keepdims=True)


def gelu_parts(v):
    k = math.sqrt(2.0 / math.pi)
    square = v * v
    t = jnp.tanh(k * v * (1.0 + 0.044715 * square))
    half = 0.5 * (1.0 + t)
    return v * half, half + 0.5 * k * v * (1.0 - t * t) * (1.0 + 3.0 * 0.044715 * square)


def split_bf(values):
    high = values.astype(BF)
    return high, (values - high.astype(F32)).astype(BF)


def exact_nn(values, chosen):
    high, low = split_bf(values)
    lower = (values - high.astype(F32) - low.astype(F32)).astype(BF)
    return nn(high, chosen) + nn(low, chosen) + nn(lower, chosen)


def devices():
    return [(zz, yy, cc, xx) for zz in range(4) for yy in range(2) for cc in range(2) for xx in range(2)]


def widen(small_full, row, k, width=1024):
    pieces = jnp.concatenate([small_full[xx, zz, yy, cc, row : row + 1, :] for zz, yy, cc, xx in devices()], 0)
    lane = lax.broadcasted_iota(jnp.int32, (128, width), 1)
    source = lax.broadcasted_iota(jnp.int32, (128, width), 0)
    pick = jnp.where(source == k * 32 + lax.rem(lane, 32), 1.0, 0.0).astype(BF)
    spread_out = nn(pieces.astype(BF), pick)
    device = lax.broadcasted_iota(jnp.int32, (32, width), 0)
    lane = lax.broadcasted_iota(jnp.int32, (32, width), 1)
    return column_sum(jnp.where(lane // 32 == device, spread_out, 0.0))


def narrow(vector, k):
    device = lax.broadcasted_iota(jnp.int32, (32, 1024), 0)
    lane = lax.broadcasted_iota(jnp.int32, (32, 1024), 1)
    source = lax.broadcasted_iota(jnp.int32, (1024, 128), 0)
    target = lax.broadcasted_iota(jnp.int32, (1024, 128), 1)
    chosen = jnp.where(target == k * 32 + lax.rem(source, 32), 1.0, 0.0).astype(BF)
    return exact_nn(jnp.where(lane // 32 == device, vector, 0.0), chosen)


def flat(value):
    return value.reshape(-1, value.shape[-1])


INPUTS = """lat_own grad_own wq wp wu wd ada cond q_bias v_bias p_bias d_bias u_bias a_bias"""
OUTPUTS = """block_mine input_mine q_out p_out u_out d_out held_a held_b held_d
    ada_out cond_out ada_bias_out bias_out"""
GROUP = (2, 4, 2, 128, 1024)
TOKENS = (1024, 1024)


def scratch():
    v, f = (lambda *s: pltpu.VMEM(s, BF)), (lambda *s: pltpu.VMEM(s, F32))
    dma, regular = pltpu.SemaphoreType.DMA, pltpu.SemaphoreType.REGULAR
    out = dict(lat=v(*TOKENS), grad=v(*TOKENS), attn_in=v(*TOKENS), mid=f(*TOKENS), branch_one=v(*TOKENS))
    out.update(mlp_in=v(*TOKENS), g_two=v(*TOKENS), mine=v(*TOKENS), theirs_a=v(*TOKENS), theirs_b=v(*TOKENS))
    out.update(buf_a=v(*GROUP), buf_b=v(*GROUP), gu=v(*GROUP), buf_c=v(*GROUP), buf_d=v(*GROUP))
    for i in range(2):
        out[f"first_a{i}"], out[f"first_b{i}"] = v(4, 2, SPLIT, 1024), v(4, 2, 128 - SPLIT, 1024)
    for i in range(3):
        out[f"second{i}"], out[f"third{i}"] = v(4, 128, 1024), v(3, 128, 1024)
    out.update(total=f(128, 1024), heads_grad=v(2, 1024, 256), lse=f(1024, 128))
    out.update(key_total=f(1024, 128), value_total=f(1024, 128))
    out.update(small=f(16, 128), small_full=f(2, 4, 2, 2, 16, 128), wide=v(128, 3072), silu=f(16, 128))
    out.update(part=f(4, 2, 2, 8, 512), near_c=f(4, 2, 8, 512), near_y=f(4, 8, 512), near_z=f(4, 8, 512))
    out.update(mods=f(2, 8, 512), vectors=f(16, 1024), up_bias=f(1, 4096), stats=f(8, 1024), columns=f(8, 1024))
    out.update(up_sums=f(2, 1, 1024), sums=f(2, 1, 768), all_mods=f(4, 2, 2, 8, 512), tall=f(128, 512))
    out.update(bias_part=f(2, 2, 2, 4, 2, 128), bias_c=f(2, 2, 4, 2, 128), bias_x=f(2, 4, 2, 128))
    out.update(bias_y=f(4, 2, 128), bias_z=f(3, 2, 128), found=f(16, 128), other=f(16, 128))
    out.update(spread_x=f(2, 2, 4, 1, 128), spread_c=f(2, 4, 1, 128), spread_y=f(2, 4, 1, 128))
    out.update(spread_z=f(4, 2, 1, 128), picked=f(8, 128), picked_other=f(8, 128))
    out.update(gather_send=dma((4, 24)), gather_recv=dma((4, 24)), gather_local=dma((4, 4)))
    out.update(scatter_send=dma((3, 28)), scatter_recv=dma((3, 28)), pair_send=dma((4, 4)), pair_recv=dma((4, 4)))
    out.update(swap_send=dma((4, 2)), swap_recv=dma((4, 2)), swap_local=dma((4,)))
    out.update(small_send=dma((4, 8)), small_recv=dma((4, 8)), load_sem=dma((12,)), free=regular)
    return out


def pairs_kernel(*refs):
    names = INPUTS.split() + OUTPUTS.split() + list(scratch())
    r = dict(zip(names, refs))
    Block(r).run()


class Block:
    def __init__(self, r):
        for name, ref in r.items():
            setattr(self, name, ref)

    def run(self):
        self.set_up()
        self.begin()
        self.attend()
        self.mlp()
        self.attend_back()
        self.end()

    def set_up(self):
        gather = lambda i, own, full, lanes: Gather(
            own, full, lanes, self.gather_send.at[i], self.gather_recv.at[i], self.gather_local.at[i]
        )
        self.q = gather(
            0, lambda h: [(self.wq.at[j, :, block(h, 256)], 256 * j, 256) for j in range(3)], self.buf_a, (0, 768)
        )
        self.p = gather(1, lambda h: [(self.wp.at[:, block(h, 256)], 768, 256)], self.buf_a, (768, 256))
        self.u = gather(2, lambda h: [(self.wu.at[:, block(h, 1024)], 0, 1024)], self.gu, (0, 1024))
        self.d = gather(3, lambda h: [(self.wd.at[:, block(h, 1024)], 0, 1024)], self.held_d, (0, 1024))
        outs = (
            lambda h: [(self.d_out.at[:, block(h, 1024)], 0, 1024)],
            lambda h: [(self.u_out.at[:, block(h, 1024)], 0, 1024)],
            lambda h: [(self.q_out.at[j, :, block(h, 256)], 256 * j, 256) for j in range(3)]
            + [(self.p_out.at[:, block(h, 256)], 768, 256)],
        )
        parts = (self.buf_d, self.buf_c, self.buf_d)
        firsts = ((self.first_a0, self.first_b0), (self.first_a1, self.first_b1), (self.first_a0, self.first_b0))
        rest = ((self.second0, self.third0), (self.second1, self.third1), (self.second2, self.third2))
        self.down, self.up, self.attn = [
            Scatter(
                parts[i], *firsts[i], *rest[i], self.total, outs[i], self.scatter_send.at[i], self.scatter_recv.at[i]
            )
            for i in range(3)
        ]
        swaps = [(self.lat_own, self.lat), (self.grad_own, self.grad)]
        self.swap_lat, self.swap_grad = [
            Swap(own, full, self.swap_send.at[i], self.swap_recv.at[i], self.swap_local.at[i])
            for i, (own, full) in enumerate(swaps)
        ]
        backs = [(self.g_two, self.block_mine), (self.branch_one, self.input_mine)]
        self.swap_block, self.swap_input = [
            SwapBack(full, out, self.swap_send.at[2 + i, 0], self.swap_recv.at[2 + i, 0], self.swap_local.at[2 + i])
            for i, (full, out) in enumerate(backs)
        ]
        self.pairs = [
            Pair(self.mine, theirs, self.pair_send.at[i], self.pair_recv.at[i])
            for i, theirs in enumerate((self.theirs_a, self.theirs_b, self.theirs_a, self.theirs_b))
        ]

    def load(self, i, source, target):
        return pltpu.make_async_copy(source, target, self.load_sem.at[i])

    def begin(self):
        z, y, c, x = place()
        q, p, u, d = self.q, self.p, self.u, self.d
        send, recv = self.small_send, self.small_recv
        little = SmallGather(self.small, self.small_full, send.at[0], recv.at[0])
        v = self.cond[...].astype(F32)
        silu = (v / (1.0 + jnp.exp(-v))).astype(BF).astype(F32)
        self.small[...] = jnp.zeros_like(self.small)
        for k in range(8):
            self.small[k : k + 1, :] = silu[:, k * 128 : (k + 1) * 128]
        for k, bias in enumerate((self.q_bias, self.v_bias, self.p_bias, self.d_bias)):
            self.small[8:9, k * 32 : (k + 1) * 32] = bias[...].astype(F32)
        self.small[9:10, :] = self.u_bias[...].astype(F32)
        a_bias = self.a_bias[...].astype(F32)
        for j in range(6):
            self.small[10 + j // 4 : 11 + j // 4, j % 4 * 32 : j % 4 * 32 + 32] = a_bias[j : j + 1, :]
        greet(partners())
        q.start_core()
        little.start()
        for group in (p, u, d):
            group.start_core()
        self.swap_lat.start()
        self.wide[...] = jnp.zeros_like(self.wide)
        ada = [self.load(j, self.ada.at[j], self.wide.at[block(c, 64), pl.ds(j * 512, 512)]) for j in range(6)]
        for copy in ada:
            copy.start()
        q.enter()
        little.step((0,), (1, 2, 3))
        self.part[...] = jnp.zeros_like(self.part)
        little.step((1, 2, 3), (4,))
        for copy in ada:
            copy.wait()
        little.step((4,), (5,))
        row = z * 2 + y
        lhs = [self.small_full[x, b // 4, b // 2 % 2, b % 2, pl.ds(row, 1), :] for b in range(16)]
        lhs = jnp.concatenate(lhs, 0)
        self.silu[...] = lhs
        for j in range(6):
            product = nn(lhs.astype(BF), self.wide[:, j * 512 : (j + 1) * 512])
            for b in range(16):
                self.part[b // 4, b // 2 % 2, b % 2, j : j + 1, :] = product[b : b + 1, :]
        near_c, near_y, near_z = self.near_c, self.near_y, self.near_z
        first = remote(self.part.at[:, :, 1 - c], near_c, send.at[1, 0], recv.at[1, 0], at(z, y, 1 - c, x))
        first.start()
        q.arrived(2)
        first.wait()
        for zz in range(4):
            for yy in range(2):
                near_c[zz, yy] = near_c[zz, yy] + self.part[zz, yy, c]
        second = remote(near_c.at[:, 1 - y], near_y, send.at[1, 1], recv.at[1, 1], at(z, 1 - y, c, x))
        second.start()
        q.turn(0)
        second.wait()
        for zz in range(4):
            near_y[zz] = near_y[zz] + near_c[zz, y]
        thirds = []
        for s in (1, 2, 3):
            to = lax.rem(z + s, 4)
            thirds.append(
                remote(near_y.at[to], near_z.at[s - 1], send.at[1, 1 + s], recv.at[1, 1 + s], at(to, y, c, x))
            )
            thirds[-1].start()
        q.arrived(1)
        for copy in thirds:
            copy.wait()
        near_z[3] = near_y[z] + near_z[0] + near_z[1] + near_z[2]
        fourth = remote(near_z.at[3], self.mods.at[1 - c], send.at[1, 5], recv.at[1, 5], at(z, y, 1 - c, 1 - x))

        @pl.when(c != x)
        def _():
            fourth.start()

        q.arrived(3)
        self.swap_lat.share()
        q.turn(2)

        @pl.when(c != x)
        def _():
            fourth.wait()

        @pl.when(c == x)
        def _():
            self.mods[c] = near_z[3]

        fifth = remote(self.mods.at[c], self.mods.at[c], send.at[1, 6], recv.at[1, 6], at(z, y, 1 - c, x))
        fifth.start()
        little.step((5,), ())
        bias = [widen(self.small_full, 8, k) for k in range(4)]
        ada_bias = [widen(self.small_full, 10 + j // 4, j % 4) for j in range(6)]
        for k, (zz, yy, cc, xx) in enumerate(devices()):
            self.up_bias[:, k * 128 : (k + 1) * 128] = self.small_full[xx, zz, yy, cc, 9:10, :]
        q.turn(1)
        fifth.wait()
        for j in range(6):
            for h in range(2):
                lanes = slice(h * 512, (h + 1) * 512)
                self.vectors[j : j + 1, lanes] = self.mods[h, j : j + 1, :] + ada_bias[j][:, lanes]
        for k in range(4):
            self.vectors[6 + k : 7 + k, :] = bias[k]
        q.turn(3)
        p.enter()
        u.enter()
        self.swap_lat.finish()

    def attend(self):
        z, y, c, x = place()
        q, p, u, d, vectors = self.q, self.p, self.u, self.d, self.vectors

        def modulated(i):
            rows = block(i, 256)
            normal, _ = normalise(self.lat[rows, :].astype(F32))
            self.attn_in[rows, :] = (normal * (1.0 + vectors[1:2, :]) + vectors[0:1, :]).astype(BF)

        loop(4, modulated)
        q.finish()
        self.swap_grad.start()

        def project(i):
            b, quarter = i // 4, lax.rem(i, 4)
            columns = pl.ds(pl.multiple_of(b * 512 + c * 256, 256), 256)
            values = nn(self.attn_in[block(quarter, 256), :], flat(self.buf_a[b, :, :, :, 0:768]))
            query = values[:, 0:256] + vectors[6:7, columns]
            value = values[:, 512:768] + vectors[7:8, columns]
            self.buf_b[b, quarter, :, :, 0:256] = query.astype(BF).reshape(2, 128, 256)
            self.buf_b[b, quarter, :, :, 256:512] = values[:, 256:512].astype(BF).reshape(2, 128, 256)
            self.buf_b[b, quarter, :, :, 512:768] = value.astype(BF).reshape(2, 128, 256)

        loop(8, project)
        for k in (2, 1, 3):
            p.arrived(k)
        for k in (0, 2, 1, 3):
            p.turn(k)
        lane = lax.broadcasted_iota(jnp.int32, (1, 128), 1)
        self.lse[...] = jnp.zeros_like(self.lse)

        def attend(i):
            pair, half = i // 2, lax.rem(i, 2)
            rows, zz = block(half, 512), pl.ds(half * 2, 2)
            b, q_at = pair // 2, pl.multiple_of(lax.rem(pair, 2) * 128, 128)
            queries = flat(self.buf_b[b, zz, :, :, pl.ds(q_at, 128)]) * BF(0.125)
            keys = flat(self.buf_b[b, :, :, :, pl.ds(q_at + 256, 128)])
            values = flat(self.buf_b[b, :, :, :, pl.ds(q_at + 512, 128)])
            result = None
            logs = self.lse[rows, :]
            for h in range(2):
                scores = nt(jnp.where(in_half(h), queries, jnp.zeros_like(queries)), keys)
                largest = jnp.max(scores, -1, keepdims=True)
                exponent = jnp.exp(scores - largest)
                summed = jnp.sum(exponent, -1, keepdims=True)
                mixture = nn(exponent.astype(BF), values) * (1.0 / summed)
                result = mixture if h == 0 else jnp.where(in_half(0), result, mixture)
                logs = jnp.where(lane == pair * 2 + h, largest + jnp.log(summed), logs)
            self.buf_b[b, zz, :, :, pl.ds(q_at + 768, 128)] = result.astype(BF).reshape(2, 2, 128, 128)
            self.lse[rows, :] = logs

            @pl.when(i == 1)
            def _():
                u.arrived(2)
                u.arrived(1)
                u.arrived(3)

            @pl.when(i == 3)
            def _():
                u.turn(0)
                d.enter()

            @pl.when(i == 5)
            def _():
                u.turn(2)
                u.turn(1)
                u.turn(3)

        loop(8, attend)
        p.finish()
        self.load(0, self.buf_a, self.held_a).start()
        pair = self.pairs[0]

        def out(i):
            zz = i
            partial = nt(flat(self.buf_b[0, zz, :, :, 768:1024]), flat(self.buf_a[0, :, :, :, 768:1024]))
            partial += nt(flat(self.buf_b[1, zz, :, :, 768:1024]), flat(self.buf_a[1, :, :, :, 768:1024]))
            pair.give(i, partial)

        loop(4, out)
        self.load(1, self.buf_b, self.held_b).start()
        self.swap_grad.share()

        def residual(i):
            rows = block(i, 256)
            branch = pair.take(i) + vectors[8:9, :]
            self.branch_one[rows, :] = branch.astype(BF)
            self.mid[rows, :] = self.lat[rows, :].astype(F32) + vectors[2:3, :] * branch

        loop(4, residual)

    def mlp(self):
        z, y, c, x = place()
        u, d, vectors, stats, down, up = self.u, self.d, self.vectors, self.stats, self.down, self.up
        active, up_grad, slope, hidden_grad = self.buf_c, self.buf_c, self.buf_a, self.buf_a
        wd, gu, mid, mlp_in, g_two, grad = self.buf_b, self.gu, self.mid, self.mlp_in, self.g_two, self.grad
        self.swap_grad.finish()
        stats[...] = jnp.zeros_like(stats)
        self.up_sums[...] = jnp.zeros_like(self.up_sums)

        def enter(i):
            rows = block(i, 256)
            normal, _ = normalise(mid[rows, :])
            mlp_in[rows, :] = (normal * (1.0 + vectors[4:5, :]) + vectors[3:4, :]).astype(BF)
            g = (grad[rows, :].astype(F32) * vectors[5:6, :]).astype(BF)
            g_two[rows, :] = g
            mine_too = jnp.where(i // 2 == c, 1.0, 0.0)
            stats[1:2, :] += column_sum(g.astype(F32)) * mine_too

        loop(4, enter)
        for k in (2, 1, 3):
            d.arrived(k)
        u.finish()
        self.load(0, self.buf_a, self.held_a).wait()
        d.turn(0)

        def ascend(i):
            b, quarter = i // 4, lax.rem(i, 4)
            columns = pl.ds(pl.multiple_of(b * 2048 + c * 1024, 1024), 1024)
            hidden = nn(mlp_in[block(quarter, 256), :], flat(gu[b])) + self.up_bias[:, columns]
            value, gradient = gelu_parts(hidden)
            active[b, quarter] = value.astype(BF).reshape(2, 128, 1024)
            slope[b, quarter] = gradient.astype(BF).reshape(2, 128, 1024)

            @pl.when(i == 5)
            def _():
                d.turn(2)
                d.turn(1)

        loop(8, ascend)
        d.turn(3)

        def down_gradient(i):
            b, half = i // 2, lax.rem(i, 2)
            value = tn(g_two[:, block(half, 512)], flat(active[b]))
            self.buf_d[b, pl.ds(half * 2, 2)] = value.astype(BF).reshape(2, 2, 128, 1024)

        loop(4, down_gradient)
        down.start()
        d.finish()
        self.load(1, self.buf_b, self.held_b).wait()
        load = self.load(2, self.held_d, wd)
        load.start()
        load.wait()
        pair, back = self.pairs[1], self.pairs[2]

        def descend(i):
            pair.give(i, nt(flat(active[0, i]), flat(wd[0])) + nt(flat(active[1, i]), flat(wd[1])))

        loop(4, descend)

        def hidden_gradient(i):
            b, quarter = i // 4, lax.rem(i, 4)
            value = nn(g_two[block(quarter, 256), :], flat(wd[b])) * flat(slope[b, quarter]).astype(F32)
            value = value.astype(BF)
            hidden_grad[b, quarter] = value.reshape(2, 128, 1024)
            self.up_sums[b] += column_sum(value.astype(F32))

        loop(8, hidden_gradient)
        self.load(3, self.held_b, self.buf_b).start()

        def leave(i):
            rows = block(i, 256)
            branch_two = pair.take(i) + vectors[9:10, :]
            g_two[rows, :] = (mid[rows, :] + vectors[5:6, :] * branch_two).astype(BF)
            stats[0:1, :] += column_sum(grad[rows, :].astype(F32) * branch_two)

        loop(4, leave)

        def descend_back(i):
            back.give(i, nt(flat(hidden_grad[0, i]), flat(gu[0])) + nt(flat(hidden_grad[1, i]), flat(gu[1])))

        loop(4, descend_back)
        down.turn(2)
        down.turn(1)

        def up_gradient(i):
            b, half = i // 2, lax.rem(i, 2)
            value = tn(mlp_in[:, block(half, 512)], flat(hidden_grad[b]))
            up_grad[b, pl.ds(half * 2, 2)] = value.astype(BF).reshape(2, 2, 128, 1024)

        loop(4, up_gradient)
        self.load(4, self.held_a, self.buf_a).start()
        up.start()
        down.turn(3)
        down.turn(0)

        def residual(i):
            rows = block(i, 256)
            dy = back.take(i)
            normal, scale = normalise(mid[rows, :])
            stats[2:3, :] += column_sum(dy)
            stats[3:4, :] += column_sum(dy * normal)
            dn = dy * (1.0 + vectors[4:5, :])
            dn = dn - jnp.mean(dn, -1, keepdims=True) - normal * jnp.mean(dn * normal, -1, keepdims=True)
            total = grad[rows, :].astype(F32) + scale * dn
            mid[rows, :] = total
            stats[4:5, :] += column_sum(total * self.branch_one[rows, :].astype(F32))
            g = (total * vectors[2:3, :]).astype(BF)
            mlp_in[rows, :] = g
            mine_too = jnp.where(i // 2 == c, 1.0, 0.0)
            stats[5:6, :] += column_sum(g.astype(F32)) * mine_too

        loop(4, residual)
        down.leave(2)

    def attend_back(self):
        z, y, c, x = place()
        vectors, stats, down, up, attn = self.vectors, self.stats, self.down, self.up, self.attn
        acts, g_one, heads_grad, sums = self.buf_b, self.mlp_in, self.heads_grad, self.sums
        weights = self.buf_a
        sums[...] = jnp.zeros_like(sums)
        self.load(3, self.held_b, self.buf_b).wait()
        self.load(4, self.held_a, self.buf_a).wait()
        down.leave(1)

        def enter(i):
            b, half = i // 2, lax.rem(i, 2)
            value = nn(g_one[block(half, 512), :], flat(weights[b, :, :, :, 768:1024]))
            heads_grad[b, block(half, 512), :] = value.astype(BF)

        loop(4, enter)

        def proj_gradient(i):
            b, half = i // 2, lax.rem(i, 2)
            value = tn(g_one[:, block(half, 512)], flat(acts[b, :, :, :, 768:1024]))
            self.buf_d[b, pl.ds(half * 2, 2), :, :, 768:1024] = value.astype(BF).reshape(2, 2, 128, 256)

        loop(4, proj_gradient)
        down.leave(3)
        lane = lax.broadcasted_iota(jnp.int32, (1, 128), 1)

        def attend(i):
            pair, quarter = i // 4, lax.rem(i, 4)
            rows = block(quarter, 256)
            b, at_lane = pair // 2, pl.multiple_of(lax.rem(pair, 2) * 128, 128)
            queries = flat(acts[b, quarter, :, :, pl.ds(at_lane, 128)]) * BF(0.125)
            keys = flat(acts[b, :, :, :, pl.ds(at_lane + 256, 128)])
            values = flat(acts[b, :, :, :, pl.ds(at_lane + 512, 128)])
            grads = heads_grad[b, rows, pl.ds(at_lane, 128)]

            @pl.when(quarter == 0)
            def _():
                self.key_total[...] = jnp.zeros_like(self.key_total)
                self.value_total[...] = jnp.zeros_like(self.value_total)

            result = None
            logs = self.lse[rows, :]
            for h in range(2):
                log = jnp.sum(jnp.where(lane == pair * 2 + h, logs, 0.0), -1, keepdims=True)
                query = jnp.where(in_half(h), queries, jnp.zeros_like(queries))
                grad = jnp.where(in_half(h), grads, jnp.zeros_like(grads))
                probs = jnp.exp(nt(query, keys) - log)
                probs_grad = nt(grad, values)
                inner = jnp.sum(probs * probs_grad, -1, keepdims=True)
                score_grad = (probs * (probs_grad - inner)).astype(BF)
                query_grad = nn(score_grad, keys)
                result = query_grad if h == 0 else jnp.where(in_half(0), result, query_grad)
                self.key_total[...] += tn(score_grad, query)
                self.value_total[...] += tn(probs.astype(BF), grad)
            result = (result * 0.125).astype(BF)
            acts[b, quarter, :, :, pl.ds(at_lane, 128)] = result.reshape(2, 128, 128)
            sums[b, :, pl.ds(at_lane, 128)] += column_sum(result.astype(F32))

            @pl.when(quarter == 3)
            def _():
                total = self.key_total[...].astype(BF)
                acts[b, :, :, :, pl.ds(at_lane + 256, 128)] = total.reshape(4, 2, 128, 128)
                total = self.value_total[...].astype(BF)
                acts[b, :, :, :, pl.ds(at_lane + 512, 128)] = total.reshape(4, 2, 128, 128)
                sums[b, :, pl.ds(at_lane + 512, 128)] = column_sum(total.astype(F32))

            @pl.when(i == 1)
            def _():
                down.leave(0)
                for to in (at(z, 1 - y, c, x), at(z, y, c, 1 - x)):
                    pl.semaphore_signal(self.free, inc=1, device_id=to, device_id_type=MESH)
                self.swap_block.start()

            @pl.when(i == 5)
            def _():
                up.turn(2)
                up.turn(1)

            @pl.when(i == 9)
            def _():
                up.turn(3)
                up.turn(0)
                down.last()

            @pl.when(i == 13)
            def _():
                up.leave(2)
                up.leave(1)

        loop(16, attend)
        up.leave(3)
        up.leave(0)

        def qkv_gradient(i):
            b, half = i // 2, lax.rem(i, 2)
            value = tn(self.attn_in[:, block(half, 512)], flat(acts[b, :, :, :, 0:768]))
            self.buf_d[b, pl.ds(half * 2, 2), :, :, 0:768] = value.astype(BF).reshape(2, 2, 128, 768)

        loop(4, qkv_gradient)
        down.finish()
        pl.semaphore_wait(self.free, 2)
        attn.start()
        pair = self.pairs[3]

        def descend(i):
            partial = nt(flat(acts[0, i, :, :, 0:768]), flat(weights[0, :, :, :, 0:768]))
            pair.give(i, partial + nt(flat(acts[1, i, :, :, 0:768]), flat(weights[1, :, :, :, 0:768])))

        loop(4, descend)
        up.last()

        def leave(i):
            rows = block(i, 256)
            dy = pair.take(i)
            normal, scale = normalise(self.lat[rows, :].astype(F32))
            stats[6:7, :] += column_sum(dy)
            stats[7:8, :] += column_sum(dy * normal)
            dn = dy * (1.0 + vectors[1:2, :])
            dn = dn - jnp.mean(dn, -1, keepdims=True) - normal * jnp.mean(dn * normal, -1, keepdims=True)
            self.branch_one[rows, :] = (self.mid[rows, :] + scale * dn).astype(BF)

        loop(4, leave)
        self.swap_input.start()
        self.swap_block.finish()

    def end(self):
        z, y, c, x = place()
        stats, sums, up_sums, attn, up = self.stats, self.sums, self.up_sums, self.attn, self.up
        send, recv, mods = self.small_send, self.small_recv, self.all_mods
        rows = [stats[k : k + 1, :] for k in (6, 7, 4, 2, 3, 0)]
        for j in range(6):
            for h in range(2):
                self.mods[h, j : j + 1, :] = rows[j][:, h * 512 : (h + 1) * 512]
        far = remote(self.mods.at[1 - x], mods.at[z, y, 1 - c], send.at[2, 0], recv.at[2, 0], at(z, y, 1 - c, 1 - x))

        @pl.when(c != x)
        def _():
            far.start()

        @pl.when(c == x)
        def _():
            mods[z, y, c] = self.mods[x]

        columns, bias_part = self.columns, self.bias_part
        columns[...] = jnp.zeros_like(columns)
        bias_part[...] = jnp.zeros_like(bias_part)
        for b in range(2):
            spot = pl.ds(pl.multiple_of(b * 512 + c * 256, 256), 256)
            columns[0:1, spot] = sums[b, :, 0:256]
            columns[1:2, spot] = sums[b, :, 512:768]
        columns[2:3, :] = stats[5:6, :]
        columns[3:4, :] = stats[1:2, :]
        pieces = narrow(columns[0:1, :], 0) + narrow(columns[1:2, :], 1)
        pieces = pieces + narrow(columns[2:3, :], 2) + narrow(columns[3:4, :], 3)
        for k, (zz, yy, cc, xx) in enumerate(devices()):
            bias_part[cc, xx, yy, zz, 0:1, :] = pieces[k : k + 1, :]
        for b in range(2):
            for i in range(8):
                bias_part[i // 2 % 2, i % 2, i // 4, b * 2 + c, 1:2, :] = up_sums[b, :, i * 128 : (i + 1) * 128]
        bias = SmallScatter(
            bias_part, self.bias_c, self.bias_x, self.bias_y, self.bias_z, self.small_send.at[0], self.small_recv.at[3]
        )
        bias.start()

        @pl.when(c != x)
        def _():
            far.wait()

        spot = mods.at[z, y, c]
        core = remote(spot, spot, send.at[2, 1], recv.at[2, 1], at(z, y, 1 - c, x))
        core.start()
        bias.step(0)
        core.wait()
        spot_y = mods.at[z, y]
        across = remote(spot_y, spot_y, send.at[2, 2], recv.at[2, 2], at(z, 1 - y, c, x))
        across.start()
        bias.step(1)
        attn.turn(2)
        across.wait()
        spot_z = mods.at[z]
        along = [
            remote(spot_z, spot_z, send.at[2, 2 + k], recv.at[2, 2 + k], at(lax.rem(z + k, 4), y, c, x))
            for k in (1, 2, 3)
        ]
        for copy in along:
            copy.start()
        bias.step(2)
        attn.turn(1)
        silu_rows = self.silu[...].astype(BF)
        for copy in along:
            copy.wait()
        total = jnp.zeros((16, 128), F32)
        bias_rows = []
        for j in range(6):
            values = jnp.concatenate([mods[b // 4, b // 2 % 2, b % 2, j : j + 1, :] for b in range(16)], 0)
            high, low = split_bf(values)
            weights = self.wide[:, j * 512 : (j + 1) * 512]
            self.tall[...] = tn(silu_rows, high) + tn(silu_rows, low)
            self.ada_out[j] = self.tall[block(c, 64), :]
            total = total + nt(high, weights) + nt(low, weights)
            bias_rows.append(column_sum(values))
        self.found[...] = total
        group = (lax.rem(z, 2) * 2 + y) * 2 + c
        source = lax.broadcasted_iota(jnp.int32, (512, 128), 0)
        target = lax.broadcasted_iota(jnp.int32, (512, 128), 1)
        chosen = jnp.where((source == group * 64 + target) & (target < 64), 1.0, 0.0).astype(BF)
        self.picked[...] = exact_nn(jnp.concatenate(bias_rows + [jnp.zeros((2, 512), F32)], 0), chosen)
        first = [
            remote(self.found, self.other, send.at[3, 0], recv.at[1, 0], at(z, y, c, 1 - x)),
            remote(self.picked, self.picked_other, send.at[3, 1], recv.at[1, 1], at(z, y, c, 1 - x)),
        ]
        for copy in first:
            copy.start()
        attn.turn(3)
        for copy in first:
            copy.wait()
        self.ada_bias_out[...] = jnp.where(z // 2 == x, self.picked[...], self.picked_other[...])
        total = self.found[...] + self.other[...]
        spread_x, spread_c, spread_y, spread_z = self.spread_x, self.spread_c, self.spread_y, self.spread_z
        for b in range(16):
            spread_x[b % 2, b // 2 % 2, b // 4] = total[b : b + 1, :]
        second = remote(spread_x.at[1 - c], spread_c, send.at[3, 2], recv.at[1, 2], at(z, y, 1 - c, x))
        second.start()
        self.bias_out[...] = bias.finish()
        attn.turn(0)
        second.wait()
        spread_c[...] = spread_c[...] + spread_x[c]
        third = remote(spread_c.at[1 - y], spread_y.at[y], send.at[3, 3], recv.at[1, 3], at(z, 1 - y, c, x))
        third.start()
        spread_y[y] = spread_c[y]
        attn.leave(2)
        third.wait()
        fourth = []
        for k in (1, 2, 3):
            to = lax.rem(z + k, 4)
            fourth.append(
                remote(spread_y.at[:, to], spread_z.at[z], send.at[3, 3 + k], recv.at[1, 3 + k], at(to, y, c, x))
            )
            fourth[-1].start()
        spread_z[z] = spread_y[:, z]
        attn.leave(1)
        for copy in fourth:
            copy.wait()
        v = self.cond[...].astype(F32)
        v = jnp.concatenate([v[:, k * 128 : (k + 1) * 128] for k in range(8)], 0)
        gate = 1.0 / (1.0 + jnp.exp(-v))
        row = jnp.concatenate([spread_z[b // 2, b % 2] for b in range(8)], 0)
        self.cond_out[...] = row * gate * (1.0 + v * (1.0 - gate))
        attn.leave(3)
        attn.leave(0)
        up.finish()
        attn.last()
        self.swap_input.finish()
        attn.finish()


def on_device_pairs(
    latents_in,
    condition,
    grad_out,
    qkv_weight,
    proj_weight,
    up_weight,
    down_weight,
    ada_weight,
    query_bias,
    value_bias,
    proj_bias,
    up_bias,
    down_bias,
    ada_bias,
):
    x = lax.axis_index("tp")
    small = [b.reshape(1, -1) for b in (query_bias, value_bias, proj_bias, down_bias, up_bias)]
    out = lambda *shape: jax.ShapeDtypeStruct(shape, F32)
    group = jax.ShapeDtypeStruct(GROUP, BF)
    rows = jax.ShapeDtypeStruct((512, 1024), BF)
    results = pl.pallas_call(
        pairs_kernel,
        out_shape=[rows, rows, out(3, 64, 512), out(64, 512), out(64, 2048), out(64, 2048)]
        + [group] * 3
        + [out(6, 64, 512), out(8, 128), out(8, 128), out(2, 128)],
        in_specs=[IN_ANY] * 7 + [IN_VMEM] * 7,
        out_specs=[IN_ANY] * 9 + [IN_VMEM] * 4,
        scratch_shapes=list(scratch().values()),
        compiler_params=pltpu.CompilerParams(
            collective_id=0, has_side_effects=True, vmem_limit_bytes=63 * MIB
        ),
        name="dit_block",
    )(
        latents_in.reshape(512, 1024), grad_out.reshape(512, 1024), qkv_weight.transpose(1, 0, 2), proj_weight.T,
        up_weight, down_weight.T, ada_weight.transpose(1, 0, 2), condition, *small, ada_bias,
    )
    block_mine, input_mine, q_out, p_out, u_out, d_out, _, _, _, ada_out, cond_out, ada_bias_out, bias_out = results
    return (
        block_mine.reshape(512, 1, 1024),
        input_mine.astype(F32).reshape(512, 1, 1024),
        lax.dynamic_slice_in_dim(cond_out, x * 4, 4, 0).reshape(1, 512),
        q_out.transpose(1, 0, 2),
        p_out.T,
        u_out,
        d_out.T,
        ada_out.transpose(1, 0, 2),
        bias_out[0, 0:32],
        bias_out[0, 32:64],
        bias_out[0, 64:96],
        bias_out[1],
        bias_out[0, 96:128],
        lax.dynamic_slice_in_dim(ada_bias_out, x * 32, 32, 1)[:6],
    )


def solution(mesh):
    shape = dict(mesh.shape)
    pairs = shape["fsdp"] == 16 and shape["tp"] == 2
    return jax.shard_map(
        on_device_pairs if pairs else on_device_general,
        mesh=mesh,
        in_specs=(
            P("tp", "fsdp", None),
            P("fsdp", None),
            P("tp", "fsdp", None),
            P("fsdp", None, "tp"),
            P("tp", "fsdp"),
            P("fsdp", "tp"),
            P("tp", "fsdp"),
            P("fsdp", None, "tp"),
            P(("fsdp", "tp")),
            P(("fsdp", "tp")),
            P(("fsdp", "tp")),
            P(("fsdp", "tp")),
            P(("fsdp", "tp")),
            P(None, ("fsdp", "tp")),
        ),
        out_specs=(
            P("tp", "fsdp", None),
            P("tp", "fsdp", None),
            P("fsdp", "tp"),
            P("fsdp", None, "tp"),
            P("tp", "fsdp"),
            P("fsdp", "tp"),
            P("tp", "fsdp"),
            P("fsdp", None, "tp"),
            P(("fsdp", "tp")),
            P(("fsdp", "tp")),
            P(("fsdp", "tp")),
            P(("fsdp", "tp")),
            P(("fsdp", "tp")),
            P(None, ("fsdp", "tp")),
        ),
        check_vma=False,
    )
```

```python
import functools
import math

import jax
import jax.numpy as jnp
from jax import lax
from jax.experimental import pallas as pl
from jax.experimental.pallas import tpu as pltpu
from jax.sharding import PartitionSpec as P


HD = 64


epsilon = 1e-06


def layer_norm(values):
    centred = values - jnp.mean(values, axis=-1, keepdims=True)
    return centred * lax.rsqrt(jnp.mean(centred * centred, axis=-1, keepdims=True) + epsilon)


def modulate(values, shift_part, scale_part):
    return layer_norm(values) * (1.0 + scale_part) + shift_part


def gelu_tanh(values):
    return jax.nn.gelu(values, approximate=True)


def gather_rows(piece):
    return lax.all_gather(piece, "tp", axis=0, tiled=True)


def gather_grads(piece):
    return lax.all_gather(piece, "tp", axis=0, tiled=True)


def scatter_rows(product, row_count):
    return lax.psum_scatter(
        product(jnp.int32(0), row_count * lax.axis_size("tp")).astype(jnp.bfloat16),
        "tp",
        scatter_dimension=0,
        tiled=True,
    ).astype(jnp.float32)


def scatter_grads(product, row_count):
    return lax.psum_scatter(
        product(jnp.int32(0), row_count * lax.axis_size("tp")).astype(jnp.bfloat16),
        "tp",
        scatter_dimension=0,
        tiled=True,
    ).astype(jnp.float32)


def split_heads(packed):
    head_count = packed.shape[3] // HD
    shaped = packed.reshape(packed.shape[0], packed.shape[1], 3, head_count, HD)
    return (shaped[:, :, 0], shaped[:, :, 1], shaped[:, :, 2])


def attend_forward(packed):
    length, latents, local_width = (packed.shape[0], packed.shape[1], packed.shape[3])
    queries, key_rows, value_rows = split_heads(packed)
    block_rows = min(512, length)
    score_scale = 1.0 / math.sqrt(HD)
    blocks = queries.reshape(length // block_rows, block_rows, latents, local_width // HD, HD)

    def one_block(q_rows):
        scores = (
            jnp.einsum("qbhd,kbhd->bhqk", q_rows, key_rows, preferred_element_type=jnp.float32)
            * score_scale
        )
        largest = jnp.max(scores, axis=-1, keepdims=True)
        exponent = jnp.exp(scores - largest)
        summed = jnp.sum(exponent, axis=-1, keepdims=True)
        weights_soft = (exponent / summed).astype(jnp.bfloat16)
        mixture = jnp.einsum(
            "bhqk,kbhd->qbhd", weights_soft, value_rows, preferred_element_type=jnp.float32
        )
        return (mixture.astype(jnp.bfloat16), largest[..., 0] + jnp.log(summed[..., 0]))

    mixture_all, log_sums = lax.map(one_block, blocks)
    return (mixture_all.reshape(length, latents, local_width), log_sums)


def attend_backward(packed, log_sums, heads_grad):
    length, latents, local_width = (packed.shape[0], packed.shape[1], packed.shape[3])
    head_count = local_width // HD
    queries, key_rows, value_rows = split_heads(packed)
    block_rows = min(512, length)
    count_blocks = length // block_rows
    score_scale = 1.0 / math.sqrt(HD)
    q_blocks = queries.reshape(count_blocks, block_rows, latents, head_count, HD)
    g_blocks = heads_grad.reshape(count_blocks, block_rows, latents, head_count, HD)

    def one_block(carried, inputs):
        key_grad, value_grad = carried
        q_rows, g_rows, log_rows = inputs
        scores = (
            jnp.einsum("qbhd,kbhd->bhqk", q_rows, key_rows, preferred_element_type=jnp.float32)
            * score_scale
        )
        weights_soft = jnp.exp(scores - log_rows[..., None])
        soft_grad = jnp.einsum(
            "qbhd,kbhd->bhqk", g_rows, value_rows, preferred_element_type=jnp.float32
        )
        inner_sum = jnp.sum(weights_soft * soft_grad, axis=-1, keepdims=True)
        score_grad = (weights_soft * (soft_grad - inner_sum)).astype(jnp.bfloat16)
        query_grad = (
            jnp.einsum("bhqk,kbhd->qbhd", score_grad, key_rows, preferred_element_type=jnp.float32)
            * score_scale
        )
        key_grad = (
            key_grad
            + jnp.einsum("bhqk,qbhd->kbhd", score_grad, q_rows, preferred_element_type=jnp.float32)
            * score_scale
        )
        value_grad = value_grad + jnp.einsum(
            "bhqk,qbhd->kbhd",
            weights_soft.astype(jnp.bfloat16),
            g_rows,
            preferred_element_type=jnp.float32,
        )
        return ((key_grad, value_grad), query_grad)

    zero_rows = jnp.zeros((length, latents, head_count, HD), jnp.float32)
    (key_grad, value_grad), query_grad = lax.scan(
        one_block, (zero_rows, zero_rows), (q_blocks, g_blocks, log_sums)
    )
    stacked = jnp.stack(
        [
            query_grad.reshape(length, latents, local_width),
            key_grad.reshape(length, latents, local_width),
            value_grad.reshape(length, latents, local_width),
        ],
        axis=2,
    )
    return stacked.astype(jnp.bfloat16)


def on_device_general(
    latents_in,
    condition,
    grad_out,
    qkv_weight,
    proj_weight,
    up_weight,
    down_weight,
    ada_weight,
    query_bias,
    value_bias,
    proj_bias,
    up_bias,
    down_bias,
    ada_bias,
):
    tp_index = lax.axis_index("tp")
    local_rows = latents_in.shape[0]
    local_width = qkv_weight.shape[2]
    local_hidden = up_weight.shape[1]
    model_width = latents_in.shape[2]
    width_start = tp_index * local_width
    hidden_start = tp_index * local_hidden
    full_qkv, full_proj, full_up, full_down, full_ada = (
        lax.all_gather(qkv_weight, "fsdp", axis=0, tiled=True),
        lax.all_gather(proj_weight, "fsdp", axis=1, tiled=True),
        lax.all_gather(up_weight, "fsdp", axis=0, tiled=True),
        lax.all_gather(down_weight, "fsdp", axis=1, tiled=True),
        lax.all_gather(ada_weight, "fsdp", axis=0, tiled=True),
    )
    bias_list = (
        lax.all_gather(query_bias, ("fsdp", "tp"), axis=0, tiled=True),
        lax.all_gather(value_bias, ("fsdp", "tp"), axis=0, tiled=True),
        lax.all_gather(proj_bias, ("fsdp", "tp"), axis=0, tiled=True),
        lax.all_gather(up_bias, ("fsdp", "tp"), axis=0, tiled=True),
        lax.all_gather(down_bias, ("fsdp", "tp"), axis=0, tiled=True),
        lax.all_gather(ada_bias, ("fsdp", "tp"), axis=1, tiled=True),
    )
    all_query, all_value, all_proj, all_up, all_down, all_ada = [
        item_bias.astype(jnp.float32) for item_bias in bias_list
    ]
    hidden_total = all_up.shape[0]
    cond_float = condition.astype(jnp.float32)
    silu_cond = jax.nn.silu(cond_float).astype(jnp.bfloat16)
    ada_cols = lax.dynamic_slice_in_dim(all_ada, width_start, local_width, 1)
    mod_part = (
        jnp.einsum("bc,ctf->btf", silu_cond, full_ada, preferred_element_type=jnp.float32)
        + ada_cols
    )
    modulation = lax.all_gather(mod_part, "tp", axis=2, tiled=True)
    shift_one, scale_one, gate_one = (modulation[:, 0], modulation[:, 1], modulation[:, 2])
    shift_two, scale_two, gate_two = (modulation[:, 3], modulation[:, 4], modulation[:, 5])
    input_float = latents_in.astype(jnp.float32)
    attn_in = modulate(input_float, shift_one, scale_one).astype(jnp.bfloat16)
    attn_full = gather_rows(attn_in)
    query_cols = lax.dynamic_slice_in_dim(all_query, width_start, local_width, 0)
    value_cols = lax.dynamic_slice_in_dim(all_value, width_start, local_width, 0)
    bias_three = jnp.stack([query_cols, jnp.zeros_like(query_cols), value_cols])
    packed = (
        jnp.einsum("sbd,dtf->sbtf", attn_full, full_qkv, preferred_element_type=jnp.float32)
        + bias_three
    ).astype(jnp.bfloat16)
    heads_out, log_sums = attend_forward(packed)

    def project_heads(first_row, row_count):
        return jnp.einsum("sbf,fd->sbd", heads_out, full_proj, preferred_element_type=jnp.float32)

    branch_one = scatter_rows(project_heads, local_rows) + all_proj
    middle = input_float + gate_one * branch_one
    mlp_in = modulate(middle, shift_two, scale_two).astype(jnp.bfloat16)
    mlp_full = gather_rows(mlp_in)
    up_cols = lax.dynamic_slice_in_dim(all_up, hidden_start, local_hidden, 0)
    hidden = (
        jnp.einsum("sbd,df->sbf", mlp_full, full_up, preferred_element_type=jnp.float32) + up_cols
    )
    active = gelu_tanh(hidden).astype(jnp.bfloat16)

    def project_hidden(first_row, row_count):
        return jnp.einsum("sbf,fd->sbd", active, full_down, preferred_element_type=jnp.float32)

    branch_two = scatter_rows(project_hidden, local_rows) + all_down
    block_out = (middle + gate_two * branch_two).astype(jnp.bfloat16)
    grad_float = grad_out.astype(jnp.float32)
    gate_two_grad = jnp.sum(grad_float * branch_two, axis=0)
    branch_two_grad = (grad_float * gate_two).astype(jnp.bfloat16)
    down_bias_part = jnp.sum(branch_two_grad.astype(jnp.float32), axis=(0, 1))
    _, gelu_pull = jax.vjp(gelu_tanh, hidden)
    branch_two_full = gather_grads(branch_two_grad)
    active_grad = jnp.einsum(
        "sbd,fd->sbf", branch_two_full, full_down, preferred_element_type=jnp.float32
    )
    down_grad = jnp.einsum(
        "sbf,sbd->fd", active, branch_two_full, preferred_element_type=jnp.float32
    )
    hidden_grad = gelu_pull(active_grad)[0].astype(jnp.bfloat16)
    up_grad = jnp.einsum("sbd,sbf->df", mlp_full, hidden_grad, preferred_element_type=jnp.float32)
    up_bias_part = lax.dynamic_update_slice(
        jnp.zeros((hidden_total,), jnp.float32),
        jnp.sum(hidden_grad.astype(jnp.float32), axis=(0, 1)),
        (hidden_start,),
    )

    def back_hidden(first_row, row_count):
        return jnp.einsum("sbf,df->sbd", hidden_grad, full_up, preferred_element_type=jnp.float32)

    mlp_in_grad = scatter_grads(back_hidden, local_rows)
    _, second_pull = jax.vjp(modulate, middle, shift_two, scale_two)
    middle_part, shift_two_grad, scale_two_grad = second_pull(mlp_in_grad)
    middle_grad = grad_float + middle_part
    gate_one_grad = jnp.sum(middle_grad * branch_one, axis=0)
    branch_one_grad = (middle_grad * gate_one).astype(jnp.bfloat16)
    proj_bias_part = jnp.sum(branch_one_grad.astype(jnp.float32), axis=(0, 1))
    branch_one_full = gather_grads(branch_one_grad)
    heads_grad = jnp.einsum(
        "sbd,fd->sbf", branch_one_full, full_proj, preferred_element_type=jnp.float32
    ).astype(jnp.bfloat16)
    proj_grad = jnp.einsum(
        "sbf,sbd->fd", heads_out, branch_one_full, preferred_element_type=jnp.float32
    )
    packed_grad = attend_backward(packed, log_sums, heads_grad)
    qkv_grad = jnp.einsum(
        "sbd,sbtf->dtf", attn_full, packed_grad, preferred_element_type=jnp.float32
    )
    packed_sums = jnp.sum(packed_grad.astype(jnp.float32), axis=(0, 1))
    zero_width = jnp.zeros((model_width,), jnp.float32)
    query_bias_part = lax.dynamic_update_slice(zero_width, packed_sums[0], (width_start,))
    value_bias_part = lax.dynamic_update_slice(zero_width, packed_sums[2], (width_start,))

    def back_packed(first_row, row_count):
        return jnp.einsum(
            "sbtf,dtf->sbd", packed_grad, full_qkv, preferred_element_type=jnp.float32
        )

    attn_in_grad = scatter_grads(back_packed, local_rows)
    _, first_pull = jax.vjp(modulate, input_float, shift_one, scale_one)
    input_part, shift_one_grad, scale_one_grad = first_pull(attn_in_grad)
    input_grad = middle_grad + input_part
    mod_grad = jnp.stack(
        [
            shift_one_grad,
            scale_one_grad,
            gate_one_grad,
            shift_two_grad,
            scale_two_grad,
            gate_two_grad,
        ],
        axis=1,
    )
    mod_cols_grad = lax.psum_scatter(
        mod_grad.astype(jnp.bfloat16), "tp", scatter_dimension=2, tiled=True
    ).astype(jnp.float32)
    ada_grad = jnp.einsum(
        "bc,btf->ctf", silu_cond.astype(jnp.float32), mod_cols_grad, precision=lax.Precision.HIGHEST
    )
    ada_bias_part = lax.dynamic_update_slice(
        jnp.zeros((6, model_width), jnp.float32), jnp.sum(mod_cols_grad, axis=0), (0, width_start)
    )
    silu_grad = jnp.einsum(
        "btf,ctf->bc", mod_cols_grad, full_ada.astype(jnp.float32), precision=lax.Precision.HIGHEST
    )
    silu_cols = lax.psum_scatter(silu_grad, "tp", scatter_dimension=1, tiled=True)
    cond_width = silu_cols.shape[1]
    cond_cols = lax.dynamic_slice_in_dim(cond_float, tp_index * cond_width, cond_width, 1)
    _, silu_pull = jax.vjp(jax.nn.silu, cond_cols)
    cond_grad = silu_pull(silu_cols)[0]
    qkv_sum, proj_sum, up_sum, down_sum, ada_sum = (
        lax.psum_scatter(
            qkv_grad.astype(jnp.bfloat16), "fsdp", scatter_dimension=0, tiled=True
        ).astype(jnp.float32),
        lax.psum_scatter(
            proj_grad.astype(jnp.bfloat16), "fsdp", scatter_dimension=1, tiled=True
        ).astype(jnp.float32),
        lax.psum_scatter(
            up_grad.astype(jnp.bfloat16), "fsdp", scatter_dimension=0, tiled=True
        ).astype(jnp.float32),
        lax.psum_scatter(
            down_grad.astype(jnp.bfloat16), "fsdp", scatter_dimension=1, tiled=True
        ).astype(jnp.float32),
        lax.psum_scatter(
            ada_grad.astype(jnp.bfloat16), "fsdp", scatter_dimension=0, tiled=True
        ).astype(jnp.float32),
    )
    query_sum, value_sum, proj_bias_sum, up_bias_sum, down_bias_sum, ada_bias_sum = (
        lax.psum_scatter(query_bias_part, ("fsdp", "tp"), scatter_dimension=0, tiled=True),
        lax.psum_scatter(value_bias_part, ("fsdp", "tp"), scatter_dimension=0, tiled=True),
        lax.psum_scatter(proj_bias_part, ("fsdp", "tp"), scatter_dimension=0, tiled=True),
        lax.psum_scatter(up_bias_part, ("fsdp", "tp"), scatter_dimension=0, tiled=True),
        lax.psum_scatter(down_bias_part, ("fsdp", "tp"), scatter_dimension=0, tiled=True),
        lax.psum_scatter(ada_bias_part, ("fsdp", "tp"), scatter_dimension=1, tiled=True),
    )
    return (
        block_out,
        input_grad,
        cond_grad,
        qkv_sum,
        proj_sum,
        up_sum,
        down_sum,
        ada_sum,
        query_sum,
        value_sum,
        proj_bias_sum,
        up_bias_sum,
        down_bias_sum,
        ada_bias_sum,
    )


MESH = pl.DeviceIdType.MESH
ANY = pl.ANY
BF = jnp.bfloat16
F32 = jnp.float32
MIB = 2**20
IN_VMEM = pl.BlockSpec(memory_space=pltpu.VMEM)
IN_ANY = pl.BlockSpec(memory_space=ANY)
SPLIT = 80


def place():
    f, x = lax.axis_index("fsdp"), lax.axis_index("tp")
    z, y, c = f // 4, lax.rem(f // 2, 2), lax.rem(f, 2)
    return z, y, c, x


def at(z, y, c, x):
    return ((z * 2 + y) * 2 + c, x)


def block(index, size):
    return pl.ds(pl.multiple_of(index * size, size), size)


def remote(src, dst, send, recv, device):
    return pltpu.make_async_remote_copy(
        src_ref=src, dst_ref=dst, send_sem=send, recv_sem=recv, device_id=device, device_id_type=MESH
    )


def loop(count, body, ticks=None):
    def step(i, carry):
        body(i)
        for k, tick in (ticks or {}).items():

            @pl.when(i == k)
            def _(tick=tick):
                tick()

        return carry

    lax.fori_loop(0, count, step, 0)


def greet(devices):
    barrier = pltpu.get_barrier_semaphore()
    for device in devices:
        pl.semaphore_signal(barrier, inc=1, device_id=device, device_id_type=MESH)
    pl.semaphore_wait(barrier, len(devices))


def partners():
    z, y, c, x = place()
    out = [at(z, y, 1 - c, x), at(z, 1 - y, c, x), at(z, y, c, 1 - x), at(z, y, 1 - c, 1 - x)]
    out.append(at(z, 1 - y, c, 1 - x))
    return out + [at(lax.rem(z + d, 4), y, c, x) for d in (1, 2, 3)]


class Gather:
    def __init__(self, own, full, lanes, send, recv, local):
        self.own, self.full, self.lanes = own, full, pl.ds(*lanes)
        self.send, self.recv, self.local = send, recv, local

    def _core(self):
        z, y, c, x = place()
        copies = []
        for i, ((near, first, width), (far, _, _)) in enumerate(zip(self.own(c), self.own(1 - c))):
            spot = self.full.at[x, z, y, block(c, 64), pl.ds(first, width)]
            copies.append(pltpu.make_async_copy(near, spot, self.local.at[i]))
            copies.append(remote(far, spot, self.send.at[i], self.recv.at[i], at(z, y, 1 - c, x)))
        return copies

    def _copy(self, kind, d):
        z, y, c, x = place()
        a, b, from_z = pl.ds(0, SPLIT), pl.ds(SPLIT, 128 - SPLIT), lax.rem(z - d + 4, 4)
        if kind == 0:
            spot, to = self.full.at[x, z, y, :, self.lanes], at(lax.rem(z + d, 4), y, c, x)
        elif kind == 1:
            spot, to = self.full.at[x, from_z, y, a, self.lanes], at(z, y, c, 1 - x)
        elif kind == 2:
            spot, to = self.full.at[x, from_z, y, b, self.lanes], at(z, 1 - y, c, x)
        elif kind == 3:
            spot, to = self.full.at[:, from_z, y, a, self.lanes], at(z, 1 - y, c, x)
        else:
            spot, to = self.full.at[x, from_z, :, b, self.lanes], at(z, y, c, 1 - x)
        return remote(spot, spot, self.send.at[8 + 4 * kind + d], self.recv.at[8 + 4 * kind + d], to)

    def start_core(self):
        for copy in self._core():
            copy.start()

    def enter(self):
        for copy in self._core():
            copy.wait()
        for d in (2, 1, 3):
            self._copy(0, d).start()

    def first(self):
        self._copy(1, 0).start()
        self._copy(2, 0).start()

    def arrived(self, d):
        self._copy(0, d).wait()
        self._copy(1, d).start()
        self._copy(2, d).start()

    def turn(self, d):
        self._copy(1, d).wait()
        self._copy(3, d).start()
        self._copy(2, d).wait()
        self._copy(4, d).start()

    def finish(self):
        for d in range(4):
            self._copy(3, d).wait()
            self._copy(4, d).wait()


class Scatter:
    def __init__(self, part, first_a, first_b, second, third, total, lanes, out, send, recv):
        self.part, self.first_a, self.first_b = part, first_a, first_b
        self.second, self.third, self.total, self.out = second, third, total, out
        self.lanes, self.send, self.recv = pl.ds(*lanes), send, recv

    def _copy(self, kind, d):
        z, y, c, x = place()
        a, b, n, to_z = pl.ds(0, SPLIT), pl.ds(SPLIT, 128 - SPLIT), self.lanes, lax.rem(z + d, 4)
        send, recv = self.send.at[4 * kind + d], self.recv.at[4 * kind + d]
        to_x, to_y = at(z, y, c, 1 - x), at(z, 1 - y, c, x)
        if kind == 0:
            return remote(self.part.at[:, to_z, 1 - y, a, n], self.first_a.at[to_z, :, :, n], send, recv, to_y)
        if kind == 1:
            return remote(self.part.at[1 - x, to_z, :, b, n], self.first_b.at[to_z, :, :, n], send, recv, to_x)
        if kind == 2:
            return remote(self.first_a.at[to_z, 1 - x, :, n], self.second.at[to_z, a, n], send, recv, to_x)
        if kind == 3:
            return remote(self.first_b.at[to_z, 1 - y, :, n], self.second.at[to_z, b, n], send, recv, to_y)
        return remote(self.second.at[to_z, :, n], self.third.at[d - 1, :, n], send, recv, at(to_z, y, c, x))

    def _core(self):
        z, y, c, x = place()
        copies = []
        for i, (target, first, width) in enumerate(self.out(c)):
            lanes = pl.ds(first, width)
            copies.append(
                remote(
                    self.total.at[block(1 - c, 64), lanes], target, self.send.at[20 + i], self.recv.at[20 + i],
                    at(z, y, 1 - c, x),
                )
            )
            copies.append(pltpu.make_async_copy(self.total.at[block(c, 64), lanes], target, self.send.at[24 + i]))
        return copies

    def _start(self, d):
        self._copy(0, d).start()
        self._copy(1, d).start()

    def start(self):
        self._start(2)
        self._start(1)

    def turn(self, d):
        z, y, c, x = place()
        to_z, n = lax.rem(z + d, 4), self.lanes
        a, b = pl.ds(0, SPLIT), pl.ds(SPLIT, 128 - SPLIT)
        self._copy(0, d).wait()
        for k in range(2):
            total = self.first_a[to_z, k, :, n].astype(F32) + self.part[k, to_z, y, a, n].astype(F32)
            self.first_a[to_z, k, :, n] = total.astype(BF)
        self._copy(2, d).start()
        self._copy(1, d).wait()
        for k in range(2):
            total = self.first_b[to_z, k, :, n].astype(F32) + self.part[x, to_z, k, b, n].astype(F32)
            self.first_b[to_z, k, :, n] = total.astype(BF)
        self._copy(3, d).start()
        if d in (1, 2):
            self._start({2: 3, 1: 0}[d])

    def leave(self, d):
        z, y, c, x = place()
        to_z, n = lax.rem(z + d, 4), self.lanes
        a, b = pl.ds(0, SPLIT), pl.ds(SPLIT, 128 - SPLIT)
        self._copy(2, d).wait()
        total = self.second[to_z, a, n].astype(F32) + self.first_a[to_z, x, :, n].astype(F32)
        self.second[to_z, a, n] = total.astype(BF)
        self._copy(3, d).wait()
        total = self.second[to_z, b, n].astype(F32) + self.first_b[to_z, y, :, n].astype(F32)
        self.second[to_z, b, n] = total.astype(BF)
        if d:
            self._copy(4, d).start()

    def last(self):
        z, y, c, x = place()
        for d in (1, 2, 3):
            self._copy(4, d).wait()
        n = self.lanes

        def add(i):
            rows = block(i, 64)
            total = self.second[z, rows, n].astype(F32)
            for d in range(3):
                total = total + self.third[d, rows, n].astype(F32)
            self.total[rows, n] = total

        loop(2, add)
        for copy in self._core():
            copy.start()

    def finish(self):
        for copy in self._core():
            copy.wait()


class Swap:
    def __init__(self, own, full, send, recv, local):
        self.own, self.full, self.send, self.recv, self.local = own, full, send, recv, local

    def _both(self, act):
        z, y, c, x = place()

        @pl.when(c != x)
        def _():
            to = at(z, y, 1 - c, 1 - x)
            act(remote(self.own, self.full.at[block(1 - c, 512)], self.send.at[0], self.recv.at[0], to))

        @pl.when(c == x)
        def _():
            act(pltpu.make_async_copy(self.own, self.full.at[block(c, 512)], self.local))

    def _core(self):
        z, y, c, x = place()
        spot = self.full.at[block(c, 512)]
        return remote(spot, spot, self.send.at[1], self.recv.at[1], at(z, y, 1 - c, x))

    def start(self):
        self._both(lambda copy: copy.start())

    def share(self):
        self._both(lambda copy: copy.wait())
        self._core().start()

    def finish(self):
        self._core().wait()


class SwapBack:
    def __init__(self, full, out, send, recv, local):
        self.full, self.out, self.send, self.recv, self.local = full, out, send, recv, local

    def _both(self, act):
        z, y, c, x = place()
        rows = self.full.at[block(c, 512)]

        @pl.when(c != x)
        def _():
            act(remote(rows, self.out, self.send, self.recv, at(z, y, 1 - c, 1 - x)))

        @pl.when(c == x)
        def _():
            act(pltpu.make_async_copy(rows, self.out, self.local))

    def start(self):
        self._both(lambda copy: copy.start())

    def finish(self):
        self._both(lambda copy: copy.wait())


class SmallGather:
    def __init__(self, own, full, send, recv):
        self.own, self.full, self.send, self.recv = own, full, send, recv

    def _copy(self, k):
        z, y, c, x = place()
        send, recv = self.send.at[k], self.recv.at[k]
        if k == 0:
            return remote(self.own, self.full.at[x, z, y, c], send, recv, at(z, y, 1 - c, x))
        if k <= 3:
            spot = self.full.at[x, z, y]
            return remote(spot, spot, send, recv, at(lax.rem(z + k, 4), y, c, x))
        if k == 4:
            spot = self.full.at[x, :, y]
            return remote(spot, spot, send, recv, at(z, 1 - y, c, x))
        spot = self.full.at[x]
        return remote(spot, spot, send, recv, at(z, y, c, 1 - x))

    def start(self):
        z, y, c, x = place()
        self.full[x, z, y, c] = self.own[...]
        self._copy(0).start()

    def step(self, done, begin):
        for k in done:
            self._copy(k).wait()
        for k in begin:
            self._copy(k).start()


class SmallScatter:
    def __init__(self, part, near_c, near_z, near, send, recv):
        self.part, self.near_c, self.near_z, self.near = part, near_c, near_z, near
        self.send, self.recv = send, recv

    def _copy(self, k):
        z, y, c, x = place()
        send, recv = self.send.at[k], self.recv.at[k]
        if k == 0:
            return remote(self.part.at[1 - c], self.near_c, send, recv, at(z, y, 1 - c, x))
        if k <= 3:
            to = lax.rem(z + k, 4)
            return remote(self.near_c.at[to], self.near_z.at[k - 1], send, recv, at(to, y, c, x))
        to_x, to_y = ((1 - x, y), (x, 1 - y), (1 - x, 1 - y))[k - 4]
        return remote(self.near_z.at[3, to_x, to_y], self.near.at[k - 4], send, recv, at(z, to_y, c, to_x))

    def start(self):
        self._copy(0).start()

    def along(self):
        z, y, c, x = place()
        self._copy(0).wait()
        self.near_c[...] = self.near_c[...] + self.part[c]
        for k in (1, 2, 3):
            self._copy(k).start()

    def across(self):
        z, y, c, x = place()
        for k in (1, 2, 3):
            self._copy(k).wait()
        self.near_z[3] = self.near_c[z] + self.near_z[0] + self.near_z[1] + self.near_z[2]
        for k in (4, 5, 6):
            self._copy(k).start()

    def finish(self):
        z, y, c, x = place()
        for k in (4, 5, 6):
            self._copy(k).wait()
        return self.near_z[3, x, y] + self.near[0] + self.near[1] + self.near[2]


class Pair:
    def __init__(self, mine, theirs, send, recv):
        self.mine, self.theirs, self.send, self.recv = mine, theirs, send, recv

    def _copy(self, i):
        z, y, c, x = place()
        rows = block(i, 256)
        return remote(
            self.mine.at[rows], self.theirs.at[rows], self.send.at[i], self.recv.at[i], at(z, y, 1 - c, x)
        )

    def give(self, i, partial):
        self.mine[block(i, 256), :] = partial.astype(BF)
        self._copy(i).start()

    def take(self, i):
        self._copy(i).wait()
        rows = block(i, 256)
        return self.mine[rows, :].astype(F32) + self.theirs[rows, :].astype(F32)


def normalise(values):
    centred = values - jnp.mean(values, axis=-1, keepdims=True)
    scale = lax.rsqrt(jnp.mean(centred * centred, axis=-1, keepdims=True) + epsilon)
    return centred * scale, scale


def nn(a, b):
    return jnp.dot(a, b, preferred_element_type=F32)


def nt(a, b):
    return lax.dot_general(a, b, (((1,), (1,)), ((), ())), preferred_element_type=F32)


def tn(a, b):
    return lax.dot_general(a, b, (((0,), (0,)), ((), ())), preferred_element_type=F32)


def in_half(h):
    return lax.broadcasted_iota(jnp.int32, (1, 128), 1) // 64 == h


def column_sum(values):
    return jnp.sum(values, 0, keepdims=True)


def gelu_parts(v):
    k = math.sqrt(2.0 / math.pi)
    square = v * v
    t = jnp.tanh(k * v * (1.0 + 0.044715 * square))
    half = 0.5 * (1.0 + t)
    return v * half, half + 0.5 * k * v * (1.0 - t * t) * (1.0 + 3.0 * 0.044715 * square)


def split_bf(values):
    high = values.astype(BF)
    return high, (values - high.astype(F32)).astype(BF)


def exact_nn(values, chosen):
    high, low = split_bf(values)
    lower = (values - high.astype(F32) - low.astype(F32)).astype(BF)
    return nn(high, chosen) + nn(low, chosen) + nn(lower, chosen)


def devices():
    return [(zz, yy, cc, xx) for zz in range(4) for yy in range(2) for cc in range(2) for xx in range(2)]


def widen(small_full, row, k, width=1024):
    pieces = jnp.concatenate([small_full[xx, zz, yy, cc, row : row + 1, :] for zz, yy, cc, xx in devices()], 0)
    lane = lax.broadcasted_iota(jnp.int32, (128, width), 1)
    source = lax.broadcasted_iota(jnp.int32, (128, width), 0)
    pick = jnp.where(source == k * 32 + lax.rem(lane, 32), 1.0, 0.0).astype(BF)
    spread_out = nn(pieces.astype(BF), pick)
    device = lax.broadcasted_iota(jnp.int32, (32, width), 0)
    lane = lax.broadcasted_iota(jnp.int32, (32, width), 1)
    return column_sum(jnp.where(lane // 32 == device, spread_out, 0.0))


def narrow(vector, k):
    device = lax.broadcasted_iota(jnp.int32, (32, 1024), 0)
    lane = lax.broadcasted_iota(jnp.int32, (32, 1024), 1)
    source = lax.broadcasted_iota(jnp.int32, (1024, 128), 0)
    target = lax.broadcasted_iota(jnp.int32, (1024, 128), 1)
    chosen = jnp.where(target == k * 32 + lax.rem(source, 32), 1.0, 0.0).astype(BF)
    return exact_nn(jnp.where(lane // 32 == device, vector, 0.0), chosen)


def flat(value):
    return value.reshape(-1, value.shape[-1])


INPUTS = """lat_own grad_own wq wp wu wd ada cond q_bias v_bias p_bias d_bias u_bias a_bias"""
OUTPUTS = """block_mine input_mine q_out p_out u_out d_out held_a held_b
    ada_out cond_out ada_bias_out bias_out"""
GROUP = (2, 4, 2, 128, 1024)
TOKENS = (1024, 1024)


def scratch():
    v, f = (lambda *s: pltpu.VMEM(s, BF)), (lambda *s: pltpu.VMEM(s, F32))
    dma, regular = pltpu.SemaphoreType.DMA, pltpu.SemaphoreType.REGULAR
    out = dict(lat=v(*TOKENS), grad=v(*TOKENS), attn_in=v(*TOKENS), mid=f(*TOKENS), branch_one=v(*TOKENS))
    out.update(mlp_in=v(*TOKENS), g_two=v(*TOKENS), mine=v(*TOKENS), theirs_a=v(*TOKENS), theirs_b=v(*TOKENS))
    out.update(buf_a=v(*GROUP), buf_b=v(*GROUP), gu=v(*GROUP), buf_c=v(*GROUP), buf_d=v(*GROUP))
    for i in range(2):
        out[f"first_a{i}"], out[f"first_b{i}"] = v(4, 2, SPLIT, 1024), v(4, 2, 128 - SPLIT, 1024)
    for i in range(3):
        out[f"second{i}"], out[f"third{i}"] = v(4, 128, 1024), v(3, 128, 1024)
    out.update(total=f(128, 1024), heads_grad=v(2, 1024, 256), lse=f(1024, 128))
    out.update(key_total=f(1024, 128), value_total=f(1024, 128))
    out.update(small=f(16, 128), small_full=f(2, 4, 2, 2, 16, 128), wide=v(128, 3072), silu=f(16, 128))
    out.update(part=f(4, 2, 2, 8, 512), near_c=f(4, 2, 8, 512), near_y=f(4, 8, 512), near_z=f(4, 8, 512))
    out.update(mods=f(2, 8, 512), vectors=f(16, 1024), up_bias=f(1, 4096), stats=f(8, 1024), columns=f(8, 1024))
    out.update(up_sums=f(2, 1, 1024), sums=f(2, 1, 768), half_mods=f(4, 2, 2, 8, 512), all_mods=f(4, 2, 2, 8, 512), tall=f(128, 512))
    out.update(bias_part=f(2, 4, 2, 2, 2, 128), bias_c=f(4, 2, 2, 2, 128), bias_z=f(4, 2, 2, 2, 128))
    out.update(bias_near=f(3, 2, 128), found=f(2, 4, 2, 1, 128), found_c=f(4, 2, 1, 128), found_z=f(4, 2, 1, 128))
    out.update(found_near=f(3, 4, 1, 128), picked=f(8, 128), picked_other=f(8, 128))
    out.update(gather_send=dma((4, 28)), gather_recv=dma((4, 28)), gather_local=dma((4, 6)))
    out.update(scatter_send=dma((4, 28)), scatter_recv=dma((4, 28)), pair_send=dma((4, 4)), pair_recv=dma((4, 4)))
    out.update(swap_send=dma((4, 2)), swap_recv=dma((4, 2)), swap_local=dma((4,)))
    out.update(small_send=dma((4, 8)), small_recv=dma((4, 8)), load_sem=dma((12,)), free=regular)
    return out


def pairs_kernel(*refs):
    names = INPUTS.split() + OUTPUTS.split() + list(scratch())
    r = dict(zip(names, refs))
    Block(r).run()


class Block:
    def __init__(self, r):
        for name, ref in r.items():
            setattr(self, name, ref)

    def run(self):
        self.set_up()
        self.begin()
        self.attend()
        self.mlp()
        self.attend_back()
        self.end()

    def set_up(self):
        gather = lambda i, own, full, lanes: Gather(
            own, full, lanes, self.gather_send.at[i], self.gather_recv.at[i], self.gather_local.at[i]
        )
        self.q = gather(
            0,
            lambda h: [
                (self.wq.at[j, :, block(2 * h + k, 128)], 256 + 384 * k + 128 * j, 128)
                for k in range(2)
                for j in range(3)
            ],
            self.buf_a,
            (256, 768),
        )
        self.p = gather(1, lambda h: [(self.wp.at[:, block(h, 256)], 0, 256)], self.buf_a, (0, 256))
        self.u = gather(2, lambda h: [(self.wu.at[:, block(h, 1024)], 0, 1024)], self.gu, (0, 1024))
        self.d = gather(3, lambda h: [(self.wd.at[:, block(h, 1024)], 0, 1024)], self.buf_b, (0, 1024))
        heads = lambda k: lambda h: [
            (self.q_out.at[j, :, block(2 * h + k, 128)], 256 + 384 * k + 128 * j, 128) for j in range(3)
        ]
        outs = (
            lambda h: [(self.d_out.at[:, block(h, 1024)], 0, 1024)],
            lambda h: [(self.u_out.at[:, block(h, 1024)], 0, 1024)],
            lambda h: heads(0)(h) + [(self.p_out.at[:, block(h, 256)], 0, 256)],
            heads(1),
        )
        firsts = ((self.first_a0, self.first_b0), (self.first_a1, self.first_b1))
        rest = ((self.second0, self.third0), (self.second1, self.third1), (self.second2, self.third2))
        plan = (
            (self.buf_d, firsts[0], rest[0], (0, 1024)),
            (self.buf_c, firsts[1], rest[1], (0, 1024)),
            (self.buf_d, firsts[0], rest[2], (0, 640)),
            (self.buf_d, firsts[0], rest[2], (640, 384)),
        )
        self.down, self.up, self.near_heads, self.far_heads = [
            Scatter(part, *first, *more, self.total, lanes, outs[i], self.scatter_send.at[i], self.scatter_recv.at[i])
            for i, (part, first, more, lanes) in enumerate(plan)
        ]
        swaps = [(self.lat_own, self.lat), (self.grad_own, self.grad)]
        self.swap_lat, self.swap_grad = [
            Swap(own, full, self.swap_send.at[i], self.swap_recv.at[i], self.swap_local.at[i])
            for i, (own, full) in enumerate(swaps)
        ]
        backs = [(self.g_two, self.block_mine), (self.branch_one, self.input_mine)]
        self.swap_block, self.swap_input = [
            SwapBack(full, out, self.swap_send.at[2 + i, 0], self.swap_recv.at[2 + i, 0], self.swap_local.at[2 + i])
            for i, (full, out) in enumerate(backs)
        ]
        self.pairs = [
            Pair(self.mine, theirs, self.pair_send.at[i], self.pair_recv.at[i])
            for i, theirs in enumerate((self.theirs_a, self.theirs_b, self.theirs_a, self.theirs_b))
        ]

    def load(self, i, source, target):
        return pltpu.make_async_copy(source, target, self.load_sem.at[i])

    def begin(self):
        z, y, c, x = place()
        q, p, u, d = self.q, self.p, self.u, self.d
        send, recv = self.small_send, self.small_recv
        little = SmallGather(self.small, self.small_full, send.at[0], recv.at[0])
        v = self.cond[...].astype(F32)
        silu = (v / (1.0 + jnp.exp(-v))).astype(BF).astype(F32)
        self.small[...] = jnp.zeros_like(self.small)
        for k in range(8):
            self.small[k : k + 1, :] = silu[:, k * 128 : (k + 1) * 128]
        for k, bias in enumerate((self.q_bias, self.v_bias, self.p_bias, self.d_bias)):
            self.small[8:9, k * 32 : (k + 1) * 32] = bias[...].astype(F32)
        self.small[9:10, :] = self.u_bias[...].astype(F32)
        a_bias = self.a_bias[...].astype(F32)
        for j in range(6):
            self.small[10 + j // 4 : 11 + j // 4, j % 4 * 32 : j % 4 * 32 + 32] = a_bias[j : j + 1, :]
        greet(partners())
        little.start()
        q.start_core()
        for group in (p, u, d):
            group.start_core()
        self.swap_lat.start()
        self.wide[...] = jnp.zeros_like(self.wide)
        ada = [self.load(j, self.ada.at[j], self.wide.at[block(c, 64), pl.ds(j * 512, 512)]) for j in range(6)]
        for copy in ada:
            copy.start()
        little.step((0,), (1, 2, 3))
        q.enter()
        p.enter()
        self.part[...] = jnp.zeros_like(self.part)
        little.step((1, 2, 3), (4,))
        for copy in ada:
            copy.wait()
        little.step((4,), (5,))
        q.first()
        row = z * 2 + y
        lhs = [self.small_full[x, b // 4, b // 2 % 2, b % 2, pl.ds(row, 1), :] for b in range(16)]
        lhs = jnp.concatenate(lhs, 0)
        self.silu[...] = lhs
        for j in range(6):
            product = nn(lhs.astype(BF), self.wide[:, j * 512 : (j + 1) * 512])
            for b in range(16):
                self.part[b // 4, b // 2 % 2, b % 2, j : j + 1, :] = product[b : b + 1, :]
        near_c, near_y, near_z = self.near_c, self.near_y, self.near_z
        first = remote(self.part.at[:, :, 1 - c], near_c, send.at[1, 0], recv.at[1, 0], at(z, y, 1 - c, x))
        first.start()
        first.wait()
        for zz in range(4):
            for yy in range(2):
                near_c[zz, yy] = near_c[zz, yy] + self.part[zz, yy, c]
        second = remote(near_c.at[:, 1 - y], near_y, send.at[1, 1], recv.at[1, 1], at(z, 1 - y, c, x))
        second.start()
        second.wait()
        for zz in range(4):
            near_y[zz] = near_y[zz] + near_c[zz, y]
        thirds = []
        for s in (1, 2, 3):
            to = lax.rem(z + s, 4)
            thirds.append(
                remote(near_y.at[to], near_z.at[s - 1], send.at[1, 1 + s], recv.at[1, 1 + s], at(to, y, c, x))
            )
            thirds[-1].start()
        u.enter()
        d.enter()
        q.turn(0)
        q.arrived(2)
        q.arrived(1)
        q.arrived(3)
        for copy in thirds:
            copy.wait()
        near_z[3] = near_y[z] + near_z[0] + near_z[1] + near_z[2]
        fourth = remote(near_z.at[3], self.mods.at[1 - c], send.at[1, 5], recv.at[1, 5], at(z, y, 1 - c, 1 - x))

        @pl.when(c != x)
        def _():
            fourth.start()

        self.swap_lat.share()
        q.turn(2)

        @pl.when(c != x)
        def _():
            fourth.wait()

        @pl.when(c == x)
        def _():
            self.mods[c] = near_z[3]

        fifth = remote(self.mods.at[c], self.mods.at[c], send.at[1, 6], recv.at[1, 6], at(z, y, 1 - c, x))
        fifth.start()
        little.step((5,), ())
        bias = [widen(self.small_full, 8, k) for k in range(4)]
        ada_bias = [widen(self.small_full, 10 + j // 4, j % 4) for j in range(6)]
        for k, (zz, yy, cc, xx) in enumerate(devices()):
            self.up_bias[:, k * 128 : (k + 1) * 128] = self.small_full[xx, zz, yy, cc, 9:10, :]
        q.turn(1)
        fifth.wait()
        for j in range(6):
            for h in range(2):
                lanes = slice(h * 512, (h + 1) * 512)
                self.vectors[j : j + 1, lanes] = self.mods[h, j : j + 1, :] + ada_bias[j][:, lanes]
        for k in range(4):
            self.vectors[6 + k : 7 + k, :] = bias[k]
        q.turn(3)
        p.first()
        for k in (2, 1, 3):
            p.arrived(k)
        u.first()
        self.swap_lat.finish()

    def attend(self):
        z, y, c, x = place()
        q, p, u, d, vectors = self.q, self.p, self.u, self.d, self.vectors

        def modulated(i):
            rows = block(i, 256)
            normal, _ = normalise(self.lat[rows, :].astype(F32))
            self.attn_in[rows, :] = (normal * (1.0 + vectors[1:2, :]) + vectors[0:1, :]).astype(BF)

        loop(4, modulated)
        q.finish()
        self.swap_grad.start()

        def project(i):
            b, quarter = i // 4, lax.rem(i, 4)
            values = nn(self.attn_in[block(quarter, 256), :], flat(self.buf_a[b, :, :, :, 256:1024]))
            for k in range(6):
                value = values[:, k * 128 : (k + 1) * 128]
                if k % 3 != 1:
                    columns = pl.ds(pl.multiple_of(b * 512 + c * 256 + k // 3 * 128, 128), 128)
                    row = 6 if k % 3 == 0 else 7
                    value = value + vectors[row : row + 1, columns]
                self.buf_d[b, quarter, :, :, 256 + k * 128 : 384 + k * 128] = value.astype(BF).reshape(2, 128, 128)

        loop(8, project)
        for k in (0, 2, 1, 3):
            p.turn(k)
        for k in (2, 1, 3):
            u.arrived(k)
        lane = lax.broadcasted_iota(jnp.int32, (1, 128), 1)
        self.lse[...] = jnp.zeros_like(self.lse)

        def attend(i):
            pair, half = i // 2, lax.rem(i, 2)
            rows, zz = block(half, 512), pl.ds(half * 2, 2)
            b, k, q_at = lax.rem(pair, 2), pair // 2, pl.multiple_of(256 + pair // 2 * 384, 128)
            queries = flat(self.buf_d[b, zz, :, :, pl.ds(q_at, 128)]) * BF(0.125)
            keys = flat(self.buf_d[b, :, :, :, pl.ds(q_at + 128, 128)])
            values = flat(self.buf_d[b, :, :, :, pl.ds(q_at + 256, 128)])
            result = None
            logs = self.lse[rows, :]
            for h in range(2):
                scores = nt(jnp.where(in_half(h), queries, jnp.zeros_like(queries)), keys)
                largest = jnp.max(scores, -1, keepdims=True)
                exponent = jnp.exp(scores - largest)
                summed = jnp.sum(exponent, -1, keepdims=True)
                mixture = nn(exponent.astype(BF), values) * (1.0 / summed)
                result = mixture if h == 0 else jnp.where(in_half(0), result, mixture)
                logs = jnp.where(lane == pair * 2 + h, largest + jnp.log(summed), logs)
            self.buf_d[b, zz, :, :, block(k, 128)] = result.astype(BF).reshape(2, 2, 128, 128)
            self.lse[rows, :] = logs

        ticks = {
            0: lambda: u.turn(0),
            3: lambda: u.turn(2),
            4: lambda: u.turn(1),
            5: lambda: u.turn(3),
        }
        loop(8, attend, ticks)
        d.first()
        p.finish()
        self.load(0, self.buf_a, self.held_a).start()
        pair = self.pairs[0]

        def out(i):
            zz = i
            partial = nt(flat(self.buf_d[0, zz, :, :, 0:256]), flat(self.buf_a[0, :, :, :, 0:256]))
            partial += nt(flat(self.buf_d[1, zz, :, :, 0:256]), flat(self.buf_a[1, :, :, :, 0:256]))
            pair.give(i, partial)

        loop(4, out)
        self.load(1, self.buf_d, self.held_b).start()
        for k in (2, 1, 3):
            d.arrived(k)
        self.swap_grad.share()

        def residual(i):
            rows = block(i, 256)
            branch = pair.take(i) + vectors[8:9, :]
            self.branch_one[rows, :] = branch.astype(BF)
            self.mid[rows, :] = self.lat[rows, :].astype(F32) + vectors[2:3, :] * branch

        loop(4, residual)

    def mlp(self):
        z, y, c, x = place()
        u, d, vectors, stats, down, up = self.u, self.d, self.vectors, self.stats, self.down, self.up
        active, up_grad, slope, hidden_grad = self.buf_c, self.buf_c, self.buf_a, self.buf_a
        wd, gu, mid, mlp_in, g_two, grad = self.buf_b, self.gu, self.mid, self.mlp_in, self.g_two, self.grad
        self.swap_grad.finish()
        stats[...] = jnp.zeros_like(stats)
        self.up_sums[...] = jnp.zeros_like(self.up_sums)

        def enter(i):
            rows = block(i, 256)
            normal, _ = normalise(mid[rows, :])
            mlp_in[rows, :] = (normal * (1.0 + vectors[4:5, :]) + vectors[3:4, :]).astype(BF)
            g = (grad[rows, :].astype(F32) * vectors[5:6, :]).astype(BF)
            g_two[rows, :] = g
            mine_too = jnp.where(i // 2 == c, 1.0, 0.0)
            stats[1:2, :] += column_sum(g.astype(F32)) * mine_too

        loop(4, enter)
        u.finish()
        self.load(0, self.buf_a, self.held_a).wait()
        d.turn(0)

        def ascend(i):
            b, quarter = i // 4, lax.rem(i, 4)
            columns = pl.ds(pl.multiple_of(b * 2048 + c * 1024, 1024), 1024)
            hidden = nn(mlp_in[block(quarter, 256), :], flat(gu[b])) + self.up_bias[:, columns]
            value, gradient = gelu_parts(hidden)
            active[b, quarter] = value.astype(BF).reshape(2, 128, 1024)
            slope[b, quarter] = gradient.astype(BF).reshape(2, 128, 1024)

        loop(8, ascend, {3: lambda: d.turn(2), 6: lambda: d.turn(1)})
        self.load(1, self.buf_d, self.held_b).wait()

        def down_gradient(i):
            b, half = i // 2, lax.rem(i, 2)
            value = tn(g_two[:, block(half, 512)], flat(active[b]))
            self.buf_d[b, pl.ds(half * 2, 2)] = value.astype(BF).reshape(2, 2, 128, 1024)

        loop(4, down_gradient, {0: lambda: d.turn(3)})
        down.start()
        d.finish()
        pair, back = self.pairs[1], self.pairs[2]

        def descend(i):
            pair.give(i, nt(flat(active[0, i]), flat(wd[0])) + nt(flat(active[1, i]), flat(wd[1])))

        loop(4, descend, {1: lambda: down.turn(2)})

        def hidden_gradient(i):
            b, quarter = i // 4, lax.rem(i, 4)
            value = nn(g_two[block(quarter, 256), :], flat(wd[b])) * flat(slope[b, quarter]).astype(F32)
            value = value.astype(BF)
            hidden_grad[b, quarter] = value.reshape(2, 128, 1024)
            self.up_sums[b] += column_sum(value.astype(F32))

        loop(8, hidden_gradient, {1: lambda: down.turn(1), 7: lambda: down.turn(3)})
        self.load(3, self.held_b, self.buf_b).start()

        def leave(i):
            rows = block(i, 256)
            branch_two = pair.take(i) + vectors[9:10, :]
            g_two[rows, :] = (mid[rows, :] + vectors[5:6, :] * branch_two).astype(BF)
            stats[0:1, :] += column_sum(grad[rows, :].astype(F32) * branch_two)

        loop(4, leave)

        def descend_back(i):
            back.give(i, nt(flat(hidden_grad[0, i]), flat(gu[0])) + nt(flat(hidden_grad[1, i]), flat(gu[1])))

        loop(4, descend_back, {0: lambda: down.turn(0), 2: lambda: down.leave(2)})

        def up_gradient(i):
            b, half = i // 2, lax.rem(i, 2)
            value = tn(mlp_in[:, block(half, 512)], flat(hidden_grad[b]))
            up_grad[b, pl.ds(half * 2, 2)] = value.astype(BF).reshape(2, 2, 128, 1024)

        loop(4, up_gradient, {0: lambda: down.leave(1), 2: lambda: down.leave(3)})
        self.load(4, self.held_a, self.buf_a).start()
        up.start()

        def residual(i):
            rows = block(i, 256)
            dy = back.take(i)
            normal, scale = normalise(mid[rows, :])
            stats[2:3, :] += column_sum(dy)
            stats[3:4, :] += column_sum(dy * normal)
            dn = dy * (1.0 + vectors[4:5, :])
            dn = dn - jnp.mean(dn, -1, keepdims=True) - normal * jnp.mean(dn * normal, -1, keepdims=True)
            total = grad[rows, :].astype(F32) + scale * dn
            mid[rows, :] = total
            stats[4:5, :] += column_sum(total * self.branch_one[rows, :].astype(F32))
            g = (total * vectors[2:3, :]).astype(BF)
            mlp_in[rows, :] = g
            mine_too = jnp.where(i // 2 == c, 1.0, 0.0)
            stats[5:6, :] += column_sum(g.astype(F32)) * mine_too

        loop(4, residual)
        down.leave(0)
        for to in (at(z, 1 - y, c, x), at(z, y, c, 1 - x)):
            pl.semaphore_signal(self.free, inc=1, device_id=to, device_id_type=MESH)

    def attend_back(self):
        z, y, c, x = place()
        vectors, stats, down, up = self.vectors, self.stats, self.down, self.up
        near, far = self.near_heads, self.far_heads
        acts, g_one, heads_grad, sums = self.buf_b, self.mlp_in, self.heads_grad, self.sums
        weights = self.buf_a
        sums[...] = jnp.zeros_like(sums)
        self.load(3, self.held_b, self.buf_b).wait()
        self.load(4, self.held_a, self.buf_a).wait()

        def enter(i):
            b, half = i // 2, lax.rem(i, 2)
            value = nn(g_one[block(half, 512), :], flat(weights[b, :, :, :, 0:256]))
            heads_grad[b, block(half, 512), :] = value.astype(BF)

        loop(4, enter)

        def proj_gradient(i):
            b, half = i // 2, lax.rem(i, 2)
            value = tn(g_one[:, block(half, 512)], flat(acts[b, :, :, :, 0:256]))
            self.buf_d[b, pl.ds(half * 2, 2), :, :, 0:256] = value.astype(BF).reshape(2, 2, 128, 256)

        loop(4, proj_gradient)
        lane = lax.broadcasted_iota(jnp.int32, (1, 128), 1)

        def attend(i, k):
            b, quarter = i // 4, lax.rem(i, 4)
            rows, at_lane = block(quarter, 256), 256 + 384 * k
            queries = flat(acts[b, quarter, :, :, at_lane : at_lane + 128]) * BF(0.125)
            keys = flat(acts[b, :, :, :, at_lane + 128 : at_lane + 256])
            values = flat(acts[b, :, :, :, at_lane + 256 : at_lane + 384])
            grads = heads_grad[b, rows, k * 128 : (k + 1) * 128]

            @pl.when(quarter == 0)
            def _():
                self.key_total[...] = jnp.zeros_like(self.key_total)
                self.value_total[...] = jnp.zeros_like(self.value_total)

            result = None
            logs = self.lse[rows, :]
            for h in range(2):
                log = jnp.sum(jnp.where(lane == (k * 2 + b) * 2 + h, logs, 0.0), -1, keepdims=True)
                query = jnp.where(in_half(h), queries, jnp.zeros_like(queries))
                grad = jnp.where(in_half(h), grads, jnp.zeros_like(grads))
                probs = jnp.exp(nt(query, keys) - log)
                probs_grad = nt(grad, values)
                inner = jnp.sum(probs * probs_grad, -1, keepdims=True)
                score_grad = (probs * (probs_grad - inner)).astype(BF)
                query_grad = nn(score_grad, keys)
                result = query_grad if h == 0 else jnp.where(in_half(0), result, query_grad)
                self.key_total[...] += tn(score_grad, query)
                self.value_total[...] += tn(probs.astype(BF), grad)
            result = (result * 0.125).astype(BF)
            acts[b, quarter, :, :, at_lane : at_lane + 128] = result.reshape(2, 128, 128)
            sums[b, :, k * 128 : (k + 1) * 128] += column_sum(result.astype(F32))

            @pl.when(quarter == 3)
            def _():
                total = self.key_total[...].astype(BF)
                acts[b, :, :, :, at_lane + 128 : at_lane + 256] = total.reshape(4, 2, 128, 128)
                total = self.value_total[...].astype(BF)
                acts[b, :, :, :, at_lane + 256 : at_lane + 384] = total.reshape(4, 2, 128, 128)
                sums[b, :, 512 + k * 128 : 640 + k * 128] = column_sum(total.astype(F32))

        def qkv_gradient(i, k):
            b, half = i // 2, lax.rem(i, 2)
            lanes = slice(256 + 384 * k, 640 + 384 * k)
            value = tn(self.attn_in[:, block(half, 512)], flat(acts[b, :, :, :, lanes]))
            self.buf_d[b, pl.ds(half * 2, 2), :, :, lanes] = value.astype(BF).reshape(2, 2, 128, 384)

        ticks = {
            0: lambda: up.turn(2),
            2: lambda: up.turn(1),
            5: lambda: up.turn(3),
        }
        loop(8, lambda i: attend(i, 0), ticks)
        up.turn(0)
        loop(4, lambda i: qkv_gradient(i, 0))
        pl.semaphore_wait(self.free, 2)
        near.start()
        up.leave(2)
        ticks = {
            0: lambda: down.last(),
            1: lambda: up.leave(1),
            2: lambda: near.turn(2),
            3: lambda: up.leave(3),
            4: lambda: near.turn(1),
            5: lambda: up.leave(0),
            6: lambda: self.swap_block.start(),
            7: lambda: near.turn(3),
        }
        loop(8, lambda i: attend(i, 1), ticks)
        pair = self.pairs[3]

        def descend(i):
            partial = nt(flat(acts[0, i, :, :, 256:1024]), flat(weights[0, :, :, :, 256:1024]))
            pair.give(i, partial + nt(flat(acts[1, i, :, :, 256:1024]), flat(weights[1, :, :, :, 256:1024])))

        loop(4, descend, {1: lambda: near.turn(0), 3: lambda: near.leave(2)})
        down.finish()

        def leave(i):
            rows = block(i, 256)
            dy = pair.take(i)
            normal, scale = normalise(self.lat[rows, :].astype(F32))
            stats[6:7, :] += column_sum(dy)
            stats[7:8, :] += column_sum(dy * normal)
            dn = dy * (1.0 + vectors[1:2, :])
            dn = dn - jnp.mean(dn, -1, keepdims=True) - normal * jnp.mean(dn * normal, -1, keepdims=True)
            self.branch_one[rows, :] = (self.mid[rows, :] + scale * dn).astype(BF)

        loop(4, leave)
        self.begin_end()
        loop(4, lambda i: qkv_gradient(i, 1), {1: lambda: near.leave(1)})
        far.start()
        self.swap_input.start()
        up.last()

    def begin_end(self):
        z, y, c, x = place()
        stats, sums, up_sums = self.stats, self.sums, self.up_sums
        rows = [stats[k : k + 1, :] for k in (6, 7, 4, 2, 3, 0)]
        for j in range(6):
            for h in range(2):
                self.mods[h, j : j + 1, :] = rows[j][:, h * 512 : (h + 1) * 512]
        self.half_mods[z, y, x] = self.mods[c]
        for d in (1, 2, 3):
            self._mods(d).start()
        columns, bias_part = self.columns, self.bias_part
        columns[...] = jnp.zeros_like(columns)
        bias_part[...] = jnp.zeros_like(bias_part)
        for b in range(2):
            spot = pl.ds(pl.multiple_of(b * 512 + c * 256, 256), 256)
            columns[0:1, spot] = sums[b, :, 0:256]
            columns[1:2, spot] = sums[b, :, 512:768]
        columns[2:3, :] = stats[5:6, :]
        columns[3:4, :] = stats[1:2, :]
        pieces = narrow(columns[0:1, :], 0) + narrow(columns[1:2, :], 1)
        pieces = pieces + narrow(columns[2:3, :], 2) + narrow(columns[3:4, :], 3)
        for k, (zz, yy, cc, xx) in enumerate(devices()):
            bias_part[cc, zz, xx, yy, 0:1, :] = pieces[k : k + 1, :]
        for b in range(2):
            for i in range(8):
                bias_part[i // 2 % 2, b * 2 + c, i % 2, i // 4, 1:2, :] = up_sums[b, :, i * 128 : (i + 1) * 128]
        self.bias = SmallScatter(
            bias_part, self.bias_c, self.bias_z, self.bias_near, self.small_send.at[0], self.small_recv.at[3]
        )
        self.bias.start()
        for d in (1, 2, 3):
            self._mods(d).wait()
        self._across(lambda copy: copy.start())
        self.bias.along()

    def _mods(self, d):
        z, y, c, x = place()
        spot = self.half_mods.at[z, y, x]
        return remote(
            spot, spot, self.small_send.at[2, d], self.small_recv.at[2, d], at(lax.rem(z + d, 4), y, c, x)
        )

    def _across(self, act):
        z, y, c, x = place()
        spot = self.half_mods.at[:, y, x]
        copy = lambda k, to: remote(spot, spot, self.small_send.at[2, k], self.small_recv.at[2, k], to)

        @pl.when(c == x)
        def _():
            act(copy(4, at(z, 1 - y, c, x)))

        @pl.when(c != x)
        def _():
            act(copy(5, at(z, y, c, 1 - x)))
            act(copy(6, at(z, 1 - y, c, 1 - x)))

    def end(self):
        z, y, c, x = place()
        up, near, far, mods, bias = self.up, self.near_heads, self.far_heads, self.all_mods, self.bias
        send, recv = self.small_send, self.small_recv
        spot = self.half_mods.at[:, y, x]

        @pl.when(c == x)
        def _():
            remote(spot, spot, send.at[2, 4], recv.at[2, 4], at(z, 1 - y, c, x)).wait()
            remote(spot, spot, send.at[2, 5], recv.at[2, 5], at(z, y, c, 1 - x)).wait_recv()
            remote(spot, spot, send.at[2, 6], recv.at[2, 6], at(z, 1 - y, c, 1 - x)).wait_recv()
            share = remote(self.half_mods, mods, send.at[2, 7], recv.at[2, 7], at(z, y, 1 - c, x))
            share.start()
            keep = self.load(5, self.half_mods, mods)
            keep.start()
            keep.wait()
            share.wait_send()

        @pl.when(c != x)
        def _():
            remote(spot, spot, send.at[2, 5], recv.at[2, 5], at(z, y, c, 1 - x)).wait_send()
            remote(spot, spot, send.at[2, 6], recv.at[2, 6], at(z, 1 - y, c, 1 - x)).wait_send()
            remote(self.half_mods, mods, send.at[2, 7], recv.at[2, 7], at(z, y, 1 - c, x)).wait_recv()

        bias.across()
        silu_rows = self.silu[...].astype(BF)
        total = jnp.zeros((16, 128), F32)
        bias_rows = []
        for j in range(6):
            values = jnp.concatenate([mods[b // 4, b // 2 % 2, b % 2, j : j + 1, :] for b in range(16)], 0)
            high, low = split_bf(values)
            weights = self.wide[:, j * 512 : (j + 1) * 512]
            self.tall[...] = tn(silu_rows, high) + tn(silu_rows, low)
            self.ada_out[j] = self.tall[block(c, 64), :]
            total = total + nt(high, weights) + nt(low, weights)
            bias_rows.append(column_sum(values))
        found, found_c, found_z, found_near = self.found, self.found_c, self.found_z, self.found_near
        for b in range(16):
            found[b % 2, b // 4, b // 2 % 2] = total[b : b + 1, :]
        core = remote(found.at[1 - c], found_c, send.at[3, 0], recv.at[1, 0], at(z, y, 1 - c, x))
        core.start()
        far.turn(2)
        group = (lax.rem(z, 2) * 2 + y) * 2 + c
        source = lax.broadcasted_iota(jnp.int32, (512, 128), 0)
        target = lax.broadcasted_iota(jnp.int32, (512, 128), 1)
        chosen = jnp.where((source == group * 64 + target) & (target < 64), 1.0, 0.0).astype(BF)
        self.picked[...] = exact_nn(jnp.concatenate(bias_rows + [jnp.zeros((2, 512), F32)], 0), chosen)
        swap = remote(self.picked, self.picked_other, send.at[3, 7], recv.at[1, 7], at(z, y, c, 1 - x))
        swap.start()
        core.wait()
        found_c[...] = found_c[...] + found[c]
        along = []
        for k in (1, 2, 3):
            to = lax.rem(z + k, 4)
            along.append(remote(found_c.at[to], found_z.at[z], send.at[3, k], recv.at[1, k], at(to, y, c, x)))
            along[-1].start()
        found_z[z] = found_c[z]
        near.leave(3)
        far.turn(1)
        near.leave(0)
        for copy in along:
            copy.wait()
        across = []
        for k, (to_y, to_x) in enumerate(((y, 1 - x), (1 - y, x), (1 - y, 1 - x))):
            across.append(
                remote(found_z.at[:, to_y], found_near.at[k], send.at[3, 4 + k], recv.at[1, 4 + k], at(z, to_y, c, to_x))
            )
            across[-1].start()
        far.turn(3)
        far.turn(0)
        up.finish()
        near.last()
        far.leave(2)
        far.leave(1)
        for copy in across:
            copy.wait()
        swap.wait()
        self.bias_out[...] = bias.finish()
        self.ada_bias_out[...] = jnp.where(z // 2 == x, self.picked[...], self.picked_other[...])
        same, other = found_z[:, y] + found_near[0], found_near[1] + found_near[2]
        rows = [jnp.where(y == b % 2, same[b // 2], other[b // 2]) for b in range(8)]
        v = self.cond[...].astype(F32)
        v = jnp.concatenate([v[:, k * 128 : (k + 1) * 128] for k in range(8)], 0)
        gate = 1.0 / (1.0 + jnp.exp(-v))
        self.cond_out[...] = jnp.concatenate(rows, 0) * gate * (1.0 + v * (1.0 - gate))
        far.leave(3)
        far.leave(0)
        near.finish()
        far.last()
        self.swap_block.finish()
        self.swap_input.finish()
        far.finish()


def on_device_pairs(
    latents_in,
    condition,
    grad_out,
    qkv_weight,
    proj_weight,
    up_weight,
    down_weight,
    ada_weight,
    query_bias,
    value_bias,
    proj_bias,
    up_bias,
    down_bias,
    ada_bias,
):
    x = lax.axis_index("tp")
    small = [b.reshape(1, -1) for b in (query_bias, value_bias, proj_bias, down_bias, up_bias)]
    out = lambda *shape: jax.ShapeDtypeStruct(shape, F32)
    group = jax.ShapeDtypeStruct(GROUP, BF)
    rows = jax.ShapeDtypeStruct((512, 1024), BF)
    results = pl.pallas_call(
        pairs_kernel,
        out_shape=[rows, rows, out(3, 64, 512), out(64, 512), out(64, 2048), out(64, 2048)]
        + [group] * 2
        + [out(6, 64, 512), out(8, 128), out(8, 128), out(2, 128)],
        in_specs=[IN_ANY] * 7 + [IN_VMEM] * 7,
        out_specs=[IN_ANY] * 8 + [IN_VMEM] * 4,
        scratch_shapes=list(scratch().values()),
        compiler_params=pltpu.CompilerParams(
            collective_id=0, has_side_effects=True, vmem_limit_bytes=63 * MIB
        ),
        name="dit_block",
    )(
        latents_in.reshape(512, 1024), grad_out.reshape(512, 1024), qkv_weight.transpose(1, 0, 2), proj_weight.T,
        up_weight, down_weight.T, ada_weight.transpose(1, 0, 2), condition, *small, ada_bias,
    )
    block_mine, input_mine, q_out, p_out, u_out, d_out, _, _, ada_out, cond_out, ada_bias_out, bias_out = results
    return (
        block_mine.reshape(512, 1, 1024),
        input_mine.astype(F32).reshape(512, 1, 1024),
        lax.dynamic_slice_in_dim(cond_out, x * 4, 4, 0).reshape(1, 512),
        q_out.transpose(1, 0, 2),
        p_out.T,
        u_out,
        d_out.T,
        ada_out.transpose(1, 0, 2),
        bias_out[0, 0:32],
        bias_out[0, 32:64],
        bias_out[0, 64:96],
        bias_out[1],
        bias_out[0, 96:128],
        lax.dynamic_slice_in_dim(ada_bias_out, x * 32, 32, 1)[:6],
    )


def solution(mesh):
    shape = dict(mesh.shape)
    pairs = shape["fsdp"] == 16 and shape["tp"] == 2
    return jax.shard_map(
        on_device_pairs if pairs else on_device_general,
        mesh=mesh,
        in_specs=(
            P("tp", "fsdp", None),
            P("fsdp", None),
            P("tp", "fsdp", None),
            P("fsdp", None, "tp"),
            P("tp", "fsdp"),
            P("fsdp", "tp"),
            P("tp", "fsdp"),
            P("fsdp", None, "tp"),
            P(("fsdp", "tp")),
            P(("fsdp", "tp")),
            P(("fsdp", "tp")),
            P(("fsdp", "tp")),
            P(("fsdp", "tp")),
            P(None, ("fsdp", "tp")),
        ),
        out_specs=(
            P("tp", "fsdp", None),
            P("tp", "fsdp", None),
            P("fsdp", "tp"),
            P("fsdp", None, "tp"),
            P("tp", "fsdp"),
            P("fsdp", "tp"),
            P("tp", "fsdp"),
            P("fsdp", None, "tp"),
            P(("fsdp", "tp")),
            P(("fsdp", "tp")),
            P(("fsdp", "tp")),
            P(("fsdp", "tp")),
            P(("fsdp", "tp")),
            P(None, ("fsdp", "tp")),
        ),
        check_vma=False,
    )
```

```python
import functools
import math

import jax
import jax.numpy as jnp
from jax import lax
from jax.experimental import pallas as pl
from jax.experimental.pallas import tpu as pltpu
from jax.sharding import PartitionSpec as P


HD = 64


epsilon = 1e-06


def layer_norm(values):
    centred = values - jnp.mean(values, axis=-1, keepdims=True)
    return centred * lax.rsqrt(jnp.mean(centred * centred, axis=-1, keepdims=True) + epsilon)


def modulate(values, shift_part, scale_part):
    return layer_norm(values) * (1.0 + scale_part) + shift_part


def gelu_tanh(values):
    return jax.nn.gelu(values, approximate=True)


def gather_rows(piece):
    return lax.all_gather(piece, "tp", axis=0, tiled=True)


def gather_grads(piece):
    return lax.all_gather(piece, "tp", axis=0, tiled=True)


def scatter_rows(product, row_count):
    return lax.psum_scatter(
        product(jnp.int32(0), row_count * lax.axis_size("tp")).astype(jnp.bfloat16),
        "tp",
        scatter_dimension=0,
        tiled=True,
    ).astype(jnp.float32)


def scatter_grads(product, row_count):
    return lax.psum_scatter(
        product(jnp.int32(0), row_count * lax.axis_size("tp")).astype(jnp.bfloat16),
        "tp",
        scatter_dimension=0,
        tiled=True,
    ).astype(jnp.float32)


def split_heads(packed):
    head_count = packed.shape[3] // HD
    shaped = packed.reshape(packed.shape[0], packed.shape[1], 3, head_count, HD)
    return (shaped[:, :, 0], shaped[:, :, 1], shaped[:, :, 2])


def attend_forward(packed):
    length, latents, local_width = (packed.shape[0], packed.shape[1], packed.shape[3])
    queries, key_rows, value_rows = split_heads(packed)
    block_rows = min(512, length)
    score_scale = 1.0 / math.sqrt(HD)
    blocks = queries.reshape(length // block_rows, block_rows, latents, local_width // HD, HD)

    def one_block(q_rows):
        scores = (
            jnp.einsum("qbhd,kbhd->bhqk", q_rows, key_rows, preferred_element_type=jnp.float32)
            * score_scale
        )
        largest = jnp.max(scores, axis=-1, keepdims=True)
        exponent = jnp.exp(scores - largest)
        summed = jnp.sum(exponent, axis=-1, keepdims=True)
        weights_soft = (exponent / summed).astype(jnp.bfloat16)
        mixture = jnp.einsum(
            "bhqk,kbhd->qbhd", weights_soft, value_rows, preferred_element_type=jnp.float32
        )
        return (mixture.astype(jnp.bfloat16), largest[..., 0] + jnp.log(summed[..., 0]))

    mixture_all, log_sums = lax.map(one_block, blocks)
    return (mixture_all.reshape(length, latents, local_width), log_sums)


def attend_backward(packed, log_sums, heads_grad):
    length, latents, local_width = (packed.shape[0], packed.shape[1], packed.shape[3])
    head_count = local_width // HD
    queries, key_rows, value_rows = split_heads(packed)
    block_rows = min(512, length)
    count_blocks = length // block_rows
    score_scale = 1.0 / math.sqrt(HD)
    q_blocks = queries.reshape(count_blocks, block_rows, latents, head_count, HD)
    g_blocks = heads_grad.reshape(count_blocks, block_rows, latents, head_count, HD)

    def one_block(carried, inputs):
        key_grad, value_grad = carried
        q_rows, g_rows, log_rows = inputs
        scores = (
            jnp.einsum("qbhd,kbhd->bhqk", q_rows, key_rows, preferred_element_type=jnp.float32)
            * score_scale
        )
        weights_soft = jnp.exp(scores - log_rows[..., None])
        soft_grad = jnp.einsum(
            "qbhd,kbhd->bhqk", g_rows, value_rows, preferred_element_type=jnp.float32
        )
        inner_sum = jnp.sum(weights_soft * soft_grad, axis=-1, keepdims=True)
        score_grad = (weights_soft * (soft_grad - inner_sum)).astype(jnp.bfloat16)
        query_grad = (
            jnp.einsum("bhqk,kbhd->qbhd", score_grad, key_rows, preferred_element_type=jnp.float32)
            * score_scale
        )
        key_grad = (
            key_grad
            + jnp.einsum("bhqk,qbhd->kbhd", score_grad, q_rows, preferred_element_type=jnp.float32)
            * score_scale
        )
        value_grad = value_grad + jnp.einsum(
            "bhqk,qbhd->kbhd",
            weights_soft.astype(jnp.bfloat16),
            g_rows,
            preferred_element_type=jnp.float32,
        )
        return ((key_grad, value_grad), query_grad)

    zero_rows = jnp.zeros((length, latents, head_count, HD), jnp.float32)
    (key_grad, value_grad), query_grad = lax.scan(
        one_block, (zero_rows, zero_rows), (q_blocks, g_blocks, log_sums)
    )
    stacked = jnp.stack(
        [
            query_grad.reshape(length, latents, local_width),
            key_grad.reshape(length, latents, local_width),
            value_grad.reshape(length, latents, local_width),
        ],
        axis=2,
    )
    return stacked.astype(jnp.bfloat16)


def on_device_general(
    latents_in,
    condition,
    grad_out,
    qkv_weight,
    proj_weight,
    up_weight,
    down_weight,
    ada_weight,
    query_bias,
    value_bias,
    proj_bias,
    up_bias,
    down_bias,
    ada_bias,
):
    tp_index = lax.axis_index("tp")
    local_rows = latents_in.shape[0]
    local_width = qkv_weight.shape[2]
    local_hidden = up_weight.shape[1]
    model_width = latents_in.shape[2]
    width_start = tp_index * local_width
    hidden_start = tp_index * local_hidden
    full_qkv, full_proj, full_up, full_down, full_ada = (
        lax.all_gather(qkv_weight, "fsdp", axis=0, tiled=True),
        lax.all_gather(proj_weight, "fsdp", axis=1, tiled=True),
        lax.all_gather(up_weight, "fsdp", axis=0, tiled=True),
        lax.all_gather(down_weight, "fsdp", axis=1, tiled=True),
        lax.all_gather(ada_weight, "fsdp", axis=0, tiled=True),
    )
    bias_list = (
        lax.all_gather(query_bias, ("fsdp", "tp"), axis=0, tiled=True),
        lax.all_gather(value_bias, ("fsdp", "tp"), axis=0, tiled=True),
        lax.all_gather(proj_bias, ("fsdp", "tp"), axis=0, tiled=True),
        lax.all_gather(up_bias, ("fsdp", "tp"), axis=0, tiled=True),
        lax.all_gather(down_bias, ("fsdp", "tp"), axis=0, tiled=True),
        lax.all_gather(ada_bias, ("fsdp", "tp"), axis=1, tiled=True),
    )
    all_query, all_value, all_proj, all_up, all_down, all_ada = [
        item_bias.astype(jnp.float32) for item_bias in bias_list
    ]
    hidden_total = all_up.shape[0]
    cond_float = condition.astype(jnp.float32)
    silu_cond = jax.nn.silu(cond_float).astype(jnp.bfloat16)
    ada_cols = lax.dynamic_slice_in_dim(all_ada, width_start, local_width, 1)
    mod_part = (
        jnp.einsum("bc,ctf->btf", silu_cond, full_ada, preferred_element_type=jnp.float32)
        + ada_cols
    )
    modulation = lax.all_gather(mod_part, "tp", axis=2, tiled=True)
    shift_one, scale_one, gate_one = (modulation[:, 0], modulation[:, 1], modulation[:, 2])
    shift_two, scale_two, gate_two = (modulation[:, 3], modulation[:, 4], modulation[:, 5])
    input_float = latents_in.astype(jnp.float32)
    attn_in = modulate(input_float, shift_one, scale_one).astype(jnp.bfloat16)
    attn_full = gather_rows(attn_in)
    query_cols = lax.dynamic_slice_in_dim(all_query, width_start, local_width, 0)
    value_cols = lax.dynamic_slice_in_dim(all_value, width_start, local_width, 0)
    bias_three = jnp.stack([query_cols, jnp.zeros_like(query_cols), value_cols])
    packed = (
        jnp.einsum("sbd,dtf->sbtf", attn_full, full_qkv, preferred_element_type=jnp.float32)
        + bias_three
    ).astype(jnp.bfloat16)
    heads_out, log_sums = attend_forward(packed)

    def project_heads(first_row, row_count):
        return jnp.einsum("sbf,fd->sbd", heads_out, full_proj, preferred_element_type=jnp.float32)

    branch_one = scatter_rows(project_heads, local_rows) + all_proj
    middle = input_float + gate_one * branch_one
    mlp_in = modulate(middle, shift_two, scale_two).astype(jnp.bfloat16)
    mlp_full = gather_rows(mlp_in)
    up_cols = lax.dynamic_slice_in_dim(all_up, hidden_start, local_hidden, 0)
    hidden = (
        jnp.einsum("sbd,df->sbf", mlp_full, full_up, preferred_element_type=jnp.float32) + up_cols
    )
    active = gelu_tanh(hidden).astype(jnp.bfloat16)

    def project_hidden(first_row, row_count):
        return jnp.einsum("sbf,fd->sbd", active, full_down, preferred_element_type=jnp.float32)

    branch_two = scatter_rows(project_hidden, local_rows) + all_down
    block_out = (middle + gate_two * branch_two).astype(jnp.bfloat16)
    grad_float = grad_out.astype(jnp.float32)
    gate_two_grad = jnp.sum(grad_float * branch_two, axis=0)
    branch_two_grad = (grad_float * gate_two).astype(jnp.bfloat16)
    down_bias_part = jnp.sum(branch_two_grad.astype(jnp.float32), axis=(0, 1))
    _, gelu_pull = jax.vjp(gelu_tanh, hidden)
    branch_two_full = gather_grads(branch_two_grad)
    active_grad = jnp.einsum(
        "sbd,fd->sbf", branch_two_full, full_down, preferred_element_type=jnp.float32
    )
    down_grad = jnp.einsum(
        "sbf,sbd->fd", active, branch_two_full, preferred_element_type=jnp.float32
    )
    hidden_grad = gelu_pull(active_grad)[0].astype(jnp.bfloat16)
    up_grad = jnp.einsum("sbd,sbf->df", mlp_full, hidden_grad, preferred_element_type=jnp.float32)
    up_bias_part = lax.dynamic_update_slice(
        jnp.zeros((hidden_total,), jnp.float32),
        jnp.sum(hidden_grad.astype(jnp.float32), axis=(0, 1)),
        (hidden_start,),
    )

    def back_hidden(first_row, row_count):
        return jnp.einsum("sbf,df->sbd", hidden_grad, full_up, preferred_element_type=jnp.float32)

    mlp_in_grad = scatter_grads(back_hidden, local_rows)
    _, second_pull = jax.vjp(modulate, middle, shift_two, scale_two)
    middle_part, shift_two_grad, scale_two_grad = second_pull(mlp_in_grad)
    middle_grad = grad_float + middle_part
    gate_one_grad = jnp.sum(middle_grad * branch_one, axis=0)
    branch_one_grad = (middle_grad * gate_one).astype(jnp.bfloat16)
    proj_bias_part = jnp.sum(branch_one_grad.astype(jnp.float32), axis=(0, 1))
    branch_one_full = gather_grads(branch_one_grad)
    heads_grad = jnp.einsum(
        "sbd,fd->sbf", branch_one_full, full_proj, preferred_element_type=jnp.float32
    ).astype(jnp.bfloat16)
    proj_grad = jnp.einsum(
        "sbf,sbd->fd", heads_out, branch_one_full, preferred_element_type=jnp.float32
    )
    packed_grad = attend_backward(packed, log_sums, heads_grad)
    qkv_grad = jnp.einsum(
        "sbd,sbtf->dtf", attn_full, packed_grad, preferred_element_type=jnp.float32
    )
    packed_sums = jnp.sum(packed_grad.astype(jnp.float32), axis=(0, 1))
    zero_width = jnp.zeros((model_width,), jnp.float32)
    query_bias_part = lax.dynamic_update_slice(zero_width, packed_sums[0], (width_start,))
    value_bias_part = lax.dynamic_update_slice(zero_width, packed_sums[2], (width_start,))

    def back_packed(first_row, row_count):
        return jnp.einsum(
            "sbtf,dtf->sbd", packed_grad, full_qkv, preferred_element_type=jnp.float32
        )

    attn_in_grad = scatter_grads(back_packed, local_rows)
    _, first_pull = jax.vjp(modulate, input_float, shift_one, scale_one)
    input_part, shift_one_grad, scale_one_grad = first_pull(attn_in_grad)
    input_grad = middle_grad + input_part
    mod_grad = jnp.stack(
        [
            shift_one_grad,
            scale_one_grad,
            gate_one_grad,
            shift_two_grad,
            scale_two_grad,
            gate_two_grad,
        ],
        axis=1,
    )
    mod_cols_grad = lax.psum_scatter(
        mod_grad.astype(jnp.bfloat16), "tp", scatter_dimension=2, tiled=True
    ).astype(jnp.float32)
    ada_grad = jnp.einsum(
        "bc,btf->ctf", silu_cond.astype(jnp.float32), mod_cols_grad, precision=lax.Precision.HIGHEST
    )
    ada_bias_part = lax.dynamic_update_slice(
        jnp.zeros((6, model_width), jnp.float32), jnp.sum(mod_cols_grad, axis=0), (0, width_start)
    )
    silu_grad = jnp.einsum(
        "btf,ctf->bc", mod_cols_grad, full_ada.astype(jnp.float32), precision=lax.Precision.HIGHEST
    )
    silu_cols = lax.psum_scatter(silu_grad, "tp", scatter_dimension=1, tiled=True)
    cond_width = silu_cols.shape[1]
    cond_cols = lax.dynamic_slice_in_dim(cond_float, tp_index * cond_width, cond_width, 1)
    _, silu_pull = jax.vjp(jax.nn.silu, cond_cols)
    cond_grad = silu_pull(silu_cols)[0]
    qkv_sum, proj_sum, up_sum, down_sum, ada_sum = (
        lax.psum_scatter(
            qkv_grad.astype(jnp.bfloat16), "fsdp", scatter_dimension=0, tiled=True
        ).astype(jnp.float32),
        lax.psum_scatter(
            proj_grad.astype(jnp.bfloat16), "fsdp", scatter_dimension=1, tiled=True
        ).astype(jnp.float32),
        lax.psum_scatter(
            up_grad.astype(jnp.bfloat16), "fsdp", scatter_dimension=0, tiled=True
        ).astype(jnp.float32),
        lax.psum_scatter(
            down_grad.astype(jnp.bfloat16), "fsdp", scatter_dimension=1, tiled=True
        ).astype(jnp.float32),
        lax.psum_scatter(
            ada_grad.astype(jnp.bfloat16), "fsdp", scatter_dimension=0, tiled=True
        ).astype(jnp.float32),
    )
    query_sum, value_sum, proj_bias_sum, up_bias_sum, down_bias_sum, ada_bias_sum = (
        lax.psum_scatter(query_bias_part, ("fsdp", "tp"), scatter_dimension=0, tiled=True),
        lax.psum_scatter(value_bias_part, ("fsdp", "tp"), scatter_dimension=0, tiled=True),
        lax.psum_scatter(proj_bias_part, ("fsdp", "tp"), scatter_dimension=0, tiled=True),
        lax.psum_scatter(up_bias_part, ("fsdp", "tp"), scatter_dimension=0, tiled=True),
        lax.psum_scatter(down_bias_part, ("fsdp", "tp"), scatter_dimension=0, tiled=True),
        lax.psum_scatter(ada_bias_part, ("fsdp", "tp"), scatter_dimension=1, tiled=True),
    )
    return (
        block_out,
        input_grad,
        cond_grad,
        qkv_sum,
        proj_sum,
        up_sum,
        down_sum,
        ada_sum,
        query_sum,
        value_sum,
        proj_bias_sum,
        up_bias_sum,
        down_bias_sum,
        ada_bias_sum,
    )


MESH = pl.DeviceIdType.MESH
ANY = pl.ANY
BF = jnp.bfloat16
F32 = jnp.float32
MIB = 2**20
IN_VMEM = pl.BlockSpec(memory_space=pltpu.VMEM)
IN_ANY = pl.BlockSpec(memory_space=ANY)
ROWS_A, ROWS_B, ROWS_W = (0, 64), (64, 48), (112, 16)
ROWS_Z = 112
FIRST = ((0, 80), (80, 48), None)


def place():
    f, x = lax.axis_index("fsdp"), lax.axis_index("tp")
    z, y, c = f // 4, lax.rem(f // 2, 2), lax.rem(f, 2)
    return z, y, c, x


def at(z, y, c, x):
    return ((z * 2 + y) * 2 + c, x)


def block(index, size):
    return pl.ds(pl.multiple_of(index * size, size), size)


def remote(src, dst, send, recv, device):
    return pltpu.make_async_remote_copy(
        src_ref=src, dst_ref=dst, send_sem=send, recv_sem=recv, device_id=device, device_id_type=MESH
    )


def loop(count, body, ticks=None):
    def step(i, carry):
        body(i)
        for k, tick in (ticks or {}).items():

            @pl.when(i == k)
            def _(tick=tick):
                tick()

        return carry

    lax.fori_loop(0, count, step, 0)


def greet(devices):
    barrier = pltpu.get_barrier_semaphore()
    for device in devices:
        pl.semaphore_signal(barrier, inc=1, device_id=device, device_id_type=MESH)
    pl.semaphore_wait(barrier, len(devices))


def partners():
    z, y, c, x = place()
    out = [at(z, y, 1 - c, x), at(z, 1 - y, c, x), at(z, y, c, 1 - x), at(z, y, 1 - c, 1 - x)]
    out.append(at(z, 1 - y, c, 1 - x))
    return out + [at(lax.rem(z + d, 4), y, c, x) for d in (1, 2, 3)]


class Gather:
    def __init__(self, own, full, lanes, send, recv, local, rows=(ROWS_A, ROWS_B, ROWS_W)):
        self.own, self.full, self.lanes, self.rows = own, full, pl.ds(*lanes), rows
        self.send, self.recv, self.local = send, recv, local

    def _core(self):
        z, y, c, x = place()
        copies = []
        for i, ((near, first, width), (far, _, _)) in enumerate(zip(self.own(c), self.own(1 - c))):
            spot = self.full.at[x, z, y, block(c, 64), pl.ds(first, width)]
            copies.append(pltpu.make_async_copy(near, spot, self.local.at[i]))
            copies.append(remote(far, spot, self.send.at[i], self.recv.at[i], at(z, y, 1 - c, x)))
        return copies

    def _copy(self, kind, d):
        z, y, c, x = place()
        a, b, w = [pl.ds(*rows) if rows else None for rows in self.rows]
        from_z = lax.rem(z - d + 4, 4)
        to_x, to_y, to_z = at(z, y, c, 1 - x), at(z, 1 - y, c, x), at(lax.rem(z + d, 4), y, c, x)
        if kind == 0:
            spot, to = self.full.at[x, z, y, pl.ds(0, sum(self.rows[1])), self.lanes], to_z
        elif kind == 1:
            spot, to = self.full.at[x, from_z, y, a, self.lanes], to_x
        elif kind == 2:
            spot, to = self.full.at[x, from_z, y, b, self.lanes], to_y
        elif kind == 3:
            spot, to = self.full.at[:, from_z, y, a, self.lanes], to_y
        elif kind == 4:
            spot, to = self.full.at[x, from_z, :, b, self.lanes], to_x
        elif kind == 5:
            spot, to = self.full.at[:, z, :, w, self.lanes], to_z
        elif d == 0:
            spot, to = self.full.at[x, z, y, w, self.lanes], to_x
        else:
            spot, to = self.full.at[:, z, y, w, self.lanes], to_y
        return remote(spot, spot, self.send.at[8 + 4 * kind + d], self.recv.at[8 + 4 * kind + d], to)

    def start_core(self):
        for copy in self._core():
            copy.start()

    def enter(self, along=(2, 1, 3)):
        for copy in self._core():
            copy.wait()
        self.pass_on(along)

    def pass_on(self, along):
        for d in along:
            self._copy(0, d).start()

    def first(self):
        if self.rows[2]:
            self._copy(6, 0).start()
        self._copy(1, 0).start()
        self._copy(2, 0).start()

    def arrived(self, d):
        self._copy(0, d).wait()
        self._copy(1, d).start()
        self._copy(2, d).start()

    def turn(self, d):
        if self.rows[2] and d == 0:
            self._copy(6, 0).wait()
            self._copy(6, 1).start()
        self._copy(1, d).wait()
        self._copy(3, d).start()
        self._copy(2, d).wait()
        self._copy(4, d).start()
        if self.rows[2] and d == 2:
            self._copy(6, 1).wait()
            for k in (2, 1, 3):
                self._copy(5, k).start()

    def finish(self):
        for d in range(4):
            self._copy(3, d).wait()
            self._copy(4, d).wait()
        if self.rows[2]:
            for d in (2, 1, 3):
                self._copy(5, d).wait()


class Scatter:
    def __init__(self, part, first_a, first_b, second, third, wide_z, wide_y, wide_x, total, lanes, out, send, recv):
        self.part, self.first_a, self.first_b = part, first_a, first_b
        self.wide_z, self.wide_y, self.wide_x = wide_z, wide_y, wide_x
        self.second, self.third, self.total, self.out = second, third, total, out
        self.lanes, self.send, self.recv = pl.ds(*lanes), send, recv

    def _copy(self, kind, d):
        z, y, c, x = place()
        a, b, w, n, to_z = pl.ds(*ROWS_A), pl.ds(*ROWS_B), pl.ds(*ROWS_W), self.lanes, lax.rem(z + d, 4)
        send, recv = self.send.at[4 * kind + d], self.recv.at[4 * kind + d]
        to_x, to_y = at(z, y, c, 1 - x), at(z, 1 - y, c, x)
        if kind == 0:
            return remote(self.part.at[:, to_z, 1 - y, a, n], self.first_a.at[to_z, :, :, n], send, recv, to_y)
        if kind == 1:
            return remote(self.part.at[1 - x, to_z, :, b, n], self.first_b.at[to_z, :, :, n], send, recv, to_x)
        if kind == 2:
            return remote(self.first_a.at[to_z, 1 - x, :, n], self.second.at[to_z, a, n], send, recv, to_x)
        if kind == 3:
            return remote(self.first_b.at[to_z, 1 - y, :, n], self.second.at[to_z, b, n], send, recv, to_y)
        if kind == 4:
            return remote(self.second.at[to_z, :, n], self.third.at[d - 1, :, n], send, recv, at(to_z, y, c, x))
        if kind == 5:
            return remote(self.part.at[:, to_z, :, w, n], self.wide_z.at[d - 1, :, :, :, n], send, recv, at(to_z, y, c, x))
        if d == 0:
            return remote(self.wide_z.at[0, :, 1 - y, :, n], self.wide_y.at[:, :, n], send, recv, to_y)
        return remote(self.wide_y.at[1 - x, :, n], self.wide_x.at[:, n], send, recv, to_x)

    def _core(self):
        z, y, c, x = place()
        copies = []
        for i, (target, first, width) in enumerate(self.out(c)):
            lanes = pl.ds(first, width)
            copies.append(
                remote(
                    self.total.at[block(1 - c, 64), lanes], target, self.send.at[28 + i], self.recv.at[28 + i],
                    at(z, y, 1 - c, x),
                )
            )
            copies.append(pltpu.make_async_copy(self.total.at[block(c, 64), lanes], target, self.send.at[32 + i]))
        return copies

    def _start(self, d):
        self._copy(0, d).start()
        self._copy(1, d).start()

    def start(self):
        for d in (2, 1, 3):
            self._copy(5, d).start()
        self._start(2)
        self._start(1)

    def turn(self, d):
        z, y, c, x = place()
        to_z, n = lax.rem(z + d, 4), self.lanes
        a, b, w = pl.ds(*ROWS_A), pl.ds(*ROWS_B), pl.ds(*ROWS_W)
        self._copy(0, d).wait()
        for k in range(2):
            total = self.first_a[to_z, k, :, n].astype(F32) + self.part[k, to_z, y, a, n].astype(F32)
            self.first_a[to_z, k, :, n] = total.astype(BF)
        self._copy(2, d).start()
        self._copy(1, d).wait()
        for k in range(2):
            total = self.first_b[to_z, k, :, n].astype(F32) + self.part[x, to_z, k, b, n].astype(F32)
            self.first_b[to_z, k, :, n] = total.astype(BF)
        self._copy(3, d).start()
        if d in (1, 2):
            self._start({2: 3, 1: 0}[d])
        elif d == 0:
            self._fold_z()

    def _fold_z(self):
        z, y, c, x = place()
        n, w = self.lanes, pl.ds(*ROWS_W)
        for k in (2, 1, 3):
            self._copy(5, k).wait()
        for k in range(2):
            total = self.part[k, z, :, w, n].astype(F32)
            for s in range(3):
                total = total + self.wide_z[s, k, :, :, n].astype(F32)
            self.wide_z[0, k, :, :, n] = total.astype(BF)
        self._copy(6, 0).start()

    def _fold_y(self):
        z, y, c, x = place()
        n = self.lanes
        self._copy(6, 0).wait()
        total = self.wide_y[:, :, n].astype(F32) + self.wide_z[0, :, y, :, n].astype(F32)
        self.wide_y[:, :, n] = total.astype(BF)
        self._copy(6, 1).start()

    def leave(self, d):
        z, y, c, x = place()
        to_z, n = lax.rem(z + d, 4), self.lanes
        a, b = pl.ds(*ROWS_A), pl.ds(*ROWS_B)
        self._copy(2, d).wait()
        total = self.second[to_z, a, n].astype(F32) + self.first_a[to_z, x, :, n].astype(F32)
        self.second[to_z, a, n] = total.astype(BF)
        self._copy(3, d).wait()
        total = self.second[to_z, b, n].astype(F32) + self.first_b[to_z, y, :, n].astype(F32)
        self.second[to_z, b, n] = total.astype(BF)
        if d:
            self._copy(4, d).start()
        if d == 1:
            self._fold_y()

    def last(self):
        z, y, c, x = place()
        n, w = self.lanes, pl.ds(*ROWS_W)
        self._copy(6, 1).wait()
        self.total[w, n] = self.wide_x[:, n].astype(F32) + self.wide_y[x, :, n].astype(F32)
        for d in (1, 2, 3):
            self._copy(4, d).wait()

        for rows in (pl.ds(*ROWS_A), pl.ds(*ROWS_B)):
            total = self.second[z, rows, n].astype(F32)
            for d in range(3):
                total = total + self.third[d, rows, n].astype(F32)
            self.total[rows, n] = total
        for copy in self._core():
            copy.start()

    def finish(self):
        for copy in self._core():
            copy.wait()


class Swap:
    def __init__(self, own, full, send, recv, local):
        self.own, self.full, self.send, self.recv, self.local = own, full, send, recv, local

    def _both(self, act):
        z, y, c, x = place()

        @pl.when(c != x)
        def _():
            to = at(z, y, 1 - c, 1 - x)
            act(remote(self.own, self.full.at[block(1 - c, 512)], self.send.at[0], self.recv.at[0], to))

        @pl.when(c == x)
        def _():
            act(pltpu.make_async_copy(self.own, self.full.at[block(c, 512)], self.local))

    def _core(self):
        z, y, c, x = place()
        spot = self.full.at[block(c, 512)]
        return remote(spot, spot, self.send.at[1], self.recv.at[1], at(z, y, 1 - c, x))

    def start(self):
        self._both(lambda copy: copy.start())

    def share(self):
        self._both(lambda copy: copy.wait())
        self._core().start()

    def finish(self):
        self._core().wait()


class SwapBack:
    def __init__(self, full, out, send, recv, local):
        self.full, self.out, self.send, self.recv, self.local = full, out, send, recv, local

    def _both(self, act):
        z, y, c, x = place()
        rows = self.full.at[block(c, 512)]

        @pl.when(c != x)
        def _():
            act(remote(rows, self.out, self.send, self.recv, at(z, y, 1 - c, 1 - x)))

        @pl.when(c == x)
        def _():
            act(pltpu.make_async_copy(rows, self.out, self.local))

    def start(self):
        self._both(lambda copy: copy.start())

    def finish(self):
        self._both(lambda copy: copy.wait())


class SmallGather:
    def __init__(self, own, full, send, recv):
        self.own, self.full, self.send, self.recv = own, full, send, recv

    def _copy(self, k):
        z, y, c, x = place()
        send, recv = self.send.at[k], self.recv.at[k]
        if k == 0:
            return remote(self.own, self.full.at[x, z, y, c], send, recv, at(z, y, 1 - c, x))
        if k <= 3:
            spot = self.full.at[x, z, y]
            return remote(spot, spot, send, recv, at(lax.rem(z + k, 4), y, c, x))
        if k == 4:
            spot = self.full.at[x, :, y]
            return remote(spot, spot, send, recv, at(z, 1 - y, c, x))
        spot = self.full.at[x]
        return remote(spot, spot, send, recv, at(z, y, c, 1 - x))

    def start(self):
        z, y, c, x = place()
        self.full[x, z, y, c] = self.own[...]
        self._copy(0).start()

    def step(self, done, begin):
        for k in done:
            self._copy(k).wait()
        for k in begin:
            self._copy(k).start()


class SmallScatter:
    def __init__(self, part, near_c, near_z, near, send, recv):
        self.part, self.near_c, self.near_z, self.near = part, near_c, near_z, near
        self.send, self.recv = send, recv

    def _copy(self, k):
        z, y, c, x = place()
        send, recv = self.send.at[k], self.recv.at[k]
        if k == 0:
            return remote(self.part.at[1 - c], self.near_c, send, recv, at(z, y, 1 - c, x))
        if k <= 3:
            to = lax.rem(z + k, 4)
            return remote(self.near_c.at[to], self.near_z.at[k - 1], send, recv, at(to, y, c, x))
        to_x, to_y = ((1 - x, y), (x, 1 - y), (1 - x, 1 - y))[k - 4]
        return remote(self.near_z.at[3, to_x, to_y], self.near.at[k - 4], send, recv, at(z, to_y, c, to_x))

    def start(self):
        self._copy(0).start()

    def along(self):
        z, y, c, x = place()
        self._copy(0).wait()
        self.near_c[...] = self.near_c[...] + self.part[c]
        for k in (1, 2, 3):
            self._copy(k).start()

    def across(self):
        z, y, c, x = place()
        for k in (1, 2, 3):
            self._copy(k).wait()
        self.near_z[3] = self.near_c[z] + self.near_z[0] + self.near_z[1] + self.near_z[2]
        for k in (4, 5, 6):
            self._copy(k).start()

    def finish(self):
        z, y, c, x = place()
        for k in (4, 5, 6):
            self._copy(k).wait()
        return self.near_z[3, x, y] + self.near[0] + self.near[1] + self.near[2]


class Pair:
    def __init__(self, mine, theirs, send, recv):
        self.mine, self.theirs, self.send, self.recv = mine, theirs, send, recv

    def _copy(self, i):
        z, y, c, x = place()
        rows = block(i, 256)
        return remote(
            self.mine.at[rows], self.theirs.at[rows], self.send.at[i], self.recv.at[i], at(z, y, 1 - c, x)
        )

    def give(self, i, partial):
        self.mine[block(i, 256), :] = partial.astype(BF)
        self._copy(i).start()

    def take(self, i):
        self._copy(i).wait()
        rows = block(i, 256)
        return self.mine[rows, :].astype(F32) + self.theirs[rows, :].astype(F32)


def normalise(values):
    centred = values - jnp.mean(values, axis=-1, keepdims=True)
    scale = lax.rsqrt(jnp.mean(centred * centred, axis=-1, keepdims=True) + epsilon)
    return centred * scale, scale


def nn(a, b):
    return jnp.dot(a, b, preferred_element_type=F32)


def nt(a, b):
    return lax.dot_general(a, b, (((1,), (1,)), ((), ())), preferred_element_type=F32)


def tn(a, b):
    return lax.dot_general(a, b, (((0,), (0,)), ((), ())), preferred_element_type=F32)


def in_half(h):
    return lax.broadcasted_iota(jnp.int32, (1, 128), 1) // 64 == h


def column_sum(values):
    return jnp.sum(values, 0, keepdims=True)


def gelu_parts(v):
    k = math.sqrt(2.0 / math.pi)
    square = v * v
    t = jnp.tanh(k * v * (1.0 + 0.044715 * square))
    half = 0.5 * (1.0 + t)
    return v * half, half + 0.5 * k * v * (1.0 - t * t) * (1.0 + 3.0 * 0.044715 * square)


def split_bf(values):
    high = values.astype(BF)
    return high, (values - high.astype(F32)).astype(BF)


def exact_nn(values, chosen):
    high, low = split_bf(values)
    lower = (values - high.astype(F32) - low.astype(F32)).astype(BF)
    return nn(high, chosen) + nn(low, chosen) + nn(lower, chosen)


def devices():
    return [(zz, yy, cc, xx) for zz in range(4) for yy in range(2) for cc in range(2) for xx in range(2)]


def widen(small_full, row, k, width=1024):
    pieces = jnp.concatenate([small_full[xx, zz, yy, cc, row : row + 1, :] for zz, yy, cc, xx in devices()], 0)
    lane = lax.broadcasted_iota(jnp.int32, (128, width), 1)
    source = lax.broadcasted_iota(jnp.int32, (128, width), 0)
    pick = jnp.where(source == k * 32 + lax.rem(lane, 32), 1.0, 0.0).astype(BF)
    spread_out = nn(pieces.astype(BF), pick)
    device = lax.broadcasted_iota(jnp.int32, (32, width), 0)
    lane = lax.broadcasted_iota(jnp.int32, (32, width), 1)
    return column_sum(jnp.where(lane // 32 == device, spread_out, 0.0))


def narrow(vector, k):
    device = lax.broadcasted_iota(jnp.int32, (32, 1024), 0)
    lane = lax.broadcasted_iota(jnp.int32, (32, 1024), 1)
    source = lax.broadcasted_iota(jnp.int32, (1024, 128), 0)
    target = lax.broadcasted_iota(jnp.int32, (1024, 128), 1)
    chosen = jnp.where(target == k * 32 + lax.rem(source, 32), 1.0, 0.0).astype(BF)
    return exact_nn(jnp.where(lane // 32 == device, vector, 0.0), chosen)


def flat(value):
    return value.reshape(-1, value.shape[-1])


INPUTS = """lat_own grad_own wq wp wu wd ada cond q_bias v_bias p_bias d_bias u_bias a_bias"""
OUTPUTS = """block_mine input_mine q_out p_out u_out d_out held_a held_b
    ada_out cond_out ada_bias_out bias_out"""
GROUP = (2, 4, 2, 128, 1024)
TOKENS = (1024, 1024)


def scratch():
    v, f = (lambda *s: pltpu.VMEM(s, BF)), (lambda *s: pltpu.VMEM(s, F32))
    dma, regular = pltpu.SemaphoreType.DMA, pltpu.SemaphoreType.REGULAR
    out = dict(lat=v(*TOKENS), grad=v(*TOKENS), attn_in=v(*TOKENS), mid=f(*TOKENS), branch_one=v(*TOKENS))
    out.update(mlp_in=v(*TOKENS), g_two=v(*TOKENS), mine=v(*TOKENS), theirs_a=v(*TOKENS), theirs_b=v(*TOKENS))
    out.update(buf_a=v(*GROUP), buf_b=v(*GROUP), gu=v(*GROUP), buf_c=v(*GROUP), buf_d=v(*GROUP))
    for i in range(2):
        out[f"first_a{i}"], out[f"first_b{i}"] = v(4, 2, ROWS_A[1], 1024), v(4, 2, ROWS_B[1], 1024)
    for i in range(3):
        out[f"second{i}"], out[f"third{i}"] = v(4, ROWS_Z, 1024), v(3, ROWS_Z, 1024)
        out[f"wide_z{i}"], out[f"wide_y{i}"] = v(3, 2, 2, ROWS_W[1], 1024), v(2, ROWS_W[1], 1024)
        out[f"wide_x{i}"] = v(ROWS_W[1], 1024)
    out.update(total=f(128, 1024), heads_grad=v(2, 1024, 256), lse=f(1024, 128))
    out.update(key_total=f(1024, 128), value_total=f(1024, 128))
    out.update(small=f(16, 128), small_full=f(2, 4, 2, 2, 16, 128), wide=v(128, 3072), silu=f(16, 128))
    out.update(part=f(2, 4, 2, 8, 512), near_c=f(4, 2, 8, 512), near_z=f(4, 2, 8, 512), near_y=f(2, 8, 512))
    out.update(mods=f(2, 8, 512), vectors=f(16, 1024), up_bias=f(1, 4096), stats=f(8, 1024), columns=f(8, 1024))
    out.update(up_sums=f(2, 1, 1024), sums=f(2, 1, 768), half_mods=f(4, 2, 2, 8, 512), all_mods=f(4, 2, 2, 8, 512), tall=f(128, 512))
    out.update(bias_part=f(2, 4, 2, 2, 2, 128), bias_c=f(4, 2, 2, 2, 128), bias_z=f(4, 2, 2, 2, 128))
    out.update(bias_near=f(3, 2, 128), found=f(2, 4, 2, 1, 128), found_c=f(4, 2, 1, 128), found_z=f(4, 2, 1, 128))
    out.update(found_near=f(3, 4, 1, 128), picked=f(8, 128), picked_other=f(8, 128))
    out.update(gather_send=dma((4, 36)), gather_recv=dma((4, 36)), gather_local=dma((4, 6)))
    out.update(scatter_send=dma((4, 36)), scatter_recv=dma((4, 36)), pair_send=dma((4, 4)), pair_recv=dma((4, 4)))
    out.update(swap_send=dma((4, 2)), swap_recv=dma((4, 2)), swap_local=dma((4,)))
    out.update(small_send=dma((4, 8)), small_recv=dma((4, 8)), load_sem=dma((12,)), free=regular)
    return out


def pairs_kernel(*refs):
    names = INPUTS.split() + OUTPUTS.split() + list(scratch())
    r = dict(zip(names, refs))
    Block(r).run()


class Block:
    def __init__(self, r):
        for name, ref in r.items():
            setattr(self, name, ref)

    def run(self):
        self.set_up()
        self.begin()
        self.attend()
        self.mlp()
        self.attend_back()
        self.end()

    def set_up(self):
        gather = lambda i, own, full, lanes, *rows: Gather(
            own, full, lanes, self.gather_send.at[i], self.gather_recv.at[i], self.gather_local.at[i], *rows
        )
        self.q = gather(
            0,
            lambda h: [
                (self.wq.at[j, :, block(2 * h + k, 128)], 256 + 384 * k + 128 * j, 128)
                for k in range(2)
                for j in range(3)
            ],
            self.buf_a,
            (256, 768),
            FIRST,
        )
        self.p = gather(1, lambda h: [(self.wp.at[:, block(h, 256)], 0, 256)], self.buf_a, (0, 256))
        self.u = gather(2, lambda h: [(self.wu.at[:, block(h, 1024)], 0, 1024)], self.gu, (0, 1024))
        self.d = gather(3, lambda h: [(self.wd.at[:, block(h, 1024)], 0, 1024)], self.buf_b, (0, 1024))
        heads = lambda k: lambda h: [
            (self.q_out.at[j, :, block(2 * h + k, 128)], 256 + 384 * k + 128 * j, 128) for j in range(3)
        ]
        outs = (
            lambda h: [(self.d_out.at[:, block(h, 1024)], 0, 1024)],
            lambda h: [(self.u_out.at[:, block(h, 1024)], 0, 1024)],
            lambda h: heads(0)(h) + [(self.p_out.at[:, block(h, 256)], 0, 256)],
            heads(1),
        )
        firsts = ((self.first_a0, self.first_b0), (self.first_a1, self.first_b1))
        rest = (
            (self.second0, self.third0, self.wide_z0, self.wide_y0, self.wide_x0),
            (self.second1, self.third1, self.wide_z1, self.wide_y1, self.wide_x1),
            (self.second2, self.third2, self.wide_z2, self.wide_y2, self.wide_x2),
        )
        plan = (
            (self.buf_d, firsts[0], rest[0], (0, 1024)),
            (self.buf_c, firsts[1], rest[1], (0, 1024)),
            (self.buf_d, firsts[0], rest[2], (0, 640)),
            (self.buf_d, firsts[0], rest[2], (640, 384)),
        )
        self.down, self.up, self.near_heads, self.far_heads = [
            Scatter(part, *first, *more, self.total, lanes, outs[i], self.scatter_send.at[i], self.scatter_recv.at[i])
            for i, (part, first, more, lanes) in enumerate(plan)
        ]
        swaps = [(self.lat_own, self.lat), (self.grad_own, self.grad)]
        self.swap_lat, self.swap_grad = [
            Swap(own, full, self.swap_send.at[i], self.swap_recv.at[i], self.swap_local.at[i])
            for i, (own, full) in enumerate(swaps)
        ]
        backs = [(self.g_two, self.block_mine), (self.branch_one, self.input_mine)]
        self.swap_block, self.swap_input = [
            SwapBack(full, out, self.swap_send.at[2 + i, 0], self.swap_recv.at[2 + i, 0], self.swap_local.at[2 + i])
            for i, (full, out) in enumerate(backs)
        ]
        self.pairs = [
            Pair(self.mine, theirs, self.pair_send.at[i], self.pair_recv.at[i])
            for i, theirs in enumerate((self.theirs_a, self.theirs_b, self.theirs_a, self.theirs_b))
        ]

    def load(self, i, source, target):
        return pltpu.make_async_copy(source, target, self.load_sem.at[i])

    def begin(self):
        z, y, c, x = place()
        q, p, u, d = self.q, self.p, self.u, self.d
        send, recv = self.small_send, self.small_recv
        little = SmallGather(self.small, self.small_full, send.at[0], recv.at[0])
        v = self.cond[...].astype(F32)
        silu = (v / (1.0 + jnp.exp(-v))).astype(BF).astype(F32)
        self.small[...] = jnp.zeros_like(self.small)
        for k in range(8):
            self.small[k : k + 1, :] = silu[:, k * 128 : (k + 1) * 128]
        for k, bias in enumerate((self.q_bias, self.v_bias, self.p_bias, self.d_bias)):
            self.small[8:9, k * 32 : (k + 1) * 32] = bias[...].astype(F32)
        self.small[9:10, :] = self.u_bias[...].astype(F32)
        a_bias = self.a_bias[...].astype(F32)
        for j in range(6):
            self.small[10 + j // 4 : 11 + j // 4, j % 4 * 32 : j % 4 * 32 + 32] = a_bias[j : j + 1, :]
        greet(partners())
        little.start()
        q.start_core()
        for group in (p, u, d):
            group.start_core()
        self.swap_lat.start()
        self.wide[...] = jnp.zeros_like(self.wide)
        ada = [self.load(j, self.ada.at[j], self.wide.at[block(c, 64), pl.ds(j * 512, 512)]) for j in range(6)]
        for copy in ada:
            copy.start()
        little.step((0,), (1, 2, 3))
        q.enter((2,))
        self.part[...] = jnp.zeros_like(self.part)
        little.step((1, 2, 3), (4,))
        q.first()
        for copy in ada:
            copy.wait()
        little.step((4,), (5,))
        row = z * 2 + y
        lhs = [self.small_full[x, b // 4, b // 2 % 2, b % 2, pl.ds(row, 1), :] for b in range(16)]
        lhs = jnp.concatenate(lhs, 0)
        self.silu[...] = lhs
        for j in range(6):
            product = nn(lhs.astype(BF), self.wide[:, j * 512 : (j + 1) * 512])
            for b in range(16):
                self.part[b % 2, b // 4, b // 2 % 2, j : j + 1, :] = product[b : b + 1, :]
        near_c, near_y, near_z = self.near_c, self.near_y, self.near_z
        first = remote(self.part.at[1 - c], near_c, send.at[1, 0], recv.at[1, 0], at(z, y, 1 - c, x))
        first.start()
        first.wait()
        near_c[...] = near_c[...] + self.part[c]
        seconds = []
        for s in (1, 2, 3):
            to = lax.rem(z + s, 4)
            seconds.append(remote(near_c.at[to], near_z.at[s - 1], send.at[1, s], recv.at[1, s], at(to, y, c, x)))
            seconds[-1].start()
        q.pass_on((1, 3))
        p.enter()
        u.enter()
        for copy in seconds:
            copy.wait()
        near_z[3] = near_c[z] + near_z[0] + near_z[1] + near_z[2]
        third = remote(near_z.at[3, 1 - y], near_y.at[0], send.at[1, 4], recv.at[1, 4], at(z, 1 - y, c, x))
        third.start()
        q.turn(0)
        third.wait()
        near_y[1] = near_y[0] + near_z[3, y]
        fourth = remote(near_y.at[1], self.mods.at[1 - c], send.at[1, 5], recv.at[1, 5], at(z, y, 1 - c, 1 - x))

        @pl.when(c != x)
        def _():
            fourth.start()

        q.arrived(2)
        q.arrived(1)
        q.arrived(3)
        d.enter()
        self.swap_lat.share()
        q.turn(2)

        @pl.when(c != x)
        def _():
            fourth.wait()

        @pl.when(c == x)
        def _():
            self.mods[c] = near_y[1]

        fifth = remote(self.mods.at[c], self.mods.at[c], send.at[1, 6], recv.at[1, 6], at(z, y, 1 - c, x))
        fifth.start()
        little.step((5,), ())
        bias = [widen(self.small_full, 8, k) for k in range(4)]
        ada_bias = [widen(self.small_full, 10 + j // 4, j % 4) for j in range(6)]
        for k, (zz, yy, cc, xx) in enumerate(devices()):
            self.up_bias[:, k * 128 : (k + 1) * 128] = self.small_full[xx, zz, yy, cc, 9:10, :]
        q.turn(1)
        fifth.wait()
        for j in range(6):
            for h in range(2):
                lanes = slice(h * 512, (h + 1) * 512)
                self.vectors[j : j + 1, lanes] = self.mods[h, j : j + 1, :] + ada_bias[j][:, lanes]
        for k in range(4):
            self.vectors[6 + k : 7 + k, :] = bias[k]
        q.turn(3)
        p.first()
        for k in (2, 1, 3):
            p.arrived(k)
        u.first()
        self.swap_lat.finish()

    def attend(self):
        z, y, c, x = place()
        q, p, u, d, vectors = self.q, self.p, self.u, self.d, self.vectors

        def modulated(i):
            rows = block(i, 256)
            normal, _ = normalise(self.lat[rows, :].astype(F32))
            self.attn_in[rows, :] = (normal * (1.0 + vectors[1:2, :]) + vectors[0:1, :]).astype(BF)

        loop(4, modulated)
        q.finish()
        self.swap_grad.start()

        def project(i):
            b, quarter = i // 4, lax.rem(i, 4)
            values = nn(self.attn_in[block(quarter, 256), :], flat(self.buf_a[b, :, :, :, 256:1024]))
            for k in range(6):
                value = values[:, k * 128 : (k + 1) * 128]
                if k % 3 != 1:
                    columns = pl.ds(pl.multiple_of(b * 512 + c * 256 + k // 3 * 128, 128), 128)
                    row = 6 if k % 3 == 0 else 7
                    value = value + vectors[row : row + 1, columns]
                self.buf_d[b, quarter, :, :, 256 + k * 128 : 384 + k * 128] = value.astype(BF).reshape(2, 128, 128)

        loop(8, project)
        for k in (0, 2, 1, 3):
            p.turn(k)
        for k in (2, 1, 3):
            u.arrived(k)
        lane = lax.broadcasted_iota(jnp.int32, (1, 128), 1)
        self.lse[...] = jnp.zeros_like(self.lse)

        def attend(i):
            pair, half = i // 2, lax.rem(i, 2)
            rows, zz = block(half, 512), pl.ds(half * 2, 2)
            b, k, q_at = lax.rem(pair, 2), pair // 2, pl.multiple_of(256 + pair // 2 * 384, 128)
            queries = flat(self.buf_d[b, zz, :, :, pl.ds(q_at, 128)]) * BF(0.125)
            keys = flat(self.buf_d[b, :, :, :, pl.ds(q_at + 128, 128)])
            values = flat(self.buf_d[b, :, :, :, pl.ds(q_at + 256, 128)])
            result = None
            logs = self.lse[rows, :]
            for h in range(2):
                scores = nt(jnp.where(in_half(h), queries, jnp.zeros_like(queries)), keys)
                largest = jnp.max(scores, -1, keepdims=True)
                exponent = jnp.exp(scores - largest)
                summed = jnp.sum(exponent, -1, keepdims=True)
                mixture = nn(exponent.astype(BF), values) * (1.0 / summed)
                result = mixture if h == 0 else jnp.where(in_half(0), result, mixture)
                logs = jnp.where(lane == pair * 2 + h, largest + jnp.log(summed), logs)
            self.buf_d[b, zz, :, :, block(k, 128)] = result.astype(BF).reshape(2, 2, 128, 128)
            self.lse[rows, :] = logs

        ticks = {
            0: lambda: u.turn(0),
            3: lambda: u.turn(2),
            4: lambda: u.turn(1),
            5: lambda: u.turn(3),
        }
        loop(8, attend, ticks)
        d.first()
        p.finish()
        self.load(0, self.buf_a, self.held_a).start()
        pair = self.pairs[0]

        def out(i):
            zz = i
            partial = nt(flat(self.buf_d[0, zz, :, :, 0:256]), flat(self.buf_a[0, :, :, :, 0:256]))
            partial += nt(flat(self.buf_d[1, zz, :, :, 0:256]), flat(self.buf_a[1, :, :, :, 0:256]))
            pair.give(i, partial)

        loop(4, out)
        self.load(1, self.buf_d, self.held_b).start()
        for k in (2, 1, 3):
            d.arrived(k)
        self.swap_grad.share()

        def residual(i):
            rows = block(i, 256)
            branch = pair.take(i) + vectors[8:9, :]
            self.branch_one[rows, :] = branch.astype(BF)
            self.mid[rows, :] = self.lat[rows, :].astype(F32) + vectors[2:3, :] * branch

        loop(4, residual)

    def mlp(self):
        z, y, c, x = place()
        u, d, vectors, stats, down, up = self.u, self.d, self.vectors, self.stats, self.down, self.up
        active, up_grad, slope, hidden_grad = self.buf_c, self.buf_c, self.buf_a, self.buf_a
        wd, gu, mid, mlp_in, g_two, grad = self.buf_b, self.gu, self.mid, self.mlp_in, self.g_two, self.grad
        self.swap_grad.finish()
        stats[...] = jnp.zeros_like(stats)
        self.up_sums[...] = jnp.zeros_like(self.up_sums)

        def enter(i):
            rows = block(i, 256)
            normal, _ = normalise(mid[rows, :])
            mlp_in[rows, :] = (normal * (1.0 + vectors[4:5, :]) + vectors[3:4, :]).astype(BF)
            g = (grad[rows, :].astype(F32) * vectors[5:6, :]).astype(BF)
            g_two[rows, :] = g
            mine_too = jnp.where(i // 2 == c, 1.0, 0.0)
            stats[1:2, :] += column_sum(g.astype(F32)) * mine_too

        loop(4, enter)
        u.finish()
        self.load(0, self.buf_a, self.held_a).wait()
        d.turn(0)

        def ascend(i):
            b, quarter = i // 4, lax.rem(i, 4)
            columns = pl.ds(pl.multiple_of(b * 2048 + c * 1024, 1024), 1024)
            hidden = nn(mlp_in[block(quarter, 256), :], flat(gu[b])) + self.up_bias[:, columns]
            value, gradient = gelu_parts(hidden)
            active[b, quarter] = value.astype(BF).reshape(2, 128, 1024)
            slope[b, quarter] = gradient.astype(BF).reshape(2, 128, 1024)

        loop(8, ascend, {3: lambda: d.turn(2), 6: lambda: d.turn(1)})
        self.load(1, self.buf_d, self.held_b).wait()

        def down_gradient(i):
            b, half = i // 2, lax.rem(i, 2)
            value = tn(g_two[:, block(half, 512)], flat(active[b]))
            self.buf_d[b, pl.ds(half * 2, 2)] = value.astype(BF).reshape(2, 2, 128, 1024)

        loop(4, down_gradient, {0: lambda: d.turn(3)})
        down.start()
        d.finish()
        pair, back = self.pairs[1], self.pairs[2]

        def descend(i):
            pair.give(i, nt(flat(active[0, i]), flat(wd[0])) + nt(flat(active[1, i]), flat(wd[1])))

        loop(4, descend, {1: lambda: down.turn(2)})

        def hidden_gradient(i):
            b, quarter = i // 4, lax.rem(i, 4)
            value = nn(g_two[block(quarter, 256), :], flat(wd[b])) * flat(slope[b, quarter]).astype(F32)
            value = value.astype(BF)
            hidden_grad[b, quarter] = value.reshape(2, 128, 1024)
            self.up_sums[b] += column_sum(value.astype(F32))

        loop(8, hidden_gradient, {1: lambda: down.turn(1), 7: lambda: down.turn(3)})
        self.load(3, self.held_b, self.buf_b).start()

        def leave(i):
            rows = block(i, 256)
            branch_two = pair.take(i) + vectors[9:10, :]
            g_two[rows, :] = (mid[rows, :] + vectors[5:6, :] * branch_two).astype(BF)
            stats[0:1, :] += column_sum(grad[rows, :].astype(F32) * branch_two)

        loop(4, leave)

        def descend_back(i):
            back.give(i, nt(flat(hidden_grad[0, i]), flat(gu[0])) + nt(flat(hidden_grad[1, i]), flat(gu[1])))

        loop(4, descend_back, {0: lambda: down.turn(0), 2: lambda: down.leave(2)})

        def up_gradient(i):
            b, half = i // 2, lax.rem(i, 2)
            value = tn(mlp_in[:, block(half, 512)], flat(hidden_grad[b]))
            up_grad[b, pl.ds(half * 2, 2)] = value.astype(BF).reshape(2, 2, 128, 1024)

        loop(4, up_gradient, {0: lambda: down.leave(1), 2: lambda: down.leave(3)})
        self.load(4, self.held_a, self.buf_a).start()
        up.start()

        def residual(i):
            rows = block(i, 256)
            dy = back.take(i)
            normal, scale = normalise(mid[rows, :])
            stats[2:3, :] += column_sum(dy)
            stats[3:4, :] += column_sum(dy * normal)
            dn = dy * (1.0 + vectors[4:5, :])
            dn = dn - jnp.mean(dn, -1, keepdims=True) - normal * jnp.mean(dn * normal, -1, keepdims=True)
            total = grad[rows, :].astype(F32) + scale * dn
            mid[rows, :] = total
            stats[4:5, :] += column_sum(total * self.branch_one[rows, :].astype(F32))
            g = (total * vectors[2:3, :]).astype(BF)
            mlp_in[rows, :] = g
            mine_too = jnp.where(i // 2 == c, 1.0, 0.0)
            stats[5:6, :] += column_sum(g.astype(F32)) * mine_too

        loop(4, residual)
        down.leave(0)
        for to in (at(z, 1 - y, c, x), at(z, y, c, 1 - x)):
            pl.semaphore_signal(self.free, inc=1, device_id=to, device_id_type=MESH)

    def attend_back(self):
        z, y, c, x = place()
        vectors, stats, down, up = self.vectors, self.stats, self.down, self.up
        near, far = self.near_heads, self.far_heads
        acts, g_one, heads_grad, sums = self.buf_b, self.mlp_in, self.heads_grad, self.sums
        weights = self.buf_a
        sums[...] = jnp.zeros_like(sums)
        self.load(3, self.held_b, self.buf_b).wait()
        self.load(4, self.held_a, self.buf_a).wait()

        def enter(i):
            b, half = i // 2, lax.rem(i, 2)
            value = nn(g_one[block(half, 512), :], flat(weights[b, :, :, :, 0:256]))
            heads_grad[b, block(half, 512), :] = value.astype(BF)

        loop(4, enter)

        def proj_gradient(i):
            b, half = i // 2, lax.rem(i, 2)
            value = tn(g_one[:, block(half, 512)], flat(acts[b, :, :, :, 0:256]))
            self.buf_d[b, pl.ds(half * 2, 2), :, :, 0:256] = value.astype(BF).reshape(2, 2, 128, 256)

        loop(4, proj_gradient)
        lane = lax.broadcasted_iota(jnp.int32, (1, 128), 1)

        def attend(i, k):
            b, quarter = i // 4, lax.rem(i, 4)
            rows, at_lane = block(quarter, 256), 256 + 384 * k
            queries = flat(acts[b, quarter, :, :, at_lane : at_lane + 128]) * BF(0.125)
            keys = flat(acts[b, :, :, :, at_lane + 128 : at_lane + 256])
            values = flat(acts[b, :, :, :, at_lane + 256 : at_lane + 384])
            grads = heads_grad[b, rows, k * 128 : (k + 1) * 128]

            @pl.when(quarter == 0)
            def _():
                self.key_total[...] = jnp.zeros_like(self.key_total)
                self.value_total[...] = jnp.zeros_like(self.value_total)

            result = None
            logs = self.lse[rows, :]
            for h in range(2):
                log = jnp.sum(jnp.where(lane == (k * 2 + b) * 2 + h, logs, 0.0), -1, keepdims=True)
                query = jnp.where(in_half(h), queries, jnp.zeros_like(queries))
                grad = jnp.where(in_half(h), grads, jnp.zeros_like(grads))
                probs = jnp.exp(nt(query, keys) - log)
                probs_grad = nt(grad, values)
                inner = jnp.sum(probs * probs_grad, -1, keepdims=True)
                score_grad = (probs * (probs_grad - inner)).astype(BF)
                query_grad = nn(score_grad, keys)
                result = query_grad if h == 0 else jnp.where(in_half(0), result, query_grad)
                self.key_total[...] += tn(score_grad, query)
                self.value_total[...] += tn(probs.astype(BF), grad)
            result = (result * 0.125).astype(BF)
            acts[b, quarter, :, :, at_lane : at_lane + 128] = result.reshape(2, 128, 128)
            sums[b, :, k * 128 : (k + 1) * 128] += column_sum(result.astype(F32))

            @pl.when(quarter == 3)
            def _():
                total = self.key_total[...].astype(BF)
                acts[b, :, :, :, at_lane + 128 : at_lane + 256] = total.reshape(4, 2, 128, 128)
                total = self.value_total[...].astype(BF)
                acts[b, :, :, :, at_lane + 256 : at_lane + 384] = total.reshape(4, 2, 128, 128)
                sums[b, :, 512 + k * 128 : 640 + k * 128] = column_sum(total.astype(F32))

        def qkv_gradient(i, k):
            b, half = i // 2, lax.rem(i, 2)
            lanes = slice(256 + 384 * k, 640 + 384 * k)
            value = tn(self.attn_in[:, block(half, 512)], flat(acts[b, :, :, :, lanes]))
            self.buf_d[b, pl.ds(half * 2, 2), :, :, lanes] = value.astype(BF).reshape(2, 2, 128, 384)

        ticks = {
            0: lambda: up.turn(2),
            2: lambda: up.turn(1),
            5: lambda: up.turn(3),
        }
        loop(8, lambda i: attend(i, 0), ticks)
        up.turn(0)
        loop(4, lambda i: qkv_gradient(i, 0))
        pl.semaphore_wait(self.free, 2)
        near.start()
        up.leave(2)
        ticks = {
            0: lambda: down.last(),
            1: lambda: up.leave(1),
            2: lambda: near.turn(2),
            3: lambda: up.leave(3),
            4: lambda: near.turn(1),
            5: lambda: up.leave(0),
            6: lambda: self.swap_block.start(),
            7: lambda: near.turn(3),
        }
        loop(8, lambda i: attend(i, 1), ticks)
        pair = self.pairs[3]

        def descend(i):
            partial = nt(flat(acts[0, i, :, :, 256:1024]), flat(weights[0, :, :, :, 256:1024]))
            pair.give(i, partial + nt(flat(acts[1, i, :, :, 256:1024]), flat(weights[1, :, :, :, 256:1024])))

        loop(4, descend, {1: lambda: near.turn(0), 3: lambda: near.leave(2)})
        down.finish()

        def leave(i):
            rows = block(i, 256)
            dy = pair.take(i)
            normal, scale = normalise(self.lat[rows, :].astype(F32))
            stats[6:7, :] += column_sum(dy)
            stats[7:8, :] += column_sum(dy * normal)
            dn = dy * (1.0 + vectors[1:2, :])
            dn = dn - jnp.mean(dn, -1, keepdims=True) - normal * jnp.mean(dn * normal, -1, keepdims=True)
            self.branch_one[rows, :] = (self.mid[rows, :] + scale * dn).astype(BF)

        loop(4, leave)
        self.begin_end()
        loop(4, lambda i: qkv_gradient(i, 1), {1: lambda: near.leave(1)})
        far.start()
        self.swap_input.start()
        up.last()

    def begin_end(self):
        z, y, c, x = place()
        stats, sums, up_sums = self.stats, self.sums, self.up_sums
        rows = [stats[k : k + 1, :] for k in (6, 7, 4, 2, 3, 0)]
        for j in range(6):
            for h in range(2):
                self.mods[h, j : j + 1, :] = rows[j][:, h * 512 : (h + 1) * 512]
        self.half_mods[z, y, x] = self.mods[c]
        for d in (1, 2, 3):
            self._mods(d).start()
        columns, bias_part = self.columns, self.bias_part
        columns[...] = jnp.zeros_like(columns)
        bias_part[...] = jnp.zeros_like(bias_part)
        for b in range(2):
            spot = pl.ds(pl.multiple_of(b * 512 + c * 256, 256), 256)
            columns[0:1, spot] = sums[b, :, 0:256]
            columns[1:2, spot] = sums[b, :, 512:768]
        columns[2:3, :] = stats[5:6, :]
        columns[3:4, :] = stats[1:2, :]
        pieces = narrow(columns[0:1, :], 0) + narrow(columns[1:2, :], 1)
        pieces = pieces + narrow(columns[2:3, :], 2) + narrow(columns[3:4, :], 3)
        for k, (zz, yy, cc, xx) in enumerate(devices()):
            bias_part[cc, zz, xx, yy, 0:1, :] = pieces[k : k + 1, :]
        for b in range(2):
            for i in range(8):
                bias_part[i // 2 % 2, b * 2 + c, i % 2, i // 4, 1:2, :] = up_sums[b, :, i * 128 : (i + 1) * 128]
        self.bias = SmallScatter(
            bias_part, self.bias_c, self.bias_z, self.bias_near, self.small_send.at[0], self.small_recv.at[3]
        )
        self.bias.start()
        for d in (1, 2, 3):
            self._mods(d).wait()
        self._across(lambda copy: copy.start())
        self.bias.along()

    def _mods(self, d):
        z, y, c, x = place()
        spot = self.half_mods.at[z, y, x]
        return remote(
            spot, spot, self.small_send.at[2, d], self.small_recv.at[2, d], at(lax.rem(z + d, 4), y, c, x)
        )

    def _across(self, act):
        z, y, c, x = place()
        spot = self.half_mods.at[:, y, x]
        copy = lambda k, to: remote(spot, spot, self.small_send.at[2, k], self.small_recv.at[2, k], to)

        @pl.when(c == x)
        def _():
            act(copy(4, at(z, 1 - y, c, x)))

        @pl.when(c != x)
        def _():
            act(copy(5, at(z, y, c, 1 - x)))
            act(copy(6, at(z, 1 - y, c, 1 - x)))

    def end(self):
        z, y, c, x = place()
        up, near, far, mods, bias = self.up, self.near_heads, self.far_heads, self.all_mods, self.bias
        send, recv = self.small_send, self.small_recv
        spot = self.half_mods.at[:, y, x]

        @pl.when(c == x)
        def _():
            remote(spot, spot, send.at[2, 4], recv.at[2, 4], at(z, 1 - y, c, x)).wait()
            remote(spot, spot, send.at[2, 5], recv.at[2, 5], at(z, y, c, 1 - x)).wait_recv()
            remote(spot, spot, send.at[2, 6], recv.at[2, 6], at(z, 1 - y, c, 1 - x)).wait_recv()
            share = remote(self.half_mods, mods, send.at[2, 7], recv.at[2, 7], at(z, y, 1 - c, x))
            share.start()
            keep = self.load(5, self.half_mods, mods)
            keep.start()
            keep.wait()
            share.wait_send()

        @pl.when(c != x)
        def _():
            remote(spot, spot, send.at[2, 5], recv.at[2, 5], at(z, y, c, 1 - x)).wait_send()
            remote(spot, spot, send.at[2, 6], recv.at[2, 6], at(z, 1 - y, c, 1 - x)).wait_send()
            remote(self.half_mods, mods, send.at[2, 7], recv.at[2, 7], at(z, y, 1 - c, x)).wait_recv()

        bias.across()
        silu_rows = self.silu[...].astype(BF)
        total = jnp.zeros((16, 128), F32)
        bias_rows = []
        for j in range(6):
            values = jnp.concatenate([mods[b // 4, b // 2 % 2, b % 2, j : j + 1, :] for b in range(16)], 0)
            high, low = split_bf(values)
            weights = self.wide[:, j * 512 : (j + 1) * 512]
            self.tall[...] = tn(silu_rows, high) + tn(silu_rows, low)
            self.ada_out[j] = self.tall[block(c, 64), :]
            total = total + nt(high, weights) + nt(low, weights)
            bias_rows.append(column_sum(values))
        found, found_c, found_z, found_near = self.found, self.found_c, self.found_z, self.found_near
        for b in range(16):
            found[b % 2, b // 4, b // 2 % 2] = total[b : b + 1, :]
        core = remote(found.at[1 - c], found_c, send.at[3, 0], recv.at[1, 0], at(z, y, 1 - c, x))
        core.start()
        far.turn(2)
        group = (lax.rem(z, 2) * 2 + y) * 2 + c
        source = lax.broadcasted_iota(jnp.int32, (512, 128), 0)
        target = lax.broadcasted_iota(jnp.int32, (512, 128), 1)
        chosen = jnp.where((source == group * 64 + target) & (target < 64), 1.0, 0.0).astype(BF)
        self.picked[...] = exact_nn(jnp.concatenate(bias_rows + [jnp.zeros((2, 512), F32)], 0), chosen)
        swap = remote(self.picked, self.picked_other, send.at[3, 7], recv.at[1, 7], at(z, y, c, 1 - x))
        swap.start()
        core.wait()
        found_c[...] = found_c[...] + found[c]
        along = []
        for k in (1, 2, 3):
            to = lax.rem(z + k, 4)
            along.append(remote(found_c.at[to], found_z.at[z], send.at[3, k], recv.at[1, k], at(to, y, c, x)))
            along[-1].start()
        found_z[z] = found_c[z]
        near.leave(3)
        far.turn(1)
        near.leave(0)
        for copy in along:
            copy.wait()
        across = []
        for k, (to_y, to_x) in enumerate(((y, 1 - x), (1 - y, x), (1 - y, 1 - x))):
            across.append(
                remote(found_z.at[:, to_y], found_near.at[k], send.at[3, 4 + k], recv.at[1, 4 + k], at(z, to_y, c, to_x))
            )
            across[-1].start()
        far.turn(3)
        far.turn(0)
        up.finish()
        near.last()
        far.leave(2)
        far.leave(1)
        for copy in across:
            copy.wait()
        swap.wait()
        self.bias_out[...] = bias.finish()
        self.ada_bias_out[...] = jnp.where(z // 2 == x, self.picked[...], self.picked_other[...])
        same, other = found_z[:, y] + found_near[0], found_near[1] + found_near[2]
        rows = [jnp.where(y == b % 2, same[b // 2], other[b // 2]) for b in range(8)]
        v = self.cond[...].astype(F32)
        v = jnp.concatenate([v[:, k * 128 : (k + 1) * 128] for k in range(8)], 0)
        gate = 1.0 / (1.0 + jnp.exp(-v))
        self.cond_out[...] = jnp.concatenate(rows, 0) * gate * (1.0 + v * (1.0 - gate))
        far.leave(3)
        far.leave(0)
        near.finish()
        far.last()
        self.swap_block.finish()
        self.swap_input.finish()
        far.finish()


def on_device_pairs(
    latents_in,
    condition,
    grad_out,
    qkv_weight,
    proj_weight,
    up_weight,
    down_weight,
    ada_weight,
    query_bias,
    value_bias,
    proj_bias,
    up_bias,
    down_bias,
    ada_bias,
):
    x = lax.axis_index("tp")
    small = [b.reshape(1, -1) for b in (query_bias, value_bias, proj_bias, down_bias, up_bias)]
    out = lambda *shape: jax.ShapeDtypeStruct(shape, F32)
    group = jax.ShapeDtypeStruct(GROUP, BF)
    rows = jax.ShapeDtypeStruct((512, 1024), BF)
    results = pl.pallas_call(
        pairs_kernel,
        out_shape=[rows, rows, out(3, 64, 512), out(64, 512), out(64, 2048), out(64, 2048)]
        + [group] * 2
        + [out(6, 64, 512), out(8, 128), out(8, 128), out(2, 128)],
        in_specs=[IN_ANY] * 7 + [IN_VMEM] * 7,
        out_specs=[IN_ANY] * 8 + [IN_VMEM] * 4,
        scratch_shapes=list(scratch().values()),
        compiler_params=pltpu.CompilerParams(
            collective_id=0, has_side_effects=True, vmem_limit_bytes=63 * MIB
        ),
        name="dit_block",
    )(
        latents_in.reshape(512, 1024), grad_out.reshape(512, 1024), qkv_weight.transpose(1, 0, 2), proj_weight.T,
        up_weight, down_weight.T, ada_weight.transpose(1, 0, 2), condition, *small, ada_bias,
    )
    block_mine, input_mine, q_out, p_out, u_out, d_out, _, _, ada_out, cond_out, ada_bias_out, bias_out = results
    return (
        block_mine.reshape(512, 1, 1024),
        input_mine.astype(F32).reshape(512, 1, 1024),
        lax.dynamic_slice_in_dim(cond_out, x * 4, 4, 0).reshape(1, 512),
        q_out.transpose(1, 0, 2),
        p_out.T,
        u_out,
        d_out.T,
        ada_out.transpose(1, 0, 2),
        bias_out[0, 0:32],
        bias_out[0, 32:64],
        bias_out[0, 64:96],
        bias_out[1],
        bias_out[0, 96:128],
        lax.dynamic_slice_in_dim(ada_bias_out, x * 32, 32, 1)[:6],
    )


def solution(mesh):
    shape = dict(mesh.shape)
    pairs = shape["fsdp"] == 16 and shape["tp"] == 2
    return jax.shard_map(
        on_device_pairs if pairs else on_device_general,
        mesh=mesh,
        in_specs=(
            P("tp", "fsdp", None),
            P("fsdp", None),
            P("tp", "fsdp", None),
            P("fsdp", None, "tp"),
            P("tp", "fsdp"),
            P("fsdp", "tp"),
            P("tp", "fsdp"),
            P("fsdp", None, "tp"),
            P(("fsdp", "tp")),
            P(("fsdp", "tp")),
            P(("fsdp", "tp")),
            P(("fsdp", "tp")),
            P(("fsdp", "tp")),
            P(None, ("fsdp", "tp")),
        ),
        out_specs=(
            P("tp", "fsdp", None),
            P("tp", "fsdp", None),
            P("fsdp", "tp"),
            P("fsdp", None, "tp"),
            P("tp", "fsdp"),
            P("fsdp", "tp"),
            P("tp", "fsdp"),
            P("fsdp", None, "tp"),
            P(("fsdp", "tp")),
            P(("fsdp", "tp")),
            P(("fsdp", "tp")),
            P(("fsdp", "tp")),
            P(("fsdp", "tp")),
            P(None, ("fsdp", "tp")),
        ),
        check_vma=False,
    )
```

```python
import functools
import math

import jax
import jax.numpy as jnp
from jax import lax
from jax.experimental import pallas as pl
from jax.experimental.pallas import tpu as pltpu
from jax.sharding import PartitionSpec as P


HD = 64


epsilon = 1e-06


def layer_norm(values):
    centred = values - jnp.mean(values, axis=-1, keepdims=True)
    return centred * lax.rsqrt(jnp.mean(centred * centred, axis=-1, keepdims=True) + epsilon)


def modulate(values, shift_part, scale_part):
    return layer_norm(values) * (1.0 + scale_part) + shift_part


def gelu_tanh(values):
    return jax.nn.gelu(values, approximate=True)


def gather_rows(piece):
    return lax.all_gather(piece, "tp", axis=0, tiled=True)


def gather_grads(piece):
    return lax.all_gather(piece, "tp", axis=0, tiled=True)


def scatter_rows(product, row_count):
    return lax.psum_scatter(
        product(jnp.int32(0), row_count * lax.axis_size("tp")).astype(jnp.bfloat16),
        "tp",
        scatter_dimension=0,
        tiled=True,
    ).astype(jnp.float32)


def scatter_grads(product, row_count):
    return lax.psum_scatter(
        product(jnp.int32(0), row_count * lax.axis_size("tp")).astype(jnp.bfloat16),
        "tp",
        scatter_dimension=0,
        tiled=True,
    ).astype(jnp.float32)


def split_heads(packed):
    head_count = packed.shape[3] // HD
    shaped = packed.reshape(packed.shape[0], packed.shape[1], 3, head_count, HD)
    return (shaped[:, :, 0], shaped[:, :, 1], shaped[:, :, 2])


def attend_forward(packed):
    length, latents, local_width = (packed.shape[0], packed.shape[1], packed.shape[3])
    queries, key_rows, value_rows = split_heads(packed)
    block_rows = min(512, length)
    score_scale = 1.0 / math.sqrt(HD)
    blocks = queries.reshape(length // block_rows, block_rows, latents, local_width // HD, HD)

    def one_block(q_rows):
        scores = (
            jnp.einsum("qbhd,kbhd->bhqk", q_rows, key_rows, preferred_element_type=jnp.float32)
            * score_scale
        )
        largest = jnp.max(scores, axis=-1, keepdims=True)
        exponent = jnp.exp(scores - largest)
        summed = jnp.sum(exponent, axis=-1, keepdims=True)
        weights_soft = (exponent / summed).astype(jnp.bfloat16)
        mixture = jnp.einsum(
            "bhqk,kbhd->qbhd", weights_soft, value_rows, preferred_element_type=jnp.float32
        )
        return (mixture.astype(jnp.bfloat16), largest[..., 0] + jnp.log(summed[..., 0]))

    mixture_all, log_sums = lax.map(one_block, blocks)
    return (mixture_all.reshape(length, latents, local_width), log_sums)


def attend_backward(packed, log_sums, heads_grad):
    length, latents, local_width = (packed.shape[0], packed.shape[1], packed.shape[3])
    head_count = local_width // HD
    queries, key_rows, value_rows = split_heads(packed)
    block_rows = min(512, length)
    count_blocks = length // block_rows
    score_scale = 1.0 / math.sqrt(HD)
    q_blocks = queries.reshape(count_blocks, block_rows, latents, head_count, HD)
    g_blocks = heads_grad.reshape(count_blocks, block_rows, latents, head_count, HD)

    def one_block(carried, inputs):
        key_grad, value_grad = carried
        q_rows, g_rows, log_rows = inputs
        scores = (
            jnp.einsum("qbhd,kbhd->bhqk", q_rows, key_rows, preferred_element_type=jnp.float32)
            * score_scale
        )
        weights_soft = jnp.exp(scores - log_rows[..., None])
        soft_grad = jnp.einsum(
            "qbhd,kbhd->bhqk", g_rows, value_rows, preferred_element_type=jnp.float32
        )
        inner_sum = jnp.sum(weights_soft * soft_grad, axis=-1, keepdims=True)
        score_grad = (weights_soft * (soft_grad - inner_sum)).astype(jnp.bfloat16)
        query_grad = (
            jnp.einsum("bhqk,kbhd->qbhd", score_grad, key_rows, preferred_element_type=jnp.float32)
            * score_scale
        )
        key_grad = (
            key_grad
            + jnp.einsum("bhqk,qbhd->kbhd", score_grad, q_rows, preferred_element_type=jnp.float32)
            * score_scale
        )
        value_grad = value_grad + jnp.einsum(
            "bhqk,qbhd->kbhd",
            weights_soft.astype(jnp.bfloat16),
            g_rows,
            preferred_element_type=jnp.float32,
        )
        return ((key_grad, value_grad), query_grad)

    zero_rows = jnp.zeros((length, latents, head_count, HD), jnp.float32)
    (key_grad, value_grad), query_grad = lax.scan(
        one_block, (zero_rows, zero_rows), (q_blocks, g_blocks, log_sums)
    )
    stacked = jnp.stack(
        [
            query_grad.reshape(length, latents, local_width),
            key_grad.reshape(length, latents, local_width),
            value_grad.reshape(length, latents, local_width),
        ],
        axis=2,
    )
    return stacked.astype(jnp.bfloat16)


def on_device_general(
    latents_in,
    condition,
    grad_out,
    qkv_weight,
    proj_weight,
    up_weight,
    down_weight,
    ada_weight,
    query_bias,
    value_bias,
    proj_bias,
    up_bias,
    down_bias,
    ada_bias,
):
    tp_index = lax.axis_index("tp")
    local_rows = latents_in.shape[0]
    local_width = qkv_weight.shape[2]
    local_hidden = up_weight.shape[1]
    model_width = latents_in.shape[2]
    width_start = tp_index * local_width
    hidden_start = tp_index * local_hidden
    full_qkv, full_proj, full_up, full_down, full_ada = (
        lax.all_gather(qkv_weight, "fsdp", axis=0, tiled=True),
        lax.all_gather(proj_weight, "fsdp", axis=1, tiled=True),
        lax.all_gather(up_weight, "fsdp", axis=0, tiled=True),
        lax.all_gather(down_weight, "fsdp", axis=1, tiled=True),
        lax.all_gather(ada_weight, "fsdp", axis=0, tiled=True),
    )
    bias_list = (
        lax.all_gather(query_bias, ("fsdp", "tp"), axis=0, tiled=True),
        lax.all_gather(value_bias, ("fsdp", "tp"), axis=0, tiled=True),
        lax.all_gather(proj_bias, ("fsdp", "tp"), axis=0, tiled=True),
        lax.all_gather(up_bias, ("fsdp", "tp"), axis=0, tiled=True),
        lax.all_gather(down_bias, ("fsdp", "tp"), axis=0, tiled=True),
        lax.all_gather(ada_bias, ("fsdp", "tp"), axis=1, tiled=True),
    )
    all_query, all_value, all_proj, all_up, all_down, all_ada = [
        item_bias.astype(jnp.float32) for item_bias in bias_list
    ]
    hidden_total = all_up.shape[0]
    cond_float = condition.astype(jnp.float32)
    silu_cond = jax.nn.silu(cond_float).astype(jnp.bfloat16)
    ada_cols = lax.dynamic_slice_in_dim(all_ada, width_start, local_width, 1)
    mod_part = (
        jnp.einsum("bc,ctf->btf", silu_cond, full_ada, preferred_element_type=jnp.float32)
        + ada_cols
    )
    modulation = lax.all_gather(mod_part, "tp", axis=2, tiled=True)
    shift_one, scale_one, gate_one = (modulation[:, 0], modulation[:, 1], modulation[:, 2])
    shift_two, scale_two, gate_two = (modulation[:, 3], modulation[:, 4], modulation[:, 5])
    input_float = latents_in.astype(jnp.float32)
    attn_in = modulate(input_float, shift_one, scale_one).astype(jnp.bfloat16)
    attn_full = gather_rows(attn_in)
    query_cols = lax.dynamic_slice_in_dim(all_query, width_start, local_width, 0)
    value_cols = lax.dynamic_slice_in_dim(all_value, width_start, local_width, 0)
    bias_three = jnp.stack([query_cols, jnp.zeros_like(query_cols), value_cols])
    packed = (
        jnp.einsum("sbd,dtf->sbtf", attn_full, full_qkv, preferred_element_type=jnp.float32)
        + bias_three
    ).astype(jnp.bfloat16)
    heads_out, log_sums = attend_forward(packed)

    def project_heads(first_row, row_count):
        return jnp.einsum("sbf,fd->sbd", heads_out, full_proj, preferred_element_type=jnp.float32)

    branch_one = scatter_rows(project_heads, local_rows) + all_proj
    middle = input_float + gate_one * branch_one
    mlp_in = modulate(middle, shift_two, scale_two).astype(jnp.bfloat16)
    mlp_full = gather_rows(mlp_in)
    up_cols = lax.dynamic_slice_in_dim(all_up, hidden_start, local_hidden, 0)
    hidden = (
        jnp.einsum("sbd,df->sbf", mlp_full, full_up, preferred_element_type=jnp.float32) + up_cols
    )
    active = gelu_tanh(hidden).astype(jnp.bfloat16)

    def project_hidden(first_row, row_count):
        return jnp.einsum("sbf,fd->sbd", active, full_down, preferred_element_type=jnp.float32)

    branch_two = scatter_rows(project_hidden, local_rows) + all_down
    block_out = (middle + gate_two * branch_two).astype(jnp.bfloat16)
    grad_float = grad_out.astype(jnp.float32)
    gate_two_grad = jnp.sum(grad_float * branch_two, axis=0)
    branch_two_grad = (grad_float * gate_two).astype(jnp.bfloat16)
    down_bias_part = jnp.sum(branch_two_grad.astype(jnp.float32), axis=(0, 1))
    _, gelu_pull = jax.vjp(gelu_tanh, hidden)
    branch_two_full = gather_grads(branch_two_grad)
    active_grad = jnp.einsum(
        "sbd,fd->sbf", branch_two_full, full_down, preferred_element_type=jnp.float32
    )
    down_grad = jnp.einsum(
        "sbf,sbd->fd", active, branch_two_full, preferred_element_type=jnp.float32
    )
    hidden_grad = gelu_pull(active_grad)[0].astype(jnp.bfloat16)
    up_grad = jnp.einsum("sbd,sbf->df", mlp_full, hidden_grad, preferred_element_type=jnp.float32)
    up_bias_part = lax.dynamic_update_slice(
        jnp.zeros((hidden_total,), jnp.float32),
        jnp.sum(hidden_grad.astype(jnp.float32), axis=(0, 1)),
        (hidden_start,),
    )

    def back_hidden(first_row, row_count):
        return jnp.einsum("sbf,df->sbd", hidden_grad, full_up, preferred_element_type=jnp.float32)

    mlp_in_grad = scatter_grads(back_hidden, local_rows)
    _, second_pull = jax.vjp(modulate, middle, shift_two, scale_two)
    middle_part, shift_two_grad, scale_two_grad = second_pull(mlp_in_grad)
    middle_grad = grad_float + middle_part
    gate_one_grad = jnp.sum(middle_grad * branch_one, axis=0)
    branch_one_grad = (middle_grad * gate_one).astype(jnp.bfloat16)
    proj_bias_part = jnp.sum(branch_one_grad.astype(jnp.float32), axis=(0, 1))
    branch_one_full = gather_grads(branch_one_grad)
    heads_grad = jnp.einsum(
        "sbd,fd->sbf", branch_one_full, full_proj, preferred_element_type=jnp.float32
    ).astype(jnp.bfloat16)
    proj_grad = jnp.einsum(
        "sbf,sbd->fd", heads_out, branch_one_full, preferred_element_type=jnp.float32
    )
    packed_grad = attend_backward(packed, log_sums, heads_grad)
    qkv_grad = jnp.einsum(
        "sbd,sbtf->dtf", attn_full, packed_grad, preferred_element_type=jnp.float32
    )
    packed_sums = jnp.sum(packed_grad.astype(jnp.float32), axis=(0, 1))
    zero_width = jnp.zeros((model_width,), jnp.float32)
    query_bias_part = lax.dynamic_update_slice(zero_width, packed_sums[0], (width_start,))
    value_bias_part = lax.dynamic_update_slice(zero_width, packed_sums[2], (width_start,))

    def back_packed(first_row, row_count):
        return jnp.einsum(
            "sbtf,dtf->sbd", packed_grad, full_qkv, preferred_element_type=jnp.float32
        )

    attn_in_grad = scatter_grads(back_packed, local_rows)
    _, first_pull = jax.vjp(modulate, input_float, shift_one, scale_one)
    input_part, shift_one_grad, scale_one_grad = first_pull(attn_in_grad)
    input_grad = middle_grad + input_part
    mod_grad = jnp.stack(
        [
            shift_one_grad,
            scale_one_grad,
            gate_one_grad,
            shift_two_grad,
            scale_two_grad,
            gate_two_grad,
        ],
        axis=1,
    )
    mod_cols_grad = lax.psum_scatter(
        mod_grad.astype(jnp.bfloat16), "tp", scatter_dimension=2, tiled=True
    ).astype(jnp.float32)
    ada_grad = jnp.einsum(
        "bc,btf->ctf", silu_cond.astype(jnp.float32), mod_cols_grad, precision=lax.Precision.HIGHEST
    )
    ada_bias_part = lax.dynamic_update_slice(
        jnp.zeros((6, model_width), jnp.float32), jnp.sum(mod_cols_grad, axis=0), (0, width_start)
    )
    silu_grad = jnp.einsum(
        "btf,ctf->bc", mod_cols_grad, full_ada.astype(jnp.float32), precision=lax.Precision.HIGHEST
    )
    silu_cols = lax.psum_scatter(silu_grad, "tp", scatter_dimension=1, tiled=True)
    cond_width = silu_cols.shape[1]
    cond_cols = lax.dynamic_slice_in_dim(cond_float, tp_index * cond_width, cond_width, 1)
    _, silu_pull = jax.vjp(jax.nn.silu, cond_cols)
    cond_grad = silu_pull(silu_cols)[0]
    qkv_sum, proj_sum, up_sum, down_sum, ada_sum = (
        lax.psum_scatter(
            qkv_grad.astype(jnp.bfloat16), "fsdp", scatter_dimension=0, tiled=True
        ).astype(jnp.float32),
        lax.psum_scatter(
            proj_grad.astype(jnp.bfloat16), "fsdp", scatter_dimension=1, tiled=True
        ).astype(jnp.float32),
        lax.psum_scatter(
            up_grad.astype(jnp.bfloat16), "fsdp", scatter_dimension=0, tiled=True
        ).astype(jnp.float32),
        lax.psum_scatter(
            down_grad.astype(jnp.bfloat16), "fsdp", scatter_dimension=1, tiled=True
        ).astype(jnp.float32),
        lax.psum_scatter(
            ada_grad.astype(jnp.bfloat16), "fsdp", scatter_dimension=0, tiled=True
        ).astype(jnp.float32),
    )
    query_sum, value_sum, proj_bias_sum, up_bias_sum, down_bias_sum, ada_bias_sum = (
        lax.psum_scatter(query_bias_part, ("fsdp", "tp"), scatter_dimension=0, tiled=True),
        lax.psum_scatter(value_bias_part, ("fsdp", "tp"), scatter_dimension=0, tiled=True),
        lax.psum_scatter(proj_bias_part, ("fsdp", "tp"), scatter_dimension=0, tiled=True),
        lax.psum_scatter(up_bias_part, ("fsdp", "tp"), scatter_dimension=0, tiled=True),
        lax.psum_scatter(down_bias_part, ("fsdp", "tp"), scatter_dimension=0, tiled=True),
        lax.psum_scatter(ada_bias_part, ("fsdp", "tp"), scatter_dimension=1, tiled=True),
    )
    return (
        block_out,
        input_grad,
        cond_grad,
        qkv_sum,
        proj_sum,
        up_sum,
        down_sum,
        ada_sum,
        query_sum,
        value_sum,
        proj_bias_sum,
        up_bias_sum,
        down_bias_sum,
        ada_bias_sum,
    )


MESH = pl.DeviceIdType.MESH
ANY = pl.ANY
BF = jnp.bfloat16
F32 = jnp.float32
MIB = 2**20
IN_VMEM = pl.BlockSpec(memory_space=pltpu.VMEM)
IN_ANY = pl.BlockSpec(memory_space=ANY)
ROWS = dict(q=[80, 48, 0], p=[64, 48, 16], u=[64, 48, 16], d=[48, 48, 32])
ROWS.update(down=[64, 48, 16], up=[64, 48, 16], near=[64, 48, 16], far=[64, 48, 16])
MOST_A, MOST_B = 64, 48


def cut(rows):
    a, b, w = rows
    return pl.ds(0, a), pl.ds(a, b), pl.ds(a + b, w), pl.ds(0, a + b)


def place():
    f, x = lax.axis_index("fsdp"), lax.axis_index("tp")
    z, y, c = f // 4, lax.rem(f // 2, 2), lax.rem(f, 2)
    return z, y, c, x


def at(z, y, c, x):
    return ((z * 2 + y) * 2 + c, x)


def block(index, size):
    return pl.ds(pl.multiple_of(index * size, size), size)


def remote(src, dst, send, recv, device):
    return pltpu.make_async_remote_copy(
        src_ref=src, dst_ref=dst, send_sem=send, recv_sem=recv, device_id=device, device_id_type=MESH
    )


def loop(count, body, ticks=None):
    def step(i, carry):
        body(i)
        for k, tick in (ticks or {}).items():

            @pl.when(i == k)
            def _(tick=tick):
                tick()

        return carry

    lax.fori_loop(0, count, step, 0)


def greet(devices):
    barrier = pltpu.get_barrier_semaphore()
    for device in devices:
        pl.semaphore_signal(barrier, inc=1, device_id=device, device_id_type=MESH)
    pl.semaphore_wait(barrier, len(devices))


def partners():
    z, y, c, x = place()
    out = [at(z, y, 1 - c, x), at(z, 1 - y, c, x), at(z, y, c, 1 - x), at(z, y, 1 - c, 1 - x)]
    out += [at(z, 1 - y, c, 1 - x), at(z, 1 - y, 1 - c, 1 - x)]
    return out + [at(lax.rem(z + d, 4), y, c, x) for d in (1, 2, 3)]


class Gather:
    def __init__(self, own, full, lanes, rows, send, recv, local):
        self.own, self.full, self.lanes, self.rows = own, full, pl.ds(*lanes), rows
        self.send, self.recv, self.local = send, recv, local

    def _core(self):
        z, y, c, x = place()
        copies = []
        for i, ((near, first, width), (far, _, _)) in enumerate(zip(self.own(c), self.own(1 - c))):
            spot = self.full.at[x, z, y, block(c, 64), pl.ds(first, width)]
            copies.append(pltpu.make_async_copy(near, spot, self.local.at[i]))
            copies.append(remote(far, spot, self.send.at[i], self.recv.at[i], at(z, y, 1 - c, x)))
        return copies

    def _copy(self, kind, d):
        z, y, c, x = place()
        a, b, w, first = cut(self.rows)
        from_z = lax.rem(z - d + 4, 4)
        to_x, to_y, to_z = at(z, y, c, 1 - x), at(z, 1 - y, c, x), at(lax.rem(z + d, 4), y, c, x)
        if kind == 0:
            spot, to = self.full.at[x, z, y, first, self.lanes], to_z
        elif kind == 1:
            spot, to = self.full.at[x, from_z, y, a, self.lanes], to_x
        elif kind == 2:
            spot, to = self.full.at[x, from_z, y, b, self.lanes], to_y
        elif kind == 3:
            spot, to = self.full.at[:, from_z, y, a, self.lanes], to_y
        elif kind == 4:
            spot, to = self.full.at[x, from_z, :, b, self.lanes], to_x
        elif kind == 5:
            spot, to = self.full.at[:, z, :, w, self.lanes], to_z
        elif d == 0:
            spot, to = self.full.at[x, z, y, w, self.lanes], to_x
        else:
            spot, to = self.full.at[:, z, y, w, self.lanes], to_y
        return remote(spot, spot, self.send.at[8 + 4 * kind + d], self.recv.at[8 + 4 * kind + d], to)

    def start_core(self):
        for copy in self._core():
            copy.start()

    def enter(self, along=(2, 1, 3)):
        for copy in self._core():
            copy.wait()
        self.pass_on(along)

    def pass_on(self, along):
        for d in along:
            self._copy(0, d).start()

    def first(self):
        if self.rows[2]:
            self._copy(6, 0).start()
        self._copy(1, 0).start()
        self._copy(2, 0).start()

    def arrived(self, d):
        self._copy(0, d).wait()
        self._copy(1, d).start()
        self._copy(2, d).start()

    def turn(self, d):
        if self.rows[2] and d == 0:
            self._copy(6, 0).wait()
            self._copy(6, 1).start()
        self._copy(1, d).wait()
        self._copy(3, d).start()
        self._copy(2, d).wait()
        self._copy(4, d).start()

    def spread(self):
        self._copy(6, 1).wait()
        for k in (2, 1, 3):
            self._copy(5, k).start()

    def finish(self):
        for d in range(4):
            self._copy(3, d).wait()
            self._copy(4, d).wait()
        if self.rows[2]:
            for d in (2, 1, 3):
                self._copy(5, d).wait()


class Scatter:
    def __init__(
        self, part, first_a, first_b, second, third, wide_z, wide_y, wide_x, total, lanes, rows, out, send, recv
    ):
        self.rows = rows
        self.part, self.first_a, self.first_b = part, first_a, first_b
        self.wide_z, self.wide_y, self.wide_x = wide_z, wide_y, wide_x
        self.second, self.third, self.total, self.out = second, third, total, out
        self.lanes, self.send, self.recv = pl.ds(*lanes), send, recv

    def _copy(self, kind, d):
        z, y, c, x = place()
        n, to_z = self.lanes, lax.rem(z + d, 4)
        a, b, w, first = cut(self.rows)
        na, nb, nw = [pl.ds(0, count) for count in self.rows]
        send, recv = self.send.at[4 * kind + d], self.recv.at[4 * kind + d]
        to_x, to_y = at(z, y, c, 1 - x), at(z, 1 - y, c, x)
        if kind == 0:
            return remote(self.part.at[:, to_z, 1 - y, a, n], self.first_a.at[to_z, :, na, n], send, recv, to_y)
        if kind == 1:
            return remote(self.part.at[1 - x, to_z, :, b, n], self.first_b.at[to_z, :, nb, n], send, recv, to_x)
        if kind == 2:
            return remote(self.first_a.at[to_z, 1 - x, na, n], self.second.at[to_z, a, n], send, recv, to_x)
        if kind == 3:
            return remote(self.first_b.at[to_z, 1 - y, nb, n], self.second.at[to_z, b, n], send, recv, to_y)
        if kind == 4:
            return remote(
                self.second.at[to_z, first, n], self.third.at[d - 1, first, n], send, recv, at(to_z, y, c, x)
            )
        if kind == 5:
            return remote(
                self.part.at[:, to_z, :, w, n], self.wide_z.at[d - 1, :, :, nw, n], send, recv, at(to_z, y, c, x)
            )
        if d == 0:
            return remote(self.wide_z.at[0, :, 1 - y, nw, n], self.wide_y.at[:, nw, n], send, recv, to_y)
        return remote(self.wide_y.at[1 - x, nw, n], self.wide_x.at[nw, n], send, recv, to_x)

    def _core(self):
        z, y, c, x = place()
        copies = []
        for i, (target, first, width) in enumerate(self.out(c)):
            lanes = pl.ds(first, width)
            copies.append(
                remote(
                    self.total.at[block(1 - c, 64), lanes], target, self.send.at[28 + i], self.recv.at[28 + i],
                    at(z, y, 1 - c, x),
                )
            )
            copies.append(pltpu.make_async_copy(self.total.at[block(c, 64), lanes], target, self.send.at[32 + i]))
        return copies

    def _start(self, d):
        self._copy(0, d).start()
        self._copy(1, d).start()

    def start(self):
        for d in (2, 1, 3):
            self._copy(5, d).start()
        for d in (2, 1, 3, 0):
            self._start(d)

    def turn(self, d):
        z, y, c, x = place()
        to_z, n = lax.rem(z + d, 4), self.lanes
        a, b, _, _ = cut(self.rows)
        na, nb, _ = [pl.ds(0, count) for count in self.rows]
        self._copy(0, d).wait()
        for k in range(2):
            total = self.first_a[to_z, k, na, n].astype(F32) + self.part[k, to_z, y, a, n].astype(F32)
            self.first_a[to_z, k, na, n] = total.astype(BF)
        self._copy(2, d).start()
        self._copy(1, d).wait()
        for k in range(2):
            total = self.first_b[to_z, k, nb, n].astype(F32) + self.part[x, to_z, k, b, n].astype(F32)
            self.first_b[to_z, k, nb, n] = total.astype(BF)
        self._copy(3, d).start()

    def fold_z(self):
        z, y, c, x = place()
        n, w, nw = self.lanes, cut(self.rows)[2], pl.ds(0, self.rows[2])
        for k in (2, 1, 3):
            self._copy(5, k).wait()
        for k in range(2):
            for j in range(2):
                total = self.part[k, z, j, w, n].astype(F32)
                for s in range(3):
                    total = total + self.wide_z[s, k, j, nw, n].astype(F32)
                self.wide_z[0, k, j, nw, n] = total.astype(BF)
        self._copy(6, 0).start()

    def fold_y(self):
        z, y, c, x = place()
        n, nw = self.lanes, pl.ds(0, self.rows[2])
        self._copy(6, 0).wait()
        for k in range(2):
            total = self.wide_y[k, nw, n].astype(F32) + self.wide_z[0, k, y, nw, n].astype(F32)
            self.wide_y[k, nw, n] = total.astype(BF)
        self._copy(6, 1).start()

    def leave(self, d):
        z, y, c, x = place()
        to_z, n = lax.rem(z + d, 4), self.lanes
        a, b, _, _ = cut(self.rows)
        na, nb, _ = [pl.ds(0, count) for count in self.rows]
        self._copy(2, d).wait()
        total = self.second[to_z, a, n].astype(F32) + self.first_a[to_z, x, na, n].astype(F32)
        self.second[to_z, a, n] = total.astype(BF)
        self._copy(3, d).wait()
        total = self.second[to_z, b, n].astype(F32) + self.first_b[to_z, y, nb, n].astype(F32)
        self.second[to_z, b, n] = total.astype(BF)
        if d:
            self._copy(4, d).start()

    def last(self):
        z, y, c, x = place()
        n, nw = self.lanes, pl.ds(0, self.rows[2])
        a, b, w, _ = cut(self.rows)
        self._copy(6, 1).wait()
        self.total[w, n] = self.wide_x[nw, n].astype(F32) + self.wide_y[x, nw, n].astype(F32)
        for d in (1, 2, 3):
            self._copy(4, d).wait()
        for rows in (a, b):
            total = self.second[z, rows, n].astype(F32)
            for d in range(3):
                total = total + self.third[d, rows, n].astype(F32)
            self.total[rows, n] = total
        for copy in self._core():
            copy.start()

    def finish(self):
        for copy in self._core():
            copy.wait()


class Swap:
    def __init__(self, own, full, send, recv, local):
        self.own, self.full, self.send, self.recv, self.local = own, full, send, recv, local

    def _both(self, act):
        z, y, c, x = place()

        @pl.when(c != x)
        def _():
            to = at(z, y, 1 - c, 1 - x)
            act(remote(self.own, self.full.at[block(1 - c, 512)], self.send.at[0], self.recv.at[0], to))

        @pl.when(c == x)
        def _():
            act(pltpu.make_async_copy(self.own, self.full.at[block(c, 512)], self.local))

    def _core(self):
        z, y, c, x = place()
        spot = self.full.at[block(c, 512)]
        return remote(spot, spot, self.send.at[1], self.recv.at[1], at(z, y, 1 - c, x))

    def start(self):
        self._both(lambda copy: copy.start())

    def share(self):
        self._both(lambda copy: copy.wait())
        self._core().start()

    def finish(self):
        self._core().wait()


class SwapBack:
    def __init__(self, full, out, send, recv, local):
        self.full, self.out, self.send, self.recv, self.local = full, out, send, recv, local

    def _both(self, act):
        z, y, c, x = place()
        rows = self.full if self.full.shape == self.out.shape else self.full.at[block(c, 512)]

        @pl.when(c != x)
        def _():
            act(remote(rows, self.out, self.send, self.recv, at(z, y, 1 - c, 1 - x)))

        @pl.when(c == x)
        def _():
            act(pltpu.make_async_copy(rows, self.out, self.local))

    def start(self):
        self._both(lambda copy: copy.start())

    def finish(self):
        self._both(lambda copy: copy.wait())


class SmallGather:
    def __init__(self, own, full, send, recv):
        self.own, self.full, self.send, self.recv = own, full, send, recv

    def _copy(self, k):
        z, y, c, x = place()
        send, recv = self.send.at[k], self.recv.at[k]
        if k == 0:
            return remote(self.own, self.full.at[x, z, y, c], send, recv, at(z, y, 1 - c, x))
        if k <= 3:
            spot = self.full.at[x, z, y]
            return remote(spot, spot, send, recv, at(lax.rem(z + k, 4), y, c, x))
        if k == 4:
            spot = self.full.at[x, :, y]
            return remote(spot, spot, send, recv, at(z, 1 - y, c, x))
        spot = self.full.at[x]
        return remote(spot, spot, send, recv, at(z, y, c, 1 - x))

    def start(self):
        z, y, c, x = place()
        self.full[x, z, y, c] = self.own[...]
        self._copy(0).start()

    def step(self, done, begin):
        for k in done:
            self._copy(k).wait()
        for k in begin:
            self._copy(k).start()


class SmallScatter:
    def __init__(self, part, near_c, near_z, near, send, recv):
        self.part, self.near_c, self.near_z, self.near = part, near_c, near_z, near
        self.send, self.recv = send, recv

    def _copy(self, k):
        z, y, c, x = place()
        send, recv = self.send.at[k], self.recv.at[k]
        if k == 0:
            return remote(self.part.at[1 - c], self.near_c, send, recv, at(z, y, 1 - c, x))
        if k <= 3:
            to = lax.rem(z + k, 4)
            return remote(self.near_c.at[to], self.near_z.at[k - 1], send, recv, at(to, y, c, x))
        to_x, to_y = ((1 - x, y), (x, 1 - y), (1 - x, 1 - y))[k - 4]
        return remote(self.near_z.at[3, to_x, to_y], self.near.at[k - 4], send, recv, at(z, to_y, c, to_x))

    def start(self):
        self._copy(0).start()

    def along(self):
        z, y, c, x = place()
        self._copy(0).wait()
        self.near_c[...] = self.near_c[...] + self.part[c]
        for k in (1, 2, 3):
            self._copy(k).start()

    def across(self):
        z, y, c, x = place()
        for k in (1, 2, 3):
            self._copy(k).wait()
        self.near_z[3] = self.near_c[z] + self.near_z[0] + self.near_z[1] + self.near_z[2]
        for k in (4, 5, 6):
            self._copy(k).start()

    def finish(self):
        z, y, c, x = place()
        for k in (4, 5, 6):
            self._copy(k).wait()
        return self.near_z[3, x, y] + self.near[0] + self.near[1] + self.near[2]


class Pair:
    def __init__(self, mine, theirs, send, recv):
        self.mine, self.theirs, self.send, self.recv = mine, theirs, send, recv

    def _copy(self, i):
        z, y, c, x = place()
        rows = block(i, 256)
        return remote(
            self.mine.at[rows], self.theirs.at[rows], self.send.at[i], self.recv.at[i], at(z, y, 1 - c, x)
        )

    def give(self, i, partial):
        self.mine[block(i, 256), :] = partial.astype(BF)
        self._copy(i).start()

    def take(self, i):
        self._copy(i).wait()
        rows = block(i, 256)
        return self.mine[rows, :].astype(F32) + self.theirs[rows, :].astype(F32)


def normalise(values):
    centred = values - jnp.mean(values, axis=-1, keepdims=True)
    scale = lax.rsqrt(jnp.mean(centred * centred, axis=-1, keepdims=True) + epsilon)
    return centred * scale, scale


def nn(a, b):
    return jnp.dot(a, b, preferred_element_type=F32)


def nt(a, b):
    return lax.dot_general(a, b, (((1,), (1,)), ((), ())), preferred_element_type=F32)


def tn(a, b):
    return lax.dot_general(a, b, (((0,), (0,)), ((), ())), preferred_element_type=F32)


def in_half(h):
    return lax.broadcasted_iota(jnp.int32, (1, 128), 1) // 64 == h


def column_sum(values):
    return jnp.sum(values, 0, keepdims=True)


def gelu_parts(v):
    k = math.sqrt(2.0 / math.pi)
    square = v * v
    t = jnp.tanh(k * v * (1.0 + 0.044715 * square))
    half = 0.5 * (1.0 + t)
    return v * half, half + 0.5 * k * v * (1.0 - t * t) * (1.0 + 3.0 * 0.044715 * square)


def split_bf(values):
    high = values.astype(BF)
    return high, (values - high.astype(F32)).astype(BF)


def exact_nn(values, chosen):
    high, low = split_bf(values)
    lower = (values - high.astype(F32) - low.astype(F32)).astype(BF)
    return nn(high, chosen) + nn(low, chosen) + nn(lower, chosen)


def devices():
    return [(zz, yy, cc, xx) for zz in range(4) for yy in range(2) for cc in range(2) for xx in range(2)]


def widen(small_full, row, k, width=1024):
    pieces = jnp.concatenate([small_full[xx, zz, yy, cc, row : row + 1, :] for zz, yy, cc, xx in devices()], 0)
    lane = lax.broadcasted_iota(jnp.int32, (128, width), 1)
    source = lax.broadcasted_iota(jnp.int32, (128, width), 0)
    pick = jnp.where(source == k * 32 + lax.rem(lane, 32), 1.0, 0.0).astype(BF)
    spread_out = nn(pieces.astype(BF), pick)
    device = lax.broadcasted_iota(jnp.int32, (32, width), 0)
    lane = lax.broadcasted_iota(jnp.int32, (32, width), 1)
    return column_sum(jnp.where(lane // 32 == device, spread_out, 0.0))


def narrow(vector, k):
    device = lax.broadcasted_iota(jnp.int32, (32, 1024), 0)
    lane = lax.broadcasted_iota(jnp.int32, (32, 1024), 1)
    source = lax.broadcasted_iota(jnp.int32, (1024, 128), 0)
    target = lax.broadcasted_iota(jnp.int32, (1024, 128), 1)
    chosen = jnp.where(target == k * 32 + lax.rem(source, 32), 1.0, 0.0).astype(BF)
    return exact_nn(jnp.where(lane // 32 == device, vector, 0.0), chosen)


def flat(value):
    return value.reshape(-1, value.shape[-1])


INPUTS = """lat_own grad_own wq wp wu wd ada cond q_bias v_bias p_bias d_bias u_bias a_bias"""
OUTPUTS = """block_mine input_mine q_out p_out u_out d_out held_a held_b
    ada_out small_out"""
GROUP = (2, 4, 2, 128, 1024)
TOKENS = (1024, 1024)


def scratch():
    v, f = (lambda *s: pltpu.VMEM(s, BF)), (lambda *s: pltpu.VMEM(s, F32))
    dma, regular = pltpu.SemaphoreType.DMA, pltpu.SemaphoreType.REGULAR
    out = dict(lat=v(*TOKENS), grad=v(*TOKENS), attn_in=v(*TOKENS), mid=f(*TOKENS), branch_one=v(*TOKENS))
    out.update(mlp_in=v(*TOKENS), g_two=v(*TOKENS), mine=v(*TOKENS), theirs_a=v(*TOKENS), theirs_b=v(*TOKENS))
    out.update(buf_a=v(*GROUP), buf_b=v(*GROUP), gu=v(*GROUP), buf_c=v(*GROUP), buf_d=v(*GROUP))
    for i in range(2):
        out[f"first_a{i}"], out[f"first_b{i}"] = v(4, 2, MOST_A, 1024), v(4, 2, MOST_B, 1024)
    for i, name in enumerate(("down", "up", "near")):
        a, b, w = ROWS[name]
        out[f"second{i}"], out[f"third{i}"] = v(4, a + b, 1024), v(3, a + b, 1024)
        out[f"wide_z{i}"], out[f"wide_y{i}"], out[f"wide_x{i}"] = v(3, 2, 2, w, 1024), v(2, w, 1024), v(w, 1024)
    out.update(total=f(128, 1024), heads_grad=v(2, 1024, 256), lse=f(1024, 128))
    out.update(key_total=f(1024, 128), value_total=f(1024, 128), input_grad=v(256, 16, 128))
    out.update(small=f(16, 128), small_full=f(2, 4, 2, 2, 16, 128), wide=v(128, 3072), silu=f(16, 128))
    out.update(part=f(2, 4, 2, 8, 512), near_c=f(4, 2, 8, 512), near_z=f(4, 2, 8, 512), near_y=f(2, 8, 512))
    out.update(mods=f(2, 8, 512), vectors=f(16, 1024), up_bias=f(1, 4096), stats=f(8, 1024), columns=f(8, 1024))
    out.update(up_sums=f(2, 1, 1024), sums=f(2, 1, 768), half_mods=f(4, 2, 2, 8, 512), all_mods=f(4, 2, 2, 8, 512), tall=f(128, 512))
    out.update(bias_part=f(2, 4, 2, 2, 2, 128), bias_c=f(4, 2, 2, 2, 128), bias_z=f(4, 2, 2, 2, 128))
    out.update(bias_near=f(3, 2, 128), found=f(2, 4, 2, 1, 128), found_c=f(4, 2, 1, 128), found_z=f(4, 2, 1, 128))
    out.update(found_near=f(3, 4, 1, 128), picked=f(8, 128), picked_other=f(8, 128))
    out.update(gather_send=dma((4, 36)), gather_recv=dma((4, 36)), gather_local=dma((4, 6)))
    out.update(scatter_send=dma((4, 36)), scatter_recv=dma((4, 36)), pair_send=dma((4, 4)), pair_recv=dma((4, 4)))
    out.update(swap_send=dma((4, 2)), swap_recv=dma((4, 2)), swap_local=dma((4,)))
    out.update(small_send=dma((4, 8)), small_recv=dma((4, 8)), load_sem=dma((12,)), free=regular)
    return out


def pairs_kernel(*refs):
    names = INPUTS.split() + OUTPUTS.split() + list(scratch())
    r = dict(zip(names, refs))
    Block(r).run()

PLAN = dict(
    b0=(("q", "enter", ()), ("q", "pass_on", (2,)),),
    b1=(("q", "first"), ("p", "enter", ()), ("u", "enter", ()), ("d", "enter", ()),),
    b3=(("q", "pass_on", (1,)), ("q", "pass_on", (3,)), ("p", "pass_on", (2,)), ("p", "pass_on", (1,)), ("p", "pass_on", (3,)), ("u", "pass_on", (2,)), ("u", "pass_on", (1,)), ("u", "pass_on", (3,)), ("q", "turn", 0),),
    b4=(("q", "arrived", 2), ("q", "arrived", 1), ("q", "arrived", 3), ("d", "pass_on", (2,)), ("d", "pass_on", (1,)), ("d", "pass_on", (3,)),),
    b5=(("q", "turn", 2), ("swap_lat", "share"),),
    b6=(("q", "turn", 1),),
    b7=(("q", "turn", 3), ("p", "first"), ("p", "arrived", 2), ("p", "arrived", 1), ("p", "arrived", 3), ("u", "first"),),
    project0=(("swap_grad", "start"),),
    project7=(("p", "turn", 0), ("p", "turn", 2), ("p", "turn", 1), ("p", "turn", 3), ("p", "spread"), ("u", "arrived", 2), ("u", "arrived", 1), ("u", "arrived", 3),),
    heads0=(("u", "turn", 0),),
    heads3=(("u", "turn", 2), ("u", "spread"),),
    heads4=(("u", "turn", 1),),
    heads5=(("u", "turn", 3),),
    heads7=(("d", "first"),),
    out3=(("d", "arrived", 2), ("d", "arrived", 1), ("d", "arrived", 3), ("swap_grad", "share"),),
    enter3=(("d", "turn", 0),),
    ascend3=(("d", "turn", 2), ("d", "spread"),),
    ascend6=(("d", "turn", 1),),
    down0=(("d", "turn", 3),),
    hidden1=(("down", "turn", 2),),
    hidden7=(("down", "turn", 1),),
    back1=(("down", "turn", 3),),
    upper0=(("down", "turn", 0),),
    upper1=(("down", "fold_z"),),
    upper2=(("down", "leave", 2),),
    rest0=(("down", "leave", 1),),
    rest1=(("down", "fold_y"),),
    rest3=(("down", "leave", 3),),
    lift3=(("down", "leave", 0), ("", "signal_free"),),
    proj3=(("swap_block", "start"),),
    near0=(("up", "turn", 2),),
    near2=(("up", "turn", 1),),
    near5=(("up", "turn", 3),),
    first0=(("up", "turn", 0), ("up", "fold_z"),),
    first3=(("up", "leave", 2), ("down", "last"),),
    far0=(("up", "leave", 1),),
    far1=(("up", "fold_y"), ("up", "leave", 3),),
    far2=(("near_heads", "turn", 2), ("up", "leave", 0),),
    far4=(("near_heads", "turn", 1),),
    far6=(("near_heads", "turn", 3),),
    far7=(("near_heads", "turn", 0), ("near_heads", "fold_z"),),
    second1=(("near_heads", "leave", 2),),
    second3=(("near_heads", "leave", 1),),
    drop1=(("near_heads", "fold_y"), ("near_heads", "leave", 3),),
    drop3=(("near_heads", "leave", 0), ("down", "finish"),),
    last0=(("far_heads", "turn", 2),),
    last2=(("far_heads", "turn", 1),),
    e0=(("swap_input", "start"), ("up", "last"),),
    e2=(("far_heads", "turn", 3),),
    e4=(("far_heads", "turn", 0), ("far_heads", "fold_z"),),
    e6=(("far_heads", "leave", 2),),
    e7=(("up", "finish"), ("far_heads", "leave", 1), ("far_heads", "fold_y"), ("near_heads", "last"),),
    e8=(("far_heads", "leave", 3), ("far_heads", "leave", 0), ("far_heads", "last"),),
)


class Block:
    def __init__(self, r):
        for name, ref in r.items():
            setattr(self, name, ref)

    def run(self):
        self.set_up()
        self.begin()
        self.attend()
        self.mlp()
        self.attend_back()
        self.end()

    def set_up(self):
        gather = lambda i, name, own, full, lanes: Gather(
            own, full, lanes, ROWS[name], self.gather_send.at[i], self.gather_recv.at[i], self.gather_local.at[i]
        )
        self.q = gather(
            0,
            "q",
            lambda h: [
                (self.wq.at[j, :, block(2 * h + k, 128)], 256 + 384 * k + 128 * j, 128)
                for k in range(2)
                for j in range(3)
            ],
            self.buf_a,
            (256, 768),
        )
        self.p = gather(1, "p", lambda h: [(self.wp.at[:, block(h, 256)], 0, 256)], self.buf_a, (0, 256))
        self.u = gather(2, "u", lambda h: [(self.wu.at[:, block(h, 1024)], 0, 1024)], self.gu, (0, 1024))
        self.d = gather(3, "d", lambda h: [(self.wd.at[:, block(h, 1024)], 0, 1024)], self.buf_b, (0, 1024))
        heads = lambda k: lambda h: [
            (self.q_out.at[j, :, block(2 * h + k, 128)], 256 + 384 * k + 128 * j, 128) for j in range(3)
        ]
        outs = (
            lambda h: [(self.d_out.at[:, block(h, 1024)], 0, 1024)],
            lambda h: [(self.u_out.at[:, block(h, 1024)], 0, 1024)],
            lambda h: heads(0)(h) + [(self.p_out.at[:, block(h, 256)], 0, 256)],
            heads(1),
        )
        firsts = ((self.first_a0, self.first_b0), (self.first_a1, self.first_b1))
        rest = (
            (self.second0, self.third0, self.wide_z0, self.wide_y0, self.wide_x0),
            (self.second1, self.third1, self.wide_z1, self.wide_y1, self.wide_x1),
            (self.second2, self.third2, self.wide_z2, self.wide_y2, self.wide_x2),
        )
        plan = (
            (self.buf_d, firsts[0], rest[0], (0, 1024), ROWS["down"]),
            (self.buf_c, firsts[1], rest[1], (0, 1024), ROWS["up"]),
            (self.buf_d, firsts[0], rest[2], (0, 640), ROWS["near"]),
            (self.buf_d, firsts[0], rest[2], (640, 384), ROWS["far"]),
        )
        self.down, self.up, self.near_heads, self.far_heads = [
            Scatter(
                part, *first, *more, self.total, lanes, rows, outs[i], self.scatter_send.at[i], self.scatter_recv.at[i]
            )
            for i, (part, first, more, lanes, rows) in enumerate(plan)
        ]
        swaps = [(self.lat_own, self.lat), (self.grad_own, self.grad)]
        self.swap_lat, self.swap_grad = [
            Swap(own, full, self.swap_send.at[i], self.swap_recv.at[i], self.swap_local.at[i])
            for i, (own, full) in enumerate(swaps)
        ]
        backs = [(self.g_two, self.block_mine), (self.input_grad, self.input_mine)]
        self.swap_block, self.swap_input = [
            SwapBack(full, out, self.swap_send.at[2 + i, 0], self.swap_recv.at[2 + i, 0], self.swap_local.at[2 + i])
            for i, (full, out) in enumerate(backs)
        ]
        self.pairs = [
            Pair(self.mine, theirs, self.pair_send.at[i], self.pair_recv.at[i])
            for i, theirs in enumerate((self.theirs_a, self.theirs_b, self.theirs_a, self.theirs_b))
        ]

    def do(self, slot):
        for owner, act, *given in PLAN.get(slot, ()):
            getattr(getattr(self, owner) if owner else self, act)(*given)

    def loop(self, count, body, name):
        loop(count, body, {i: (lambda s=name + str(i): self.do(s)) for i in range(count) if name + str(i) in PLAN})

    def signal_free(self):
        z, y, c, x = place()
        for to in (at(z, 1 - y, c, x), at(z, y, c, 1 - x)):
            pl.semaphore_signal(self.free, inc=1, device_id=to, device_id_type=MESH)

    def load(self, i, source, target):
        return pltpu.make_async_copy(source, target, self.load_sem.at[i])

    def begin(self):
        z, y, c, x = place()
        q, p, u, d = self.q, self.p, self.u, self.d
        send, recv = self.small_send, self.small_recv
        little = SmallGather(self.small, self.small_full, send.at[0], recv.at[0])
        v = self.cond[...].astype(F32)
        silu = (v / (1.0 + jnp.exp(-v))).astype(BF).astype(F32)
        self.small[...] = jnp.zeros_like(self.small)
        for k in range(8):
            self.small[k : k + 1, :] = silu[:, k * 128 : (k + 1) * 128]
        for k, bias in enumerate((self.q_bias, self.v_bias, self.p_bias, self.d_bias)):
            self.small[8:9, k * 32 : (k + 1) * 32] = bias[...].astype(F32)
        self.small[9:10, :] = self.u_bias[...].astype(F32)
        a_bias = self.a_bias[...].astype(F32)
        for j in range(6):
            self.small[10 + j // 4 : 11 + j // 4, j % 4 * 32 : j % 4 * 32 + 32] = a_bias[j : j + 1, :]
        greet(partners())
        little.start()
        q.start_core()
        for group in (p, u, d):
            group.start_core()
        self.swap_lat.start()
        self.wide[...] = jnp.zeros_like(self.wide)
        ada = [self.load(j, self.ada.at[j], self.wide.at[block(c, 64), pl.ds(j * 512, 512)]) for j in range(6)]
        for copy in ada:
            copy.start()
        little.step((0,), (1, 2, 3))
        self.do("b0")
        self.part[...] = jnp.zeros_like(self.part)
        little.step((1, 2, 3), (4,))
        self.do("b1")
        for copy in ada:
            copy.wait()
        little.step((4,), (5,))
        self.do("b2")
        row = z * 2 + y
        lhs = [self.small_full[x, b // 4, b // 2 % 2, b % 2, pl.ds(row, 1), :] for b in range(16)]
        lhs = jnp.concatenate(lhs, 0)
        self.silu[...] = lhs
        for j in range(6):
            product = nn(lhs.astype(BF), self.wide[:, j * 512 : (j + 1) * 512])
            for b in range(16):
                self.part[b % 2, b // 4, b // 2 % 2, j : j + 1, :] = product[b : b + 1, :]
        near_c, near_y, near_z = self.near_c, self.near_y, self.near_z
        first = remote(self.part.at[1 - c], near_c, send.at[1, 0], recv.at[1, 0], at(z, y, 1 - c, x))
        first.start()
        first.wait()
        near_c[...] = near_c[...] + self.part[c]
        seconds = []
        for s in (1, 2, 3):
            to = lax.rem(z + s, 4)
            seconds.append(remote(near_c.at[to], near_z.at[s - 1], send.at[1, s], recv.at[1, s], at(to, y, c, x)))
            seconds[-1].start()
        self.do("b3")
        for copy in seconds:
            copy.wait()
        near_z[3] = near_c[z] + near_z[0] + near_z[1] + near_z[2]
        self._partials(lambda copy: copy.start())
        self.do("b4")
        self._partials(lambda copy: copy.wait())
        self.mods[c] = near_y[0] + near_y[1]
        fifth = remote(self.mods.at[c], self.mods.at[c], send.at[1, 6], recv.at[1, 6], at(z, y, 1 - c, x))
        fifth.start()
        self.do("b5")
        little.step((5,), ())
        bias = [widen(self.small_full, 8, k) for k in range(4)]
        ada_bias = [widen(self.small_full, 10 + j // 4, j % 4) for j in range(6)]
        for k, (zz, yy, cc, xx) in enumerate(devices()):
            self.up_bias[:, k * 128 : (k + 1) * 128] = self.small_full[xx, zz, yy, cc, 9:10, :]
        self.do("b6")
        fifth.wait()
        for j in range(6):
            for h in range(2):
                lanes = slice(h * 512, (h + 1) * 512)
                self.vectors[j : j + 1, lanes] = self.mods[h, j : j + 1, :] + ada_bias[j][:, lanes]
        for k in range(4):
            self.vectors[6 + k : 7 + k, :] = bias[k]
        self.do("b7")
        self.swap_lat.finish()

    def _partials(self, act):
        z, y, c, x = place()
        for k, to_y in enumerate((y, 1 - y)):
            sems = self.small_send.at[1, 4 + k], self.small_recv.at[1, 4 + k]
            source, target = self.near_z.at[3, to_y], self.near_y.at[y]

            @pl.when(c != x)
            def _():
                act(remote(source, target, *sems, at(z, to_y, 1 - c, 1 - x)))

            @pl.when(c == x)
            def _():
                if k:
                    act(remote(source, target, *sems, at(z, to_y, c, x)))
                else:
                    act(pltpu.make_async_copy(source, target, self.load_sem.at[6]))

    def attend(self):
        z, y, c, x = place()
        q, p, u, d, vectors = self.q, self.p, self.u, self.d, self.vectors

        def modulated(i):
            rows = block(i, 256)
            normal, _ = normalise(self.lat[rows, :].astype(F32))
            self.attn_in[rows, :] = (normal * (1.0 + vectors[1:2, :]) + vectors[0:1, :]).astype(BF)

        self.loop(4, modulated, "normal")
        q.finish()

        def project(i):
            b, quarter = i // 4, lax.rem(i, 4)
            values = nn(self.attn_in[block(quarter, 256), :], flat(self.buf_a[b, :, :, :, 256:1024]))
            for k in range(6):
                value = values[:, k * 128 : (k + 1) * 128]
                if k % 3 != 1:
                    columns = pl.ds(pl.multiple_of(b * 512 + c * 256 + k // 3 * 128, 128), 128)
                    row = 6 if k % 3 == 0 else 7
                    value = value + vectors[row : row + 1, columns]
                self.buf_d[b, quarter, :, :, 256 + k * 128 : 384 + k * 128] = value.astype(BF).reshape(2, 128, 128)

        self.loop(8, project, "project")
        lane = lax.broadcasted_iota(jnp.int32, (1, 128), 1)
        self.lse[...] = jnp.zeros_like(self.lse)

        def attend(i):
            pair, half = i // 2, lax.rem(i, 2)
            rows, zz = block(half, 512), pl.ds(half * 2, 2)
            b, k, q_at = lax.rem(pair, 2), pair // 2, pl.multiple_of(256 + pair // 2 * 384, 128)
            queries = flat(self.buf_d[b, zz, :, :, pl.ds(q_at, 128)]) * BF(0.125)
            keys = flat(self.buf_d[b, :, :, :, pl.ds(q_at + 128, 128)])
            values = flat(self.buf_d[b, :, :, :, pl.ds(q_at + 256, 128)])
            result = None
            logs = self.lse[rows, :]
            for h in range(2):
                scores = nt(jnp.where(in_half(h), queries, jnp.zeros_like(queries)), keys)
                largest = jnp.max(scores, -1, keepdims=True)
                exponent = jnp.exp(scores - largest)
                summed = jnp.sum(exponent, -1, keepdims=True)
                mixture = nn(exponent.astype(BF), values) * (1.0 / summed)
                result = mixture if h == 0 else jnp.where(in_half(0), result, mixture)
                logs = jnp.where(lane == pair * 2 + h, largest + jnp.log(summed), logs)
            self.buf_d[b, zz, :, :, block(k, 128)] = result.astype(BF).reshape(2, 2, 128, 128)
            self.lse[rows, :] = logs

        self.loop(8, attend, "heads")
        p.finish()
        self.load(0, self.buf_a, self.held_a).start()
        pair = self.pairs[0]

        def out(i):
            zz = i
            partial = nt(flat(self.buf_d[0, zz, :, :, 0:256]), flat(self.buf_a[0, :, :, :, 0:256]))
            partial += nt(flat(self.buf_d[1, zz, :, :, 0:256]), flat(self.buf_a[1, :, :, :, 0:256]))
            pair.give(i, partial)

        self.loop(4, out, "out")
        self.load(1, self.buf_d, self.held_b).start()

        def residual(i):
            rows = block(i, 256)
            branch = pair.take(i) + vectors[8:9, :]
            self.branch_one[rows, :] = branch.astype(BF)
            self.mid[rows, :] = self.lat[rows, :].astype(F32) + vectors[2:3, :] * branch

        self.loop(4, residual, "middle")

    def mlp(self):
        z, y, c, x = place()
        u, d, vectors, stats, down, up = self.u, self.d, self.vectors, self.stats, self.down, self.up
        active, up_grad, slope, hidden_grad = self.buf_c, self.buf_c, self.buf_a, self.buf_a
        wd, gu, mid, mlp_in, g_two, grad = self.buf_b, self.gu, self.mid, self.mlp_in, self.g_two, self.grad
        self.swap_grad.finish()
        stats[...] = jnp.zeros_like(stats)
        self.up_sums[...] = jnp.zeros_like(self.up_sums)

        def enter(i):
            rows = block(i, 256)
            normal, _ = normalise(mid[rows, :])
            mlp_in[rows, :] = (normal * (1.0 + vectors[4:5, :]) + vectors[3:4, :]).astype(BF)
            g = (grad[rows, :].astype(F32) * vectors[5:6, :]).astype(BF)
            g_two[rows, :] = g
            mine_too = jnp.where(i // 2 == c, 1.0, 0.0)
            stats[1:2, :] += column_sum(g.astype(F32)) * mine_too

        self.loop(4, enter, "enter")
        u.finish()
        self.load(0, self.buf_a, self.held_a).wait()

        def ascend(i):
            b, quarter = i // 4, lax.rem(i, 4)
            columns = pl.ds(pl.multiple_of(b * 2048 + c * 1024, 1024), 1024)
            hidden = nn(mlp_in[block(quarter, 256), :], flat(gu[b])) + self.up_bias[:, columns]
            value, gradient = gelu_parts(hidden)
            active[b, quarter] = value.astype(BF).reshape(2, 128, 1024)
            slope[b, quarter] = gradient.astype(BF).reshape(2, 128, 1024)

        self.loop(8, ascend, "ascend")
        self.load(1, self.buf_d, self.held_b).wait()

        def down_gradient(i):
            b, half = i // 2, lax.rem(i, 2)
            value = tn(g_two[:, block(half, 512)], flat(active[b]))
            self.buf_d[b, pl.ds(half * 2, 2)] = value.astype(BF).reshape(2, 2, 128, 1024)

        self.loop(4, down_gradient, "down")
        down.start()
        d.finish()
        pair, back = self.pairs[1], self.pairs[2]

        def descend(i):
            pair.give(i, nt(flat(active[0, i]), flat(wd[0])) + nt(flat(active[1, i]), flat(wd[1])))

        self.loop(4, descend, "descend")

        def hidden_gradient(i):
            b, quarter = i // 4, lax.rem(i, 4)
            value = nn(g_two[block(quarter, 256), :], flat(wd[b])) * flat(slope[b, quarter]).astype(F32)
            value = value.astype(BF)
            hidden_grad[b, quarter] = value.reshape(2, 128, 1024)
            self.up_sums[b] += column_sum(value.astype(F32))

        self.loop(8, hidden_gradient, "hidden")
        self.load(3, self.held_b, self.buf_b).start()

        def leave(i):
            rows = block(i, 256)
            branch_two = pair.take(i) + vectors[9:10, :]
            g_two[rows, :] = (mid[rows, :] + vectors[5:6, :] * branch_two).astype(BF)
            stats[0:1, :] += column_sum(grad[rows, :].astype(F32) * branch_two)

        self.loop(4, leave, "leave")

        def descend_back(i):
            back.give(i, nt(flat(hidden_grad[0, i]), flat(gu[0])) + nt(flat(hidden_grad[1, i]), flat(gu[1])))

        self.loop(4, descend_back, "back")

        def up_gradient(i):
            b, half = i // 2, lax.rem(i, 2)
            value = tn(mlp_in[:, block(half, 512)], flat(hidden_grad[b]))
            up_grad[b, pl.ds(half * 2, 2)] = value.astype(BF).reshape(2, 2, 128, 1024)

        self.loop(4, up_gradient, "upper")
        self.load(4, self.held_a, self.buf_a).start()
        up.start()

        def residual(i):
            rows = block(i, 256)
            dy = back.take(i)
            normal, scale = normalise(mid[rows, :])
            stats[2:3, :] += column_sum(dy)
            stats[3:4, :] += column_sum(dy * normal)
            dn = dy * (1.0 + vectors[4:5, :])
            dn = dn - jnp.mean(dn, -1, keepdims=True) - normal * jnp.mean(dn * normal, -1, keepdims=True)
            total = grad[rows, :].astype(F32) + scale * dn
            mid[rows, :] = total
            stats[4:5, :] += column_sum(total * self.branch_one[rows, :].astype(F32))
            g = (total * vectors[2:3, :]).astype(BF)
            mlp_in[rows, :] = g
            mine_too = jnp.where(i // 2 == c, 1.0, 0.0)
            stats[5:6, :] += column_sum(g.astype(F32)) * mine_too

        self.loop(4, residual, "rest")

    def attend_back(self):
        z, y, c, x = place()
        vectors, stats, down, up = self.vectors, self.stats, self.down, self.up
        near, far = self.near_heads, self.far_heads
        acts, g_one, heads_grad, sums = self.buf_b, self.mlp_in, self.heads_grad, self.sums
        weights = self.buf_a
        sums[...] = jnp.zeros_like(sums)
        self.load(3, self.held_b, self.buf_b).wait()
        self.load(4, self.held_a, self.buf_a).wait()

        def enter(i):
            b, half = i // 2, lax.rem(i, 2)
            value = nn(g_one[block(half, 512), :], flat(weights[b, :, :, :, 0:256]))
            heads_grad[b, block(half, 512), :] = value.astype(BF)

        self.loop(4, enter, "lift")

        def proj_gradient(i):
            b, half = i // 2, lax.rem(i, 2)
            value = tn(g_one[:, block(half, 512)], flat(acts[b, :, :, :, 0:256]))
            self.buf_d[b, pl.ds(half * 2, 2), :, :, 0:256] = value.astype(BF).reshape(2, 2, 128, 256)

        self.loop(4, proj_gradient, "proj")
        lane = lax.broadcasted_iota(jnp.int32, (1, 128), 1)

        def attend(i, k):
            b, quarter = i // 4, lax.rem(i, 4)
            rows, at_lane = block(quarter, 256), 256 + 384 * k
            queries = flat(acts[b, quarter, :, :, at_lane : at_lane + 128]) * BF(0.125)
            keys = flat(acts[b, :, :, :, at_lane + 128 : at_lane + 256])
            values = flat(acts[b, :, :, :, at_lane + 256 : at_lane + 384])
            grads = heads_grad[b, rows, k * 128 : (k + 1) * 128]

            @pl.when(quarter == 0)
            def _():
                self.key_total[...] = jnp.zeros_like(self.key_total)
                self.value_total[...] = jnp.zeros_like(self.value_total)

            result = None
            logs = self.lse[rows, :]
            for h in range(2):
                log = jnp.sum(jnp.where(lane == (k * 2 + b) * 2 + h, logs, 0.0), -1, keepdims=True)
                query = jnp.where(in_half(h), queries, jnp.zeros_like(queries))
                grad = jnp.where(in_half(h), grads, jnp.zeros_like(grads))
                probs = jnp.exp(nt(query, keys) - log)
                probs_grad = nt(grad, values)
                inner = jnp.sum(probs * probs_grad, -1, keepdims=True)
                score_grad = (probs * (probs_grad - inner)).astype(BF)
                query_grad = nn(score_grad, keys)
                result = query_grad if h == 0 else jnp.where(in_half(0), result, query_grad)
                self.key_total[...] += tn(score_grad, query)
                self.value_total[...] += tn(probs.astype(BF), grad)
            result = (result * 0.125).astype(BF)
            acts[b, quarter, :, :, at_lane : at_lane + 128] = result.reshape(2, 128, 128)
            sums[b, :, k * 128 : (k + 1) * 128] += column_sum(result.astype(F32))

            @pl.when(quarter == 3)
            def _():
                total = self.key_total[...].astype(BF)
                acts[b, :, :, :, at_lane + 128 : at_lane + 256] = total.reshape(4, 2, 128, 128)
                total = self.value_total[...].astype(BF)
                acts[b, :, :, :, at_lane + 256 : at_lane + 384] = total.reshape(4, 2, 128, 128)
                sums[b, :, 512 + k * 128 : 640 + k * 128] = column_sum(total.astype(F32))

        def qkv_gradient(i, k):
            b, half = i // 2, lax.rem(i, 2)
            lanes = slice(256 + 384 * k, 640 + 384 * k)
            value = tn(self.attn_in[:, block(half, 512)], flat(acts[b, :, :, :, lanes]))
            self.buf_d[b, pl.ds(half * 2, 2), :, :, lanes] = value.astype(BF).reshape(2, 2, 128, 384)

        self.loop(8, lambda i: attend(i, 0), "near")
        self.loop(4, lambda i: qkv_gradient(i, 0), "first")
        pl.semaphore_wait(self.free, 2)
        near.start()
        self.loop(8, lambda i: attend(i, 1), "far")
        self.loop(4, lambda i: qkv_gradient(i, 1), "second")
        far.start()
        self.do("s0")
        pair = self.pairs[3]

        def descend(i):
            partial = nt(flat(acts[0, i, :, :, 256:1024]), flat(weights[0, :, :, :, 256:1024]))
            pair.give(i, partial + nt(flat(acts[1, i, :, :, 256:1024]), flat(weights[1, :, :, :, 256:1024])))

        self.loop(4, descend, "drop")

        def leave(i):
            rows = block(i, 256)
            dy = pair.take(i)
            normal, scale = normalise(self.lat[rows, :].astype(F32))
            stats[6:7, :] += column_sum(dy)
            stats[7:8, :] += column_sum(dy * normal)
            dn = dy * (1.0 + vectors[1:2, :])
            dn = dn - jnp.mean(dn, -1, keepdims=True) - normal * jnp.mean(dn * normal, -1, keepdims=True)
            total = self.mid[rows, :] + scale * dn

            @pl.when(i // 2 == c)
            def _():
                for half in range(2):
                    for k in range(8):
                        part = total[half * 128 : (half + 1) * 128, k * 128 : (k + 1) * 128]
                        self.key_total[pl.ds(k, 128, stride=8), :] = part
                    values = self.key_total[...].astype(BF).reshape(64, 16, 128)
                    self.input_grad[block(lax.rem(i, 2) * 2 + half, 64)] = values

        self.loop(4, leave, "last")
        self.begin_end()

    def begin_end(self):
        z, y, c, x = place()
        stats, sums, up_sums = self.stats, self.sums, self.up_sums
        rows = [stats[k : k + 1, :] for k in (6, 7, 4, 2, 3, 0)]
        for j in range(6):
            for h in range(2):
                self.mods[h, j : j + 1, :] = rows[j][:, h * 512 : (h + 1) * 512]
        self.half_mods[z, y, x] = self.mods[c]
        for d in (1, 2, 3):
            self._mods(d).start()
        self.do("e0")
        columns, bias_part = self.columns, self.bias_part
        columns[...] = jnp.zeros_like(columns)
        bias_part[...] = jnp.zeros_like(bias_part)
        for b in range(2):
            spot = pl.ds(pl.multiple_of(b * 512 + c * 256, 256), 256)
            columns[0:1, spot] = sums[b, :, 0:256]
            columns[1:2, spot] = sums[b, :, 512:768]
        columns[2:3, :] = stats[5:6, :]
        columns[3:4, :] = stats[1:2, :]
        pieces = narrow(columns[0:1, :], 0) + narrow(columns[1:2, :], 1)
        pieces = pieces + narrow(columns[2:3, :], 2) + narrow(columns[3:4, :], 3)
        for k, (zz, yy, cc, xx) in enumerate(devices()):
            bias_part[cc, zz, xx, yy, 0:1, :] = pieces[k : k + 1, :]
        for b in range(2):
            for i in range(8):
                bias_part[i // 2 % 2, b * 2 + c, i % 2, i // 4, 1:2, :] = up_sums[b, :, i * 128 : (i + 1) * 128]
        self.bias = SmallScatter(
            bias_part, self.bias_c, self.bias_z, self.bias_near, self.small_send.at[0], self.small_recv.at[3]
        )
        self.bias.start()
        self.do("e1")
        for d in (1, 2, 3):
            self._mods(d).wait()
        self._across(lambda copy: copy.start())
        self.bias.along()
        self.do("e2")

    def _mods(self, d):
        z, y, c, x = place()
        spot = self.half_mods.at[z, y, x]
        return remote(
            spot, spot, self.small_send.at[2, d], self.small_recv.at[2, d], at(lax.rem(z + d, 4), y, c, x)
        )

    def _across(self, act):
        z, y, c, x = place()
        spot = self.half_mods.at[:, y, x]
        copy = lambda k, to: remote(spot, spot, self.small_send.at[2, k], self.small_recv.at[2, k], to)

        @pl.when(c == x)
        def _():
            act(copy(4, at(z, 1 - y, c, x)))

        @pl.when(c != x)
        def _():
            act(copy(5, at(z, y, c, 1 - x)))
            act(copy(6, at(z, 1 - y, c, 1 - x)))

    def end(self):
        z, y, c, x = place()
        up, near, far, mods, bias = self.up, self.near_heads, self.far_heads, self.all_mods, self.bias
        send, recv = self.small_send, self.small_recv
        spot = self.half_mods.at[:, y, x]

        @pl.when(c == x)
        def _():
            remote(spot, spot, send.at[2, 4], recv.at[2, 4], at(z, 1 - y, c, x)).wait()
            remote(spot, spot, send.at[2, 5], recv.at[2, 5], at(z, y, c, 1 - x)).wait_recv()
            remote(spot, spot, send.at[2, 6], recv.at[2, 6], at(z, 1 - y, c, 1 - x)).wait_recv()
            share = remote(self.half_mods, mods, send.at[2, 7], recv.at[2, 7], at(z, y, 1 - c, x))
            share.start()
            keep = self.load(5, self.half_mods, mods)
            keep.start()
            keep.wait()
            share.wait_send()

        @pl.when(c != x)
        def _():
            remote(spot, spot, send.at[2, 5], recv.at[2, 5], at(z, y, c, 1 - x)).wait_send()
            remote(spot, spot, send.at[2, 6], recv.at[2, 6], at(z, 1 - y, c, 1 - x)).wait_send()
            remote(self.half_mods, mods, send.at[2, 7], recv.at[2, 7], at(z, y, 1 - c, x)).wait_recv()

        bias.across()
        self.do("e3")
        silu_rows = self.silu[...].astype(BF)
        total = jnp.zeros((16, 128), F32)
        bias_rows = []
        for j in range(6):
            values = jnp.concatenate([mods[b // 4, b // 2 % 2, b % 2, j : j + 1, :] for b in range(16)], 0)
            high, low = split_bf(values)
            weights = self.wide[:, j * 512 : (j + 1) * 512]
            self.tall[...] = tn(silu_rows, high) + tn(silu_rows, low)
            self.ada_out[j] = self.tall[block(c, 64), :]
            total = total + nt(high, weights) + nt(low, weights)
            bias_rows.append(column_sum(values))
        found, found_c, found_z, found_near = self.found, self.found_c, self.found_z, self.found_near
        for b in range(16):
            found[b % 2, b // 4, b // 2 % 2] = total[b : b + 1, :]
        core = remote(found.at[1 - c], found_c, send.at[3, 0], recv.at[1, 0], at(z, y, 1 - c, x))
        core.start()
        self.do("e4")
        group = (lax.rem(z, 2) * 2 + y) * 2 + c
        source = lax.broadcasted_iota(jnp.int32, (512, 128), 0)
        target = lax.broadcasted_iota(jnp.int32, (512, 128), 1)
        chosen = jnp.where((source == group * 64 + target) & (target < 64), 1.0, 0.0).astype(BF)
        self.picked[...] = exact_nn(jnp.concatenate(bias_rows + [jnp.zeros((2, 512), F32)], 0), chosen)
        swap = remote(self.picked, self.picked_other, send.at[3, 7], recv.at[1, 7], at(z, y, c, 1 - x))
        swap.start()
        self.do("e5")
        core.wait()
        found_c[...] = found_c[...] + found[c]
        along = []
        for k in (1, 2, 3):
            to = lax.rem(z + k, 4)
            along.append(remote(found_c.at[to], found_z.at[z], send.at[3, k], recv.at[1, k], at(to, y, c, x)))
            along[-1].start()
        found_z[z] = found_c[z]
        self.do("e6")
        for copy in along:
            copy.wait()
        across = []
        for k, (to_y, to_x) in enumerate(((y, 1 - x), (1 - y, x), (1 - y, 1 - x))):
            across.append(
                remote(found_z.at[:, to_y], found_near.at[k], send.at[3, 4 + k], recv.at[1, 4 + k], at(z, to_y, c, to_x))
            )
            across[-1].start()
        self.do("e7")
        for copy in across:
            copy.wait()
        swap.wait()
        self.small_out[...] = jnp.zeros_like(self.small_out)
        self.small_out[4:6, :] = bias.finish()
        picked = jnp.where(z // 2 == x, self.picked[...], self.picked_other[...])
        self.small_out[8:16, 0:32] = jnp.where(x == 0, picked[:, 0:32], picked[:, 32:64])
        same, other = found_z[:, y] + found_near[0], found_near[1] + found_near[2]
        rows = [jnp.where(y == b % 2, same[b // 2], other[b // 2]) for b in range(8)]
        v = self.cond[...].astype(F32)
        v = jnp.concatenate([v[:, k * 128 : (k + 1) * 128] for k in range(8)], 0)
        gate = 1.0 / (1.0 + jnp.exp(-v))
        row = jnp.concatenate(rows, 0) * gate * (1.0 + v * (1.0 - gate))
        self.small_out[0:4, :] = jnp.where(x == 0, row[0:4], row[4:8])
        self.do("e8")
        near.finish()
        self.swap_block.finish()
        self.swap_input.finish()
        far.finish()


def on_device_pairs(
    latents_in,
    condition,
    grad_out,
    qkv_weight,
    proj_weight,
    up_weight,
    down_weight,
    ada_weight,
    query_bias,
    value_bias,
    proj_bias,
    up_bias,
    down_bias,
    ada_bias,
):
    small = [b.reshape(1, -1) for b in (query_bias, value_bias, proj_bias, down_bias, up_bias)]
    out = lambda *shape: jax.ShapeDtypeStruct(shape, F32)
    group = jax.ShapeDtypeStruct(GROUP, BF)
    rows = jax.ShapeDtypeStruct((512, 1024), BF)
    results = pl.pallas_call(
        pairs_kernel,
        out_shape=[rows, jax.ShapeDtypeStruct((256, 16, 128), BF), out(3, 64, 512), out(64, 512), out(64, 2048), out(64, 2048)]
        + [group] * 2
        + [out(6, 64, 512), out(16, 128)],
        in_specs=[IN_ANY] * 7 + [IN_VMEM] * 7,
        out_specs=[IN_ANY] * 8 + [IN_VMEM] * 2,
        scratch_shapes=list(scratch().values()),
        compiler_params=pltpu.CompilerParams(
            collective_id=0, has_side_effects=True, vmem_limit_bytes=63 * MIB + MIB // 2
        ),
        name="dit_block",
    )(
        latents_in.reshape(512, 1024), grad_out.reshape(512, 1024), qkv_weight.transpose(1, 0, 2), proj_weight.T,
        up_weight, down_weight.T, ada_weight.transpose(1, 0, 2), condition, *small, ada_bias,
    )
    block_mine, input_mine, q_out, p_out, u_out, d_out, _, _, ada_out, small_out = results
    return (
        block_mine.reshape(512, 1, 1024),
        input_mine.astype(F32).reshape(512, 1, 1024),
        small_out[0:4].reshape(1, 512),
        q_out.transpose(1, 0, 2),
        p_out.T,
        u_out,
        d_out.T,
        ada_out.transpose(1, 0, 2),
        small_out[4, 0:32],
        small_out[4, 32:64],
        small_out[4, 64:96],
        small_out[5],
        small_out[4, 96:128],
        small_out[8:14, 0:32],
    )


def solution(mesh):
    shape = dict(mesh.shape)
    pairs = shape["fsdp"] == 16 and shape["tp"] == 2
    return jax.shard_map(
        on_device_pairs if pairs else on_device_general,
        mesh=mesh,
        in_specs=(
            P("tp", "fsdp", None),
            P("fsdp", None),
            P("tp", "fsdp", None),
            P("fsdp", None, "tp"),
            P("tp", "fsdp"),
            P("fsdp", "tp"),
            P("tp", "fsdp"),
            P("fsdp", None, "tp"),
            P(("fsdp", "tp")),
            P(("fsdp", "tp")),
            P(("fsdp", "tp")),
            P(("fsdp", "tp")),
            P(("fsdp", "tp")),
            P(None, ("fsdp", "tp")),
        ),
        out_specs=(
            P("tp", "fsdp", None),
            P("tp", "fsdp", None),
            P("fsdp", "tp"),
            P("fsdp", None, "tp"),
            P("tp", "fsdp"),
            P("fsdp", "tp"),
            P("tp", "fsdp"),
            P("fsdp", None, "tp"),
            P(("fsdp", "tp")),
            P(("fsdp", "tp")),
            P(("fsdp", "tp")),
            P(("fsdp", "tp")),
            P(("fsdp", "tp")),
            P(None, ("fsdp", "tp")),
        ),
        check_vma=False,
    )
```

```python
import functools
import math

import jax
import jax.numpy as jnp
from jax import lax
from jax.experimental import pallas as pl
from jax.experimental.pallas import tpu as pltpu
from jax.sharding import PartitionSpec as P


HD = 64


epsilon = 1e-06


def layer_norm(values):
    centred = values - jnp.mean(values, axis=-1, keepdims=True)
    return centred * lax.rsqrt(jnp.mean(centred * centred, axis=-1, keepdims=True) + epsilon)


def modulate(values, shift_part, scale_part):
    return layer_norm(values) * (1.0 + scale_part) + shift_part


def gelu_tanh(values):
    return jax.nn.gelu(values, approximate=True)


def gather_rows(piece):
    return lax.all_gather(piece, "tp", axis=0, tiled=True)


def gather_grads(piece):
    return lax.all_gather(piece, "tp", axis=0, tiled=True)


def scatter_rows(product, row_count):
    return lax.psum_scatter(
        product(jnp.int32(0), row_count * lax.axis_size("tp")).astype(jnp.bfloat16),
        "tp",
        scatter_dimension=0,
        tiled=True,
    ).astype(jnp.float32)


def scatter_grads(product, row_count):
    return lax.psum_scatter(
        product(jnp.int32(0), row_count * lax.axis_size("tp")).astype(jnp.bfloat16),
        "tp",
        scatter_dimension=0,
        tiled=True,
    ).astype(jnp.float32)


def split_heads(packed):
    head_count = packed.shape[3] // HD
    shaped = packed.reshape(packed.shape[0], packed.shape[1], 3, head_count, HD)
    return (shaped[:, :, 0], shaped[:, :, 1], shaped[:, :, 2])


def attend_forward(packed):
    length, latents, local_width = (packed.shape[0], packed.shape[1], packed.shape[3])
    queries, key_rows, value_rows = split_heads(packed)
    block_rows = min(512, length)
    score_scale = 1.0 / math.sqrt(HD)
    blocks = queries.reshape(length // block_rows, block_rows, latents, local_width // HD, HD)

    def one_block(q_rows):
        scores = (
            jnp.einsum("qbhd,kbhd->bhqk", q_rows, key_rows, preferred_element_type=jnp.float32)
            * score_scale
        )
        largest = jnp.max(scores, axis=-1, keepdims=True)
        exponent = jnp.exp(scores - largest)
        summed = jnp.sum(exponent, axis=-1, keepdims=True)
        weights_soft = (exponent / summed).astype(jnp.bfloat16)
        mixture = jnp.einsum(
            "bhqk,kbhd->qbhd", weights_soft, value_rows, preferred_element_type=jnp.float32
        )
        return (mixture.astype(jnp.bfloat16), largest[..., 0] + jnp.log(summed[..., 0]))

    mixture_all, log_sums = lax.map(one_block, blocks)
    return (mixture_all.reshape(length, latents, local_width), log_sums)


def attend_backward(packed, log_sums, heads_grad):
    length, latents, local_width = (packed.shape[0], packed.shape[1], packed.shape[3])
    head_count = local_width // HD
    queries, key_rows, value_rows = split_heads(packed)
    block_rows = min(512, length)
    count_blocks = length // block_rows
    score_scale = 1.0 / math.sqrt(HD)
    q_blocks = queries.reshape(count_blocks, block_rows, latents, head_count, HD)
    g_blocks = heads_grad.reshape(count_blocks, block_rows, latents, head_count, HD)

    def one_block(carried, inputs):
        key_grad, value_grad = carried
        q_rows, g_rows, log_rows = inputs
        scores = (
            jnp.einsum("qbhd,kbhd->bhqk", q_rows, key_rows, preferred_element_type=jnp.float32)
            * score_scale
        )
        weights_soft = jnp.exp(scores - log_rows[..., None])
        soft_grad = jnp.einsum(
            "qbhd,kbhd->bhqk", g_rows, value_rows, preferred_element_type=jnp.float32
        )
        inner_sum = jnp.sum(weights_soft * soft_grad, axis=-1, keepdims=True)
        score_grad = (weights_soft * (soft_grad - inner_sum)).astype(jnp.bfloat16)
        query_grad = (
            jnp.einsum("bhqk,kbhd->qbhd", score_grad, key_rows, preferred_element_type=jnp.float32)
            * score_scale
        )
        key_grad = (
            key_grad
            + jnp.einsum("bhqk,qbhd->kbhd", score_grad, q_rows, preferred_element_type=jnp.float32)
            * score_scale
        )
        value_grad = value_grad + jnp.einsum(
            "bhqk,qbhd->kbhd",
            weights_soft.astype(jnp.bfloat16),
            g_rows,
            preferred_element_type=jnp.float32,
        )
        return ((key_grad, value_grad), query_grad)

    zero_rows = jnp.zeros((length, latents, head_count, HD), jnp.float32)
    (key_grad, value_grad), query_grad = lax.scan(
        one_block, (zero_rows, zero_rows), (q_blocks, g_blocks, log_sums)
    )
    stacked = jnp.stack(
        [
            query_grad.reshape(length, latents, local_width),
            key_grad.reshape(length, latents, local_width),
            value_grad.reshape(length, latents, local_width),
        ],
        axis=2,
    )
    return stacked.astype(jnp.bfloat16)


def on_device_general(
    latents_in,
    condition,
    grad_out,
    qkv_weight,
    proj_weight,
    up_weight,
    down_weight,
    ada_weight,
    query_bias,
    value_bias,
    proj_bias,
    up_bias,
    down_bias,
    ada_bias,
):
    tp_index = lax.axis_index("tp")
    local_rows = latents_in.shape[0]
    local_width = qkv_weight.shape[2]
    local_hidden = up_weight.shape[1]
    model_width = latents_in.shape[2]
    width_start = tp_index * local_width
    hidden_start = tp_index * local_hidden
    full_qkv, full_proj, full_up, full_down, full_ada = (
        lax.all_gather(qkv_weight, "fsdp", axis=0, tiled=True),
        lax.all_gather(proj_weight, "fsdp", axis=1, tiled=True),
        lax.all_gather(up_weight, "fsdp", axis=0, tiled=True),
        lax.all_gather(down_weight, "fsdp", axis=1, tiled=True),
        lax.all_gather(ada_weight, "fsdp", axis=0, tiled=True),
    )
    bias_list = (
        lax.all_gather(query_bias, ("fsdp", "tp"), axis=0, tiled=True),
        lax.all_gather(value_bias, ("fsdp", "tp"), axis=0, tiled=True),
        lax.all_gather(proj_bias, ("fsdp", "tp"), axis=0, tiled=True),
        lax.all_gather(up_bias, ("fsdp", "tp"), axis=0, tiled=True),
        lax.all_gather(down_bias, ("fsdp", "tp"), axis=0, tiled=True),
        lax.all_gather(ada_bias, ("fsdp", "tp"), axis=1, tiled=True),
    )
    all_query, all_value, all_proj, all_up, all_down, all_ada = [
        item_bias.astype(jnp.float32) for item_bias in bias_list
    ]
    hidden_total = all_up.shape[0]
    cond_float = condition.astype(jnp.float32)
    silu_cond = jax.nn.silu(cond_float).astype(jnp.bfloat16)
    ada_cols = lax.dynamic_slice_in_dim(all_ada, width_start, local_width, 1)
    mod_part = (
        jnp.einsum("bc,ctf->btf", silu_cond, full_ada, preferred_element_type=jnp.float32)
        + ada_cols
    )
    modulation = lax.all_gather(mod_part, "tp", axis=2, tiled=True)
    shift_one, scale_one, gate_one = (modulation[:, 0], modulation[:, 1], modulation[:, 2])
    shift_two, scale_two, gate_two = (modulation[:, 3], modulation[:, 4], modulation[:, 5])
    input_float = latents_in.astype(jnp.float32)
    attn_in = modulate(input_float, shift_one, scale_one).astype(jnp.bfloat16)
    attn_full = gather_rows(attn_in)
    query_cols = lax.dynamic_slice_in_dim(all_query, width_start, local_width, 0)
    value_cols = lax.dynamic_slice_in_dim(all_value, width_start, local_width, 0)
    bias_three = jnp.stack([query_cols, jnp.zeros_like(query_cols), value_cols])
    packed = (
        jnp.einsum("sbd,dtf->sbtf", attn_full, full_qkv, preferred_element_type=jnp.float32)
        + bias_three
    ).astype(jnp.bfloat16)
    heads_out, log_sums = attend_forward(packed)

    def project_heads(first_row, row_count):
        return jnp.einsum("sbf,fd->sbd", heads_out, full_proj, preferred_element_type=jnp.float32)

    branch_one = scatter_rows(project_heads, local_rows) + all_proj
    middle = input_float + gate_one * branch_one
    mlp_in = modulate(middle, shift_two, scale_two).astype(jnp.bfloat16)
    mlp_full = gather_rows(mlp_in)
    up_cols = lax.dynamic_slice_in_dim(all_up, hidden_start, local_hidden, 0)
    hidden = (
        jnp.einsum("sbd,df->sbf", mlp_full, full_up, preferred_element_type=jnp.float32) + up_cols
    )
    active = gelu_tanh(hidden).astype(jnp.bfloat16)

    def project_hidden(first_row, row_count):
        return jnp.einsum("sbf,fd->sbd", active, full_down, preferred_element_type=jnp.float32)

    branch_two = scatter_rows(project_hidden, local_rows) + all_down
    block_out = (middle + gate_two * branch_two).astype(jnp.bfloat16)
    grad_float = grad_out.astype(jnp.float32)
    gate_two_grad = jnp.sum(grad_float * branch_two, axis=0)
    branch_two_grad = (grad_float * gate_two).astype(jnp.bfloat16)
    down_bias_part = jnp.sum(branch_two_grad.astype(jnp.float32), axis=(0, 1))
    _, gelu_pull = jax.vjp(gelu_tanh, hidden)
    branch_two_full = gather_grads(branch_two_grad)
    active_grad = jnp.einsum(
        "sbd,fd->sbf", branch_two_full, full_down, preferred_element_type=jnp.float32
    )
    down_grad = jnp.einsum(
        "sbf,sbd->fd", active, branch_two_full, preferred_element_type=jnp.float32
    )
    hidden_grad = gelu_pull(active_grad)[0].astype(jnp.bfloat16)
    up_grad = jnp.einsum("sbd,sbf->df", mlp_full, hidden_grad, preferred_element_type=jnp.float32)
    up_bias_part = lax.dynamic_update_slice(
        jnp.zeros((hidden_total,), jnp.float32),
        jnp.sum(hidden_grad.astype(jnp.float32), axis=(0, 1)),
        (hidden_start,),
    )

    def back_hidden(first_row, row_count):
        return jnp.einsum("sbf,df->sbd", hidden_grad, full_up, preferred_element_type=jnp.float32)

    mlp_in_grad = scatter_grads(back_hidden, local_rows)
    _, second_pull = jax.vjp(modulate, middle, shift_two, scale_two)
    middle_part, shift_two_grad, scale_two_grad = second_pull(mlp_in_grad)
    middle_grad = grad_float + middle_part
    gate_one_grad = jnp.sum(middle_grad * branch_one, axis=0)
    branch_one_grad = (middle_grad * gate_one).astype(jnp.bfloat16)
    proj_bias_part = jnp.sum(branch_one_grad.astype(jnp.float32), axis=(0, 1))
    branch_one_full = gather_grads(branch_one_grad)
    heads_grad = jnp.einsum(
        "sbd,fd->sbf", branch_one_full, full_proj, preferred_element_type=jnp.float32
    ).astype(jnp.bfloat16)
    proj_grad = jnp.einsum(
        "sbf,sbd->fd", heads_out, branch_one_full, preferred_element_type=jnp.float32
    )
    packed_grad = attend_backward(packed, log_sums, heads_grad)
    qkv_grad = jnp.einsum(
        "sbd,sbtf->dtf", attn_full, packed_grad, preferred_element_type=jnp.float32
    )
    packed_sums = jnp.sum(packed_grad.astype(jnp.float32), axis=(0, 1))
    zero_width = jnp.zeros((model_width,), jnp.float32)
    query_bias_part = lax.dynamic_update_slice(zero_width, packed_sums[0], (width_start,))
    value_bias_part = lax.dynamic_update_slice(zero_width, packed_sums[2], (width_start,))

    def back_packed(first_row, row_count):
        return jnp.einsum(
            "sbtf,dtf->sbd", packed_grad, full_qkv, preferred_element_type=jnp.float32
        )

    attn_in_grad = scatter_grads(back_packed, local_rows)
    _, first_pull = jax.vjp(modulate, input_float, shift_one, scale_one)
    input_part, shift_one_grad, scale_one_grad = first_pull(attn_in_grad)
    input_grad = middle_grad + input_part
    mod_grad = jnp.stack(
        [
            shift_one_grad,
            scale_one_grad,
            gate_one_grad,
            shift_two_grad,
            scale_two_grad,
            gate_two_grad,
        ],
        axis=1,
    )
    mod_cols_grad = lax.psum_scatter(
        mod_grad.astype(jnp.bfloat16), "tp", scatter_dimension=2, tiled=True
    ).astype(jnp.float32)
    ada_grad = jnp.einsum(
        "bc,btf->ctf", silu_cond.astype(jnp.float32), mod_cols_grad, precision=lax.Precision.HIGHEST
    )
    ada_bias_part = lax.dynamic_update_slice(
        jnp.zeros((6, model_width), jnp.float32), jnp.sum(mod_cols_grad, axis=0), (0, width_start)
    )
    silu_grad = jnp.einsum(
        "btf,ctf->bc", mod_cols_grad, full_ada.astype(jnp.float32), precision=lax.Precision.HIGHEST
    )
    silu_cols = lax.psum_scatter(silu_grad, "tp", scatter_dimension=1, tiled=True)
    cond_width = silu_cols.shape[1]
    cond_cols = lax.dynamic_slice_in_dim(cond_float, tp_index * cond_width, cond_width, 1)
    _, silu_pull = jax.vjp(jax.nn.silu, cond_cols)
    cond_grad = silu_pull(silu_cols)[0]
    qkv_sum, proj_sum, up_sum, down_sum, ada_sum = (
        lax.psum_scatter(
            qkv_grad.astype(jnp.bfloat16), "fsdp", scatter_dimension=0, tiled=True
        ).astype(jnp.float32),
        lax.psum_scatter(
            proj_grad.astype(jnp.bfloat16), "fsdp", scatter_dimension=1, tiled=True
        ).astype(jnp.float32),
        lax.psum_scatter(
            up_grad.astype(jnp.bfloat16), "fsdp", scatter_dimension=0, tiled=True
        ).astype(jnp.float32),
        lax.psum_scatter(
            down_grad.astype(jnp.bfloat16), "fsdp", scatter_dimension=1, tiled=True
        ).astype(jnp.float32),
        lax.psum_scatter(
            ada_grad.astype(jnp.bfloat16), "fsdp", scatter_dimension=0, tiled=True
        ).astype(jnp.float32),
    )
    query_sum, value_sum, proj_bias_sum, up_bias_sum, down_bias_sum, ada_bias_sum = (
        lax.psum_scatter(query_bias_part, ("fsdp", "tp"), scatter_dimension=0, tiled=True),
        lax.psum_scatter(value_bias_part, ("fsdp", "tp"), scatter_dimension=0, tiled=True),
        lax.psum_scatter(proj_bias_part, ("fsdp", "tp"), scatter_dimension=0, tiled=True),
        lax.psum_scatter(up_bias_part, ("fsdp", "tp"), scatter_dimension=0, tiled=True),
        lax.psum_scatter(down_bias_part, ("fsdp", "tp"), scatter_dimension=0, tiled=True),
        lax.psum_scatter(ada_bias_part, ("fsdp", "tp"), scatter_dimension=1, tiled=True),
    )
    return (
        block_out,
        input_grad,
        cond_grad,
        qkv_sum,
        proj_sum,
        up_sum,
        down_sum,
        ada_sum,
        query_sum,
        value_sum,
        proj_bias_sum,
        up_bias_sum,
        down_bias_sum,
        ada_bias_sum,
    )


MESH = pl.DeviceIdType.MESH
ANY = pl.ANY
BF = jnp.bfloat16
F32 = jnp.float32
MIB = 2**20
IN_VMEM = pl.BlockSpec(memory_space=pltpu.VMEM)
IN_ANY = pl.BlockSpec(memory_space=ANY)
ROWS = dict(q=[80, 48, 0], p=[64, 48, 16], u=[48, 48, 32], d=[48, 48, 32])
ROWS.update(down=[64, 48, 16], up=[64, 48, 16], near=[64, 48, 16], far=[64, 48, 16])
MOST_A, MOST_B = 64, 48


def cut(rows):
    a, b, w = rows
    return pl.ds(0, a), pl.ds(a, b), pl.ds(a + b, w), pl.ds(0, a + b)


def place():
    f, x = lax.axis_index("fsdp"), lax.axis_index("tp")
    z, y, c = f // 4, lax.rem(f // 2, 2), lax.rem(f, 2)
    return z, y, c, x


def at(z, y, c, x):
    return ((z * 2 + y) * 2 + c, x)


def block(index, size):
    return pl.ds(pl.multiple_of(index * size, size), size)


def remote(src, dst, send, recv, device):
    return pltpu.make_async_remote_copy(
        src_ref=src, dst_ref=dst, send_sem=send, recv_sem=recv, device_id=device, device_id_type=MESH
    )


def loop(count, body, ticks=None):
    def step(i, carry):
        body(i)
        for k, tick in (ticks or {}).items():

            @pl.when(i == k)
            def _(tick=tick):
                tick()

        return carry

    lax.fori_loop(0, count, step, 0)


def greet(devices):
    barrier = pltpu.get_barrier_semaphore()
    for device in devices:
        pl.semaphore_signal(barrier, inc=1, device_id=device, device_id_type=MESH)
    pl.semaphore_wait(barrier, len(devices))


def partners():
    z, y, c, x = place()
    out = [at(z, y, 1 - c, x), at(z, 1 - y, c, x), at(z, y, c, 1 - x), at(z, y, 1 - c, 1 - x)]
    out += [at(z, 1 - y, c, 1 - x), at(z, 1 - y, 1 - c, 1 - x)]
    return out + [at(lax.rem(z + d, 4), y, c, x) for d in (1, 2, 3)]


class Gather:
    def __init__(self, own, full, lanes, rows, send, recv, local):
        self.own, self.full, self.lanes, self.rows = own, full, pl.ds(*lanes), rows
        self.send, self.recv, self.local = send, recv, local

    def _core(self):
        z, y, c, x = place()
        copies = []
        for i, ((near, first, width), (far, _, _)) in enumerate(zip(self.own(c), self.own(1 - c))):
            spot = self.full.at[x, z, y, block(c, 64), pl.ds(first, width)]
            copies.append(pltpu.make_async_copy(near, spot, self.local.at[i]))
            copies.append(remote(far, spot, self.send.at[i], self.recv.at[i], at(z, y, 1 - c, x)))
        return copies

    def _copy(self, kind, d):
        z, y, c, x = place()
        a, b, w, first = cut(self.rows)
        from_z = lax.rem(z - d + 4, 4)
        to_x, to_y, to_z = at(z, y, c, 1 - x), at(z, 1 - y, c, x), at(lax.rem(z + d, 4), y, c, x)
        if kind == 0:
            spot, to = self.full.at[x, z, y, first, self.lanes], to_z
        elif kind == 1:
            spot, to = self.full.at[x, from_z, y, a, self.lanes], to_x
        elif kind == 2:
            spot, to = self.full.at[x, from_z, y, b, self.lanes], to_y
        elif kind == 3:
            spot, to = self.full.at[:, from_z, y, a, self.lanes], to_y
        elif kind == 4:
            spot, to = self.full.at[x, from_z, :, b, self.lanes], to_x
        elif kind == 5:
            spot, to = self.full.at[:, z, :, w, self.lanes], to_z
        elif d == 0:
            spot, to = self.full.at[x, z, y, w, self.lanes], to_x
        else:
            spot, to = self.full.at[:, z, y, w, self.lanes], to_y
        return remote(spot, spot, self.send.at[8 + 4 * kind + d], self.recv.at[8 + 4 * kind + d], to)

    def start_core(self):
        for copy in self._core():
            copy.start()

    def enter(self, along=(2, 1, 3)):
        for copy in self._core():
            copy.wait()
        self.pass_on(along)

    def pass_on(self, along):
        for d in along:
            self._copy(0, d).start()

    def first(self):
        if self.rows[2]:
            self._copy(6, 0).start()
        self._copy(1, 0).start()
        self._copy(2, 0).start()

    def arrived(self, d):
        self._copy(0, d).wait()
        self._copy(1, d).start()
        self._copy(2, d).start()

    def turn(self, d):
        if self.rows[2] and d == 0:
            self._copy(6, 0).wait()
            self._copy(6, 1).start()
        self._copy(1, d).wait()
        self._copy(3, d).start()
        self._copy(2, d).wait()
        self._copy(4, d).start()

    def spread(self):
        self._copy(6, 1).wait()
        for k in (2, 1, 3):
            self._copy(5, k).start()

    def finish(self):
        for d in range(4):
            self._copy(3, d).wait()
            self._copy(4, d).wait()
        if self.rows[2]:
            for d in (2, 1, 3):
                self._copy(5, d).wait()


class Scatter:
    def __init__(
        self, part, first_a, first_b, second, third, wide_z, wide_y, wide_x, total, lanes, rows, out, send, recv
    ):
        self.rows = rows
        self.part, self.first_a, self.first_b = part, first_a, first_b
        self.wide_z, self.wide_y, self.wide_x = wide_z, wide_y, wide_x
        self.second, self.third, self.total, self.out = second, third, total, out
        self.lanes, self.send, self.recv = pl.ds(*lanes), send, recv

    def _copy(self, kind, d):
        z, y, c, x = place()
        n, to_z = self.lanes, lax.rem(z + d, 4)
        a, b, w, first = cut(self.rows)
        na, nb, nw = [pl.ds(0, count) for count in self.rows]
        send, recv = self.send.at[4 * kind + d], self.recv.at[4 * kind + d]
        to_x, to_y = at(z, y, c, 1 - x), at(z, 1 - y, c, x)
        if kind == 0:
            return remote(self.part.at[:, to_z, 1 - y, a, n], self.first_a.at[to_z, :, na, n], send, recv, to_y)
        if kind == 1:
            return remote(self.part.at[1 - x, to_z, :, b, n], self.first_b.at[to_z, :, nb, n], send, recv, to_x)
        if kind == 2:
            return remote(self.first_a.at[to_z, 1 - x, na, n], self.second.at[to_z, a, n], send, recv, to_x)
        if kind == 3:
            return remote(self.first_b.at[to_z, 1 - y, nb, n], self.second.at[to_z, b, n], send, recv, to_y)
        if kind == 4:
            return remote(
                self.second.at[to_z, first, n], self.third.at[d - 1, first, n], send, recv, at(to_z, y, c, x)
            )
        if kind == 5:
            return remote(
                self.part.at[:, to_z, :, w, n], self.wide_z.at[d - 1, :, :, nw, n], send, recv, at(to_z, y, c, x)
            )
        if d == 0:
            return remote(self.wide_z.at[0, :, 1 - y, nw, n], self.wide_y.at[:, nw, n], send, recv, to_y)
        return remote(self.wide_y.at[1 - x, nw, n], self.wide_x.at[nw, n], send, recv, to_x)

    def _core(self):
        z, y, c, x = place()
        copies = []
        for i, (target, first, width) in enumerate(self.out(c)):
            lanes = pl.ds(first, width)
            copies.append(
                remote(
                    self.total.at[block(1 - c, 64), lanes], target, self.send.at[28 + i], self.recv.at[28 + i],
                    at(z, y, 1 - c, x),
                )
            )
            copies.append(pltpu.make_async_copy(self.total.at[block(c, 64), lanes], target, self.send.at[32 + i]))
        return copies

    def _start(self, d):
        self._copy(0, d).start()
        self._copy(1, d).start()

    def start(self):
        for d in (2, 1, 3):
            self._copy(5, d).start()
        for d in (2, 1, 3, 0):
            self._start(d)

    def turn(self, d):
        z, y, c, x = place()
        to_z, n = lax.rem(z + d, 4), self.lanes
        a, b, _, _ = cut(self.rows)
        na, nb, _ = [pl.ds(0, count) for count in self.rows]
        self._copy(0, d).wait()
        for k in range(2):
            total = self.first_a[to_z, k, na, n].astype(F32) + self.part[k, to_z, y, a, n].astype(F32)
            self.first_a[to_z, k, na, n] = total.astype(BF)
        self._copy(2, d).start()
        self._copy(1, d).wait()
        for k in range(2):
            total = self.first_b[to_z, k, nb, n].astype(F32) + self.part[x, to_z, k, b, n].astype(F32)
            self.first_b[to_z, k, nb, n] = total.astype(BF)
        self._copy(3, d).start()

    def fold_z(self):
        z, y, c, x = place()
        n, w, nw = self.lanes, cut(self.rows)[2], pl.ds(0, self.rows[2])
        for k in (2, 1, 3):
            self._copy(5, k).wait()
        for k in range(2):
            for j in range(2):
                total = self.part[k, z, j, w, n].astype(F32)
                for s in range(3):
                    total = total + self.wide_z[s, k, j, nw, n].astype(F32)
                self.wide_z[0, k, j, nw, n] = total.astype(BF)
        self._copy(6, 0).start()

    def fold_y(self):
        z, y, c, x = place()
        n, nw = self.lanes, pl.ds(0, self.rows[2])
        self._copy(6, 0).wait()
        for k in range(2):
            total = self.wide_y[k, nw, n].astype(F32) + self.wide_z[0, k, y, nw, n].astype(F32)
            self.wide_y[k, nw, n] = total.astype(BF)
        self._copy(6, 1).start()

    def leave(self, d):
        z, y, c, x = place()
        to_z, n = lax.rem(z + d, 4), self.lanes
        a, b, _, _ = cut(self.rows)
        na, nb, _ = [pl.ds(0, count) for count in self.rows]
        self._copy(2, d).wait()
        total = self.second[to_z, a, n].astype(F32) + self.first_a[to_z, x, na, n].astype(F32)
        self.second[to_z, a, n] = total.astype(BF)
        self._copy(3, d).wait()
        total = self.second[to_z, b, n].astype(F32) + self.first_b[to_z, y, nb, n].astype(F32)
        self.second[to_z, b, n] = total.astype(BF)
        if d:
            self._copy(4, d).start()

    def last(self):
        z, y, c, x = place()
        n, nw = self.lanes, pl.ds(0, self.rows[2])
        a, b, w, _ = cut(self.rows)
        self._copy(6, 1).wait()
        self.total[w, n] = self.wide_x[nw, n].astype(F32) + self.wide_y[x, nw, n].astype(F32)
        for d in (1, 2, 3):
            self._copy(4, d).wait()
        for rows in (a, b):
            total = self.second[z, rows, n].astype(F32)
            for d in range(3):
                total = total + self.third[d, rows, n].astype(F32)
            self.total[rows, n] = total
        for copy in self._core():
            copy.start()

    def finish(self):
        for copy in self._core():
            copy.wait()


class Swap:
    def __init__(self, own, full, send, recv, local):
        self.own, self.full, self.send, self.recv, self.local = own, full, send, recv, local

    def _both(self, act):
        z, y, c, x = place()

        @pl.when(c != x)
        def _():
            to = at(z, y, 1 - c, 1 - x)
            act(remote(self.own, self.full.at[block(1 - c, 512)], self.send.at[0], self.recv.at[0], to))

        @pl.when(c == x)
        def _():
            act(pltpu.make_async_copy(self.own, self.full.at[block(c, 512)], self.local))

    def _core(self):
        z, y, c, x = place()
        spot = self.full.at[block(c, 512)]
        return remote(spot, spot, self.send.at[1], self.recv.at[1], at(z, y, 1 - c, x))

    def start(self):
        self._both(lambda copy: copy.start())

    def share(self):
        self._both(lambda copy: copy.wait())
        self._core().start()

    def finish(self):
        self._core().wait()


class SwapBack:
    def __init__(self, full, out, send, recv, local):
        self.full, self.out, self.send, self.recv, self.local = full, out, send, recv, local

    def _both(self, act):
        z, y, c, x = place()
        rows = self.full if self.full.shape == self.out.shape else self.full.at[block(c, 512)]

        @pl.when(c != x)
        def _():
            act(remote(rows, self.out, self.send, self.recv, at(z, y, 1 - c, 1 - x)))

        @pl.when(c == x)
        def _():
            act(pltpu.make_async_copy(rows, self.out, self.local))

    def start(self):
        self._both(lambda copy: copy.start())

    def finish(self):
        self._both(lambda copy: copy.wait())


class SmallGather:
    def __init__(self, own, full, send, recv):
        self.own, self.full, self.send, self.recv = own, full, send, recv

    def _copy(self, k):
        z, y, c, x = place()
        send, recv = self.send.at[k], self.recv.at[k]
        if k == 0:
            return remote(self.own, self.full.at[x, z, y, c], send, recv, at(z, y, 1 - c, x))
        if k <= 3:
            spot = self.full.at[x, z, y]
            return remote(spot, spot, send, recv, at(lax.rem(z + k, 4), y, c, x))
        if k == 4:
            spot = self.full.at[x, :, y]
            return remote(spot, spot, send, recv, at(z, 1 - y, c, x))
        spot = self.full.at[x]
        return remote(spot, spot, send, recv, at(z, y, c, 1 - x))

    def start(self):
        z, y, c, x = place()
        self.full[x, z, y, c] = self.own[...]
        self._copy(0).start()

    def step(self, done, begin):
        for k in done:
            self._copy(k).wait()
        for k in begin:
            self._copy(k).start()


class SmallScatter:
    def __init__(self, part, near_c, near_z, near, send, recv):
        self.part, self.near_c, self.near_z, self.near = part, near_c, near_z, near
        self.send, self.recv = send, recv

    def _copy(self, k):
        z, y, c, x = place()
        send, recv = self.send.at[k], self.recv.at[k]
        if k == 0:
            return remote(self.part.at[1 - c], self.near_c, send, recv, at(z, y, 1 - c, x))
        if k <= 3:
            to = lax.rem(z + k, 4)
            return remote(self.near_c.at[to], self.near_z.at[k - 1], send, recv, at(to, y, c, x))
        to_x, to_y = ((1 - x, y), (x, 1 - y), (1 - x, 1 - y))[k - 4]
        return remote(self.near_z.at[3, to_x, to_y], self.near.at[k - 4], send, recv, at(z, to_y, c, to_x))

    def start(self):
        self._copy(0).start()

    def along(self):
        z, y, c, x = place()
        self._copy(0).wait()
        self.near_c[...] = self.near_c[...] + self.part[c]
        for k in (1, 2, 3):
            self._copy(k).start()

    def across(self):
        z, y, c, x = place()
        for k in (1, 2, 3):
            self._copy(k).wait()
        self.near_z[3] = self.near_c[z] + self.near_z[0] + self.near_z[1] + self.near_z[2]
        for k in (4, 5, 6):
            self._copy(k).start()

    def finish(self):
        z, y, c, x = place()
        for k in (4, 5, 6):
            self._copy(k).wait()
        return self.near_z[3, x, y] + self.near[0] + self.near[1] + self.near[2]


class Pair:
    def __init__(self, mine, theirs, send, recv):
        self.mine, self.theirs, self.send, self.recv = mine, theirs, send, recv

    def _copy(self, i):
        z, y, c, x = place()
        rows = block(i, 256)
        return remote(
            self.mine.at[rows], self.theirs.at[rows], self.send.at[i], self.recv.at[i], at(z, y, 1 - c, x)
        )

    def give(self, i, partial):
        self.mine[block(i, 256), :] = partial.astype(BF)
        self._copy(i).start()

    def take(self, i):
        self._copy(i).wait()
        rows = block(i, 256)
        return self.mine[rows, :].astype(F32) + self.theirs[rows, :].astype(F32)


def normalise(values):
    centred = values - jnp.mean(values, axis=-1, keepdims=True)
    scale = lax.rsqrt(jnp.mean(centred * centred, axis=-1, keepdims=True) + epsilon)
    return centred * scale, scale


def nn(a, b):
    return jnp.dot(a, b, preferred_element_type=F32)


def nt(a, b):
    return lax.dot_general(a, b, (((1,), (1,)), ((), ())), preferred_element_type=F32)


def tn(a, b):
    return lax.dot_general(a, b, (((0,), (0,)), ((), ())), preferred_element_type=F32)


def in_half(h):
    return lax.broadcasted_iota(jnp.int32, (1, 128), 1) // 64 == h


def column_sum(values):
    return jnp.sum(values, 0, keepdims=True)


def gelu_parts(v):
    k = math.sqrt(2.0 / math.pi)
    square = v * v
    t = jnp.tanh(k * v * (1.0 + 0.044715 * square))
    half = 0.5 * (1.0 + t)
    return v * half, half + 0.5 * k * v * (1.0 - t * t) * (1.0 + 3.0 * 0.044715 * square)


def split_bf(values):
    high = values.astype(BF)
    return high, (values - high.astype(F32)).astype(BF)


def exact_nn(values, chosen):
    high, low = split_bf(values)
    lower = (values - high.astype(F32) - low.astype(F32)).astype(BF)
    return nn(high, chosen) + nn(low, chosen) + nn(lower, chosen)


def devices():
    return [(zz, yy, cc, xx) for zz in range(4) for yy in range(2) for cc in range(2) for xx in range(2)]


def widen(small_full, row, k, width=1024):
    pieces = jnp.concatenate([small_full[xx, zz, yy, cc, row : row + 1, :] for zz, yy, cc, xx in devices()], 0)
    lane = lax.broadcasted_iota(jnp.int32, (128, width), 1)
    source = lax.broadcasted_iota(jnp.int32, (128, width), 0)
    pick = jnp.where(source == k * 32 + lax.rem(lane, 32), 1.0, 0.0).astype(BF)
    spread_out = nn(pieces.astype(BF), pick)
    device = lax.broadcasted_iota(jnp.int32, (32, width), 0)
    lane = lax.broadcasted_iota(jnp.int32, (32, width), 1)
    return column_sum(jnp.where(lane // 32 == device, spread_out, 0.0))


def narrow(vector, k):
    device = lax.broadcasted_iota(jnp.int32, (32, 1024), 0)
    lane = lax.broadcasted_iota(jnp.int32, (32, 1024), 1)
    source = lax.broadcasted_iota(jnp.int32, (1024, 128), 0)
    target = lax.broadcasted_iota(jnp.int32, (1024, 128), 1)
    chosen = jnp.where(target == k * 32 + lax.rem(source, 32), 1.0, 0.0).astype(BF)
    return exact_nn(jnp.where(lane // 32 == device, vector, 0.0), chosen)


def flat(value):
    return value.reshape(-1, value.shape[-1])


INPUTS = """lat_own grad_own wq wp wu wd ada cond q_bias v_bias p_bias d_bias u_bias a_bias"""
OUTPUTS = """block_mine input_mine q_out p_out u_out d_out held_a held_b
    ada_out small_out"""
GROUP = (2, 4, 2, 128, 1024)
TOKENS = (1024, 1024)


def scratch():
    v, f = (lambda *s: pltpu.VMEM(s, BF)), (lambda *s: pltpu.VMEM(s, F32))
    dma, regular = pltpu.SemaphoreType.DMA, pltpu.SemaphoreType.REGULAR
    out = dict(lat=v(*TOKENS), grad=v(*TOKENS), attn_in=v(*TOKENS), mid=f(*TOKENS), branch_one=v(*TOKENS))
    out.update(mlp_in=v(*TOKENS), g_two=v(*TOKENS), mine=v(*TOKENS), theirs_a=v(*TOKENS), theirs_b=v(*TOKENS))
    out.update(buf_a=v(*GROUP), buf_b=v(*GROUP), gu=v(*GROUP), buf_c=v(*GROUP), buf_d=v(*GROUP))
    for i in range(2):
        out[f"first_a{i}"], out[f"first_b{i}"] = v(4, 2, MOST_A, 1024), v(4, 2, MOST_B, 1024)
    for i, name in enumerate(("down", "up", "near")):
        a, b, w = ROWS[name]
        out[f"second{i}"], out[f"third{i}"] = v(4, a + b, 1024), v(3, a + b, 1024)
        out[f"wide_z{i}"], out[f"wide_y{i}"], out[f"wide_x{i}"] = v(3, 2, 2, w, 1024), v(2, w, 1024), v(w, 1024)
    out.update(total=f(128, 1024), heads_grad=v(2, 1024, 256), lse=f(1024, 128))
    out.update(key_total=f(1024, 128), value_total=f(1024, 128), input_grad=v(256, 16, 128))
    out.update(small=f(16, 128), small_full=f(2, 4, 2, 2, 16, 128), wide=v(128, 3072), silu=f(16, 128))
    out.update(part=f(2, 4, 2, 8, 512), near_c=f(4, 2, 8, 512), near_z=f(4, 2, 8, 512), near_y=f(2, 8, 512))
    out.update(mods=f(2, 8, 512), vectors=f(16, 1024), up_bias=f(1, 4096), stats=f(8, 1024), columns=f(8, 1024))
    out.update(up_sums=f(2, 1, 1024), sums=f(2, 1, 768), half_mods=f(4, 2, 2, 8, 512), all_mods=f(4, 2, 2, 8, 512), tall=f(128, 512))
    out.update(bias_part=f(2, 4, 2, 2, 2, 128), bias_c=f(4, 2, 2, 2, 128), bias_z=f(4, 2, 2, 2, 128))
    out.update(bias_near=f(3, 2, 128), found=f(2, 4, 2, 1, 128), found_c=f(4, 2, 1, 128), found_z=f(4, 2, 1, 128))
    out.update(found_near=f(3, 4, 1, 128), picked=f(8, 128), picked_other=f(8, 128))
    out.update(gather_send=dma((4, 36)), gather_recv=dma((4, 36)), gather_local=dma((4, 6)))
    out.update(scatter_send=dma((4, 36)), scatter_recv=dma((4, 36)), pair_send=dma((4, 4)), pair_recv=dma((4, 4)))
    out.update(swap_send=dma((4, 2)), swap_recv=dma((4, 2)), swap_local=dma((4,)))
    out.update(small_send=dma((4, 8)), small_recv=dma((4, 8)), load_sem=dma((12,)), free=regular)
    return out


def pairs_kernel(*refs):
    names = INPUTS.split() + OUTPUTS.split() + list(scratch())
    r = dict(zip(names, refs))
    Block(r).run()

PLAN = dict(
    b0=(("q", "enter", ()), ("q", "pass_on", (2,)),),
    b1=(("q", "first"), ("p", "enter", ()), ("u", "enter", ()), ("d", "enter", ()),),
    b3=(("q", "pass_on", (1,)), ("q", "pass_on", (3,)), ("p", "pass_on", (2,)), ("p", "pass_on", (1,)), ("p", "pass_on", (3,)), ("u", "pass_on", (2,)), ("u", "pass_on", (1,)), ("u", "pass_on", (3,)), ("q", "turn", 0),),
    b4=(("q", "arrived", 2), ("q", "arrived", 1), ("q", "arrived", 3), ("d", "pass_on", (2,)), ("d", "pass_on", (1,)), ("d", "pass_on", (3,)),),
    b5=(("q", "turn", 2), ("swap_lat", "share"),),
    b6=(("q", "turn", 1),),
    b7=(("q", "turn", 3), ("p", "first"), ("p", "arrived", 2), ("p", "arrived", 1), ("p", "arrived", 3), ("u", "first"),),
    project0=(("swap_grad", "start"),),
    project7=(("p", "turn", 0), ("p", "turn", 2), ("p", "turn", 1), ("p", "turn", 3), ("p", "spread"), ("u", "arrived", 2), ("u", "arrived", 1), ("u", "arrived", 3),),
    heads0=(("u", "turn", 0),),
    heads3=(("u", "turn", 2), ("u", "spread"),),
    heads4=(("u", "turn", 1),),
    heads5=(("u", "turn", 3),),
    heads7=(("d", "first"),),
    out3=(("d", "arrived", 2), ("d", "arrived", 1), ("d", "arrived", 3), ("swap_grad", "share"),),
    enter3=(("d", "turn", 0),),
    ascend3=(("d", "turn", 2), ("d", "spread"),),
    ascend6=(("d", "turn", 1),),
    down0=(("d", "turn", 3),),
    hidden1=(("down", "turn", 2),),
    hidden7=(("down", "turn", 1),),
    back1=(("down", "turn", 3),),
    upper0=(("down", "turn", 0),),
    upper1=(("down", "fold_z"),),
    upper2=(("down", "leave", 2),),
    rest0=(("down", "leave", 1),),
    rest1=(("down", "fold_y"),),
    rest3=(("down", "leave", 3),),
    lift3=(("down", "leave", 0), ("", "signal_free"),),
    proj3=(("swap_block", "start"),),
    near0=(("up", "turn", 2),),
    near2=(("up", "turn", 1),),
    near5=(("up", "turn", 3),),
    first0=(("up", "turn", 0), ("up", "fold_z"),),
    first3=(("up", "leave", 2), ("down", "last"),),
    far0=(("up", "leave", 1),),
    far1=(("up", "fold_y"), ("up", "leave", 3),),
    far2=(("near_heads", "turn", 2), ("up", "leave", 0),),
    far4=(("near_heads", "turn", 1),),
    far6=(("near_heads", "turn", 3),),
    far7=(("near_heads", "turn", 0), ("near_heads", "fold_z"),),
    second1=(("near_heads", "leave", 2),),
    second3=(("near_heads", "leave", 1),),
    drop1=(("near_heads", "fold_y"), ("near_heads", "leave", 3),),
    drop3=(("near_heads", "leave", 0), ("down", "finish"),),
    last0=(("far_heads", "turn", 2),),
    last2=(("far_heads", "turn", 1),),
    e0=(("swap_input", "start"), ("up", "last"),),
    e2=(("far_heads", "turn", 3),),
    e4=(("far_heads", "turn", 0), ("far_heads", "fold_z"),),
    e6=(("far_heads", "leave", 2),),
    e7=(("up", "finish"), ("far_heads", "leave", 1), ("far_heads", "fold_y"), ("near_heads", "last"),),
    e8=(("far_heads", "leave", 3), ("far_heads", "leave", 0), ("far_heads", "last"),),
)


class Block:
    def __init__(self, r):
        for name, ref in r.items():
            setattr(self, name, ref)

    def run(self):
        self.set_up()
        self.begin()
        self.attend()
        self.mlp()
        self.attend_back()
        self.end()

    def set_up(self):
        gather = lambda i, name, own, full, lanes: Gather(
            own, full, lanes, ROWS[name], self.gather_send.at[i], self.gather_recv.at[i], self.gather_local.at[i]
        )
        self.q = gather(
            0,
            "q",
            lambda h: [
                (self.wq.at[j, :, block(2 * h + k, 128)], 256 + 384 * k + 128 * j, 128)
                for k in range(2)
                for j in range(3)
            ],
            self.buf_a,
            (256, 768),
        )
        self.p = gather(1, "p", lambda h: [(self.wp.at[:, block(h, 256)], 0, 256)], self.buf_a, (0, 256))
        self.u = gather(2, "u", lambda h: [(self.wu.at[:, block(h, 1024)], 0, 1024)], self.gu, (0, 1024))
        self.d = gather(3, "d", lambda h: [(self.wd.at[:, block(h, 1024)], 0, 1024)], self.buf_b, (0, 1024))
        heads = lambda k: lambda h: [
            (self.q_out.at[j, :, block(2 * h + k, 128)], 256 + 384 * k + 128 * j, 128) for j in range(3)
        ]
        outs = (
            lambda h: [(self.d_out.at[:, block(h, 1024)], 0, 1024)],
            lambda h: [(self.u_out.at[:, block(h, 1024)], 0, 1024)],
            lambda h: heads(0)(h) + [(self.p_out.at[:, block(h, 256)], 0, 256)],
            heads(1),
        )
        firsts = ((self.first_a0, self.first_b0), (self.first_a1, self.first_b1))
        rest = (
            (self.second0, self.third0, self.wide_z0, self.wide_y0, self.wide_x0),
            (self.second1, self.third1, self.wide_z1, self.wide_y1, self.wide_x1),
            (self.second2, self.third2, self.wide_z2, self.wide_y2, self.wide_x2),
        )
        plan = (
            (self.buf_d, firsts[0], rest[0], (0, 1024), ROWS["down"]),
            (self.buf_c, firsts[1], rest[1], (0, 1024), ROWS["up"]),
            (self.buf_d, firsts[0], rest[2], (0, 640), ROWS["near"]),
            (self.buf_d, firsts[0], rest[2], (640, 384), ROWS["far"]),
        )
        self.down, self.up, self.near_heads, self.far_heads = [
            Scatter(
                part, *first, *more, self.total, lanes, rows, outs[i], self.scatter_send.at[i], self.scatter_recv.at[i]
            )
            for i, (part, first, more, lanes, rows) in enumerate(plan)
        ]
        swaps = [(self.lat_own, self.lat), (self.grad_own, self.grad)]
        self.swap_lat, self.swap_grad = [
            Swap(own, full, self.swap_send.at[i], self.swap_recv.at[i], self.swap_local.at[i])
            for i, (own, full) in enumerate(swaps)
        ]
        backs = [(self.g_two, self.block_mine), (self.input_grad, self.input_mine)]
        self.swap_block, self.swap_input = [
            SwapBack(full, out, self.swap_send.at[2 + i, 0], self.swap_recv.at[2 + i, 0], self.swap_local.at[2 + i])
            for i, (full, out) in enumerate(backs)
        ]
        self.pairs = [
            Pair(self.mine, theirs, self.pair_send.at[i], self.pair_recv.at[i])
            for i, theirs in enumerate((self.theirs_a, self.theirs_b, self.theirs_a, self.theirs_b))
        ]

    def do(self, slot):
        for owner, act, *given in PLAN.get(slot, ()):
            getattr(getattr(self, owner) if owner else self, act)(*given)

    def loop(self, count, body, name):
        loop(count, body, {i: (lambda s=name + str(i): self.do(s)) for i in range(count) if name + str(i) in PLAN})

    def signal_free(self):
        z, y, c, x = place()
        for to in (at(z, 1 - y, c, x), at(z, y, c, 1 - x)):
            pl.semaphore_signal(self.free, inc=1, device_id=to, device_id_type=MESH)

    def load(self, i, source, target):
        return pltpu.make_async_copy(source, target, self.load_sem.at[i])

    def begin(self):
        z, y, c, x = place()
        q, p, u, d = self.q, self.p, self.u, self.d
        send, recv = self.small_send, self.small_recv
        little = SmallGather(self.small, self.small_full, send.at[0], recv.at[0])
        v = self.cond[...].astype(F32)
        silu = (v / (1.0 + jnp.exp(-v))).astype(BF).astype(F32)
        self.small[...] = jnp.zeros_like(self.small)
        for k in range(8):
            self.small[k : k + 1, :] = silu[:, k * 128 : (k + 1) * 128]
        for k, bias in enumerate((self.q_bias, self.v_bias, self.p_bias, self.d_bias)):
            self.small[8:9, k * 32 : (k + 1) * 32] = bias[...].astype(F32)
        self.small[9:10, :] = self.u_bias[...].astype(F32)
        a_bias = self.a_bias[...].astype(F32)
        for j in range(6):
            self.small[10 + j // 4 : 11 + j // 4, j % 4 * 32 : j % 4 * 32 + 32] = a_bias[j : j + 1, :]
        greet(partners())
        little.start()
        q.start_core()
        for group in (p, u, d):
            group.start_core()
        self.swap_lat.start()
        self.wide[...] = jnp.zeros_like(self.wide)
        ada = [self.load(j, self.ada.at[j], self.wide.at[block(c, 64), pl.ds(j * 512, 512)]) for j in range(6)]
        for copy in ada:
            copy.start()
        little.step((0,), (1, 2, 3))
        self.do("b0")
        self.part[...] = jnp.zeros_like(self.part)
        little.step((1, 2, 3), (4,))
        self.do("b1")
        for copy in ada:
            copy.wait()
        little.step((4,), (5,))
        self.do("b2")
        row = z * 2 + y
        lhs = [self.small_full[x, b // 4, b // 2 % 2, b % 2, pl.ds(row, 1), :] for b in range(16)]
        lhs = jnp.concatenate(lhs, 0)
        self.silu[...] = lhs
        for j in range(6):
            product = nn(lhs.astype(BF), self.wide[:, j * 512 : (j + 1) * 512])
            for b in range(16):
                self.part[b % 2, b // 4, b // 2 % 2, j : j + 1, :] = product[b : b + 1, :]
        near_c, near_y, near_z = self.near_c, self.near_y, self.near_z
        first = remote(self.part.at[1 - c], near_c, send.at[1, 0], recv.at[1, 0], at(z, y, 1 - c, x))
        first.start()
        first.wait()
        near_c[...] = near_c[...] + self.part[c]
        seconds = []
        for s in (1, 2, 3):
            to = lax.rem(z + s, 4)
            seconds.append(remote(near_c.at[to], near_z.at[s - 1], send.at[1, s], recv.at[1, s], at(to, y, c, x)))
            seconds[-1].start()
        self.do("b3")
        for copy in seconds:
            copy.wait()
        near_z[3] = near_c[z] + near_z[0] + near_z[1] + near_z[2]
        self._partials(lambda copy: copy.start())
        self.do("b4")
        self._partials(lambda copy: copy.wait())
        self.mods[c] = near_y[0] + near_y[1]
        fifth = remote(self.mods.at[c], self.mods.at[c], send.at[1, 6], recv.at[1, 6], at(z, y, 1 - c, x))
        fifth.start()
        self.do("b5")
        little.step((5,), ())
        bias = [widen(self.small_full, 8, k) for k in range(4)]
        ada_bias = [widen(self.small_full, 10 + j // 4, j % 4) for j in range(6)]
        for k, (zz, yy, cc, xx) in enumerate(devices()):
            self.up_bias[:, k * 128 : (k + 1) * 128] = self.small_full[xx, zz, yy, cc, 9:10, :]
        self.do("b6")
        fifth.wait()
        for j in range(6):
            for h in range(2):
                lanes = slice(h * 512, (h + 1) * 512)
                self.vectors[j : j + 1, lanes] = self.mods[h, j : j + 1, :] + ada_bias[j][:, lanes]
        for k in range(4):
            self.vectors[6 + k : 7 + k, :] = bias[k]
        self.do("b7")
        self.swap_lat.finish()

    def _partials(self, act):
        z, y, c, x = place()
        for k, to_y in enumerate((y, 1 - y)):
            sems = self.small_send.at[1, 4 + k], self.small_recv.at[1, 4 + k]
            source, target = self.near_z.at[3, to_y], self.near_y.at[y]

            @pl.when(c != x)
            def _():
                act(remote(source, target, *sems, at(z, to_y, 1 - c, 1 - x)))

            @pl.when(c == x)
            def _():
                if k:
                    act(remote(source, target, *sems, at(z, to_y, c, x)))
                else:
                    act(pltpu.make_async_copy(source, target, self.load_sem.at[6]))

    def attend(self):
        z, y, c, x = place()
        q, p, u, d, vectors = self.q, self.p, self.u, self.d, self.vectors

        def modulated(i):
            rows = block(i, 256)
            normal, _ = normalise(self.lat[rows, :].astype(F32))
            self.attn_in[rows, :] = (normal * (1.0 + vectors[1:2, :]) + vectors[0:1, :]).astype(BF)

        self.loop(4, modulated, "normal")
        q.finish()

        def project(i):
            b, quarter = i // 4, lax.rem(i, 4)
            values = nn(self.attn_in[block(quarter, 256), :], flat(self.buf_a[b, :, :, :, 256:1024]))
            for k in range(6):
                value = values[:, k * 128 : (k + 1) * 128]
                if k % 3 != 1:
                    columns = pl.ds(pl.multiple_of(b * 512 + c * 256 + k // 3 * 128, 128), 128)
                    row = 6 if k % 3 == 0 else 7
                    value = value + vectors[row : row + 1, columns]
                self.buf_d[b, quarter, :, :, 256 + k * 128 : 384 + k * 128] = value.astype(BF).reshape(2, 128, 128)

        self.loop(8, project, "project")
        lane = lax.broadcasted_iota(jnp.int32, (1, 128), 1)
        self.lse[...] = jnp.zeros_like(self.lse)

        def attend(i):
            pair, half = i // 2, lax.rem(i, 2)
            rows, zz = block(half, 512), pl.ds(half * 2, 2)
            b, k, q_at = lax.rem(pair, 2), pair // 2, pl.multiple_of(256 + pair // 2 * 384, 128)
            queries = flat(self.buf_d[b, zz, :, :, pl.ds(q_at, 128)]) * BF(0.125)
            keys = flat(self.buf_d[b, :, :, :, pl.ds(q_at + 128, 128)])
            values = flat(self.buf_d[b, :, :, :, pl.ds(q_at + 256, 128)])
            result = None
            logs = self.lse[rows, :]
            for h in range(2):
                scores = nt(jnp.where(in_half(h), queries, jnp.zeros_like(queries)), keys)
                largest = jnp.max(scores, -1, keepdims=True)
                exponent = jnp.exp(scores - largest)
                summed = jnp.sum(exponent, -1, keepdims=True)
                mixture = nn(exponent.astype(BF), values) * (1.0 / summed)
                result = mixture if h == 0 else jnp.where(in_half(0), result, mixture)
                logs = jnp.where(lane == pair * 2 + h, largest + jnp.log(summed), logs)
            self.buf_d[b, zz, :, :, block(k, 128)] = result.astype(BF).reshape(2, 2, 128, 128)
            self.lse[rows, :] = logs

        self.loop(8, attend, "heads")
        p.finish()
        self.load(0, self.buf_a, self.held_a).start()
        pair = self.pairs[0]

        def out(i):
            zz = i
            partial = nt(flat(self.buf_d[0, zz, :, :, 0:256]), flat(self.buf_a[0, :, :, :, 0:256]))
            partial += nt(flat(self.buf_d[1, zz, :, :, 0:256]), flat(self.buf_a[1, :, :, :, 0:256]))
            pair.give(i, partial)

        self.loop(4, out, "out")
        self.load(1, self.buf_d, self.held_b).start()

        def residual(i):
            rows = block(i, 256)
            branch = pair.take(i) + vectors[8:9, :]
            self.branch_one[rows, :] = branch.astype(BF)
            self.mid[rows, :] = self.lat[rows, :].astype(F32) + vectors[2:3, :] * branch

        self.loop(4, residual, "middle")

    def mlp(self):
        z, y, c, x = place()
        u, d, vectors, stats, down, up = self.u, self.d, self.vectors, self.stats, self.down, self.up
        active, up_grad, slope, hidden_grad = self.buf_c, self.buf_c, self.buf_a, self.buf_a
        wd, gu, mid, mlp_in, g_two, grad = self.buf_b, self.gu, self.mid, self.mlp_in, self.g_two, self.grad
        self.swap_grad.finish()
        stats[...] = jnp.zeros_like(stats)
        self.up_sums[...] = jnp.zeros_like(self.up_sums)

        def enter(i):
            rows = block(i, 256)
            normal, _ = normalise(mid[rows, :])
            mlp_in[rows, :] = (normal * (1.0 + vectors[4:5, :]) + vectors[3:4, :]).astype(BF)
            g = (grad[rows, :].astype(F32) * vectors[5:6, :]).astype(BF)
            g_two[rows, :] = g
            mine_too = jnp.where(i // 2 == c, 1.0, 0.0)
            stats[1:2, :] += column_sum(g.astype(F32)) * mine_too

        self.loop(4, enter, "enter")
        u.finish()
        self.load(0, self.buf_a, self.held_a).wait()

        def ascend(i):
            b, quarter = i // 4, lax.rem(i, 4)
            columns = pl.ds(pl.multiple_of(b * 2048 + c * 1024, 1024), 1024)
            hidden = nn(mlp_in[block(quarter, 256), :], flat(gu[b])) + self.up_bias[:, columns]
            value, gradient = gelu_parts(hidden)
            active[b, quarter] = value.astype(BF).reshape(2, 128, 1024)
            slope[b, quarter] = gradient.astype(BF).reshape(2, 128, 1024)

        self.loop(8, ascend, "ascend")
        self.load(1, self.buf_d, self.held_b).wait()

        def down_gradient(i):
            b, half = i // 2, lax.rem(i, 2)
            value = tn(g_two[:, block(half, 512)], flat(active[b]))
            self.buf_d[b, pl.ds(half * 2, 2)] = value.astype(BF).reshape(2, 2, 128, 1024)

        self.loop(4, down_gradient, "down")
        down.start()
        d.finish()
        pair, back = self.pairs[1], self.pairs[2]

        def descend(i):
            pair.give(i, nt(flat(active[0, i]), flat(wd[0])) + nt(flat(active[1, i]), flat(wd[1])))

        self.loop(4, descend, "descend")

        def hidden_gradient(i):
            b, quarter = i // 4, lax.rem(i, 4)
            value = nn(g_two[block(quarter, 256), :], flat(wd[b])) * flat(slope[b, quarter]).astype(F32)
            value = value.astype(BF)
            hidden_grad[b, quarter] = value.reshape(2, 128, 1024)
            self.up_sums[b] += column_sum(value.astype(F32))

        self.loop(8, hidden_gradient, "hidden")
        self.load(3, self.held_b, self.buf_b).start()

        def leave(i):
            rows = block(i, 256)
            branch_two = pair.take(i) + vectors[9:10, :]
            g_two[rows, :] = (mid[rows, :] + vectors[5:6, :] * branch_two).astype(BF)
            stats[0:1, :] += column_sum(grad[rows, :].astype(F32) * branch_two)

        self.loop(4, leave, "leave")

        def descend_back(i):
            back.give(i, nt(flat(hidden_grad[0, i]), flat(gu[0])) + nt(flat(hidden_grad[1, i]), flat(gu[1])))

        self.loop(4, descend_back, "back")

        def up_gradient(i):
            b, half = i // 2, lax.rem(i, 2)
            value = tn(mlp_in[:, block(half, 512)], flat(hidden_grad[b]))
            up_grad[b, pl.ds(half * 2, 2)] = value.astype(BF).reshape(2, 2, 128, 1024)

        self.loop(4, up_gradient, "upper")
        self.load(4, self.held_a, self.buf_a).start()
        up.start()

        def residual(i):
            rows = block(i, 256)
            dy = back.take(i)
            normal, scale = normalise(mid[rows, :])
            stats[2:3, :] += column_sum(dy)
            stats[3:4, :] += column_sum(dy * normal)
            dn = dy * (1.0 + vectors[4:5, :])
            dn = dn - jnp.mean(dn, -1, keepdims=True) - normal * jnp.mean(dn * normal, -1, keepdims=True)
            total = grad[rows, :].astype(F32) + scale * dn
            mid[rows, :] = total
            stats[4:5, :] += column_sum(total * self.branch_one[rows, :].astype(F32))
            g = (total * vectors[2:3, :]).astype(BF)
            mlp_in[rows, :] = g
            mine_too = jnp.where(i // 2 == c, 1.0, 0.0)
            stats[5:6, :] += column_sum(g.astype(F32)) * mine_too

        self.loop(4, residual, "rest")

    def attend_back(self):
        z, y, c, x = place()
        vectors, stats, down, up = self.vectors, self.stats, self.down, self.up
        near, far = self.near_heads, self.far_heads
        acts, g_one, heads_grad, sums = self.buf_b, self.mlp_in, self.heads_grad, self.sums
        weights = self.buf_a
        sums[...] = jnp.zeros_like(sums)
        self.load(3, self.held_b, self.buf_b).wait()
        self.load(4, self.held_a, self.buf_a).wait()

        def enter(i):
            b, half = i // 2, lax.rem(i, 2)
            value = nn(g_one[block(half, 512), :], flat(weights[b, :, :, :, 0:256]))
            heads_grad[b, block(half, 512), :] = value.astype(BF)

        self.loop(4, enter, "lift")

        def proj_gradient(i):
            b, half = i // 2, lax.rem(i, 2)
            value = tn(g_one[:, block(half, 512)], flat(acts[b, :, :, :, 0:256]))
            self.buf_d[b, pl.ds(half * 2, 2), :, :, 0:256] = value.astype(BF).reshape(2, 2, 128, 256)

        self.loop(4, proj_gradient, "proj")
        lane = lax.broadcasted_iota(jnp.int32, (1, 128), 1)

        def attend(i, k):
            b, quarter = i // 4, lax.rem(i, 4)
            rows, at_lane = block(quarter, 256), 256 + 384 * k
            queries = flat(acts[b, quarter, :, :, at_lane : at_lane + 128]) * BF(0.125)
            keys = flat(acts[b, :, :, :, at_lane + 128 : at_lane + 256])
            values = flat(acts[b, :, :, :, at_lane + 256 : at_lane + 384])
            grads = heads_grad[b, rows, k * 128 : (k + 1) * 128]

            @pl.when(quarter == 0)
            def _():
                self.key_total[...] = jnp.zeros_like(self.key_total)
                self.value_total[...] = jnp.zeros_like(self.value_total)

            result = None
            logs = self.lse[rows, :]
            for h in range(2):
                log = jnp.sum(jnp.where(lane == (k * 2 + b) * 2 + h, logs, 0.0), -1, keepdims=True)
                query = jnp.where(in_half(h), queries, jnp.zeros_like(queries))
                grad = jnp.where(in_half(h), grads, jnp.zeros_like(grads))
                probs = jnp.exp(nt(query, keys) - log)
                probs_grad = nt(grad, values)
                inner = jnp.sum(probs * probs_grad, -1, keepdims=True)
                score_grad = (probs * (probs_grad - inner)).astype(BF)
                query_grad = nn(score_grad, keys)
                result = query_grad if h == 0 else jnp.where(in_half(0), result, query_grad)
                self.key_total[...] += tn(score_grad, query)
                self.value_total[...] += tn(probs.astype(BF), grad)
            result = (result * 0.125).astype(BF)
            acts[b, quarter, :, :, at_lane : at_lane + 128] = result.reshape(2, 128, 128)
            sums[b, :, k * 128 : (k + 1) * 128] += column_sum(result.astype(F32))

            @pl.when(quarter == 3)
            def _():
                total = self.key_total[...].astype(BF)
                acts[b, :, :, :, at_lane + 128 : at_lane + 256] = total.reshape(4, 2, 128, 128)
                total = self.value_total[...].astype(BF)
                acts[b, :, :, :, at_lane + 256 : at_lane + 384] = total.reshape(4, 2, 128, 128)
                sums[b, :, 512 + k * 128 : 640 + k * 128] = column_sum(total.astype(F32))

        def qkv_gradient(i, k):
            b, half = i // 2, lax.rem(i, 2)
            lanes = slice(256 + 384 * k, 640 + 384 * k)
            value = tn(self.attn_in[:, block(half, 512)], flat(acts[b, :, :, :, lanes]))
            self.buf_d[b, pl.ds(half * 2, 2), :, :, lanes] = value.astype(BF).reshape(2, 2, 128, 384)

        self.loop(8, lambda i: attend(i, 0), "near")
        self.loop(4, lambda i: qkv_gradient(i, 0), "first")
        pl.semaphore_wait(self.free, 2)
        near.start()
        self.loop(8, lambda i: attend(i, 1), "far")
        self.loop(4, lambda i: qkv_gradient(i, 1), "second")
        far.start()
        self.do("s0")
        pair = self.pairs[3]

        def descend(i):
            partial = nt(flat(acts[0, i, :, :, 256:1024]), flat(weights[0, :, :, :, 256:1024]))
            pair.give(i, partial + nt(flat(acts[1, i, :, :, 256:1024]), flat(weights[1, :, :, :, 256:1024])))

        self.loop(4, descend, "drop")

        def leave(i):
            rows = block(i, 256)
            dy = pair.take(i)
            normal, scale = normalise(self.lat[rows, :].astype(F32))
            stats[6:7, :] += column_sum(dy)
            stats[7:8, :] += column_sum(dy * normal)
            dn = dy * (1.0 + vectors[1:2, :])
            dn = dn - jnp.mean(dn, -1, keepdims=True) - normal * jnp.mean(dn * normal, -1, keepdims=True)
            total = self.mid[rows, :] + scale * dn

            @pl.when(i // 2 == c)
            def _():
                for half in range(2):
                    for k in range(8):
                        part = total[half * 128 : (half + 1) * 128, k * 128 : (k + 1) * 128]
                        self.key_total[pl.ds(k, 128, stride=8), :] = part
                    values = self.key_total[...].astype(BF).reshape(64, 16, 128)
                    self.input_grad[block(lax.rem(i, 2) * 2 + half, 64)] = values

        self.loop(4, leave, "last")
        self.begin_end()

    def begin_end(self):
        z, y, c, x = place()
        stats, sums, up_sums = self.stats, self.sums, self.up_sums
        rows = [stats[k : k + 1, :] for k in (6, 7, 4, 2, 3, 0)]
        for j in range(6):
            for h in range(2):
                self.mods[h, j : j + 1, :] = rows[j][:, h * 512 : (h + 1) * 512]
        self.half_mods[z, y, x] = self.mods[c]
        for d in (1, 2, 3):
            self._mods(d).start()
        self.do("e0")
        columns, bias_part = self.columns, self.bias_part
        columns[...] = jnp.zeros_like(columns)
        bias_part[...] = jnp.zeros_like(bias_part)
        for b in range(2):
            spot = pl.ds(pl.multiple_of(b * 512 + c * 256, 256), 256)
            columns[0:1, spot] = sums[b, :, 0:256]
            columns[1:2, spot] = sums[b, :, 512:768]
        columns[2:3, :] = stats[5:6, :]
        columns[3:4, :] = stats[1:2, :]
        pieces = narrow(columns[0:1, :], 0) + narrow(columns[1:2, :], 1)
        pieces = pieces + narrow(columns[2:3, :], 2) + narrow(columns[3:4, :], 3)
        for k, (zz, yy, cc, xx) in enumerate(devices()):
            bias_part[cc, zz, xx, yy, 0:1, :] = pieces[k : k + 1, :]
        for b in range(2):
            for i in range(8):
                bias_part[i // 2 % 2, b * 2 + c, i % 2, i // 4, 1:2, :] = up_sums[b, :, i * 128 : (i + 1) * 128]
        self.bias = SmallScatter(
            bias_part, self.bias_c, self.bias_z, self.bias_near, self.small_send.at[0], self.small_recv.at[3]
        )
        self.bias.start()
        self.do("e1")
        for d in (1, 2, 3):
            self._mods(d).wait()
        self._across(lambda copy: copy.start())
        self.bias.along()
        self.do("e2")

    def _mods(self, d):
        z, y, c, x = place()
        spot = self.half_mods.at[z, y, x]
        return remote(
            spot, spot, self.small_send.at[2, d], self.small_recv.at[2, d], at(lax.rem(z + d, 4), y, c, x)
        )

    def _across(self, act):
        z, y, c, x = place()
        spot = self.half_mods.at[:, y, x]
        copy = lambda k, to: remote(spot, spot, self.small_send.at[2, k], self.small_recv.at[2, k], to)

        @pl.when(c == x)
        def _():
            act(copy(4, at(z, 1 - y, c, x)))

        @pl.when(c != x)
        def _():
            act(copy(5, at(z, y, c, 1 - x)))
            act(copy(6, at(z, 1 - y, c, 1 - x)))

    def end(self):
        z, y, c, x = place()
        up, near, far, mods, bias = self.up, self.near_heads, self.far_heads, self.all_mods, self.bias
        send, recv = self.small_send, self.small_recv
        spot = self.half_mods.at[:, y, x]

        @pl.when(c == x)
        def _():
            remote(spot, spot, send.at[2, 4], recv.at[2, 4], at(z, 1 - y, c, x)).wait()
            remote(spot, spot, send.at[2, 5], recv.at[2, 5], at(z, y, c, 1 - x)).wait_recv()
            remote(spot, spot, send.at[2, 6], recv.at[2, 6], at(z, 1 - y, c, 1 - x)).wait_recv()
            share = remote(self.half_mods, mods, send.at[2, 7], recv.at[2, 7], at(z, y, 1 - c, x))
            share.start()
            keep = self.load(5, self.half_mods, mods)
            keep.start()
            keep.wait()
            share.wait_send()

        @pl.when(c != x)
        def _():
            remote(spot, spot, send.at[2, 5], recv.at[2, 5], at(z, y, c, 1 - x)).wait_send()
            remote(spot, spot, send.at[2, 6], recv.at[2, 6], at(z, 1 - y, c, 1 - x)).wait_send()
            remote(self.half_mods, mods, send.at[2, 7], recv.at[2, 7], at(z, y, 1 - c, x)).wait_recv()

        bias.across()
        self.do("e3")
        silu_rows = self.silu[...].astype(BF)
        total = jnp.zeros((16, 128), F32)
        bias_rows = []
        for j in range(6):
            values = jnp.concatenate([mods[b // 4, b // 2 % 2, b % 2, j : j + 1, :] for b in range(16)], 0)
            high, low = split_bf(values)
            weights = self.wide[:, j * 512 : (j + 1) * 512]
            self.tall[...] = tn(silu_rows, high) + tn(silu_rows, low)
            self.ada_out[j] = self.tall[block(c, 64), :]
            total = total + nt(high, weights) + nt(low, weights)
            bias_rows.append(column_sum(values))
        found, found_c, found_z, found_near = self.found, self.found_c, self.found_z, self.found_near
        for b in range(16):
            found[b % 2, b // 4, b // 2 % 2] = total[b : b + 1, :]
        core = remote(found.at[1 - c], found_c, send.at[3, 0], recv.at[1, 0], at(z, y, 1 - c, x))
        core.start()
        self.do("e4")
        group = (lax.rem(z, 2) * 2 + y) * 2 + c
        source = lax.broadcasted_iota(jnp.int32, (512, 128), 0)
        target = lax.broadcasted_iota(jnp.int32, (512, 128), 1)
        chosen = jnp.where((source == group * 64 + target) & (target < 64), 1.0, 0.0).astype(BF)
        self.picked[...] = exact_nn(jnp.concatenate(bias_rows + [jnp.zeros((2, 512), F32)], 0), chosen)
        swap = remote(self.picked, self.picked_other, send.at[3, 7], recv.at[1, 7], at(z, y, c, 1 - x))
        swap.start()
        self.do("e5")
        core.wait()
        found_c[...] = found_c[...] + found[c]
        along = []
        for k in (1, 2, 3):
            to = lax.rem(z + k, 4)
            along.append(remote(found_c.at[to], found_z.at[z], send.at[3, k], recv.at[1, k], at(to, y, c, x)))
            along[-1].start()
        found_z[z] = found_c[z]
        self.do("e6")
        for copy in along:
            copy.wait()
        across = []
        for k, (to_y, to_x) in enumerate(((y, 1 - x), (1 - y, x), (1 - y, 1 - x))):
            across.append(
                remote(found_z.at[:, to_y], found_near.at[k], send.at[3, 4 + k], recv.at[1, 4 + k], at(z, to_y, c, to_x))
            )
            across[-1].start()
        self.do("e7")
        for copy in across:
            copy.wait()
        swap.wait()
        self.small_out[...] = jnp.zeros_like(self.small_out)
        self.small_out[4:6, :] = bias.finish()
        picked = jnp.where(z // 2 == x, self.picked[...], self.picked_other[...])
        self.small_out[8:16, 0:32] = jnp.where(x == 0, picked[:, 0:32], picked[:, 32:64])
        same, other = found_z[:, y] + found_near[0], found_near[1] + found_near[2]
        rows = [jnp.where(y == b % 2, same[b // 2], other[b // 2]) for b in range(8)]
        v = self.cond[...].astype(F32)
        v = jnp.concatenate([v[:, k * 128 : (k + 1) * 128] for k in range(8)], 0)
        gate = 1.0 / (1.0 + jnp.exp(-v))
        row = jnp.concatenate(rows, 0) * gate * (1.0 + v * (1.0 - gate))
        self.small_out[0:4, :] = jnp.where(x == 0, row[0:4], row[4:8])
        self.do("e8")
        near.finish()
        self.swap_block.finish()
        self.swap_input.finish()
        far.finish()


def on_device_pairs(
    latents_in,
    condition,
    grad_out,
    qkv_weight,
    proj_weight,
    up_weight,
    down_weight,
    ada_weight,
    query_bias,
    value_bias,
    proj_bias,
    up_bias,
    down_bias,
    ada_bias,
):
    small = [b.reshape(1, -1) for b in (query_bias, value_bias, proj_bias, down_bias, up_bias)]
    out = lambda *shape: jax.ShapeDtypeStruct(shape, F32)
    group = jax.ShapeDtypeStruct(GROUP, BF)
    rows = jax.ShapeDtypeStruct((512, 1024), BF)
    results = pl.pallas_call(
        pairs_kernel,
        out_shape=[rows, jax.ShapeDtypeStruct((256, 16, 128), BF), out(3, 64, 512), out(64, 512), out(64, 2048), out(64, 2048)]
        + [group] * 2
        + [out(6, 64, 512), out(16, 128)],
        in_specs=[IN_ANY] * 7 + [IN_VMEM] * 7,
        out_specs=[IN_ANY] * 8 + [IN_VMEM] * 2,
        scratch_shapes=list(scratch().values()),
        compiler_params=pltpu.CompilerParams(
            collective_id=0, has_side_effects=True, vmem_limit_bytes=63 * MIB + MIB // 2
        ),
        name="dit_block",
    )(
        latents_in.reshape(512, 1024), grad_out.reshape(512, 1024), qkv_weight.transpose(1, 0, 2), proj_weight.T,
        up_weight, down_weight.T, ada_weight.transpose(1, 0, 2), condition, *small, ada_bias,
    )
    block_mine, input_mine, q_out, p_out, u_out, d_out, _, _, ada_out, small_out = results
    return (
        block_mine.reshape(512, 1, 1024),
        input_mine.astype(F32).reshape(512, 1, 1024),
        small_out[0:4].reshape(1, 512),
        q_out.transpose(1, 0, 2),
        p_out.T,
        u_out,
        d_out.T,
        ada_out.transpose(1, 0, 2),
        small_out[4, 0:32],
        small_out[4, 32:64],
        small_out[4, 64:96],
        small_out[5],
        small_out[4, 96:128],
        small_out[8:14, 0:32],
    )


def solution(mesh):
    shape = dict(mesh.shape)
    pairs = shape["fsdp"] == 16 and shape["tp"] == 2
    return jax.shard_map(
        on_device_pairs if pairs else on_device_general,
        mesh=mesh,
        in_specs=(
            P("tp", "fsdp", None),
            P("fsdp", None),
            P("tp", "fsdp", None),
            P("fsdp", None, "tp"),
            P("tp", "fsdp"),
            P("fsdp", "tp"),
            P("tp", "fsdp"),
            P("fsdp", None, "tp"),
            P(("fsdp", "tp")),
            P(("fsdp", "tp")),
            P(("fsdp", "tp")),
            P(("fsdp", "tp")),
            P(("fsdp", "tp")),
            P(None, ("fsdp", "tp")),
        ),
        out_specs=(
            P("tp", "fsdp", None),
            P("tp", "fsdp", None),
            P("fsdp", "tp"),
            P("fsdp", None, "tp"),
            P("tp", "fsdp"),
            P("fsdp", "tp"),
            P("tp", "fsdp"),
            P("fsdp", None, "tp"),
            P(("fsdp", "tp")),
            P(("fsdp", "tp")),
            P(("fsdp", "tp")),
            P(("fsdp", "tp")),
            P(("fsdp", "tp")),
            P(None, ("fsdp", "tp")),
        ),
        check_vma=False,
    )
```

```python
import functools
import math

import jax
import jax.numpy as jnp
from jax import lax
from jax.experimental import pallas as pl
from jax.experimental.pallas import tpu as pltpu
from jax.sharding import PartitionSpec as P


HD = 64


epsilon = 1e-06


def layer_norm(values):
    centred = values - jnp.mean(values, axis=-1, keepdims=True)
    return centred * lax.rsqrt(jnp.mean(centred * centred, axis=-1, keepdims=True) + epsilon)


def modulate(values, shift_part, scale_part):
    return layer_norm(values) * (1.0 + scale_part) + shift_part


def gelu_tanh(values):
    return jax.nn.gelu(values, approximate=True)


def gather_rows(piece):
    return lax.all_gather(piece, "tp", axis=0, tiled=True)


def gather_grads(piece):
    return lax.all_gather(piece, "tp", axis=0, tiled=True)


def scatter_rows(product, row_count):
    return lax.psum_scatter(
        product(jnp.int32(0), row_count * lax.axis_size("tp")).astype(jnp.bfloat16),
        "tp",
        scatter_dimension=0,
        tiled=True,
    ).astype(jnp.float32)


def scatter_grads(product, row_count):
    return lax.psum_scatter(
        product(jnp.int32(0), row_count * lax.axis_size("tp")).astype(jnp.bfloat16),
        "tp",
        scatter_dimension=0,
        tiled=True,
    ).astype(jnp.float32)


def split_heads(packed):
    head_count = packed.shape[3] // HD
    shaped = packed.reshape(packed.shape[0], packed.shape[1], 3, head_count, HD)
    return (shaped[:, :, 0], shaped[:, :, 1], shaped[:, :, 2])


def attend_forward(packed):
    length, latents, local_width = (packed.shape[0], packed.shape[1], packed.shape[3])
    queries, key_rows, value_rows = split_heads(packed)
    block_rows = min(512, length)
    score_scale = 1.0 / math.sqrt(HD)
    blocks = queries.reshape(length // block_rows, block_rows, latents, local_width // HD, HD)

    def one_block(q_rows):
        scores = (
            jnp.einsum("qbhd,kbhd->bhqk", q_rows, key_rows, preferred_element_type=jnp.float32)
            * score_scale
        )
        largest = jnp.max(scores, axis=-1, keepdims=True)
        exponent = jnp.exp(scores - largest)
        summed = jnp.sum(exponent, axis=-1, keepdims=True)
        weights_soft = (exponent / summed).astype(jnp.bfloat16)
        mixture = jnp.einsum(
            "bhqk,kbhd->qbhd", weights_soft, value_rows, preferred_element_type=jnp.float32
        )
        return (mixture.astype(jnp.bfloat16), largest[..., 0] + jnp.log(summed[..., 0]))

    mixture_all, log_sums = lax.map(one_block, blocks)
    return (mixture_all.reshape(length, latents, local_width), log_sums)


def attend_backward(packed, log_sums, heads_grad):
    length, latents, local_width = (packed.shape[0], packed.shape[1], packed.shape[3])
    head_count = local_width // HD
    queries, key_rows, value_rows = split_heads(packed)
    block_rows = min(512, length)
    count_blocks = length // block_rows
    score_scale = 1.0 / math.sqrt(HD)
    q_blocks = queries.reshape(count_blocks, block_rows, latents, head_count, HD)
    g_blocks = heads_grad.reshape(count_blocks, block_rows, latents, head_count, HD)

    def one_block(carried, inputs):
        key_grad, value_grad = carried
        q_rows, g_rows, log_rows = inputs
        scores = (
            jnp.einsum("qbhd,kbhd->bhqk", q_rows, key_rows, preferred_element_type=jnp.float32)
            * score_scale
        )
        weights_soft = jnp.exp(scores - log_rows[..., None])
        soft_grad = jnp.einsum(
            "qbhd,kbhd->bhqk", g_rows, value_rows, preferred_element_type=jnp.float32
        )
        inner_sum = jnp.sum(weights_soft * soft_grad, axis=-1, keepdims=True)
        score_grad = (weights_soft * (soft_grad - inner_sum)).astype(jnp.bfloat16)
        query_grad = (
            jnp.einsum("bhqk,kbhd->qbhd", score_grad, key_rows, preferred_element_type=jnp.float32)
            * score_scale
        )
        key_grad = (
            key_grad
            + jnp.einsum("bhqk,qbhd->kbhd", score_grad, q_rows, preferred_element_type=jnp.float32)
            * score_scale
        )
        value_grad = value_grad + jnp.einsum(
            "bhqk,qbhd->kbhd",
            weights_soft.astype(jnp.bfloat16),
            g_rows,
            preferred_element_type=jnp.float32,
        )
        return ((key_grad, value_grad), query_grad)

    zero_rows = jnp.zeros((length, latents, head_count, HD), jnp.float32)
    (key_grad, value_grad), query_grad = lax.scan(
        one_block, (zero_rows, zero_rows), (q_blocks, g_blocks, log_sums)
    )
    stacked = jnp.stack(
        [
            query_grad.reshape(length, latents, local_width),
            key_grad.reshape(length, latents, local_width),
            value_grad.reshape(length, latents, local_width),
        ],
        axis=2,
    )
    return stacked.astype(jnp.bfloat16)


def on_device_general(
    latents_in,
    condition,
    grad_out,
    qkv_weight,
    proj_weight,
    up_weight,
    down_weight,
    ada_weight,
    query_bias,
    value_bias,
    proj_bias,
    up_bias,
    down_bias,
    ada_bias,
):
    tp_index = lax.axis_index("tp")
    local_rows = latents_in.shape[0]
    local_width = qkv_weight.shape[2]
    local_hidden = up_weight.shape[1]
    model_width = latents_in.shape[2]
    width_start = tp_index * local_width
    hidden_start = tp_index * local_hidden
    full_qkv, full_proj, full_up, full_down, full_ada = (
        lax.all_gather(qkv_weight, "fsdp", axis=0, tiled=True),
        lax.all_gather(proj_weight, "fsdp", axis=1, tiled=True),
        lax.all_gather(up_weight, "fsdp", axis=0, tiled=True),
        lax.all_gather(down_weight, "fsdp", axis=1, tiled=True),
        lax.all_gather(ada_weight, "fsdp", axis=0, tiled=True),
    )
    bias_list = (
        lax.all_gather(query_bias, ("fsdp", "tp"), axis=0, tiled=True),
        lax.all_gather(value_bias, ("fsdp", "tp"), axis=0, tiled=True),
        lax.all_gather(proj_bias, ("fsdp", "tp"), axis=0, tiled=True),
        lax.all_gather(up_bias, ("fsdp", "tp"), axis=0, tiled=True),
        lax.all_gather(down_bias, ("fsdp", "tp"), axis=0, tiled=True),
        lax.all_gather(ada_bias, ("fsdp", "tp"), axis=1, tiled=True),
    )
    all_query, all_value, all_proj, all_up, all_down, all_ada = [
        item_bias.astype(jnp.float32) for item_bias in bias_list
    ]
    hidden_total = all_up.shape[0]
    cond_float = condition.astype(jnp.float32)
    silu_cond = jax.nn.silu(cond_float).astype(jnp.bfloat16)
    ada_cols = lax.dynamic_slice_in_dim(all_ada, width_start, local_width, 1)
    mod_part = (
        jnp.einsum("bc,ctf->btf", silu_cond, full_ada, preferred_element_type=jnp.float32)
        + ada_cols
    )
    modulation = lax.all_gather(mod_part, "tp", axis=2, tiled=True)
    shift_one, scale_one, gate_one = (modulation[:, 0], modulation[:, 1], modulation[:, 2])
    shift_two, scale_two, gate_two = (modulation[:, 3], modulation[:, 4], modulation[:, 5])
    input_float = latents_in.astype(jnp.float32)
    attn_in = modulate(input_float, shift_one, scale_one).astype(jnp.bfloat16)
    attn_full = gather_rows(attn_in)
    query_cols = lax.dynamic_slice_in_dim(all_query, width_start, local_width, 0)
    value_cols = lax.dynamic_slice_in_dim(all_value, width_start, local_width, 0)
    bias_three = jnp.stack([query_cols, jnp.zeros_like(query_cols), value_cols])
    packed = (
        jnp.einsum("sbd,dtf->sbtf", attn_full, full_qkv, preferred_element_type=jnp.float32)
        + bias_three
    ).astype(jnp.bfloat16)
    heads_out, log_sums = attend_forward(packed)

    def project_heads(first_row, row_count):
        return jnp.einsum("sbf,fd->sbd", heads_out, full_proj, preferred_element_type=jnp.float32)

    branch_one = scatter_rows(project_heads, local_rows) + all_proj
    middle = input_float + gate_one * branch_one
    mlp_in = modulate(middle, shift_two, scale_two).astype(jnp.bfloat16)
    mlp_full = gather_rows(mlp_in)
    up_cols = lax.dynamic_slice_in_dim(all_up, hidden_start, local_hidden, 0)
    hidden = (
        jnp.einsum("sbd,df->sbf", mlp_full, full_up, preferred_element_type=jnp.float32) + up_cols
    )
    active = gelu_tanh(hidden).astype(jnp.bfloat16)

    def project_hidden(first_row, row_count):
        return jnp.einsum("sbf,fd->sbd", active, full_down, preferred_element_type=jnp.float32)

    branch_two = scatter_rows(project_hidden, local_rows) + all_down
    block_out = (middle + gate_two * branch_two).astype(jnp.bfloat16)
    grad_float = grad_out.astype(jnp.float32)
    gate_two_grad = jnp.sum(grad_float * branch_two, axis=0)
    branch_two_grad = (grad_float * gate_two).astype(jnp.bfloat16)
    down_bias_part = jnp.sum(branch_two_grad.astype(jnp.float32), axis=(0, 1))
    _, gelu_pull = jax.vjp(gelu_tanh, hidden)
    branch_two_full = gather_grads(branch_two_grad)
    active_grad = jnp.einsum(
        "sbd,fd->sbf", branch_two_full, full_down, preferred_element_type=jnp.float32
    )
    down_grad = jnp.einsum(
        "sbf,sbd->fd", active, branch_two_full, preferred_element_type=jnp.float32
    )
    hidden_grad = gelu_pull(active_grad)[0].astype(jnp.bfloat16)
    up_grad = jnp.einsum("sbd,sbf->df", mlp_full, hidden_grad, preferred_element_type=jnp.float32)
    up_bias_part = lax.dynamic_update_slice(
        jnp.zeros((hidden_total,), jnp.float32),
        jnp.sum(hidden_grad.astype(jnp.float32), axis=(0, 1)),
        (hidden_start,),
    )

    def back_hidden(first_row, row_count):
        return jnp.einsum("sbf,df->sbd", hidden_grad, full_up, preferred_element_type=jnp.float32)

    mlp_in_grad = scatter_grads(back_hidden, local_rows)
    _, second_pull = jax.vjp(modulate, middle, shift_two, scale_two)
    middle_part, shift_two_grad, scale_two_grad = second_pull(mlp_in_grad)
    middle_grad = grad_float + middle_part
    gate_one_grad = jnp.sum(middle_grad * branch_one, axis=0)
    branch_one_grad = (middle_grad * gate_one).astype(jnp.bfloat16)
    proj_bias_part = jnp.sum(branch_one_grad.astype(jnp.float32), axis=(0, 1))
    branch_one_full = gather_grads(branch_one_grad)
    heads_grad = jnp.einsum(
        "sbd,fd->sbf", branch_one_full, full_proj, preferred_element_type=jnp.float32
    ).astype(jnp.bfloat16)
    proj_grad = jnp.einsum(
        "sbf,sbd->fd", heads_out, branch_one_full, preferred_element_type=jnp.float32
    )
    packed_grad = attend_backward(packed, log_sums, heads_grad)
    qkv_grad = jnp.einsum(
        "sbd,sbtf->dtf", attn_full, packed_grad, preferred_element_type=jnp.float32
    )
    packed_sums = jnp.sum(packed_grad.astype(jnp.float32), axis=(0, 1))
    zero_width = jnp.zeros((model_width,), jnp.float32)
    query_bias_part = lax.dynamic_update_slice(zero_width, packed_sums[0], (width_start,))
    value_bias_part = lax.dynamic_update_slice(zero_width, packed_sums[2], (width_start,))

    def back_packed(first_row, row_count):
        return jnp.einsum(
            "sbtf,dtf->sbd", packed_grad, full_qkv, preferred_element_type=jnp.float32
        )

    attn_in_grad = scatter_grads(back_packed, local_rows)
    _, first_pull = jax.vjp(modulate, input_float, shift_one, scale_one)
    input_part, shift_one_grad, scale_one_grad = first_pull(attn_in_grad)
    input_grad = middle_grad + input_part
    mod_grad = jnp.stack(
        [
            shift_one_grad,
            scale_one_grad,
            gate_one_grad,
            shift_two_grad,
            scale_two_grad,
            gate_two_grad,
        ],
        axis=1,
    )
    mod_cols_grad = lax.psum_scatter(
        mod_grad.astype(jnp.bfloat16), "tp", scatter_dimension=2, tiled=True
    ).astype(jnp.float32)
    ada_grad = jnp.einsum(
        "bc,btf->ctf", silu_cond.astype(jnp.float32), mod_cols_grad, precision=lax.Precision.HIGHEST
    )
    ada_bias_part = lax.dynamic_update_slice(
        jnp.zeros((6, model_width), jnp.float32), jnp.sum(mod_cols_grad, axis=0), (0, width_start)
    )
    silu_grad = jnp.einsum(
        "btf,ctf->bc", mod_cols_grad, full_ada.astype(jnp.float32), precision=lax.Precision.HIGHEST
    )
    silu_cols = lax.psum_scatter(silu_grad, "tp", scatter_dimension=1, tiled=True)
    cond_width = silu_cols.shape[1]
    cond_cols = lax.dynamic_slice_in_dim(cond_float, tp_index * cond_width, cond_width, 1)
    _, silu_pull = jax.vjp(jax.nn.silu, cond_cols)
    cond_grad = silu_pull(silu_cols)[0]
    qkv_sum, proj_sum, up_sum, down_sum, ada_sum = (
        lax.psum_scatter(
            qkv_grad.astype(jnp.bfloat16), "fsdp", scatter_dimension=0, tiled=True
        ).astype(jnp.float32),
        lax.psum_scatter(
            proj_grad.astype(jnp.bfloat16), "fsdp", scatter_dimension=1, tiled=True
        ).astype(jnp.float32),
        lax.psum_scatter(
            up_grad.astype(jnp.bfloat16), "fsdp", scatter_dimension=0, tiled=True
        ).astype(jnp.float32),
        lax.psum_scatter(
            down_grad.astype(jnp.bfloat16), "fsdp", scatter_dimension=1, tiled=True
        ).astype(jnp.float32),
        lax.psum_scatter(
            ada_grad.astype(jnp.bfloat16), "fsdp", scatter_dimension=0, tiled=True
        ).astype(jnp.float32),
    )
    query_sum, value_sum, proj_bias_sum, up_bias_sum, down_bias_sum, ada_bias_sum = (
        lax.psum_scatter(query_bias_part, ("fsdp", "tp"), scatter_dimension=0, tiled=True),
        lax.psum_scatter(value_bias_part, ("fsdp", "tp"), scatter_dimension=0, tiled=True),
        lax.psum_scatter(proj_bias_part, ("fsdp", "tp"), scatter_dimension=0, tiled=True),
        lax.psum_scatter(up_bias_part, ("fsdp", "tp"), scatter_dimension=0, tiled=True),
        lax.psum_scatter(down_bias_part, ("fsdp", "tp"), scatter_dimension=0, tiled=True),
        lax.psum_scatter(ada_bias_part, ("fsdp", "tp"), scatter_dimension=1, tiled=True),
    )
    return (
        block_out,
        input_grad,
        cond_grad,
        qkv_sum,
        proj_sum,
        up_sum,
        down_sum,
        ada_sum,
        query_sum,
        value_sum,
        proj_bias_sum,
        up_bias_sum,
        down_bias_sum,
        ada_bias_sum,
    )


MESH = pl.DeviceIdType.MESH
ANY = pl.ANY
BF = jnp.bfloat16
F32 = jnp.float32
MIB = 2**20
IN_VMEM = pl.BlockSpec(memory_space=pltpu.VMEM)
IN_ANY = pl.BlockSpec(memory_space=ANY)
ROWS = dict(q=[80, 48, 0], p=[48, 48, 32], u=[48, 48, 32], d=[48, 48, 32])
ROWS.update(down=[64, 48, 16], up=[64, 48, 16], near=[64, 48, 16], far=[64, 48, 16])
MOST_A, MOST_B = 64, 48


def cut(rows):
    a, b, w = rows
    return pl.ds(0, a), pl.ds(a, b), pl.ds(a + b, w), pl.ds(0, a + b)


def place():
    f, x = lax.axis_index("fsdp"), lax.axis_index("tp")
    z, y, c = f // 4, lax.rem(f // 2, 2), lax.rem(f, 2)
    return z, y, c, x


def at(z, y, c, x):
    return ((z * 2 + y) * 2 + c, x)


def block(index, size):
    return pl.ds(pl.multiple_of(index * size, size), size)


def remote(src, dst, send, recv, device):
    return pltpu.make_async_remote_copy(
        src_ref=src, dst_ref=dst, send_sem=send, recv_sem=recv, device_id=device, device_id_type=MESH
    )


def loop(count, body, ticks=None):
    def step(i, carry):
        body(i)
        for k, tick in (ticks or {}).items():

            @pl.when(i == k)
            def _(tick=tick):
                tick()

        return carry

    lax.fori_loop(0, count, step, 0)


def greet(devices):
    barrier = pltpu.get_barrier_semaphore()
    for device in devices:
        pl.semaphore_signal(barrier, inc=1, device_id=device, device_id_type=MESH)
    pl.semaphore_wait(barrier, len(devices))


def partners():
    z, y, c, x = place()
    out = [at(z, y, 1 - c, x), at(z, 1 - y, c, x), at(z, y, c, 1 - x), at(z, y, 1 - c, 1 - x)]
    out += [at(z, 1 - y, c, 1 - x), at(z, 1 - y, 1 - c, 1 - x)]
    return out + [at(lax.rem(z + d, 4), y, c, x) for d in (1, 2, 3)]


class Gather:
    def __init__(self, own, full, lanes, rows, send, recv, local):
        self.own, self.full, self.lanes, self.rows = own, full, pl.ds(*lanes), rows
        self.send, self.recv, self.local = send, recv, local

    def _core(self):
        z, y, c, x = place()
        copies = []
        for i, ((near, first, width), (far, _, _)) in enumerate(zip(self.own(c), self.own(1 - c))):
            spot = self.full.at[x, z, y, block(c, 64), pl.ds(first, width)]
            copies.append(pltpu.make_async_copy(near, spot, self.local.at[i]))
            copies.append(remote(far, spot, self.send.at[i], self.recv.at[i], at(z, y, 1 - c, x)))
        return copies

    def _copy(self, kind, d):
        z, y, c, x = place()
        a, b, w, first = cut(self.rows)
        from_z = lax.rem(z - d + 4, 4)
        to_x, to_y, to_z = at(z, y, c, 1 - x), at(z, 1 - y, c, x), at(lax.rem(z + d, 4), y, c, x)
        if kind == 0:
            spot, to = self.full.at[x, z, y, first, self.lanes], to_z
        elif kind == 1:
            spot, to = self.full.at[x, from_z, y, a, self.lanes], to_x
        elif kind == 2:
            spot, to = self.full.at[x, from_z, y, b, self.lanes], to_y
        elif kind == 3:
            spot, to = self.full.at[:, from_z, y, a, self.lanes], to_y
        elif kind == 4:
            spot, to = self.full.at[x, from_z, :, b, self.lanes], to_x
        elif kind == 5:
            spot, to = self.full.at[:, z, :, w, self.lanes], to_z
        elif d == 0:
            spot, to = self.full.at[x, z, y, w, self.lanes], to_x
        else:
            spot, to = self.full.at[:, z, y, w, self.lanes], to_y
        return remote(spot, spot, self.send.at[8 + 4 * kind + d], self.recv.at[8 + 4 * kind + d], to)

    def start_core(self):
        for copy in self._core():
            copy.start()

    def enter(self, along=(2, 1, 3)):
        for copy in self._core():
            copy.wait()
        self.pass_on(along)

    def pass_on(self, along):
        for d in along:
            self._copy(0, d).start()

    def first(self):
        if self.rows[2]:
            self._copy(6, 0).start()
        self._copy(1, 0).start()
        self._copy(2, 0).start()

    def arrived(self, d):
        self._copy(0, d).wait()
        self._copy(1, d).start()
        self._copy(2, d).start()

    def turn(self, d):
        if self.rows[2] and d == 0:
            self._copy(6, 0).wait()
            self._copy(6, 1).start()
        self._copy(1, d).wait()
        self._copy(3, d).start()
        self._copy(2, d).wait()
        self._copy(4, d).start()

    def spread(self):
        self._copy(6, 1).wait()
        for k in (2, 1, 3):
            self._copy(5, k).start()

    def finish(self):
        for d in range(4):
            self._copy(3, d).wait()
            self._copy(4, d).wait()
        if self.rows[2]:
            for d in (2, 1, 3):
                self._copy(5, d).wait()


class Scatter:
    def __init__(
        self, part, first_a, first_b, second, third, wide_z, wide_y, wide_x, total, lanes, rows, out, send, recv
    ):
        self.rows = rows
        self.part, self.first_a, self.first_b = part, first_a, first_b
        self.wide_z, self.wide_y, self.wide_x = wide_z, wide_y, wide_x
        self.second, self.third, self.total, self.out = second, third, total, out
        self.lanes, self.send, self.recv = pl.ds(*lanes), send, recv

    def _copy(self, kind, d):
        z, y, c, x = place()
        n, to_z = self.lanes, lax.rem(z + d, 4)
        a, b, w, first = cut(self.rows)
        na, nb, nw = [pl.ds(0, count) for count in self.rows]
        send, recv = self.send.at[4 * kind + d], self.recv.at[4 * kind + d]
        to_x, to_y = at(z, y, c, 1 - x), at(z, 1 - y, c, x)
        if kind == 0:
            return remote(self.part.at[:, to_z, 1 - y, a, n], self.first_a.at[to_z, :, na, n], send, recv, to_y)
        if kind == 1:
            return remote(self.part.at[1 - x, to_z, :, b, n], self.first_b.at[to_z, :, nb, n], send, recv, to_x)
        if kind == 2:
            return remote(self.first_a.at[to_z, 1 - x, na, n], self.second.at[to_z, a, n], send, recv, to_x)
        if kind == 3:
            return remote(self.first_b.at[to_z, 1 - y, nb, n], self.second.at[to_z, b, n], send, recv, to_y)
        if kind == 4:
            return remote(
                self.second.at[to_z, first, n], self.third.at[d - 1, first, n], send, recv, at(to_z, y, c, x)
            )
        if kind == 5:
            return remote(
                self.part.at[:, to_z, :, w, n], self.wide_z.at[d - 1, :, :, nw, n], send, recv, at(to_z, y, c, x)
            )
        if d == 0:
            return remote(self.wide_z.at[0, :, 1 - y, nw, n], self.wide_y.at[:, nw, n], send, recv, to_y)
        return remote(self.wide_y.at[1 - x, nw, n], self.wide_x.at[nw, n], send, recv, to_x)

    def _core(self):
        z, y, c, x = place()
        copies = []
        for i, (target, first, width) in enumerate(self.out(c)):
            lanes = pl.ds(first, width)
            copies.append(
                remote(
                    self.total.at[block(1 - c, 64), lanes], target, self.send.at[28 + i], self.recv.at[28 + i],
                    at(z, y, 1 - c, x),
                )
            )
            copies.append(pltpu.make_async_copy(self.total.at[block(c, 64), lanes], target, self.send.at[32 + i]))
        return copies

    def _start(self, d):
        self._copy(0, d).start()
        self._copy(1, d).start()

    def start(self):
        for d in (2, 1, 3):
            self._copy(5, d).start()
        for d in (2, 1, 3, 0):
            self._start(d)

    def turn(self, d):
        z, y, c, x = place()
        to_z, n = lax.rem(z + d, 4), self.lanes
        a, b, _, _ = cut(self.rows)
        na, nb, _ = [pl.ds(0, count) for count in self.rows]
        self._copy(0, d).wait()
        for k in range(2):
            total = self.first_a[to_z, k, na, n].astype(F32) + self.part[k, to_z, y, a, n].astype(F32)
            self.first_a[to_z, k, na, n] = total.astype(BF)
        self._copy(2, d).start()
        self._copy(1, d).wait()
        for k in range(2):
            total = self.first_b[to_z, k, nb, n].astype(F32) + self.part[x, to_z, k, b, n].astype(F32)
            self.first_b[to_z, k, nb, n] = total.astype(BF)
        self._copy(3, d).start()

    def fold_z(self):
        z, y, c, x = place()
        n, w, nw = self.lanes, cut(self.rows)[2], pl.ds(0, self.rows[2])
        for k in (2, 1, 3):
            self._copy(5, k).wait()
        for k in range(2):
            for j in range(2):
                total = self.part[k, z, j, w, n].astype(F32)
                for s in range(3):
                    total = total + self.wide_z[s, k, j, nw, n].astype(F32)
                self.wide_z[0, k, j, nw, n] = total.astype(BF)
        self._copy(6, 0).start()

    def fold_y(self):
        z, y, c, x = place()
        n, nw = self.lanes, pl.ds(0, self.rows[2])
        self._copy(6, 0).wait()
        for k in range(2):
            total = self.wide_y[k, nw, n].astype(F32) + self.wide_z[0, k, y, nw, n].astype(F32)
            self.wide_y[k, nw, n] = total.astype(BF)
        self._copy(6, 1).start()

    def leave(self, d):
        z, y, c, x = place()
        to_z, n = lax.rem(z + d, 4), self.lanes
        a, b, _, _ = cut(self.rows)
        na, nb, _ = [pl.ds(0, count) for count in self.rows]
        self._copy(2, d).wait()
        total = self.second[to_z, a, n].astype(F32) + self.first_a[to_z, x, na, n].astype(F32)
        self.second[to_z, a, n] = total.astype(BF)
        self._copy(3, d).wait()
        total = self.second[to_z, b, n].astype(F32) + self.first_b[to_z, y, nb, n].astype(F32)
        self.second[to_z, b, n] = total.astype(BF)
        if d:
            self._copy(4, d).start()

    def last(self):
        z, y, c, x = place()
        n, nw = self.lanes, pl.ds(0, self.rows[2])
        a, b, w, _ = cut(self.rows)
        self._copy(6, 1).wait()
        self.total[w, n] = self.wide_x[nw, n].astype(F32) + self.wide_y[x, nw, n].astype(F32)
        for d in (1, 2, 3):
            self._copy(4, d).wait()
        for rows in (a, b):
            total = self.second[z, rows, n].astype(F32)
            for d in range(3):
                total = total + self.third[d, rows, n].astype(F32)
            self.total[rows, n] = total
        for copy in self._core():
            copy.start()

    def finish(self):
        for copy in self._core():
            copy.wait()


class Swap:
    def __init__(self, own, full, send, recv, local):
        self.own, self.full, self.send, self.recv, self.local = own, full, send, recv, local

    def _both(self, act):
        z, y, c, x = place()

        @pl.when(c != x)
        def _():
            to = at(z, y, 1 - c, 1 - x)
            act(remote(self.own, self.full.at[block(1 - c, 512)], self.send.at[0], self.recv.at[0], to))

        @pl.when(c == x)
        def _():
            act(pltpu.make_async_copy(self.own, self.full.at[block(c, 512)], self.local))

    def _core(self):
        z, y, c, x = place()
        spot = self.full.at[block(c, 512)]
        return remote(spot, spot, self.send.at[1], self.recv.at[1], at(z, y, 1 - c, x))

    def start(self):
        self._both(lambda copy: copy.start())

    def share(self):
        self._both(lambda copy: copy.wait())
        self._core().start()

    def finish(self):
        self._core().wait()


class SwapBack:
    def __init__(self, full, out, send, recv, local):
        self.full, self.out, self.send, self.recv, self.local = full, out, send, recv, local

    def _both(self, act):
        z, y, c, x = place()
        rows = self.full if self.full.shape == self.out.shape else self.full.at[block(c, 512)]

        @pl.when(c != x)
        def _():
            act(remote(rows, self.out, self.send, self.recv, at(z, y, 1 - c, 1 - x)))

        @pl.when(c == x)
        def _():
            act(pltpu.make_async_copy(rows, self.out, self.local))

    def start(self):
        self._both(lambda copy: copy.start())

    def finish(self):
        self._both(lambda copy: copy.wait())


class SmallGather:
    def __init__(self, own, full, send, recv):
        self.own, self.full, self.send, self.recv = own, full, send, recv

    def _copy(self, k):
        z, y, c, x = place()
        send, recv = self.send.at[k], self.recv.at[k]
        if k == 0:
            return remote(self.own, self.full.at[x, z, y, c], send, recv, at(z, y, 1 - c, x))
        if k <= 3:
            spot = self.full.at[x, z, y]
            return remote(spot, spot, send, recv, at(lax.rem(z + k, 4), y, c, x))
        if k == 4:
            spot = self.full.at[x, :, y]
            return remote(spot, spot, send, recv, at(z, 1 - y, c, x))
        spot = self.full.at[x]
        return remote(spot, spot, send, recv, at(z, y, c, 1 - x))

    def start(self):
        z, y, c, x = place()
        self.full[x, z, y, c] = self.own[...]
        self._copy(0).start()

    def step(self, done, begin):
        for k in done:
            self._copy(k).wait()
        for k in begin:
            self._copy(k).start()


class SmallScatter:
    def __init__(self, part, near_c, near_z, near, send, recv):
        self.part, self.near_c, self.near_z, self.near = part, near_c, near_z, near
        self.send, self.recv = send, recv

    def _copy(self, k):
        z, y, c, x = place()
        send, recv = self.send.at[k], self.recv.at[k]
        if k == 0:
            return remote(self.part.at[1 - c], self.near_c, send, recv, at(z, y, 1 - c, x))
        if k <= 3:
            to = lax.rem(z + k, 4)
            return remote(self.near_c.at[to], self.near_z.at[k - 1], send, recv, at(to, y, c, x))
        to_x, to_y = ((1 - x, y), (x, 1 - y), (1 - x, 1 - y))[k - 4]
        return remote(self.near_z.at[3, to_x, to_y], self.near.at[k - 4], send, recv, at(z, to_y, c, to_x))

    def start(self):
        self._copy(0).start()

    def along(self):
        z, y, c, x = place()
        self._copy(0).wait()
        self.near_c[...] = self.near_c[...] + self.part[c]
        for k in (1, 2, 3):
            self._copy(k).start()

    def across(self):
        z, y, c, x = place()
        for k in (1, 2, 3):
            self._copy(k).wait()
        self.near_z[3] = self.near_c[z] + self.near_z[0] + self.near_z[1] + self.near_z[2]
        for k in (4, 5, 6):
            self._copy(k).start()

    def finish(self):
        z, y, c, x = place()
        for k in (4, 5, 6):
            self._copy(k).wait()
        return self.near_z[3, x, y] + self.near[0] + self.near[1] + self.near[2]


class Pair:
    def __init__(self, mine, theirs, send, recv):
        self.mine, self.theirs, self.send, self.recv = mine, theirs, send, recv

    def _copy(self, i):
        z, y, c, x = place()
        rows = block(i, 256)
        return remote(
            self.mine.at[rows], self.theirs.at[rows], self.send.at[i], self.recv.at[i], at(z, y, 1 - c, x)
        )

    def give(self, i, partial):
        self.mine[block(i, 256), :] = partial.astype(BF)
        self._copy(i).start()

    def take(self, i):
        self._copy(i).wait()
        rows = block(i, 256)
        return self.mine[rows, :].astype(F32) + self.theirs[rows, :].astype(F32)


def normalise(values):
    centred = values - jnp.mean(values, axis=-1, keepdims=True)
    scale = lax.rsqrt(jnp.mean(centred * centred, axis=-1, keepdims=True) + epsilon)
    return centred * scale, scale


def nn(a, b):
    return jnp.dot(a, b, preferred_element_type=F32)


def nt(a, b):
    return lax.dot_general(a, b, (((1,), (1,)), ((), ())), preferred_element_type=F32)


def tn(a, b):
    return lax.dot_general(a, b, (((0,), (0,)), ((), ())), preferred_element_type=F32)


def in_half(h):
    return lax.broadcasted_iota(jnp.int32, (1, 128), 1) // 64 == h


def column_sum(values):
    return jnp.sum(values, 0, keepdims=True)


def gelu_parts(v):
    k = math.sqrt(2.0 / math.pi)
    square = v * v
    t = jnp.tanh(k * v * (1.0 + 0.044715 * square))
    half = 0.5 * (1.0 + t)
    return v * half, half + 0.5 * k * v * (1.0 - t * t) * (1.0 + 3.0 * 0.044715 * square)


def split_bf(values):
    high = values.astype(BF)
    return high, (values - high.astype(F32)).astype(BF)


def exact_nn(values, chosen):
    high, low = split_bf(values)
    lower = (values - high.astype(F32) - low.astype(F32)).astype(BF)
    return nn(high, chosen) + nn(low, chosen) + nn(lower, chosen)


def devices():
    return [(zz, yy, cc, xx) for zz in range(4) for yy in range(2) for cc in range(2) for xx in range(2)]


def widen(small_full, row, k, width=1024):
    pieces = jnp.concatenate([small_full[xx, zz, yy, cc, row : row + 1, :] for zz, yy, cc, xx in devices()], 0)
    lane = lax.broadcasted_iota(jnp.int32, (128, width), 1)
    source = lax.broadcasted_iota(jnp.int32, (128, width), 0)
    pick = jnp.where(source == k * 32 + lax.rem(lane, 32), 1.0, 0.0).astype(BF)
    spread_out = nn(pieces.astype(BF), pick)
    device = lax.broadcasted_iota(jnp.int32, (32, width), 0)
    lane = lax.broadcasted_iota(jnp.int32, (32, width), 1)
    return column_sum(jnp.where(lane // 32 == device, spread_out, 0.0))


def narrow(vector, k):
    device = lax.broadcasted_iota(jnp.int32, (32, 1024), 0)
    lane = lax.broadcasted_iota(jnp.int32, (32, 1024), 1)
    source = lax.broadcasted_iota(jnp.int32, (1024, 128), 0)
    target = lax.broadcasted_iota(jnp.int32, (1024, 128), 1)
    chosen = jnp.where(target == k * 32 + lax.rem(source, 32), 1.0, 0.0).astype(BF)
    return exact_nn(jnp.where(lane // 32 == device, vector, 0.0), chosen)


def flat(value):
    return value.reshape(-1, value.shape[-1])


INPUTS = """lat_own grad_own wq wp wu wd ada cond q_bias v_bias p_bias d_bias u_bias a_bias"""
OUTPUTS = """block_mine input_mine q_out p_out u_out d_out held_a held_b
    ada_out small_out"""
GROUP = (2, 4, 2, 128, 1024)
TOKENS = (1024, 1024)


def scratch():
    v, f = (lambda *s: pltpu.VMEM(s, BF)), (lambda *s: pltpu.VMEM(s, F32))
    dma, regular = pltpu.SemaphoreType.DMA, pltpu.SemaphoreType.REGULAR
    out = dict(lat=v(*TOKENS), grad=v(*TOKENS), attn_in=v(*TOKENS), mid=f(*TOKENS), branch_one=v(*TOKENS))
    out.update(mlp_in=v(*TOKENS), g_two=v(*TOKENS), mine=v(*TOKENS), theirs_a=v(*TOKENS), theirs_b=v(*TOKENS))
    out.update(buf_a=v(*GROUP), buf_b=v(*GROUP), gu=v(*GROUP), buf_c=v(*GROUP), buf_d=v(*GROUP))
    for i in range(2):
        out[f"first_a{i}"], out[f"first_b{i}"] = v(4, 2, MOST_A, 1024), v(4, 2, MOST_B, 1024)
    for i, name in enumerate(("down", "up", "near")):
        a, b, w = ROWS[name]
        out[f"second{i}"], out[f"third{i}"] = v(4, a + b, 1024), v(3, a + b, 1024)
        out[f"wide_z{i}"], out[f"wide_y{i}"], out[f"wide_x{i}"] = v(3, 2, 2, w, 1024), v(2, w, 1024), v(w, 1024)
    out.update(total=f(128, 1024), heads_grad=v(2, 1024, 256), lse=f(1024, 128))
    out.update(key_total=f(1024, 128), value_total=f(1024, 128), input_grad=v(256, 16, 128))
    out.update(small=f(16, 128), small_full=f(2, 4, 2, 2, 16, 128), wide=v(128, 3072), silu=f(16, 128))
    out.update(part=f(2, 4, 2, 8, 512), near_c=f(4, 2, 8, 512), near_z=f(4, 2, 8, 512), near_y=f(2, 8, 512))
    out.update(mods=f(2, 8, 512), vectors=f(16, 1024), up_bias=f(1, 4096), stats=f(8, 1024), columns=f(8, 1024))
    out.update(up_sums=f(2, 1, 1024), sums=f(2, 1, 768), half_mods=f(4, 2, 2, 8, 512), all_mods=f(4, 2, 2, 8, 512), tall=f(128, 512))
    out.update(bias_part=f(2, 4, 2, 2, 2, 128), bias_c=f(4, 2, 2, 2, 128), bias_z=f(4, 2, 2, 2, 128))
    out.update(bias_near=f(3, 2, 128), found=f(2, 4, 2, 1, 128), found_c=f(4, 2, 1, 128), found_z=f(4, 2, 1, 128))
    out.update(found_near=f(3, 4, 1, 128), picked=f(8, 128), picked_other=f(8, 128))
    out.update(gather_send=dma((4, 36)), gather_recv=dma((4, 36)), gather_local=dma((4, 6)))
    out.update(scatter_send=dma((4, 36)), scatter_recv=dma((4, 36)), pair_send=dma((4, 4)), pair_recv=dma((4, 4)))
    out.update(swap_send=dma((4, 2)), swap_recv=dma((4, 2)), swap_local=dma((4,)))
    out.update(small_send=dma((4, 8)), small_recv=dma((4, 8)), load_sem=dma((12,)), free=regular)
    return out


def pairs_kernel(*refs):
    names = INPUTS.split() + OUTPUTS.split() + list(scratch())
    r = dict(zip(names, refs))
    Block(r).run()

PLAN = dict(
    b0=(("q", "enter", ()), ("q", "pass_on", (2,)),),
    b1=(("q", "first"), ("p", "enter", ()), ("u", "enter", ()), ("d", "enter", ()),),
    b3=(("q", "pass_on", (1,)), ("q", "pass_on", (3,)), ("p", "pass_on", (2,)), ("p", "pass_on", (1,)), ("p", "pass_on", (3,)), ("u", "pass_on", (2,)), ("u", "pass_on", (1,)), ("u", "pass_on", (3,)), ("q", "turn", 0),),
    b4=(("q", "arrived", 2), ("q", "arrived", 1), ("q", "arrived", 3), ("d", "pass_on", (2,)), ("d", "pass_on", (1,)), ("d", "pass_on", (3,)),),
    b5=(("q", "turn", 2), ("swap_lat", "share"),),
    b6=(("q", "turn", 1),),
    b7=(("q", "turn", 3), ("p", "first"), ("p", "arrived", 2), ("p", "arrived", 1), ("p", "arrived", 3), ("u", "first"),),
    project0=(("swap_grad", "start"),),
    project7=(("p", "turn", 0), ("p", "turn", 2), ("p", "turn", 1), ("p", "turn", 3), ("p", "spread"), ("u", "arrived", 2), ("u", "arrived", 1), ("u", "arrived", 3),),
    heads0=(("u", "turn", 0),),
    heads3=(("u", "turn", 2), ("u", "spread"),),
    heads4=(("u", "turn", 1),),
    heads5=(("u", "turn", 3),),
    heads7=(("d", "first"),),
    out3=(("d", "arrived", 2), ("d", "arrived", 1), ("d", "arrived", 3), ("swap_grad", "share"),),
    enter3=(("d", "turn", 0),),
    ascend3=(("d", "turn", 2), ("d", "spread"),),
    ascend6=(("d", "turn", 1),),
    down0=(("d", "turn", 3),),
    hidden1=(("down", "turn", 2),),
    hidden7=(("down", "turn", 1),),
    back1=(("down", "turn", 3),),
    upper0=(("down", "turn", 0),),
    upper1=(("down", "fold_z"),),
    upper2=(("down", "leave", 2),),
    rest0=(("down", "leave", 1),),
    rest1=(("down", "fold_y"),),
    rest3=(("down", "leave", 3),),
    lift3=(("down", "leave", 0), ("", "signal_free"),),
    proj3=(("swap_block", "start"),),
    near0=(("up", "turn", 2),),
    near2=(("up", "turn", 1),),
    near5=(("up", "turn", 3),),
    first0=(("up", "turn", 0), ("up", "fold_z"),),
    first3=(("up", "leave", 2), ("down", "last"),),
    far0=(("up", "leave", 1),),
    far1=(("up", "fold_y"), ("up", "leave", 3),),
    far2=(("near_heads", "turn", 2), ("up", "leave", 0),),
    far4=(("near_heads", "turn", 1),),
    far6=(("near_heads", "turn", 3),),
    far7=(("near_heads", "turn", 0), ("near_heads", "fold_z"),),
    second1=(("near_heads", "leave", 2),),
    second3=(("near_heads", "leave", 1),),
    drop1=(("near_heads", "fold_y"), ("near_heads", "leave", 3),),
    drop3=(("near_heads", "leave", 0), ("down", "finish"),),
    last0=(("far_heads", "turn", 2),),
    last2=(("far_heads", "turn", 1),),
    e0=(("swap_input", "start"), ("up", "last"),),
    e2=(("far_heads", "turn", 3),),
    e4=(("far_heads", "turn", 0), ("far_heads", "fold_z"),),
    e6=(("far_heads", "leave", 2),),
    e7=(("up", "finish"), ("far_heads", "leave", 1), ("far_heads", "fold_y"), ("near_heads", "last"),),
    e8=(("far_heads", "leave", 3), ("far_heads", "leave", 0), ("far_heads", "last"),),
)


class Block:
    def __init__(self, r):
        for name, ref in r.items():
            setattr(self, name, ref)

    def run(self):
        self.set_up()
        self.begin()
        self.attend()
        self.mlp()
        self.attend_back()
        self.end()

    def set_up(self):
        gather = lambda i, name, own, full, lanes: Gather(
            own, full, lanes, ROWS[name], self.gather_send.at[i], self.gather_recv.at[i], self.gather_local.at[i]
        )
        self.q = gather(
            0,
            "q",
            lambda h: [
                (self.wq.at[j, :, block(2 * h + k, 128)], 256 + 384 * k + 128 * j, 128)
                for k in range(2)
                for j in range(3)
            ],
            self.buf_a,
            (256, 768),
        )
        self.p = gather(1, "p", lambda h: [(self.wp.at[:, block(h, 256)], 0, 256)], self.buf_a, (0, 256))
        self.u = gather(2, "u", lambda h: [(self.wu.at[:, block(h, 1024)], 0, 1024)], self.gu, (0, 1024))
        self.d = gather(3, "d", lambda h: [(self.wd.at[:, block(h, 1024)], 0, 1024)], self.buf_b, (0, 1024))
        heads = lambda k: lambda h: [
            (self.q_out.at[j, :, block(2 * h + k, 128)], 256 + 384 * k + 128 * j, 128) for j in range(3)
        ]
        outs = (
            lambda h: [(self.d_out.at[:, block(h, 1024)], 0, 1024)],
            lambda h: [(self.u_out.at[:, block(h, 1024)], 0, 1024)],
            lambda h: heads(0)(h) + [(self.p_out.at[:, block(h, 256)], 0, 256)],
            heads(1),
        )
        firsts = ((self.first_a0, self.first_b0), (self.first_a1, self.first_b1))
        rest = (
            (self.second0, self.third0, self.wide_z0, self.wide_y0, self.wide_x0),
            (self.second1, self.third1, self.wide_z1, self.wide_y1, self.wide_x1),
            (self.second2, self.third2, self.wide_z2, self.wide_y2, self.wide_x2),
        )
        plan = (
            (self.buf_d, firsts[0], rest[0], (0, 1024), ROWS["down"]),
            (self.buf_c, firsts[1], rest[1], (0, 1024), ROWS["up"]),
            (self.buf_d, firsts[0], rest[2], (0, 640), ROWS["near"]),
            (self.buf_d, firsts[0], rest[2], (640, 384), ROWS["far"]),
        )
        self.down, self.up, self.near_heads, self.far_heads = [
            Scatter(
                part, *first, *more, self.total, lanes, rows, outs[i], self.scatter_send.at[i], self.scatter_recv.at[i]
            )
            for i, (part, first, more, lanes, rows) in enumerate(plan)
        ]
        swaps = [(self.lat_own, self.lat), (self.grad_own, self.grad)]
        self.swap_lat, self.swap_grad = [
            Swap(own, full, self.swap_send.at[i], self.swap_recv.at[i], self.swap_local.at[i])
            for i, (own, full) in enumerate(swaps)
        ]
        backs = [(self.g_two, self.block_mine), (self.input_grad, self.input_mine)]
        self.swap_block, self.swap_input = [
            SwapBack(full, out, self.swap_send.at[2 + i, 0], self.swap_recv.at[2 + i, 0], self.swap_local.at[2 + i])
            for i, (full, out) in enumerate(backs)
        ]
        self.pairs = [
            Pair(self.mine, theirs, self.pair_send.at[i], self.pair_recv.at[i])
            for i, theirs in enumerate((self.theirs_a, self.theirs_b, self.theirs_a, self.theirs_b))
        ]

    def do(self, slot):
        for owner, act, *given in PLAN.get(slot, ()):
            getattr(getattr(self, owner) if owner else self, act)(*given)

    def loop(self, count, body, name):
        loop(count, body, {i: (lambda s=name + str(i): self.do(s)) for i in range(count) if name + str(i) in PLAN})

    def signal_free(self):
        z, y, c, x = place()
        for to in (at(z, 1 - y, c, x), at(z, y, c, 1 - x)):
            pl.semaphore_signal(self.free, inc=1, device_id=to, device_id_type=MESH)

    def load(self, i, source, target):
        return pltpu.make_async_copy(source, target, self.load_sem.at[i])

    def begin(self):
        z, y, c, x = place()
        q, p, u, d = self.q, self.p, self.u, self.d
        send, recv = self.small_send, self.small_recv
        little = SmallGather(self.small, self.small_full, send.at[0], recv.at[0])
        v = self.cond[...].astype(F32)
        silu = (v / (1.0 + jnp.exp(-v))).astype(BF).astype(F32)
        self.small[...] = jnp.zeros_like(self.small)
        for k in range(8):
            self.small[k : k + 1, :] = silu[:, k * 128 : (k + 1) * 128]
        for k, bias in enumerate((self.q_bias, self.v_bias, self.p_bias, self.d_bias)):
            self.small[8:9, k * 32 : (k + 1) * 32] = bias[...].astype(F32)
        self.small[9:10, :] = self.u_bias[...].astype(F32)
        a_bias = self.a_bias[...].astype(F32)
        for j in range(6):
            self.small[10 + j // 4 : 11 + j // 4, j % 4 * 32 : j % 4 * 32 + 32] = a_bias[j : j + 1, :]
        greet(partners())
        little.start()
        q.start_core()
        for group in (p, u, d):
            group.start_core()
        self.swap_lat.start()
        self.wide[...] = jnp.zeros_like(self.wide)
        ada = [self.load(j, self.ada.at[j], self.wide.at[block(c, 64), pl.ds(j * 512, 512)]) for j in range(6)]
        for copy in ada:
            copy.start()
        little.step((0,), (1, 2, 3))
        self.do("b0")
        self.part[...] = jnp.zeros_like(self.part)
        little.step((1, 2, 3), (4,))
        self.do("b1")
        for copy in ada:
            copy.wait()
        little.step((4,), (5,))
        self.do("b2")
        row = z * 2 + y
        lhs = [self.small_full[x, b // 4, b // 2 % 2, b % 2, pl.ds(row, 1), :] for b in range(16)]
        lhs = jnp.concatenate(lhs, 0)
        self.silu[...] = lhs
        for j in range(6):
            product = nn(lhs.astype(BF), self.wide[:, j * 512 : (j + 1) * 512])
            for b in range(16):
                self.part[b % 2, b // 4, b // 2 % 2, j : j + 1, :] = product[b : b + 1, :]
        near_c, near_y, near_z = self.near_c, self.near_y, self.near_z
        first = remote(self.part.at[1 - c], near_c, send.at[1, 0], recv.at[1, 0], at(z, y, 1 - c, x))
        first.start()
        first.wait()
        near_c[...] = near_c[...] + self.part[c]
        seconds = []
        for s in (1, 2, 3):
            to = lax.rem(z + s, 4)
            seconds.append(remote(near_c.at[to], near_z.at[s - 1], send.at[1, s], recv.at[1, s], at(to, y, c, x)))
            seconds[-1].start()
        self.do("b3")
        for copy in seconds:
            copy.wait()
        near_z[3] = near_c[z] + near_z[0] + near_z[1] + near_z[2]
        self._partials(lambda copy: copy.start())
        self.do("b4")
        self._partials(lambda copy: copy.wait())
        self.mods[c] = near_y[0] + near_y[1]
        fifth = remote(self.mods.at[c], self.mods.at[c], send.at[1, 6], recv.at[1, 6], at(z, y, 1 - c, x))
        fifth.start()
        self.do("b5")
        little.step((5,), ())
        bias = [widen(self.small_full, 8, k) for k in range(4)]
        ada_bias = [widen(self.small_full, 10 + j // 4, j % 4) for j in range(6)]
        for k, (zz, yy, cc, xx) in enumerate(devices()):
            self.up_bias[:, k * 128 : (k + 1) * 128] = self.small_full[xx, zz, yy, cc, 9:10, :]
        self.do("b6")
        fifth.wait()
        for j in range(6):
            for h in range(2):
                lanes = slice(h * 512, (h + 1) * 512)
                self.vectors[j : j + 1, lanes] = self.mods[h, j : j + 1, :] + ada_bias[j][:, lanes]
        for k in range(4):
            self.vectors[6 + k : 7 + k, :] = bias[k]
        self.do("b7")
        self.swap_lat.finish()

    def _partials(self, act):
        z, y, c, x = place()
        for k, to_y in enumerate((y, 1 - y)):
            sems = self.small_send.at[1, 4 + k], self.small_recv.at[1, 4 + k]
            source, target = self.near_z.at[3, to_y], self.near_y.at[y]

            @pl.when(c != x)
            def _():
                act(remote(source, target, *sems, at(z, to_y, 1 - c, 1 - x)))

            @pl.when(c == x)
            def _():
                if k:
                    act(remote(source, target, *sems, at(z, to_y, c, x)))
                else:
                    act(pltpu.make_async_copy(source, target, self.load_sem.at[6]))

    def attend(self):
        z, y, c, x = place()
        q, p, u, d, vectors = self.q, self.p, self.u, self.d, self.vectors

        def modulated(i):
            rows = block(i, 256)
            normal, _ = normalise(self.lat[rows, :].astype(F32))
            self.attn_in[rows, :] = (normal * (1.0 + vectors[1:2, :]) + vectors[0:1, :]).astype(BF)

        self.loop(4, modulated, "normal")
        q.finish()

        def project(i):
            b, quarter = i // 4, lax.rem(i, 4)
            values = nn(self.attn_in[block(quarter, 256), :], flat(self.buf_a[b, :, :, :, 256:1024]))
            for k in range(6):
                value = values[:, k * 128 : (k + 1) * 128]
                if k % 3 != 1:
                    columns = pl.ds(pl.multiple_of(b * 512 + c * 256 + k // 3 * 128, 128), 128)
                    row = 6 if k % 3 == 0 else 7
                    value = value + vectors[row : row + 1, columns]
                self.buf_d[b, quarter, :, :, 256 + k * 128 : 384 + k * 128] = value.astype(BF).reshape(2, 128, 128)

        self.loop(8, project, "project")
        lane = lax.broadcasted_iota(jnp.int32, (1, 128), 1)
        self.lse[...] = jnp.zeros_like(self.lse)

        def attend(i):
            pair, half = i // 2, lax.rem(i, 2)
            rows, zz = block(half, 512), pl.ds(half * 2, 2)
            b, k, q_at = lax.rem(pair, 2), pair // 2, pl.multiple_of(256 + pair // 2 * 384, 128)
            queries = flat(self.buf_d[b, zz, :, :, pl.ds(q_at, 128)]) * BF(0.125)
            keys = flat(self.buf_d[b, :, :, :, pl.ds(q_at + 128, 128)])
            values = flat(self.buf_d[b, :, :, :, pl.ds(q_at + 256, 128)])
            result = None
            logs = self.lse[rows, :]
            for h in range(2):
                scores = nt(jnp.where(in_half(h), queries, jnp.zeros_like(queries)), keys)
                largest = jnp.max(scores, -1, keepdims=True)
                exponent = jnp.exp(scores - largest)
                summed = jnp.sum(exponent, -1, keepdims=True)
                mixture = nn(exponent.astype(BF), values) * (1.0 / summed)
                result = mixture if h == 0 else jnp.where(in_half(0), result, mixture)
                logs = jnp.where(lane == pair * 2 + h, largest + jnp.log(summed), logs)
            self.buf_d[b, zz, :, :, block(k, 128)] = result.astype(BF).reshape(2, 2, 128, 128)
            self.lse[rows, :] = logs

        self.loop(8, attend, "heads")
        p.finish()
        self.load(0, self.buf_a, self.held_a).start()
        pair = self.pairs[0]

        def out(i):
            zz = i
            partial = nt(flat(self.buf_d[0, zz, :, :, 0:256]), flat(self.buf_a[0, :, :, :, 0:256]))
            partial += nt(flat(self.buf_d[1, zz, :, :, 0:256]), flat(self.buf_a[1, :, :, :, 0:256]))
            pair.give(i, partial)

        self.loop(4, out, "out")
        self.load(1, self.buf_d, self.held_b).start()

        def residual(i):
            rows = block(i, 256)
            branch = pair.take(i) + vectors[8:9, :]
            self.branch_one[rows, :] = branch.astype(BF)
            self.mid[rows, :] = self.lat[rows, :].astype(F32) + vectors[2:3, :] * branch

        self.loop(4, residual, "middle")

    def mlp(self):
        z, y, c, x = place()
        u, d, vectors, stats, down, up = self.u, self.d, self.vectors, self.stats, self.down, self.up
        active, up_grad, slope, hidden_grad = self.buf_c, self.buf_c, self.buf_a, self.buf_a
        wd, gu, mid, mlp_in, g_two, grad = self.buf_b, self.gu, self.mid, self.mlp_in, self.g_two, self.grad
        self.swap_grad.finish()
        stats[...] = jnp.zeros_like(stats)
        self.up_sums[...] = jnp.zeros_like(self.up_sums)

        def enter(i):
            rows = block(i, 256)
            normal, _ = normalise(mid[rows, :])
            mlp_in[rows, :] = (normal * (1.0 + vectors[4:5, :]) + vectors[3:4, :]).astype(BF)
            g = (grad[rows, :].astype(F32) * vectors[5:6, :]).astype(BF)
            g_two[rows, :] = g
            mine_too = jnp.where(i // 2 == c, 1.0, 0.0)
            stats[1:2, :] += column_sum(g.astype(F32)) * mine_too

        self.loop(4, enter, "enter")
        u.finish()
        self.load(0, self.buf_a, self.held_a).wait()

        def ascend(i):
            b, quarter = i // 4, lax.rem(i, 4)
            columns = pl.ds(pl.multiple_of(b * 2048 + c * 1024, 1024), 1024)
            hidden = nn(mlp_in[block(quarter, 256), :], flat(gu[b])) + self.up_bias[:, columns]
            value, gradient = gelu_parts(hidden)
            active[b, quarter] = value.astype(BF).reshape(2, 128, 1024)
            slope[b, quarter] = gradient.astype(BF).reshape(2, 128, 1024)

        self.loop(8, ascend, "ascend")
        self.load(1, self.buf_d, self.held_b).wait()

        def down_gradient(i):
            b, half = i // 2, lax.rem(i, 2)
            value = tn(g_two[:, block(half, 512)], flat(active[b]))
            self.buf_d[b, pl.ds(half * 2, 2)] = value.astype(BF).reshape(2, 2, 128, 1024)

        self.loop(4, down_gradient, "down")
        down.start()
        d.finish()
        pair, back = self.pairs[1], self.pairs[2]

        def descend(i):
            pair.give(i, nt(flat(active[0, i]), flat(wd[0])) + nt(flat(active[1, i]), flat(wd[1])))

        self.loop(4, descend, "descend")

        def hidden_gradient(i):
            b, quarter = i // 4, lax.rem(i, 4)
            value = nn(g_two[block(quarter, 256), :], flat(wd[b])) * flat(slope[b, quarter]).astype(F32)
            value = value.astype(BF)
            hidden_grad[b, quarter] = value.reshape(2, 128, 1024)
            self.up_sums[b] += column_sum(value.astype(F32))

        self.loop(8, hidden_gradient, "hidden")
        self.load(3, self.held_b, self.buf_b).start()

        def leave(i):
            rows = block(i, 256)
            branch_two = pair.take(i) + vectors[9:10, :]
            g_two[rows, :] = (mid[rows, :] + vectors[5:6, :] * branch_two).astype(BF)
            stats[0:1, :] += column_sum(grad[rows, :].astype(F32) * branch_two)

        self.loop(4, leave, "leave")

        def descend_back(i):
            back.give(i, nt(flat(hidden_grad[0, i]), flat(gu[0])) + nt(flat(hidden_grad[1, i]), flat(gu[1])))

        self.loop(4, descend_back, "back")

        def up_gradient(i):
            b, half = i // 2, lax.rem(i, 2)
            value = tn(mlp_in[:, block(half, 512)], flat(hidden_grad[b]))
            up_grad[b, pl.ds(half * 2, 2)] = value.astype(BF).reshape(2, 2, 128, 1024)

        self.loop(4, up_gradient, "upper")
        self.load(4, self.held_a, self.buf_a).start()
        up.start()

        def residual(i):
            rows = block(i, 256)
            dy = back.take(i)
            normal, scale = normalise(mid[rows, :])
            stats[2:3, :] += column_sum(dy)
            stats[3:4, :] += column_sum(dy * normal)
            dn = dy * (1.0 + vectors[4:5, :])
            dn = dn - jnp.mean(dn, -1, keepdims=True) - normal * jnp.mean(dn * normal, -1, keepdims=True)
            total = grad[rows, :].astype(F32) + scale * dn
            mid[rows, :] = total
            stats[4:5, :] += column_sum(total * self.branch_one[rows, :].astype(F32))
            g = (total * vectors[2:3, :]).astype(BF)
            mlp_in[rows, :] = g
            mine_too = jnp.where(i // 2 == c, 1.0, 0.0)
            stats[5:6, :] += column_sum(g.astype(F32)) * mine_too

        self.loop(4, residual, "rest")

    def attend_back(self):
        z, y, c, x = place()
        vectors, stats, down, up = self.vectors, self.stats, self.down, self.up
        near, far = self.near_heads, self.far_heads
        acts, g_one, heads_grad, sums = self.buf_b, self.mlp_in, self.heads_grad, self.sums
        weights = self.buf_a
        sums[...] = jnp.zeros_like(sums)
        self.load(3, self.held_b, self.buf_b).wait()
        self.load(4, self.held_a, self.buf_a).wait()

        def enter(i):
            b, half = i // 2, lax.rem(i, 2)
            value = nn(g_one[block(half, 512), :], flat(weights[b, :, :, :, 0:256]))
            heads_grad[b, block(half, 512), :] = value.astype(BF)

        self.loop(4, enter, "lift")

        def proj_gradient(i):
            b, half = i // 2, lax.rem(i, 2)
            value = tn(g_one[:, block(half, 512)], flat(acts[b, :, :, :, 0:256]))
            self.buf_d[b, pl.ds(half * 2, 2), :, :, 0:256] = value.astype(BF).reshape(2, 2, 128, 256)

        self.loop(4, proj_gradient, "proj")
        lane = lax.broadcasted_iota(jnp.int32, (1, 128), 1)

        def attend(i, k):
            b, quarter = i // 4, lax.rem(i, 4)
            rows, at_lane = block(quarter, 256), 256 + 384 * k
            queries = flat(acts[b, quarter, :, :, at_lane : at_lane + 128]) * BF(0.125)
            keys = flat(acts[b, :, :, :, at_lane + 128 : at_lane + 256])
            values = flat(acts[b, :, :, :, at_lane + 256 : at_lane + 384])
            grads = heads_grad[b, rows, k * 128 : (k + 1) * 128]

            @pl.when(quarter == 0)
            def _():
                self.key_total[...] = jnp.zeros_like(self.key_total)
                self.value_total[...] = jnp.zeros_like(self.value_total)

            result = None
            logs = self.lse[rows, :]
            for h in range(2):
                log = jnp.sum(jnp.where(lane == (k * 2 + b) * 2 + h, logs, 0.0), -1, keepdims=True)
                query = jnp.where(in_half(h), queries, jnp.zeros_like(queries))
                grad = jnp.where(in_half(h), grads, jnp.zeros_like(grads))
                probs = jnp.exp(nt(query, keys) - log)
                probs_grad = nt(grad, values)
                inner = jnp.sum(probs * probs_grad, -1, keepdims=True)
                score_grad = (probs * (probs_grad - inner)).astype(BF)
                query_grad = nn(score_grad, keys)
                result = query_grad if h == 0 else jnp.where(in_half(0), result, query_grad)
                self.key_total[...] += tn(score_grad, query)
                self.value_total[...] += tn(probs.astype(BF), grad)
            result = (result * 0.125).astype(BF)
            acts[b, quarter, :, :, at_lane : at_lane + 128] = result.reshape(2, 128, 128)
            sums[b, :, k * 128 : (k + 1) * 128] += column_sum(result.astype(F32))

            @pl.when(quarter == 3)
            def _():
                total = self.key_total[...].astype(BF)
                acts[b, :, :, :, at_lane + 128 : at_lane + 256] = total.reshape(4, 2, 128, 128)
                total = self.value_total[...].astype(BF)
                acts[b, :, :, :, at_lane + 256 : at_lane + 384] = total.reshape(4, 2, 128, 128)
                sums[b, :, 512 + k * 128 : 640 + k * 128] = column_sum(total.astype(F32))

        def qkv_gradient(i, k):
            b, half = i // 2, lax.rem(i, 2)
            lanes = slice(256 + 384 * k, 640 + 384 * k)
            value = tn(self.attn_in[:, block(half, 512)], flat(acts[b, :, :, :, lanes]))
            self.buf_d[b, pl.ds(half * 2, 2), :, :, lanes] = value.astype(BF).reshape(2, 2, 128, 384)

        self.loop(8, lambda i: attend(i, 0), "near")
        self.loop(4, lambda i: qkv_gradient(i, 0), "first")
        pl.semaphore_wait(self.free, 2)
        near.start()
        self.loop(8, lambda i: attend(i, 1), "far")
        self.loop(4, lambda i: qkv_gradient(i, 1), "second")
        far.start()
        self.do("s0")
        pair = self.pairs[3]

        def descend(i):
            partial = nt(flat(acts[0, i, :, :, 256:1024]), flat(weights[0, :, :, :, 256:1024]))
            pair.give(i, partial + nt(flat(acts[1, i, :, :, 256:1024]), flat(weights[1, :, :, :, 256:1024])))

        self.loop(4, descend, "drop")

        def leave(i):
            rows = block(i, 256)
            dy = pair.take(i)
            normal, scale = normalise(self.lat[rows, :].astype(F32))
            stats[6:7, :] += column_sum(dy)
            stats[7:8, :] += column_sum(dy * normal)
            dn = dy * (1.0 + vectors[1:2, :])
            dn = dn - jnp.mean(dn, -1, keepdims=True) - normal * jnp.mean(dn * normal, -1, keepdims=True)
            total = self.mid[rows, :] + scale * dn

            @pl.when(i // 2 == c)
            def _():
                for half in range(2):
                    for k in range(8):
                        part = total[half * 128 : (half + 1) * 128, k * 128 : (k + 1) * 128]
                        self.key_total[pl.ds(k, 128, stride=8), :] = part
                    values = self.key_total[...].astype(BF).reshape(64, 16, 128)
                    self.input_grad[block(lax.rem(i, 2) * 2 + half, 64)] = values

        self.loop(4, leave, "last")
        self.begin_end()

    def begin_end(self):
        z, y, c, x = place()
        stats, sums, up_sums = self.stats, self.sums, self.up_sums
        rows = [stats[k : k + 1, :] for k in (6, 7, 4, 2, 3, 0)]
        for j in range(6):
            for h in range(2):
                self.mods[h, j : j + 1, :] = rows[j][:, h * 512 : (h + 1) * 512]
        self.half_mods[z, y, x] = self.mods[c]
        for d in (1, 2, 3):
            self._mods(d).start()
        self.do("e0")
        columns, bias_part = self.columns, self.bias_part
        columns[...] = jnp.zeros_like(columns)
        bias_part[...] = jnp.zeros_like(bias_part)
        for b in range(2):
            spot = pl.ds(pl.multiple_of(b * 512 + c * 256, 256), 256)
            columns[0:1, spot] = sums[b, :, 0:256]
            columns[1:2, spot] = sums[b, :, 512:768]
        columns[2:3, :] = stats[5:6, :]
        columns[3:4, :] = stats[1:2, :]
        pieces = narrow(columns[0:1, :], 0) + narrow(columns[1:2, :], 1)
        pieces = pieces + narrow(columns[2:3, :], 2) + narrow(columns[3:4, :], 3)
        for k, (zz, yy, cc, xx) in enumerate(devices()):
            bias_part[cc, zz, xx, yy, 0:1, :] = pieces[k : k + 1, :]
        for b in range(2):
            for i in range(8):
                bias_part[i // 2 % 2, b * 2 + c, i % 2, i // 4, 1:2, :] = up_sums[b, :, i * 128 : (i + 1) * 128]
        self.bias = SmallScatter(
            bias_part, self.bias_c, self.bias_z, self.bias_near, self.small_send.at[0], self.small_recv.at[3]
        )
        self.bias.start()
        self.do("e1")
        for d in (1, 2, 3):
            self._mods(d).wait()
        self._across(lambda copy: copy.start())
        self.bias.along()
        self.do("e2")

    def _mods(self, d):
        z, y, c, x = place()
        spot = self.half_mods.at[z, y, x]
        return remote(
            spot, spot, self.small_send.at[2, d], self.small_recv.at[2, d], at(lax.rem(z + d, 4), y, c, x)
        )

    def _across(self, act):
        z, y, c, x = place()
        spot = self.half_mods.at[:, y, x]
        copy = lambda k, to: remote(spot, spot, self.small_send.at[2, k], self.small_recv.at[2, k], to)

        @pl.when(c == x)
        def _():
            act(copy(4, at(z, 1 - y, c, x)))

        @pl.when(c != x)
        def _():
            act(copy(5, at(z, y, c, 1 - x)))
            act(copy(6, at(z, 1 - y, c, 1 - x)))

    def end(self):
        z, y, c, x = place()
        up, near, far, mods, bias = self.up, self.near_heads, self.far_heads, self.all_mods, self.bias
        send, recv = self.small_send, self.small_recv
        spot = self.half_mods.at[:, y, x]

        @pl.when(c == x)
        def _():
            remote(spot, spot, send.at[2, 4], recv.at[2, 4], at(z, 1 - y, c, x)).wait()
            remote(spot, spot, send.at[2, 5], recv.at[2, 5], at(z, y, c, 1 - x)).wait_recv()
            remote(spot, spot, send.at[2, 6], recv.at[2, 6], at(z, 1 - y, c, 1 - x)).wait_recv()
            share = remote(self.half_mods, mods, send.at[2, 7], recv.at[2, 7], at(z, y, 1 - c, x))
            share.start()
            keep = self.load(5, self.half_mods, mods)
            keep.start()
            keep.wait()
            share.wait_send()

        @pl.when(c != x)
        def _():
            remote(spot, spot, send.at[2, 5], recv.at[2, 5], at(z, y, c, 1 - x)).wait_send()
            remote(spot, spot, send.at[2, 6], recv.at[2, 6], at(z, 1 - y, c, 1 - x)).wait_send()
            remote(self.half_mods, mods, send.at[2, 7], recv.at[2, 7], at(z, y, 1 - c, x)).wait_recv()

        bias.across()
        self.do("e3")
        silu_rows = self.silu[...].astype(BF)
        total = jnp.zeros((16, 128), F32)
        bias_rows = []
        for j in range(6):
            values = jnp.concatenate([mods[b // 4, b // 2 % 2, b % 2, j : j + 1, :] for b in range(16)], 0)
            high, low = split_bf(values)
            weights = self.wide[:, j * 512 : (j + 1) * 512]
            self.tall[...] = tn(silu_rows, high) + tn(silu_rows, low)
            self.ada_out[j] = self.tall[block(c, 64), :]
            total = total + nt(high, weights) + nt(low, weights)
            bias_rows.append(column_sum(values))
        found, found_c, found_z, found_near = self.found, self.found_c, self.found_z, self.found_near
        for b in range(16):
            found[b % 2, b // 4, b // 2 % 2] = total[b : b + 1, :]
        core = remote(found.at[1 - c], found_c, send.at[3, 0], recv.at[1, 0], at(z, y, 1 - c, x))
        core.start()
        self.do("e4")
        group = (lax.rem(z, 2) * 2 + y) * 2 + c
        source = lax.broadcasted_iota(jnp.int32, (512, 128), 0)
        target = lax.broadcasted_iota(jnp.int32, (512, 128), 1)
        chosen = jnp.where((source == group * 64 + target) & (target < 64), 1.0, 0.0).astype(BF)
        self.picked[...] = exact_nn(jnp.concatenate(bias_rows + [jnp.zeros((2, 512), F32)], 0), chosen)
        swap = remote(self.picked, self.picked_other, send.at[3, 7], recv.at[1, 7], at(z, y, c, 1 - x))
        swap.start()
        self.do("e5")
        core.wait()
        found_c[...] = found_c[...] + found[c]
        along = []
        for k in (1, 2, 3):
            to = lax.rem(z + k, 4)
            along.append(remote(found_c.at[to], found_z.at[z], send.at[3, k], recv.at[1, k], at(to, y, c, x)))
            along[-1].start()
        found_z[z] = found_c[z]
        self.do("e6")
        for copy in along:
            copy.wait()
        across = []
        for k, (to_y, to_x) in enumerate(((y, 1 - x), (1 - y, x), (1 - y, 1 - x))):
            across.append(
                remote(found_z.at[:, to_y], found_near.at[k], send.at[3, 4 + k], recv.at[1, 4 + k], at(z, to_y, c, to_x))
            )
            across[-1].start()
        self.do("e7")
        for copy in across:
            copy.wait()
        swap.wait()
        self.small_out[...] = jnp.zeros_like(self.small_out)
        self.small_out[4:6, :] = bias.finish()
        picked = jnp.where(z // 2 == x, self.picked[...], self.picked_other[...])
        self.small_out[8:16, 0:32] = jnp.where(x == 0, picked[:, 0:32], picked[:, 32:64])
        same, other = found_z[:, y] + found_near[0], found_near[1] + found_near[2]
        rows = [jnp.where(y == b % 2, same[b // 2], other[b // 2]) for b in range(8)]
        v = self.cond[...].astype(F32)
        v = jnp.concatenate([v[:, k * 128 : (k + 1) * 128] for k in range(8)], 0)
        gate = 1.0 / (1.0 + jnp.exp(-v))
        row = jnp.concatenate(rows, 0) * gate * (1.0 + v * (1.0 - gate))
        self.small_out[0:4, :] = jnp.where(x == 0, row[0:4], row[4:8])
        self.do("e8")
        near.finish()
        self.swap_block.finish()
        self.swap_input.finish()
        far.finish()


def on_device_pairs(
    latents_in,
    condition,
    grad_out,
    qkv_weight,
    proj_weight,
    up_weight,
    down_weight,
    ada_weight,
    query_bias,
    value_bias,
    proj_bias,
    up_bias,
    down_bias,
    ada_bias,
):
    small = [b.reshape(1, -1) for b in (query_bias, value_bias, proj_bias, down_bias, up_bias)]
    out = lambda *shape: jax.ShapeDtypeStruct(shape, F32)
    group = jax.ShapeDtypeStruct(GROUP, BF)
    rows = jax.ShapeDtypeStruct((512, 1024), BF)
    results = pl.pallas_call(
        pairs_kernel,
        out_shape=[rows, jax.ShapeDtypeStruct((256, 16, 128), BF), out(3, 64, 512), out(64, 512), out(64, 2048), out(64, 2048)]
        + [group] * 2
        + [out(6, 64, 512), out(16, 128)],
        in_specs=[IN_ANY] * 7 + [IN_VMEM] * 7,
        out_specs=[IN_ANY] * 8 + [IN_VMEM] * 2,
        scratch_shapes=list(scratch().values()),
        compiler_params=pltpu.CompilerParams(
            collective_id=0, has_side_effects=True, vmem_limit_bytes=63 * MIB + MIB // 2
        ),
        name="dit_block",
    )(
        latents_in.reshape(512, 1024), grad_out.reshape(512, 1024), qkv_weight.transpose(1, 0, 2), proj_weight.T,
        up_weight, down_weight.T, ada_weight.transpose(1, 0, 2), condition, *small, ada_bias,
    )
    block_mine, input_mine, q_out, p_out, u_out, d_out, _, _, ada_out, small_out = results
    return (
        block_mine.reshape(512, 1, 1024),
        input_mine.astype(F32).reshape(512, 1, 1024),
        small_out[0:4].reshape(1, 512),
        q_out.transpose(1, 0, 2),
        p_out.T,
        u_out,
        d_out.T,
        ada_out.transpose(1, 0, 2),
        small_out[4, 0:32],
        small_out[4, 32:64],
        small_out[4, 64:96],
        small_out[5],
        small_out[4, 96:128],
        small_out[8:14, 0:32],
    )


def solution(mesh):
    shape = dict(mesh.shape)
    pairs = shape["fsdp"] == 16 and shape["tp"] == 2
    return jax.shard_map(
        on_device_pairs if pairs else on_device_general,
        mesh=mesh,
        in_specs=(
            P("tp", "fsdp", None),
            P("fsdp", None),
            P("tp", "fsdp", None),
            P("fsdp", None, "tp"),
            P("tp", "fsdp"),
            P("fsdp", "tp"),
            P("tp", "fsdp"),
            P("fsdp", None, "tp"),
            P(("fsdp", "tp")),
            P(("fsdp", "tp")),
            P(("fsdp", "tp")),
            P(("fsdp", "tp")),
            P(("fsdp", "tp")),
            P(None, ("fsdp", "tp")),
        ),
        out_specs=(
            P("tp", "fsdp", None),
            P("tp", "fsdp", None),
            P("fsdp", "tp"),
            P("fsdp", None, "tp"),
            P("tp", "fsdp"),
            P("fsdp", "tp"),
            P("tp", "fsdp"),
            P("fsdp", None, "tp"),
            P(("fsdp", "tp")),
            P(("fsdp", "tp")),
            P(("fsdp", "tp")),
            P(("fsdp", "tp")),
            P(("fsdp", "tp")),
            P(None, ("fsdp", "tp")),
        ),
        check_vma=False,
    )
```
